32 devices in a mesh: groups: 2 (over x), blk: 4 (over y, core), sub: 4 (over z).
Axes of the slice: x: 2, y: 2, z: 4, core: 2. Of those that a mesh axis runs over, the one named last changes fastest.
Arguments:
- teacher: bfloat16 [4096, 1024], P(('groups', 'blk', 'sub')), parts along dimension 0, may hold values from -8 to 8
- student: bfloat16 [4096, 384], P(('groups', 'blk', 'sub')), parts along dimension 0, may hold values from -0.25 to 0.25
Outputs:
- student_grad: float32 [4096, 384], P(('groups', 'blk', 'sub')), parts along dimension 0
- distill_loss: float32 [2], P('groups'), parts along dimension 0
The draws below stay inside these ranges and needn't reach their ends.
There are 2 independent parts, one for each index of `groups`. The reference program is written for one: setup_inputs(seed, part) draws one part's arguments, and reference() takes and returns one part's arrays. A program takes and returns all parts, laid end to end along the dimension named above; each array names one. Nothing has to cross between parts.
All inputs are finite; a program needn't handle non-finite values.
Results may differ from the reference program's by a relative error of at most 0.00085.
Values may be sent and summed in bfloat16 or wider, within the bound.
No kernel may reach another device: no remote copies, remote signals or barrier semaphores. Data moves between devices by JAX's collectives and lax.ppermute only.
A program may use at most 64 MiB of HBM per device.

```python
import math
import jax
import jax.numpy as jnp
from jax import lax

TEACHER_D = 1024
STUDENT_D = 384
TOKENS = 2048


def common_rows(key, ramp_top):
    scale_key = jax.random.fold_in(key, 0)
    entry_key = jax.random.fold_in(key, 1)
    col_key = jax.random.fold_in(key, 3)
    row_scale = jnp.exp(jax.random.uniform(scale_key, (TOKENS,), jnp.float32, math.log(0.3), math.log(3.0)))
    ramp = 1.0 + (ramp_top - 1.0) * jnp.arange(TOKENS, dtype=jnp.float32) / max(TOKENS - 1, 1)
    row_scale = row_scale * ramp
    col_scale = jnp.exp(jax.random.uniform(col_key, (TEACHER_D,), jnp.float32, math.log(0.9), math.log(1.1)))
    bell = jnp.clip(jax.random.normal(entry_key, (TOKENS, TEACHER_D), jnp.float32), -5.0, 5.0)
    entries = bell
    values = entries * col_scale[None, :] * row_scale[:, None]
    return (values, row_scale)


def draw_teacher(key, part):
    values, row_scale = common_rows(key, 3.0)
    values = jnp.clip(values / math.sqrt(TEACHER_D), -8.0, 8.0)
    return values.astype(jnp.bfloat16)


def draw_student(key, part):
    values, row_scale = common_rows(key, 3.0)
    key = jax.random.fold_in(key, 23)
    column_key, level_key, noise_key = jax.random.split(key, 3)
    columns = jax.random.permutation(column_key, TEACHER_D)[:STUDENT_D]
    noise_level = jnp.exp(jax.random.uniform(level_key, (TOKENS,), jnp.float32, math.log(0.15), math.log(0.45)))
    noise = jnp.clip(jax.random.normal(noise_key, (TOKENS, STUDENT_D), jnp.float32), -5.0, 5.0)
    picked = values[:, columns]
    mixed = picked + (noise_level * row_scale)[:, None] * noise
    mixed = jnp.clip(mixed * (0.008 / math.sqrt(STUDENT_D)), -0.25, 0.25)
    return mixed.astype(jnp.bfloat16)


def setup_inputs(seed: int = 0, part: int = 0) -> dict:
    seeds = jax.random.split(jax.random.key(seed), 3)
    part_splits = jax.random.split(jax.random.fold_in(seeds[2], part), 3)
    teacher = draw_teacher(jax.random.fold_in(jax.random.fold_in(seeds[2], part), 71), part)
    student = draw_student(jax.random.fold_in(jax.random.fold_in(seeds[2], part), 71), part)
    return dict(teacher=teacher, student=student)


FLOOR = 0.01
EPSILON = 1e-06

def moments(values):
    as_float = values.astype(jnp.float32)
    norms = lax.optimization_barrier(jnp.sum(as_float * as_float, axis=1))
    centre = lax.optimization_barrier(jnp.mean(as_float, axis=0))
    spread = 2.0 * (jnp.sum(norms) / TOKENS - jnp.sum(centre * centre)) + EPSILON
    return (norms, centre, spread)

def reference(teacher, student):
    norms_teacher, centre_teacher, spread_teacher = moments(teacher)
    norms_student, centre_student, spread_student = moments(student)
    block_rows = min(512, TOKENS)
    count_blocks = TOKENS // block_rows
    all_index = jnp.arange(TOKENS, dtype=jnp.int32)

    def one_block(number):
        start = (number * block_rows).astype(jnp.int32)
        part_teacher = lax.dynamic_slice_in_dim(teacher, start, block_rows, 0)
        part_student = lax.dynamic_slice_in_dim(student, start, block_rows, 0)
        here_teacher = lax.dynamic_slice_in_dim(norms_teacher, start, block_rows, 0)
        here_student = lax.dynamic_slice_in_dim(norms_student, start, block_rows, 0)
        gram_teacher = jnp.dot(part_teacher, teacher.T, preferred_element_type=jnp.float32)
        gram_student = jnp.dot(part_student, student.T, preferred_element_type=jnp.float32)
        square_teacher = jnp.maximum(here_teacher[:, None] + norms_teacher[None, :] - 2.0 * gram_teacher, 0.0)
        square_student = jnp.maximum(here_student[:, None] + norms_student[None, :] - 2.0 * gram_student, 0.0)
        scaled_teacher = jnp.sqrt(square_teacher / spread_teacher + FLOOR)
        scaled_student = jnp.sqrt(square_student / spread_student + FLOOR)
        residue = scaled_student - scaled_teacher
        magnitude = jnp.abs(residue)
        huber_value = jnp.where(magnitude < 1.0, 0.5 * residue * residue, magnitude - 0.5)
        slope = jnp.clip(residue, -1.0, 1.0)
        row_index = start + jnp.arange(block_rows, dtype=jnp.int32)
        pair_mask = (row_index[:, None] != all_index[None, :]).astype(jnp.float32)
        loss_part = jnp.sum(huber_value * pair_mask)
        spread_part = -jnp.sum(slope * square_student / scaled_student * pair_mask)
        weights = (slope / (spread_student * scaled_student) * pair_mask).astype(jnp.bfloat16)
        row_weight = lax.optimization_barrier(jnp.sum(weights.astype(jnp.float32), axis=1))
        gradient = part_student.astype(jnp.float32) * row_weight[:, None] - jnp.dot(weights, student, preferred_element_type=jnp.float32)
        return (loss_part, spread_part, gradient)
    losses, spreads, gradients = lax.map(one_block, jnp.arange(count_blocks, dtype=jnp.int32))
    pair_count = float(TOKENS) * float(TOKENS - 1)
    direct = gradients.reshape(TOKENS, STUDENT_D)
    spread_total = jnp.sum(spreads)
    correction = 2.0 * spread_total / (pair_count * spread_student * spread_student)
    student_grad = 2.0 / float(TOKENS - 1) * direct + correction * (student.astype(jnp.float32) - centre_student[None, :])
    distill_loss = (jnp.sum(losses) / pair_count).reshape(1)
    return (student_grad, distill_loss)
```

```python
import functools

import jax
import jax.numpy as jnp
from jax import lax
from jax.experimental import pallas as pl
from jax.experimental.pallas import tpu as pltpu
from jax.sharding import PartitionSpec as P

FLOOR = 0.01
EPSILON = 1e-06
LANES = 128
WHOLE = pl.BlockSpec(memory_space=pltpu.VMEM)


def exchange(value, axis, distance):
    size = lax.axis_size(axis)
    return lax.ppermute(value, axis, [(i, i ^ distance) for i in range(size)])


def shifted(value, axis, distance):
    size = lax.axis_size(axis)
    return lax.ppermute(value, axis, [(i, (i + distance) % size) for i in range(size)])


def stats_kernel(t_ref, s_ref, out_ref):
    t = t_ref[...].astype(jnp.float32)
    s = s_ref[...].astype(jnp.float32)
    t_width, s_width = t.shape[1], s.shape[1]
    out_ref[:, :t_width] = jnp.sum(t, axis=0, keepdims=True)
    out_ref[:, t_width : t_width + s_width] = jnp.sum(s, axis=0, keepdims=True)
    square_t = jnp.sum(jnp.sum(t * t, axis=0, keepdims=True), axis=1, keepdims=True)
    square_s = jnp.sum(jnp.sum(s * s, axis=0, keepdims=True), axis=1, keepdims=True)
    lane = lax.broadcasted_iota(jnp.int32, (1, LANES), 1)
    out_ref[:, t_width + s_width :] = jnp.where(
        lane == 0, square_t, jnp.where(lane == 1, square_s, 0.0)
    )


def spreads_of(stats, t_width, s_width, total_rows):
    centre_t = stats[:, :t_width] / total_rows
    centre_s = stats[:, t_width : t_width + s_width] / total_rows
    square_t = stats[:, t_width + s_width : t_width + s_width + 1]
    square_s = stats[:, t_width + s_width + 1 : t_width + s_width + 2]
    spread_t = (
        2.0 * (square_t / total_rows - jnp.sum(centre_t * centre_t, axis=1, keepdims=True)) + EPSILON
    )
    spread_s = (
        2.0 * (square_s / total_rows - jnp.sum(centre_s * centre_s, axis=1, keepdims=True)) + EPSILON
    )
    return spread_t, spread_s, centre_s


def column_norms(ref):
    value = ref[...].astype(jnp.float32)
    return jnp.sum(value * value, axis=1, keepdims=True)


def diagonal(rows):
    return lax.broadcasted_iota(jnp.int32, (rows, rows), 0) == lax.broadcasted_iota(
        jnp.int32, (rows, rows), 1
    )


def as_row(column):
    return jnp.sum(jnp.where(diagonal(column.shape[0]), column, 0.0), axis=0, keepdims=True)


def with_ones(ref):
    return jnp.concatenate([ref[...], jnp.ones((ref.shape[0], LANES), ref.dtype)], axis=1)


def pair_tile(v, c, inv_t, inv_s, own):
    (vt, vs, nvt, nvs), (ct, cs, nct, ncs) = v, c
    last = (((1,), (1,)), ((), ()))
    gram_t = lax.dot_general(vt[...], ct[...], last, preferred_element_type=jnp.float32)
    gram_s = lax.dot_general(vs[...], cs[...], last, preferred_element_type=jnp.float32)
    square_t = jnp.maximum(nvt + nct - 2.0 * gram_t, 0.0)
    square_s = jnp.maximum(nvs + ncs - 2.0 * gram_s, 0.0)
    under_t = square_t * inv_t + FLOOR
    under_s = square_s * inv_s + FLOOR
    inverse_s = lax.rsqrt(under_s)
    residue = under_s * inverse_s - under_t * lax.rsqrt(under_t)
    slope = jnp.clip(residue, -1.0, 1.0)
    huber = slope * (residue - 0.5 * slope)
    pull = slope * inverse_s
    if own:
        diag = diagonal(pull.shape[0])
        pull = jnp.where(diag, 0.0, pull)
        huber = jnp.where(diag, 0.0, huber)
    weights = (pull * inv_s).astype(jnp.bfloat16)
    return (
        weights,
        jnp.sum(huber, axis=0, keepdims=True),
        jnp.sum(pull * square_s, axis=0, keepdims=True),
    )


def direct_of(ref, summed):
    width = ref.shape[1]
    row_weight = summed[:, width:]
    spread_out = jnp.concatenate([row_weight] * (width // LANES), axis=1)
    return ref[...].astype(jnp.float32) * spread_out - summed[:, :width]


def early_kernel(n_blk, steps, total_rows, *refs):
    refs = list(refs)
    plane = [(refs.pop(0), refs.pop(0)) for _ in range(n_blk)]
    line = [plane[0]] + [(refs.pop(0), refs.pop(0)) for _ in range(steps - 1)]
    stats_refs = refs.pop(0), refs.pop(0)
    n_sub_stats = stats_refs[1].shape[0]
    own_ref = refs.pop(0)
    back_refs = [refs.pop(0) for _ in range(steps - 1)]
    acc_ref, norm_ref, total_ref, sums_ref = refs
    t_width, s_width = plane[0][0].shape[1], plane[0][1].shape[1]
    stats = stats_refs[0][...]
    for i in range(n_sub_stats):
        stats = stats + stats_refs[1][i]
    total_ref[...] = stats
    spread_t, spread_s, _ = spreads_of(stats, t_width, s_width, total_rows)
    inv_t, inv_s = 1.0 / spread_t, 1.0 / spread_s
    cols = []
    for d, (t, s) in enumerate(plane):
        nt, ns = as_row(column_norms(t)), as_row(column_norms(s))
        norm_ref[d : d + 1, :LANES] = nt
        norm_ref[d : d + 1, LANES:] = ns
        cols.append((t, s, nt, ns))
    loss = jnp.zeros((1, LANES), jnp.float32)
    spread = jnp.zeros((1, LANES), jnp.float32)
    for k, (t, s) in enumerate(line):
        v = (t, s, column_norms(t), column_norms(s))
        summed = None
        for d in range(n_blk):
            weights, loss_part, spread_part = pair_tile(v, cols[d], inv_t, inv_s, k == 0 and d == 0)
            factor = 1.0 if k == 0 else 2.0
            loss = loss + factor * loss_part
            spread = spread + factor * spread_part
            term = jnp.dot(weights, with_ones(cols[d][1]), preferred_element_type=jnp.float32)
            summed = term if summed is None else summed + term
            if k > 0:
                back = lax.dot_general(
                    weights,
                    with_ones(s),
                    (((0,), (0,)), ((), ())),
                    preferred_element_type=jnp.float32,
                )
                acc_ref[d] = back if k == 1 else acc_ref[d] + back
        if k == 0:
            own_ref[...] = direct_of(s, summed)
        else:
            back_refs[k - 1][...] = direct_of(s, summed)
    if steps == 1:
        acc_ref[...] = jnp.zeros_like(acc_ref)
    sums_ref[0:1, :] = loss
    sums_ref[1:2, :] = spread


def late_kernel(n_blk, total_rows, *refs):
    refs = list(refs)
    plane = [(refs.pop(0), refs.pop(0)) for _ in range(n_blk)]
    t, s, stats_ref, acc_ref, norm_ref, early_sums = (refs.pop(0) for _ in range(6))
    out_refs = [refs.pop(0) for _ in range(n_blk)]
    (sums_ref,) = refs
    t_width, s_width = t.shape[1], s.shape[1]
    spread_t, spread_s, _ = spreads_of(stats_ref[...], t_width, s_width, total_rows)
    inv_t, inv_s = 1.0 / spread_t, 1.0 / spread_s
    v = (t, s, column_norms(t), column_norms(s))
    loss = early_sums[0:1, :]
    spread = early_sums[1:2, :]
    for d in range(n_blk):
        ct, cs = plane[d]
        c = (ct, cs, norm_ref[d : d + 1, :LANES], norm_ref[d : d + 1, LANES:])
        weights, loss_part, spread_part = pair_tile(v, c, inv_t, inv_s, False)
        loss = loss + loss_part
        spread = spread + spread_part
        back = lax.dot_general(
            weights, with_ones(s), (((0,), (0,)), ((), ())), preferred_element_type=jnp.float32
        )
        out_refs[d][...] = direct_of(cs, acc_ref[d] + back)
    sums_ref[0:1, :] = loss
    sums_ref[1:2, :] = spread


def final_kernel(n_parts, n_sums, total_rows, *refs):
    refs = list(refs)
    student_ref, stats_ref = refs.pop(0), refs.pop(0)
    parts = [refs.pop(0) for _ in range(n_parts)]
    sums = [refs.pop(0) for _ in range(n_sums)]
    grad_ref, loss_ref = refs
    s_width = student_ref.shape[1]
    t_width = stats_ref.shape[1] - s_width - LANES
    direct = parts[0][...]
    for part in parts[1:]:
        direct = direct + part[...]
    both = sums[0][...]
    for one in sums[1:]:
        both = both + one[...]
    both = jnp.sum(both, axis=1, keepdims=True)
    loss_total, spread_total = both[0:1, :], -both[1:2, :]
    _, spread_s, centre = spreads_of(stats_ref[...], t_width, s_width, total_rows)
    pairs = total_rows * (total_rows - 1.0)
    correction = 2.0 * spread_total / (pairs * spread_s * spread_s)
    grad_ref[...] = (2.0 / (total_rows - 1.0)) * direct + correction * (
        student_ref[...].astype(jnp.float32) - centre
    )
    loss_ref[...] = jnp.broadcast_to(loss_total / pairs, loss_ref.shape)


def call(kernel, out_shape, operands, flops):
    nbytes = sum(x.size * x.dtype.itemsize for x in operands)
    return pl.pallas_call(
        kernel,
        out_shape=out_shape,
        in_specs=[WHOLE] * len(operands),
        out_specs=jax.tree.map(lambda _: WHOLE, out_shape),
        compiler_params=pltpu.CompilerParams(vmem_limit_bytes=48 * 1024 * 1024),
        cost_estimate=pl.CostEstimate(flops=flops, bytes_accessed=nbytes, transcendentals=0),
    )(*operands)


def per_device(teacher, student):
    rows, t_width = teacher.shape
    s_width = student.shape[1]
    n_blk = lax.axis_size("blk")
    n_sub = lax.axis_size("sub")
    total_rows = float(rows * n_blk * n_sub)
    half = n_sub // 2
    f32 = functools.partial(jax.ShapeDtypeStruct, dtype=jnp.float32)

    line = [(teacher, student)]
    for _ in range(half):
        line.append(tuple(shifted(x, "sub", 1) for x in line[-1]))
    plane = [(teacher, student)]
    for d in range(1, n_blk):
        plane.append(tuple(exchange(x, "blk", d) for x in (teacher, student)))

    stats = call(
        stats_kernel, f32((1, t_width + s_width + LANES)), (teacher, student), 4 * teacher.size
    )
    for_plane = stats
    for d in range(1, n_blk):
        for_plane = for_plane + exchange(stats, "blk", d)
    others = [exchange(for_plane, "sub", d) for d in range(1, n_sub)]

    pair_flops = 2 * rows * rows * n_blk * (t_width + 3 * s_width)
    flat_plane = [x for pair in plane for x in pair]
    flat_line = [x for pair in line[1:half] for x in pair]
    out_shape = (
        [f32((rows, s_width))] * half
        + [f32((n_blk, rows, s_width + LANES)), f32((n_blk, 2 * LANES))]
        + [f32(stats.shape), f32((2, LANES))]
    )
    *tiles, acc, norms, totals, early_sums = call(
        functools.partial(early_kernel, n_blk, half, total_rows),
        out_shape,
        flat_plane + flat_line + [for_plane, jnp.stack(others)],
        half * pair_flops,
    )
    own, backs = tiles[0], tiles[1:]
    returned = [shifted(x, "sub", -k) for k, x in enumerate(backs, 1)]
    *shares, sums = call(
        functools.partial(late_kernel, n_blk, total_rows),
        [f32((rows, s_width))] * n_blk + [f32((2, LANES))],
        flat_plane + list(line[half]) + [totals, acc, norms, early_sums],
        pair_flops,
    )
    plane_sums = sums
    for d in range(1, n_blk):
        plane_sums = plane_sums + exchange(sums, "blk", d)
    all_sums = [plane_sums] + [exchange(plane_sums, "sub", d) for d in range(1, n_sub)]
    received = [exchange(shares[d], "blk", d) for d in range(1, n_blk)]
    parts = [own, shares[0]] + returned + received
    grad, loss = call(
        functools.partial(final_kernel, len(parts), len(all_sums), total_rows),
        [f32((rows, s_width)), f32((1, LANES))],
        [student, totals] + parts + all_sums,
        8 * student.size,
    )
    return grad, loss[0, :1]


def solution(mesh):
    placed = P(("groups", "blk", "sub"), None)
    return jax.shard_map(
        per_device,
        mesh=mesh,
        in_specs=(placed, placed),
        out_specs=(placed, P("groups")),
        check_vma=False,
    )
```

```python
import functools

import jax
import jax.numpy as jnp
from jax import lax
from jax.experimental import pallas as pl
from jax.experimental.pallas import tpu as pltpu
from jax.sharding import PartitionSpec as P

FLOOR = 0.01
EPSILON = 1e-06
LANES = 128
WHOLE = pl.BlockSpec(memory_space=pltpu.VMEM)


def exchange(value, axis, distance):
    size = lax.axis_size(axis)
    return lax.ppermute(value, axis, [(i, i ^ distance) for i in range(size)])


def shifted(value, axis, distance):
    size = lax.axis_size(axis)
    return lax.ppermute(value, axis, [(i, (i + distance) % size) for i in range(size)])


def pack_kernel(t_hbm, s_hbm, packed_ref, stats_ref, sems):
    t_width, s_width = t_hbm.shape[1], s_hbm.shape[1]
    copies = [
        pltpu.make_async_copy(t_hbm, packed_ref.at[:, :t_width], sems.at[0]),
        pltpu.make_async_copy(s_hbm, packed_ref.at[:, t_width:], sems.at[1]),
    ]
    for copy in copies:
        copy.start()
    for copy in copies:
        copy.wait()
    value = packed_ref[...].astype(jnp.float32)
    squares = jnp.sum(value * value, axis=0, keepdims=True)
    square_t = jnp.sum(squares[:, :t_width], axis=1, keepdims=True)
    square_s = jnp.sum(squares[:, t_width:], axis=1, keepdims=True)
    lane = lax.broadcasted_iota(jnp.int32, (1, LANES), 1)
    last = jnp.where(lane == 0, square_t, jnp.where(lane == 1, square_s, 0.0))
    row = jnp.concatenate([jnp.sum(value, axis=0, keepdims=True), last], axis=1)
    stats_ref[...] = jnp.broadcast_to(row[None], stats_ref.shape)


def spreads_of(stats, t_width, s_width, total_rows):
    centre_t = stats[:, :t_width] / total_rows
    centre_s = stats[:, t_width : t_width + s_width] / total_rows
    square_t = stats[:, t_width + s_width : t_width + s_width + 1]
    square_s = stats[:, t_width + s_width + 1 : t_width + s_width + 2]
    spread_t = (
        2.0 * (square_t / total_rows - jnp.sum(centre_t * centre_t, axis=1, keepdims=True)) + EPSILON
    )
    spread_s = (
        2.0 * (square_s / total_rows - jnp.sum(centre_s * centre_s, axis=1, keepdims=True)) + EPSILON
    )
    return spread_t, spread_s, centre_s


def halves(ref, t_width):
    return ref.at[:, :t_width], ref.at[:, t_width:]


def column_norms(ref):
    value = ref[...].astype(jnp.float32)
    return jnp.sum(value * value, axis=1, keepdims=True)


def diagonal(rows):
    return lax.broadcasted_iota(jnp.int32, (rows, rows), 0) == lax.broadcasted_iota(
        jnp.int32, (rows, rows), 1
    )


def as_row(column):
    return jnp.sum(jnp.where(diagonal(column.shape[0]), column, 0.0), axis=0, keepdims=True)


def with_ones(ref):
    return jnp.concatenate([ref[...], jnp.ones((ref.shape[0], LANES), ref.dtype)], axis=1)


def pair_tile(v, c, inv_t, inv_s, own):
    (vt, vs, nvt, nvs), (ct, cs, nct, ncs) = v, c
    last = (((1,), (1,)), ((), ()))
    gram_t = lax.dot_general(vt[...], ct[...], last, preferred_element_type=jnp.float32)
    gram_s = lax.dot_general(vs[...], cs[...], last, preferred_element_type=jnp.float32)
    square_t = jnp.maximum(nvt + nct - 2.0 * gram_t, 0.0)
    square_s = jnp.maximum(nvs + ncs - 2.0 * gram_s, 0.0)
    under_t = square_t * inv_t + FLOOR
    under_s = square_s * inv_s + FLOOR
    inverse_s = lax.rsqrt(under_s)
    residue = under_s * inverse_s - under_t * lax.rsqrt(under_t)
    slope = jnp.clip(residue, -1.0, 1.0)
    huber = slope * (residue - 0.5 * slope)
    pull = slope * inverse_s
    if own:
        diag = diagonal(pull.shape[0])
        pull = jnp.where(diag, 0.0, pull)
        huber = jnp.where(diag, 0.0, huber)
    weights = (pull * inv_s).astype(jnp.bfloat16)
    return (
        weights,
        jnp.sum(huber, axis=0, keepdims=True),
        jnp.sum(pull * square_s, axis=0, keepdims=True),
    )


def direct_of(ref, summed):
    width = ref.shape[1]
    row_weight = summed[:, width:]
    spread_out = jnp.concatenate([row_weight] * (width // LANES), axis=1)
    return ref[...].astype(jnp.float32) * spread_out - summed[:, :width]


def early_kernel(n_blk, steps, t_width, total_rows, *refs):
    refs = list(refs)
    plane = [halves(refs.pop(0), t_width) for _ in range(n_blk)]
    line = [plane[0]] + [halves(refs.pop(0), t_width) for _ in range(steps - 1)]
    stats_ref, own_ref = refs.pop(0), refs.pop(0)
    back_refs = [refs.pop(0) for _ in range(steps - 1)]
    acc_ref, norm_ref, total_ref, sums_ref = refs
    s_width = plane[0][1].shape[1]
    stats = jnp.sum(stats_ref[...], axis=0)
    total_ref[...] = stats
    spread_t, spread_s, _ = spreads_of(stats, t_width, s_width, total_rows)
    inv_t, inv_s = 1.0 / spread_t, 1.0 / spread_s
    cols = []
    for d, (t, s) in enumerate(plane):
        nt, ns = as_row(column_norms(t)), as_row(column_norms(s))
        norm_ref[d : d + 1, :LANES] = nt
        norm_ref[d : d + 1, LANES:] = ns
        cols.append((t, s, nt, ns))
    loss = jnp.zeros((1, LANES), jnp.float32)
    spread = jnp.zeros((1, LANES), jnp.float32)
    for k, (t, s) in enumerate(line):
        v = (t, s, column_norms(t), column_norms(s))
        summed = None
        for d in range(n_blk):
            weights, loss_part, spread_part = pair_tile(v, cols[d], inv_t, inv_s, k == 0 and d == 0)
            factor = 1.0 if k == 0 else 2.0
            loss = loss + factor * loss_part
            spread = spread + factor * spread_part
            term = jnp.dot(weights, with_ones(cols[d][1]), preferred_element_type=jnp.float32)
            summed = term if summed is None else summed + term
            if k > 0:
                back = lax.dot_general(
                    weights,
                    with_ones(s),
                    (((0,), (0,)), ((), ())),
                    preferred_element_type=jnp.float32,
                )
                acc_ref[d] = back if k == 1 else acc_ref[d] + back
        if k == 0:
            own_ref[...] = direct_of(s, summed)
        else:
            back_refs[k - 1][...] = direct_of(s, summed)
    if steps == 1:
        acc_ref[...] = jnp.zeros_like(acc_ref)
    sums_ref[0:1, :] = loss
    sums_ref[1:2, :] = spread


def late_kernel(n_blk, t_width, total_rows, *refs):
    refs = list(refs)
    plane = [halves(refs.pop(0), t_width) for _ in range(n_blk)]
    t, s = halves(refs.pop(0), t_width)
    stats_ref, acc_ref, norm_ref, early_sums = (refs.pop(0) for _ in range(4))
    out_refs = [refs.pop(0) for _ in range(n_blk)]
    (sums_ref,) = refs
    s_width = s.shape[1]
    spread_t, spread_s, _ = spreads_of(stats_ref[...], t_width, s_width, total_rows)
    inv_t, inv_s = 1.0 / spread_t, 1.0 / spread_s
    v = (t, s, column_norms(t), column_norms(s))
    loss = early_sums[0:1, :]
    spread = early_sums[1:2, :]
    for d in range(n_blk):
        ct, cs = plane[d]
        c = (ct, cs, norm_ref[d : d + 1, :LANES], norm_ref[d : d + 1, LANES:])
        weights, loss_part, spread_part = pair_tile(v, c, inv_t, inv_s, False)
        loss = loss + loss_part
        spread = spread + spread_part
        back = lax.dot_general(
            weights, with_ones(s), (((0,), (0,)), ((), ())), preferred_element_type=jnp.float32
        )
        out_refs[d][...] = direct_of(cs, acc_ref[d] + back)
    for i in range(sums_ref.shape[0]):
        sums_ref[i, 0:1, :] = loss
        sums_ref[i, 1:2, :] = spread


def final_kernel(n_parts, total_rows, *refs):
    refs = list(refs)
    student_ref, stats_ref = refs.pop(0), refs.pop(0)
    parts = [refs.pop(0) for _ in range(n_parts)]
    sums_ref, grad_ref, loss_ref = refs
    s_width = student_ref.shape[1]
    t_width = stats_ref.shape[1] - s_width - LANES
    direct = parts[0][...]
    for part in parts[1:]:
        direct = direct + part[...]
    both = jnp.sum(jnp.sum(sums_ref[...], axis=0), axis=1, keepdims=True)
    loss_total, spread_total = both[0:1, :], -both[1:2, :]
    _, spread_s, centre = spreads_of(stats_ref[...], t_width, s_width, total_rows)
    pairs = total_rows * (total_rows - 1.0)
    correction = 2.0 * spread_total / (pairs * spread_s * spread_s)
    grad_ref[...] = (2.0 / (total_rows - 1.0)) * direct + correction * (
        student_ref[...].astype(jnp.float32) - centre
    )
    loss_ref[...] = jnp.broadcast_to(loss_total / pairs, loss_ref.shape)


def call(kernel, out_shape, operands, flops, vmem=48, **more):
    nbytes = sum(x.size * x.dtype.itemsize for x in operands)
    in_specs = more.pop("in_specs", [WHOLE] * len(operands))
    return pl.pallas_call(
        kernel,
        out_shape=out_shape,
        in_specs=in_specs,
        out_specs=jax.tree.map(lambda _: WHOLE, out_shape),
        compiler_params=pltpu.CompilerParams(vmem_limit_bytes=vmem * 1024 * 1024),
        cost_estimate=pl.CostEstimate(flops=flops, bytes_accessed=nbytes, transcendentals=0),
        **more,
    )(*operands)


def to_all(value):
    return lax.all_to_all(value, ("blk", "sub"), 0, 0, tiled=True)


def per_device(teacher, student):
    rows, t_width = teacher.shape
    s_width = student.shape[1]
    n_blk = lax.axis_size("blk")
    n_sub = lax.axis_size("sub")
    n_all = n_blk * n_sub
    total_rows = float(rows * n_all)
    half = n_sub // 2
    f32 = functools.partial(jax.ShapeDtypeStruct, dtype=jnp.float32)

    packed, stats = call(
        pack_kernel,
        [
            jax.ShapeDtypeStruct((rows, t_width + s_width), teacher.dtype),
            f32((n_all, 1, t_width + s_width + LANES)),
        ],
        (teacher, student),
        4 * teacher.size,
        vmem=62,
        in_specs=[pl.BlockSpec(memory_space=pl.ANY)] * 2,
        scratch_shapes=[pltpu.SemaphoreType.DMA((2,))],
    )
    line = [packed]
    for _ in range(half):
        line.append(shifted(line[-1], "sub", 1))
    plane = [packed]
    distance = n_blk // 2
    while distance:
        plane = plane + [exchange(x, "blk", distance) for x in plane]
        distance //= 2
    distances = [0]
    distance = n_blk // 2
    while distance:
        distances = distances + [x ^ distance for x in distances]
        distance //= 2
    stats = to_all(stats)

    pair_flops = 2 * rows * rows * n_blk * (t_width + 3 * s_width)
    out_shape = (
        [f32((rows, s_width))] * half
        + [f32((n_blk, rows, s_width + LANES)), f32((n_blk, 2 * LANES))]
        + [f32(stats.shape[1:]), f32((2, LANES))]
    )
    *tiles, acc, norms, totals, early_sums = call(
        functools.partial(early_kernel, n_blk, half, t_width, total_rows),
        out_shape,
        plane + line[1:half] + [stats],
        half * pair_flops,
    )
    own, backs = tiles[0], tiles[1:]
    returned = [shifted(x, "sub", -k) for k, x in enumerate(backs, 1)]
    *shares, sums = call(
        functools.partial(late_kernel, n_blk, t_width, total_rows),
        [f32((rows, s_width))] * n_blk + [f32((n_all, 2, LANES))],
        plane + [line[half], totals, acc, norms, early_sums],
        pair_flops,
    )
    received = [exchange(share, "blk", d) for share, d in zip(shares[1:], distances[1:])]
    all_sums = to_all(sums)
    parts = [own, shares[0]] + returned + received
    grad, loss = call(
        functools.partial(final_kernel, len(parts), total_rows),
        [f32((rows, s_width)), f32((1, LANES))],
        [student, totals] + parts + [all_sums],
        8 * student.size,
    )
    return grad, loss[0, :1]


def solution(mesh):
    placed = P(("groups", "blk", "sub"), None)
    return jax.shard_map(
        per_device,
        mesh=mesh,
        in_specs=(placed, placed),
        out_specs=(placed, P("groups")),
        check_vma=False,
    )
```

```python
import functools

import jax
import jax.numpy as jnp
from jax import lax
from jax.experimental import pallas as pl
from jax.experimental.pallas import tpu as pltpu
from jax.sharding import PartitionSpec as P

FLOOR = 0.01
EPSILON = 1e-06
LANES = 128
WHOLE = pl.BlockSpec(memory_space=pltpu.VMEM)


def exchange(value, axis, distance):
    size = lax.axis_size(axis)
    return lax.ppermute(value, axis, [(i, i ^ distance) for i in range(size)])


def shifted(value, axis, distance):
    size = lax.axis_size(axis)
    return lax.ppermute(value, axis, [(i, (i + distance) % size) for i in range(size)])


def pack_kernel(t_hbm, s_hbm, packed_ref, sems):
    t_width = t_hbm.shape[1]
    copies = [
        pltpu.make_async_copy(t_hbm, packed_ref.at[:, :t_width], sems.at[0]),
        pltpu.make_async_copy(s_hbm, packed_ref.at[:, t_width:], sems.at[1]),
    ]
    for copy in copies:
        copy.start()
    for copy in copies:
        copy.wait()


def stats_kernel(t_width, packed_ref, stats_ref):
    value = packed_ref[...].astype(jnp.float32)
    squares = jnp.sum(value * value, axis=0, keepdims=True)
    square_t = jnp.sum(squares[:, :t_width], axis=1, keepdims=True)
    square_s = jnp.sum(squares[:, t_width:], axis=1, keepdims=True)
    lane = lax.broadcasted_iota(jnp.int32, (1, LANES), 1)
    width = value.shape[1]
    stats_ref[:, :width] = jnp.sum(value, axis=0, keepdims=True)
    stats_ref[:, width:] = jnp.where(lane == 0, square_t, jnp.where(lane == 1, square_s, 0.0))


def spreads_of(stats, t_width, s_width, total_rows):
    centre_t = stats[:, :t_width] / total_rows
    centre_s = stats[:, t_width : t_width + s_width] / total_rows
    square_t = stats[:, t_width + s_width : t_width + s_width + 1]
    square_s = stats[:, t_width + s_width + 1 : t_width + s_width + 2]
    spread_t = (
        2.0 * (square_t / total_rows - jnp.sum(centre_t * centre_t, axis=1, keepdims=True)) + EPSILON
    )
    spread_s = (
        2.0 * (square_s / total_rows - jnp.sum(centre_s * centre_s, axis=1, keepdims=True)) + EPSILON
    )
    return spread_t, spread_s, centre_s


def halves(ref, t_width):
    return ref.at[:, :t_width], ref.at[:, t_width:]


def column_norms(ref):
    value = ref[...].astype(jnp.float32)
    return jnp.sum(value * value, axis=1, keepdims=True)


def diagonal(rows):
    return lax.broadcasted_iota(jnp.int32, (rows, rows), 0) == lax.broadcasted_iota(
        jnp.int32, (rows, rows), 1
    )


def as_row(column):
    return jnp.sum(jnp.where(diagonal(column.shape[0]), column, 0.0), axis=0, keepdims=True)


def with_ones(ref):
    return jnp.concatenate([ref[...], jnp.ones((ref.shape[0], LANES), ref.dtype)], axis=1)


def pair_tile(v, c, inv_t, inv_s, own):
    (vt, vs, nvt, nvs), (ct, cs, nct, ncs) = v, c
    last = (((1,), (1,)), ((), ()))
    gram_t = lax.dot_general(vt[...], ct[...], last, preferred_element_type=jnp.float32)
    gram_s = lax.dot_general(vs[...], cs[...], last, preferred_element_type=jnp.float32)
    square_t = jnp.maximum(nvt + nct - 2.0 * gram_t, 0.0)
    square_s = jnp.maximum(nvs + ncs - 2.0 * gram_s, 0.0)
    under_t = square_t * inv_t + FLOOR
    under_s = square_s * inv_s + FLOOR
    inverse_s = lax.rsqrt(under_s)
    residue = under_s * inverse_s - under_t * lax.rsqrt(under_t)
    slope = jnp.clip(residue, -1.0, 1.0)
    huber = slope * (residue - 0.5 * slope)
    pull = slope * inverse_s
    if own:
        diag = diagonal(pull.shape[0])
        pull = jnp.where(diag, 0.0, pull)
        huber = jnp.where(diag, 0.0, huber)
    weights = (pull * inv_s).astype(jnp.bfloat16)
    return (
        weights,
        jnp.sum(huber, axis=0, keepdims=True),
        jnp.sum(pull * square_s, axis=0, keepdims=True),
    )


def direct_of(ref, summed):
    width = ref.shape[1]
    row_weight = summed[:, width:]
    spread_out = jnp.concatenate([row_weight] * (width // LANES), axis=1)
    return ref[...].astype(jnp.float32) * spread_out - summed[:, :width]


def early_kernel(n_blk, steps, t_width, total_rows, *refs):
    refs = list(refs)
    plane = [halves(refs.pop(0), t_width) for _ in range(n_blk)]
    line = [plane[0]] + [halves(refs.pop(0), t_width) for _ in range(steps - 1)]
    stats_refs = refs.pop(0), refs.pop(0)
    own_ref = refs.pop(0)
    back_refs = [refs.pop(0) for _ in range(steps - 1)]
    acc_ref, norm_ref, total_ref, sums_ref = refs
    s_width = plane[0][1].shape[1]
    stats = stats_refs[0][...] + stats_refs[1][...]
    total_ref[...] = stats
    spread_t, spread_s, _ = spreads_of(stats, t_width, s_width, total_rows)
    inv_t, inv_s = 1.0 / spread_t, 1.0 / spread_s
    cols = []
    for d, (t, s) in enumerate(plane):
        nt, ns = as_row(column_norms(t)), as_row(column_norms(s))
        norm_ref[d : d + 1, :LANES] = nt
        norm_ref[d : d + 1, LANES:] = ns
        cols.append((t, s, nt, ns))
    loss = jnp.zeros((1, LANES), jnp.float32)
    spread = jnp.zeros((1, LANES), jnp.float32)
    for k, (t, s) in enumerate(line):
        v = (t, s, column_norms(t), column_norms(s))
        summed = None
        for d in range(n_blk):
            weights, loss_part, spread_part = pair_tile(v, cols[d], inv_t, inv_s, k == 0 and d == 0)
            factor = 1.0 if k == 0 else 2.0
            loss = loss + factor * loss_part
            spread = spread + factor * spread_part
            term = jnp.dot(weights, with_ones(cols[d][1]), preferred_element_type=jnp.float32)
            summed = term if summed is None else summed + term
            if k > 0:
                back = lax.dot_general(
                    weights,
                    with_ones(s),
                    (((0,), (0,)), ((), ())),
                    preferred_element_type=jnp.float32,
                )
                acc_ref[d] = back if k == 1 else acc_ref[d] + back
        if k == 0:
            own_ref[...] = direct_of(s, summed)
        else:
            back_refs[k - 1][...] = direct_of(s, summed)
    if steps == 1:
        acc_ref[...] = jnp.zeros_like(acc_ref)
    sums_ref[0:1, :] = loss
    sums_ref[1:2, :] = spread


def late_kernel(n_blk, t_width, total_rows, *refs):
    refs = list(refs)
    plane = [halves(refs.pop(0), t_width) for _ in range(n_blk)]
    t, s = halves(refs.pop(0), t_width)
    stats_ref, acc_ref, norm_ref, early_sums = (refs.pop(0) for _ in range(4))
    out_refs = [refs.pop(0) for _ in range(n_blk)]
    (sums_ref,) = refs
    s_width = s.shape[1]
    spread_t, spread_s, _ = spreads_of(stats_ref[...], t_width, s_width, total_rows)
    inv_t, inv_s = 1.0 / spread_t, 1.0 / spread_s
    v = (t, s, column_norms(t), column_norms(s))
    loss = early_sums[0:1, :]
    spread = early_sums[1:2, :]
    for d in range(n_blk):
        ct, cs = plane[d]
        c = (ct, cs, norm_ref[d : d + 1, :LANES], norm_ref[d : d + 1, LANES:])
        weights, loss_part, spread_part = pair_tile(v, c, inv_t, inv_s, False)
        loss = loss + loss_part
        spread = spread + spread_part
        back = lax.dot_general(
            weights, with_ones(s), (((0,), (0,)), ((), ())), preferred_element_type=jnp.float32
        )
        out_refs[d][...] = direct_of(cs, acc_ref[d] + back)
    sums_ref[0:1, :] = loss
    sums_ref[1:2, :] = spread


def final_kernel(n_parts, t_width, total_rows, *refs):
    refs = list(refs)
    packed_ref, stats_ref = refs.pop(0), refs.pop(0)
    parts = [refs.pop(0) for _ in range(n_parts)]
    *sums, grad_ref, loss_ref = refs
    student_ref = packed_ref.at[:, t_width:]
    s_width = student_ref.shape[1]
    direct = parts[0][...]
    for part in parts[1:]:
        direct = direct + part[...]
    both = sums[0][...]
    for one in sums[1:]:
        both = both + one[...]
    both = jnp.sum(both, axis=1, keepdims=True)
    loss_total, spread_total = both[0:1, :], -both[1:2, :]
    _, spread_s, centre = spreads_of(stats_ref[...], t_width, s_width, total_rows)
    pairs = total_rows * (total_rows - 1.0)
    correction = 2.0 * spread_total / (pairs * spread_s * spread_s)
    grad_ref[...] = (2.0 / (total_rows - 1.0)) * direct + correction * (
        student_ref[...].astype(jnp.float32) - centre
    )
    loss_ref[...] = jnp.broadcast_to(loss_total / pairs, loss_ref.shape)


def call(kernel, out_shape, operands, flops, vmem=48, **more):
    nbytes = sum(x.size * x.dtype.itemsize for x in operands)
    in_specs = more.pop("in_specs", [WHOLE] * len(operands))
    return pl.pallas_call(
        kernel,
        out_shape=out_shape,
        in_specs=in_specs,
        out_specs=jax.tree.map(lambda _: WHOLE, out_shape),
        compiler_params=pltpu.CompilerParams(vmem_limit_bytes=vmem * 1024 * 1024),
        cost_estimate=pl.CostEstimate(flops=flops, bytes_accessed=nbytes, transcendentals=0),
        **more,
    )(*operands)


def gathered(value, axis):
    return [value] + [exchange(value, axis, d) for d in range(1, lax.axis_size(axis))]


def halvings(axis):
    size = lax.axis_size(axis)
    return [size >> i for i in range(1, size.bit_length())]


def per_device(teacher, student):
    rows, t_width = teacher.shape
    s_width = student.shape[1]
    n_blk = lax.axis_size("blk")
    n_sub = lax.axis_size("sub")
    n_all = n_blk * n_sub
    total_rows = float(rows * n_all)
    half = n_sub // 2
    f32 = functools.partial(jax.ShapeDtypeStruct, dtype=jnp.float32)

    packed = call(
        pack_kernel,
        jax.ShapeDtypeStruct((rows, t_width + s_width), teacher.dtype),
        (teacher, student),
        0,
        vmem=62,
        in_specs=[pl.BlockSpec(memory_space=pl.ANY)] * 2,
        scratch_shapes=[pltpu.SemaphoreType.DMA((2,))],
    )
    line = [packed]
    for _ in range(half):
        line.append(shifted(line[-1], "sub", 1))
    plane, distances = [packed], [0]
    for distance in halvings("blk"):
        plane = plane + [exchange(x, "blk", distance) for x in plane]
        distances = distances + [x ^ distance for x in distances]
    stats = call(
        functools.partial(stats_kernel, t_width),
        f32((1, t_width + s_width + LANES)),
        (packed,),
        4 * packed.size,
    )
    stats = functools.reduce(jnp.add, gathered(stats, "sub"))
    for distance in halvings("blk")[:-1]:
        stats = stats + exchange(stats, "blk", distance)
    stats_other = exchange(stats, "blk", 1)

    pair_flops = 2 * rows * rows * n_blk * (t_width + 3 * s_width)
    out_shape = (
        [f32((rows, s_width))] * half
        + [f32((n_blk, rows, s_width + LANES)), f32((n_blk, 2 * LANES))]
        + [f32(stats.shape), f32((2, LANES))]
    )
    *tiles, acc, norms, totals, early_sums = call(
        functools.partial(early_kernel, n_blk, half, t_width, total_rows),
        out_shape,
        plane + line[1:half] + [stats, stats_other],
        half * pair_flops,
    )
    own, backs = tiles[0], tiles[1:]
    returned = [shifted(x, "sub", -k) for k, x in enumerate(backs, 1)]
    *shares, sums = call(
        functools.partial(late_kernel, n_blk, t_width, total_rows),
        [f32((rows, s_width))] * n_blk + [f32((2, LANES))],
        plane + [line[half], totals, acc, norms, early_sums],
        pair_flops,
    )
    received = [exchange(share, "blk", d) for share, d in zip(shares[1:], distances[1:])]
    sums, returned = lax.optimization_barrier((sums, returned))
    sums = functools.reduce(jnp.add, gathered(sums, "sub"))
    for distance in halvings("blk")[:-1]:
        sums = sums + exchange(sums, "blk", distance)
    all_sums = [sums, exchange(sums, "blk", 1)]
    parts = [own, shares[0]] + returned + received
    grad, loss = call(
        functools.partial(final_kernel, len(parts), t_width, total_rows),
        [f32((rows, s_width)), f32((1, LANES))],
        [packed, totals] + parts + all_sums,
        8 * student.size,
    )
    return grad, loss[0, :1]


def solution(mesh):
    placed = P(("groups", "blk", "sub"), None)
    return jax.shard_map(
        per_device,
        mesh=mesh,
        in_specs=(placed, placed),
        out_specs=(placed, P("groups")),
        check_vma=False,
    )
```

```python
import functools

import jax
import jax.numpy as jnp
from jax import lax
from jax.experimental import pallas as pl
from jax.experimental.pallas import tpu as pltpu
from jax.sharding import PartitionSpec as P

FLOOR = 0.01
EPSILON = 1e-06
LANES = 128
SUBLANES = 8
PARTS = 2
WHOLE = pl.BlockSpec(memory_space=pltpu.VMEM)


def exchange(value, axis, distance):
    size = lax.axis_size(axis)
    return lax.ppermute(value, axis, [(i, i ^ distance) for i in range(size)])


def shifted(value, axis, distance):
    size = lax.axis_size(axis)
    return lax.ppermute(value, axis, [(i, (i + distance) % size) for i in range(size)])


def pack_kernel(t_hbm, s_hbm, packed_hbm, *rest):
    *part_refs, sems = rest
    t_width = t_hbm.shape[1]
    rows = part_refs[0].shape[0]
    copies = []
    for i, ref in enumerate([*part_refs, packed_hbm]):
        start = i * rows if ref is not packed_hbm else 0
        for j, (source, column) in enumerate(((t_hbm, 0), (s_hbm, t_width))):
            copies.append(
                pltpu.make_async_copy(
                    source.at[start : start + ref.shape[0], :],
                    ref.at[:, column : column + source.shape[1]],
                    sems.at[2 * i + j],
                )
            )
    for copy in copies:
        copy.start()
    for copy in copies:
        copy.wait()


def stats_kernel(t_width, packed_ref, stats_ref):
    value = packed_ref[...].astype(jnp.float32)
    squares = jnp.sum(value * value, axis=0, keepdims=True)
    square_t = jnp.sum(squares[:, :t_width], axis=1, keepdims=True)
    square_s = jnp.sum(squares[:, t_width:], axis=1, keepdims=True)
    lane = lax.broadcasted_iota(jnp.int32, (1, LANES), 1)
    width = value.shape[1]
    stats_ref[:, :width] = jnp.sum(value, axis=0, keepdims=True)
    stats_ref[:, width:] = jnp.where(lane == 0, square_t, jnp.where(lane == 1, square_s, 0.0))


def spreads_of(stats, t_width, s_width, total_rows):
    centre_t = stats[:, :t_width] / total_rows
    centre_s = stats[:, t_width : t_width + s_width] / total_rows
    square_t = stats[:, t_width + s_width : t_width + s_width + 1]
    square_s = stats[:, t_width + s_width + 1 : t_width + s_width + 2]
    spread_t = (
        2.0 * (square_t / total_rows - jnp.sum(centre_t * centre_t, axis=1, keepdims=True)) + EPSILON
    )
    spread_s = (
        2.0 * (square_s / total_rows - jnp.sum(centre_s * centre_s, axis=1, keepdims=True)) + EPSILON
    )
    return spread_t, spread_s, centre_s


def halves(ref, t_width):
    return ref.at[:, :t_width], ref.at[:, t_width:]


def column_norms(ref):
    value = ref[...].astype(jnp.float32)
    return jnp.sum(value * value, axis=1, keepdims=True)


def diagonal(rows):
    return lax.broadcasted_iota(jnp.int32, (rows, rows), 0) == lax.broadcasted_iota(
        jnp.int32, (rows, rows), 1
    )


def as_row(column):
    return jnp.sum(jnp.where(diagonal(column.shape[0]), column, 0.0), axis=0, keepdims=True)


def with_ones(ref):
    return jnp.concatenate([ref[...], jnp.ones((ref.shape[0], LANES), ref.dtype)], axis=1)


def dot_rows(weights, value):
    return lax.dot_general(
        weights, value, (((0,), (0,)), ((), ())), preferred_element_type=jnp.float32
    )


def pair_tile(v, c, inv_t, inv_s, own):
    (vt, vs, nvt, nvs), (ct, cs, nct, ncs) = v, c
    last = (((1,), (1,)), ((), ()))
    gram_t = lax.dot_general(vt[...], ct[...], last, preferred_element_type=jnp.float32)
    gram_s = lax.dot_general(vs[...], cs[...], last, preferred_element_type=jnp.float32)
    square_t = jnp.maximum(nvt + nct - 2.0 * gram_t, 0.0)
    square_s = jnp.maximum(nvs + ncs - 2.0 * gram_s, 0.0)
    under_t = square_t * inv_t + FLOOR
    under_s = square_s * inv_s + FLOOR
    inverse_s = lax.rsqrt(under_s)
    residue = under_s * inverse_s - under_t * lax.rsqrt(under_t)
    slope = jnp.clip(residue, -1.0, 1.0)
    huber = slope * (residue - 0.5 * slope)
    pull = slope * inverse_s
    if own:
        diag = diagonal(pull.shape[0])
        pull = jnp.where(diag, 0.0, pull)
        huber = jnp.where(diag, 0.0, huber)
    weights = (pull * inv_s).astype(jnp.bfloat16)
    return (
        weights,
        jnp.sum(huber, axis=0, keepdims=True),
        jnp.sum(pull * square_s, axis=0, keepdims=True),
    )


def direct_of(ref, summed):
    width = ref.shape[1]
    row_weight = summed[:, width:]
    spread_out = jnp.concatenate([row_weight] * (width // LANES), axis=1)
    return ref[...].astype(jnp.float32) * spread_out - summed[:, :width]


def early_kernel(n_blk, steps, t_width, total_rows, *refs):
    refs = list(refs)
    plane = [halves(refs.pop(0), t_width) for _ in range(n_blk)]
    line = [[plane[0]]]
    for _ in range(steps - 1):
        line.append([halves(refs.pop(0), t_width) for _ in range(PARTS)])
    stats_refs = refs.pop(0), refs.pop(0)
    own_ref = refs.pop(0)
    back_refs = [refs.pop(0) for _ in range(steps - 1)]
    acc_ref, norm_ref, total_ref, sums_ref = refs
    s_width = plane[0][1].shape[1]
    stats = stats_refs[0][...] + stats_refs[1][...]
    total_ref[...] = stats
    spread_t, spread_s, _ = spreads_of(stats, t_width, s_width, total_rows)
    inv_t, inv_s = 1.0 / spread_t, 1.0 / spread_s
    cols = []
    for d, (t, s) in enumerate(plane):
        nt, ns = as_row(column_norms(t)), as_row(column_norms(s))
        norm_ref[d : d + 1, :LANES] = nt
        norm_ref[d : d + 1, LANES:] = ns
        cols.append((t, s, nt, ns))
    loss = jnp.zeros((1, LANES), jnp.float32)
    spread = jnp.zeros((1, LANES), jnp.float32)
    if steps == 1:
        acc_ref[...] = jnp.zeros_like(acc_ref)
    for k, parts in enumerate(line):
        for p, (t, s) in enumerate(parts):
            v = (t, s, column_norms(t), column_norms(s))
            summed = None
            for d in range(n_blk):
                own = k == 0 and d == 0
                weights, loss_part, spread_part = pair_tile(v, cols[d], inv_t, inv_s, own)
                factor = 1.0 if k == 0 else 2.0
                loss = loss + factor * loss_part
                spread = spread + factor * spread_part
                term = jnp.dot(weights, with_ones(cols[d][1]), preferred_element_type=jnp.float32)
                summed = term if summed is None else summed + term
                if k > 0:
                    back = dot_rows(weights, with_ones(s))
                    acc_ref[d] = back if k == 1 and p == 0 else acc_ref[d] + back
            if k == 0:
                own_ref[...] = direct_of(s, summed)
            else:
                start = p * s.shape[0]
                back_refs[k - 1][start : start + s.shape[0], :] = direct_of(s, summed)
    sums_ref[0:1, :] = loss
    sums_ref[1:2, :] = spread


def late_kernel(n_blk, t_width, total_rows, *refs):
    refs = list(refs)
    plane = [halves(refs.pop(0), t_width) for _ in range(n_blk)]
    parts = [halves(refs.pop(0), t_width) for _ in range(PARTS)]
    stats_ref, acc_ref, norm_ref, early_sums, keep_ref, give_ref = refs
    rows, s_width = plane[0][1].shape
    spread_t, spread_s, _ = spreads_of(stats_ref[...], t_width, s_width, total_rows)
    inv_t, inv_s = 1.0 / spread_t, 1.0 / spread_s
    loss = early_sums[0:1, :]
    spread = early_sums[1:2, :]
    visits = [(t, s, column_norms(t), column_norms(s)) for t, s in parts]
    for d in range(n_blk):
        ct, cs = plane[d]
        c = (ct, cs, norm_ref[d : d + 1, :LANES], norm_ref[d : d + 1, LANES:])
        summed = acc_ref[d]
        for v in visits:
            weights, loss_part, spread_part = pair_tile(v, c, inv_t, inv_s, False)
            loss = loss + loss_part
            spread = spread + spread_part
            summed = summed + dot_rows(weights, with_ones(v[1]))
        to_ref = keep_ref if d < n_blk // 2 else give_ref
        start = d % (n_blk // 2) * rows
        to_ref[start : start + rows, :] = direct_of(cs, summed)
    for ref in (keep_ref, give_ref):
        ref[-SUBLANES:, :] = jnp.zeros((SUBLANES, s_width), jnp.float32)
        ref[-SUBLANES : 1 - SUBLANES, :LANES] = loss
        ref[1 - SUBLANES : 2 - SUBLANES, :LANES] = spread


def halve_kernel(rows, keep_ref, got_ref, *out_refs):
    if len(out_refs) == 3:
        out_refs[2][...] = keep_ref[-SUBLANES:, :LANES] + got_ref[-SUBLANES:, :LANES]
    out_refs[0][...] = keep_ref[:rows, :] + got_ref[:rows, :]
    out_refs[1][...] = keep_ref[rows : 2 * rows, :] + got_ref[rows : 2 * rows, :]


def final_kernel(n_parts, t_width, total_rows, *refs):
    refs = list(refs)
    packed_ref, stats_ref = refs.pop(0), refs.pop(0)
    parts = [refs.pop(0) for _ in range(n_parts)]
    *sums, grad_ref, loss_ref = refs
    student_ref = packed_ref.at[:, t_width:]
    s_width = student_ref.shape[1]
    direct = parts[0][...]
    for part in parts[1:]:
        direct = direct + part[...]
    both = sums[0][...]
    for one in sums[1:]:
        both = both + one[...]
    both = jnp.sum(both, axis=1, keepdims=True)
    loss_total, spread_total = both[0:1, :], -both[1:2, :]
    _, spread_s, centre = spreads_of(stats_ref[...], t_width, s_width, total_rows)
    pairs = total_rows * (total_rows - 1.0)
    correction = 2.0 * spread_total / (pairs * spread_s * spread_s)
    grad_ref[...] = (2.0 / (total_rows - 1.0)) * direct + correction * (
        student_ref[...].astype(jnp.float32) - centre
    )
    loss_ref[...] = jnp.broadcast_to(loss_total / pairs, loss_ref.shape)


def call(kernel, out_shape, operands, flops, vmem=48, **more):
    nbytes = sum(x.size * x.dtype.itemsize for x in operands)
    in_specs = more.pop("in_specs", [WHOLE] * len(operands))
    out_specs = more.pop("out_specs", jax.tree.map(lambda _: WHOLE, out_shape))
    return pl.pallas_call(
        kernel,
        out_shape=out_shape,
        in_specs=in_specs,
        out_specs=out_specs,
        compiler_params=pltpu.CompilerParams(vmem_limit_bytes=vmem * 1024 * 1024),
        cost_estimate=pl.CostEstimate(flops=flops, bytes_accessed=nbytes, transcendentals=0),
        **more,
    )(*operands)


def gathered(value, axis):
    return [value] + [exchange(value, axis, d) for d in range(1, lax.axis_size(axis))]


def halvings(axis):
    size = lax.axis_size(axis)
    return [size >> i for i in range(1, size.bit_length())]


def per_device(teacher, student):
    rows, t_width = teacher.shape
    s_width = student.shape[1]
    n_blk = lax.axis_size("blk")
    n_sub = lax.axis_size("sub")
    n_all = n_blk * n_sub
    total_rows = float(rows * n_all)
    half = n_sub // 2
    f32 = functools.partial(jax.ShapeDtypeStruct, dtype=jnp.float32)

    whole = pl.BlockSpec(memory_space=pl.ANY)
    shapes = [(rows, t_width + s_width)] + [(rows // PARTS, t_width + s_width)] * PARTS
    packed, *parts = call(
        pack_kernel,
        [jax.ShapeDtypeStruct(shape, teacher.dtype) for shape in shapes],
        (teacher, student),
        0,
        vmem=62,
        in_specs=[whole] * 2,
        out_specs=[whole] * len(shapes),
        scratch_shapes=[pltpu.SemaphoreType.DMA((2 * len(shapes),))],
    )
    line = [parts]
    for _ in range(half):
        line.append([shifted(x, "sub", 1) for x in line[-1]])
    stats = call(
        functools.partial(stats_kernel, t_width),
        f32((1, t_width + s_width + LANES)),
        (packed,),
        4 * packed.size,
    )
    plane = [packed]
    for distance in halvings("blk"):
        if distance == 1:
            plane = list(lax.optimization_barrier(tuple(plane)))
        plane = plane + [exchange(x, "blk", distance) for x in plane]
    stats = functools.reduce(jnp.add, gathered(stats, "sub"))
    for distance in halvings("blk")[:-1]:
        stats = stats + exchange(stats, "blk", distance)
    stats_other = exchange(stats, "blk", 1)

    pair_flops = 2 * rows * rows * n_blk * (t_width + 3 * s_width)
    out_shape = (
        [f32((rows, s_width))] * half
        + [f32((n_blk, rows, s_width + LANES)), f32((n_blk, 2 * LANES))]
        + [f32(stats.shape), f32((2, LANES))]
    )
    *tiles, acc, norms, totals, early_sums = call(
        functools.partial(early_kernel, n_blk, half, t_width, total_rows),
        out_shape,
        plane + [x for pair in line[1:half] for x in pair] + [stats, stats_other],
        half * pair_flops,
    )
    own, backs = tiles[0], tiles[1:]
    returned = [shifted(x, "sub", -k) for k, x in enumerate(backs, 1)]
    mine = f32((rows * n_blk // 2 + SUBLANES, s_width))
    keep, give = call(
        functools.partial(late_kernel, n_blk, t_width, total_rows),
        [mine, mine],
        plane + line[half] + [totals, acc, norms, early_sums],
        pair_flops,
    )
    got = exchange(give, "blk", 1)
    tiles, distance = n_blk // 2, 2
    while tiles > 1:
        tiles //= 2
        out_shape = [f32((rows * tiles, s_width))] * 2
        if distance == 2:
            out_shape = out_shape + [f32((SUBLANES, LANES))]
        keep, give, *rest = call(
            functools.partial(halve_kernel, rows * tiles), out_shape, (keep, got), 2 * keep.size
        )
        got = exchange(give, "blk", distance)
        if distance == 2:
            sums = functools.reduce(jnp.add, gathered(rest[0], "sub"))
        distance *= 2
    all_sums = [sums]
    for distance in halvings("blk")[:-1]:
        all_sums = [sum(all_sums[1:], all_sums[0])]
        all_sums.append(exchange(all_sums[0], "blk", distance))
    parts = [own, keep, got] + returned
    grad, loss = call(
        functools.partial(final_kernel, len(parts), t_width, total_rows),
        [f32((rows, s_width)), f32((1, LANES))],
        [packed, totals] + parts + all_sums,
        8 * student.size,
    )
    return grad, loss[0, :1]


def solution(mesh):
    placed = P(("groups", "blk", "sub"), None)
    return jax.shard_map(
        per_device,
        mesh=mesh,
        in_specs=(placed, placed),
        out_specs=(placed, P("groups")),
        check_vma=False,
    )
```

```python
import functools

import jax
import jax.numpy as jnp
from jax import lax
from jax.experimental import pallas as pl
from jax.experimental.pallas import tpu as pltpu
from jax.sharding import PartitionSpec as P

FLOOR = 0.01
EPSILON = 1e-06
LANES = 128
CHUNK = 256
WHOLE = pl.BlockSpec(memory_space=pltpu.VMEM)


def exchange(value, axis, distance):
    size = lax.axis_size(axis)
    return lax.ppermute(value, axis, [(i, i ^ distance) for i in range(size)])


def shifted(value, axis, distance):
    size = lax.axis_size(axis)
    return lax.ppermute(value, axis, [(i, (i + distance) % size) for i in range(size)])


def pack_kernel(t_hbm, s_hbm, packed_ref, stats_ref, sems):
    t_width = t_hbm.shape[1]
    copies = [
        pltpu.make_async_copy(t_hbm, packed_ref.at[:, :t_width], sems.at[0]),
        pltpu.make_async_copy(s_hbm, packed_ref.at[:, t_width:], sems.at[1]),
    ]
    for copy in copies:
        copy.start()
    for copy in copies:
        copy.wait()
    value = packed_ref[...].astype(jnp.float32)
    squares = jnp.sum(value * value, axis=0, keepdims=True)
    square_t = jnp.sum(squares[:, :t_width], axis=1, keepdims=True)
    square_s = jnp.sum(squares[:, t_width:], axis=1, keepdims=True)
    lane = lax.broadcasted_iota(jnp.int32, (1, LANES), 1)
    width = value.shape[1]
    stats_ref[:, :width] = jnp.sum(value, axis=0, keepdims=True)
    stats_ref[:, width:] = jnp.where(lane == 0, square_t, jnp.where(lane == 1, square_s, 0.0))


def spreads_of(stats, t_width, s_width, total_rows):
    centre_t = stats[:, :t_width] / total_rows
    centre_s = stats[:, t_width : t_width + s_width] / total_rows
    square_t = stats[:, t_width + s_width : t_width + s_width + 1]
    square_s = stats[:, t_width + s_width + 1 : t_width + s_width + 2]
    spread_t = (
        2.0 * (square_t / total_rows - jnp.sum(centre_t * centre_t, axis=1, keepdims=True)) + EPSILON
    )
    spread_s = (
        2.0 * (square_s / total_rows - jnp.sum(centre_s * centre_s, axis=1, keepdims=True)) + EPSILON
    )
    return spread_t, spread_s, centre_s


def norms_of(value):
    value = value.astype(jnp.float32)
    return jnp.sum(value * value, axis=1, keepdims=True)


def as_row(column):
    rows = column.shape[0]
    row = lax.broadcasted_iota(jnp.int32, (rows, rows), 0)
    same = row == lax.broadcasted_iota(jnp.int32, (rows, rows), 1)
    return jnp.sum(jnp.where(same, column, 0.0), axis=0, keepdims=True)


def with_ones(value):
    return jnp.concatenate([value, jnp.ones((value.shape[0], LANES), value.dtype)], axis=1)


def visiting(ref, t_width):
    t, s = ref[:, :t_width], ref[:, t_width:]
    return t, s, as_row(norms_of(t)), as_row(norms_of(s))


def pair_tile(c, v, inv_t, inv_s, own):
    (ct, cs, nct, ncs), (vt, vs, nvt, nvs) = c, v
    last = (((1,), (1,)), ((), ()))
    gram_t = lax.dot_general(ct, vt, last, preferred_element_type=jnp.float32)
    gram_s = lax.dot_general(cs, vs, last, preferred_element_type=jnp.float32)
    square_t = jnp.maximum(nct + nvt - 2.0 * gram_t, 0.0)
    square_s = jnp.maximum(ncs + nvs - 2.0 * gram_s, 0.0)
    under_t = square_t * inv_t + FLOOR
    under_s = square_s * inv_s + FLOOR
    inverse_s = lax.rsqrt(under_s)
    residue = under_s * inverse_s - under_t * lax.rsqrt(under_t)
    slope = jnp.clip(residue, -1.0, 1.0)
    huber = slope * (residue - 0.5 * slope)
    pull = slope * inverse_s
    if own:
        row = lax.broadcasted_iota(jnp.int32, pull.shape, 0)
        same = row == lax.broadcasted_iota(jnp.int32, pull.shape, 1)
        pull = jnp.where(same, 0.0, pull)
        huber = jnp.where(same, 0.0, huber)
    weights = (pull * inv_s).astype(jnp.bfloat16)
    return (
        weights,
        jnp.sum(huber, axis=0, keepdims=True),
        jnp.sum(pull * square_s, axis=0, keepdims=True),
    )


def direct_of(rows, summed):
    width = rows.shape[1]
    row_weight = jnp.concatenate([summed[:, width:]] * (width // LANES), axis=1)
    return rows.astype(jnp.float32) * row_weight - summed[:, :width]


def chunks_of(ref):
    for h in range(ref.shape[0]):
        for start in range(0, ref.shape[1], CHUNK):
            yield h, pl.ds(start, min(CHUNK, ref.shape[1] - start))


def early_kernel(n_blk, steps, t_width, total_rows, *refs):
    refs = list(refs)
    tiles = [refs.pop(0) for _ in range(n_blk)]
    line = [tiles[0]] + [refs.pop(0) for _ in range(steps - 1)]
    *stats_refs, own_ref = refs[: -4 - steps]
    back_refs = refs[-4 - steps : -5]
    acc_ref, norm_ref, total_ref, sums_ref, plane_ref = refs[-5:]
    rows = own_ref.shape[0]
    for d, ref in enumerate(tiles):
        start = d % (n_blk // 2) * rows
        plane_ref[d // (n_blk // 2), start : start + rows, :] = ref[...]
    s_width = own_ref.shape[1]
    stats = stats_refs[0][...]
    for ref in stats_refs[1:]:
        stats = stats + ref[...]
    total_ref[...] = stats
    spread_t, spread_s, _ = spreads_of(stats, t_width, s_width, total_rows)
    inv_t, inv_s = 1.0 / spread_t, 1.0 / spread_s
    loss = jnp.zeros((1, LANES), jnp.float32)
    spread = jnp.zeros((1, LANES), jnp.float32)
    if steps == 1:
        acc_ref[...] = jnp.zeros_like(acc_ref)
    for h, at in chunks_of(plane_ref):
        norm_ref[h, 0, at, :] = jnp.broadcast_to(norms_of(plane_ref[h, at, :t_width]), (at.size, LANES))
        norm_ref[h, 1, at, :] = jnp.broadcast_to(norms_of(plane_ref[h, at, t_width:]), (at.size, LANES))
    for k, ref in enumerate(line):
        v = visiting(ref, t_width)
        factor = 1.0 if k == 0 else 2.0
        summed = None
        for h, at in chunks_of(plane_ref):
            cs = plane_ref[h, at, t_width:]
            c = (plane_ref[h, at, :t_width], cs, norm_ref[h, 0, at, :], norm_ref[h, 1, at, :])
            own = k == 0 and h == 0 and at.start == 0
            weights, loss_part, spread_part = pair_tile(c, v, inv_t, inv_s, own)
            loss = loss + factor * loss_part
            spread = spread + factor * spread_part
            term = lax.dot_general(
                weights,
                with_ones(cs),
                (((0,), (0,)), ((), ())),
                preferred_element_type=jnp.float32,
            )
            summed = term if summed is None else summed + term
            if k > 0:
                back = jnp.dot(weights, with_ones(v[1]), preferred_element_type=jnp.float32)
                acc_ref[h, at, :] = back if k == 1 else acc_ref[h, at, :] + back
        to_ref = own_ref if k == 0 else back_refs[k - 1]
        to_ref[...] = direct_of(v[1], summed)
    sums_ref[0:1, :] = loss
    sums_ref[1:2, :] = spread


def late_kernel(t_width, total_rows, *refs):
    plane_ref, ref, stats_ref, acc_ref, norm_ref, early_sums, keep_ref, give_ref, sums_ref = refs
    s_width = keep_ref.shape[1]
    spread_t, spread_s, _ = spreads_of(stats_ref[...], t_width, s_width, total_rows)
    inv_t, inv_s = 1.0 / spread_t, 1.0 / spread_s
    loss = early_sums[0:1, :]
    spread = early_sums[1:2, :]
    v = visiting(ref, t_width)
    for h, at in chunks_of(plane_ref):
        cs = plane_ref[h, at, t_width:]
        c = (plane_ref[h, at, :t_width], cs, norm_ref[h, 0, at, :], norm_ref[h, 1, at, :])
        weights, loss_part, spread_part = pair_tile(c, v, inv_t, inv_s, False)
        loss = loss + loss_part
        spread = spread + spread_part
        back = jnp.dot(weights, with_ones(v[1]), preferred_element_type=jnp.float32)
        to_ref = (keep_ref, give_ref)[h]
        to_ref[at, :] = direct_of(cs, acc_ref[h, at, :] + back)
    sums_ref[0:1, :] = loss
    sums_ref[1:2, :] = spread


def halve_kernel(rows, keep_ref, got_ref, *out_refs):
    out_refs[0][...] = keep_ref[:rows, :] + got_ref[:rows, :]
    out_refs[1][...] = keep_ref[rows : 2 * rows, :] + got_ref[rows : 2 * rows, :]


def add_kernel(*refs):
    *parts, out_ref = refs
    total = parts[0][...]
    for part in parts[1:]:
        total = total + part[...]
    out_ref[...] = total


def final_kernel(t_width, total_rows, packed_ref, stats_ref, direct_ref, *refs):
    *sums, grad_ref, loss_ref = refs
    rows, s_width = direct_ref.shape
    both = sums[0][...]
    for one in sums[1:]:
        both = both + one[...]
    both = jnp.sum(both, axis=1, keepdims=True)
    loss_total, spread_total = both[0:1, :], -both[1:2, :]
    _, spread_s, centre = spreads_of(stats_ref[...], t_width, s_width, total_rows)
    pairs = total_rows * (total_rows - 1.0)
    correction = 2.0 * spread_total / (pairs * spread_s * spread_s)
    student = packed_ref[:, t_width:].astype(jnp.float32)
    grad_ref[...] = (2.0 / (total_rows - 1.0)) * direct_ref[...] + correction * (student - centre)
    loss_ref[...] = jnp.broadcast_to(loss_total / pairs, loss_ref.shape)


def call(kernel, out_shape, operands, flops, vmem=48, **more):
    nbytes = sum(x.size * x.dtype.itemsize for x in operands)
    in_specs = more.pop("in_specs", [WHOLE] * len(operands))
    out_specs = more.pop("out_specs", jax.tree.map(lambda _: WHOLE, out_shape))
    return pl.pallas_call(
        kernel,
        out_shape=out_shape,
        in_specs=in_specs,
        out_specs=out_specs,
        compiler_params=pltpu.CompilerParams(vmem_limit_bytes=vmem * 1024 * 1024),
        cost_estimate=pl.CostEstimate(flops=flops, bytes_accessed=nbytes, transcendentals=0),
        **more,
    )(*operands)


def gathered(value, axis):
    return [value] + [exchange(value, axis, d) for d in range(1, lax.axis_size(axis))]


def halvings(axis):
    size = lax.axis_size(axis)
    return [size >> i for i in range(1, size.bit_length())]


def per_device(teacher, student):
    rows, t_width = teacher.shape
    s_width = student.shape[1]
    n_blk = lax.axis_size("blk")
    n_sub = lax.axis_size("sub")
    total_rows = float(rows * n_blk * n_sub)
    half = n_sub // 2
    side = rows * n_blk // 2
    f32 = functools.partial(jax.ShapeDtypeStruct, dtype=jnp.float32)

    packed, stats = call(
        pack_kernel,
        [
            jax.ShapeDtypeStruct((rows, t_width + s_width), teacher.dtype),
            f32((1, t_width + s_width + LANES)),
        ],
        (teacher, student),
        4 * teacher.size,
        vmem=62,
        in_specs=[pl.BlockSpec(memory_space=pl.ANY)] * 2,
        scratch_shapes=[pltpu.SemaphoreType.DMA((2,))],
    )
    line = [packed, shifted(packed, "sub", 1)]
    tz = [exchange(stats, "sub", d) for d in range(1, n_sub)]
    line[1], *tz = lax.optimization_barrier((line[1], *tz))
    for _ in range(half - 1):
        line.append(shifted(line[-1], "sub", 1))
    stats = functools.reduce(jnp.add, [stats] + tz)
    tiles = [packed]
    for distance in halvings("blk"):
        if distance == 1:
            *tiles, line[1] = lax.optimization_barrier((*tiles, line[1]))
        else:
            stats = stats + exchange(stats, "blk", distance)
        tiles = tiles + [exchange(x, "blk", distance) for x in tiles]
    stats = [stats, exchange(stats, "blk", 1)]

    pair_flops = 2 * rows * rows * n_blk * (t_width + 3 * s_width)
    out_shape = (
        [f32((rows, s_width))] * half
        + [f32((2, side, s_width + LANES)), f32((2, 2, side, LANES))]
        + [f32(stats[0].shape), f32((2, LANES))]
        + [jax.ShapeDtypeStruct((2, side, t_width + s_width), packed.dtype)]
    )
    *tiles, acc, norms, totals, early_sums, plane = call(
        functools.partial(early_kernel, n_blk, half, t_width, total_rows),
        out_shape,
        tiles + line[1:half] + stats,
        half * pair_flops,
    )
    own, backs = tiles[0], tiles[1:]
    returned = [shifted(x, "sub", -k) for k, x in enumerate(backs, 1)]
    keep, give, sums = call(
        functools.partial(late_kernel, t_width, total_rows),
        [f32((side, s_width))] * 2 + [f32((2, LANES))],
        [plane, line[half], totals, acc, norms, early_sums],
        pair_flops,
    )
    give, returned = lax.optimization_barrier((give, returned))
    got = exchange(give, "blk", 1)
    for distance in halvings("blk")[:-1]:
        sums = sums + exchange(sums, "blk", distance)
    tiles, distance = n_blk // 2, 2
    while tiles > 1:
        tiles //= 2
        out_shape = [f32((rows * tiles, s_width))] * 2
        keep, give = call(
            functools.partial(halve_kernel, rows * tiles), out_shape, (keep, got), 2 * keep.size
        )
        if tiles == n_blk // 4:
            give, sums = lax.optimization_barrier((give, sums))
        got = exchange(give, "blk", distance)
        distance *= 2
    sums = gathered(sums, "sub")
    direct = call(add_kernel, f32((rows, s_width)), [own, keep, got] + returned, 4 * own.size)
    *sums, direct = lax.optimization_barrier((*sums, direct))
    sums = functools.reduce(jnp.add, sums)
    all_sums = [sums, exchange(sums, "blk", 1)]
    grad, loss = call(
        functools.partial(final_kernel, t_width, total_rows),
        [f32((rows, s_width)), f32((1, LANES))],
        [packed, totals, direct] + all_sums,
        8 * student.size,
    )
    return grad, loss[0, :1]


def solution(mesh):
    placed = P(("groups", "blk", "sub"), None)
    return jax.shard_map(
        per_device,
        mesh=mesh,
        in_specs=(placed, placed),
        out_specs=(placed, P("groups")),
        check_vma=False,
    )
```

```python
import functools

import jax
import jax.numpy as jnp
from jax import lax
from jax.experimental import pallas as pl
from jax.experimental.pallas import tpu as pltpu
from jax.sharding import PartitionSpec as P

FLOOR = 0.01
EPSILON = 1e-06
LANES = 128
CHUNK = 256
WHOLE = pl.BlockSpec(memory_space=pltpu.VMEM)


def exchange(value, axis, distance):
    size = lax.axis_size(axis)
    return lax.ppermute(value, axis, [(i, i ^ distance) for i in range(size)])


def shifted(value, axis, distance):
    size = lax.axis_size(axis)
    return lax.ppermute(value, axis, [(i, (i + distance) % size) for i in range(size)])


def stats_kernel(t_width, packed_ref, stats_ref):
    value = packed_ref[...].astype(jnp.float32)
    squares = jnp.sum(value * value, axis=0, keepdims=True)
    square_t = jnp.sum(squares[:, :t_width], axis=1, keepdims=True)
    square_s = jnp.sum(squares[:, t_width:], axis=1, keepdims=True)
    lane = lax.broadcasted_iota(jnp.int32, (1, LANES), 1)
    width = value.shape[1]
    stats_ref[:, :width] = jnp.sum(value, axis=0, keepdims=True)
    stats_ref[:, width:] = jnp.where(lane == 0, square_t, jnp.where(lane == 1, square_s, 0.0))


def spreads_of(stats, t_width, s_width, total_rows):
    centre_t = stats[:, :t_width] / total_rows
    centre_s = stats[:, t_width : t_width + s_width] / total_rows
    square_t = stats[:, t_width + s_width : t_width + s_width + 1]
    square_s = stats[:, t_width + s_width + 1 : t_width + s_width + 2]
    spread_t = (
        2.0 * (square_t / total_rows - jnp.sum(centre_t * centre_t, axis=1, keepdims=True)) + EPSILON
    )
    spread_s = (
        2.0 * (square_s / total_rows - jnp.sum(centre_s * centre_s, axis=1, keepdims=True)) + EPSILON
    )
    return spread_t, spread_s, centre_s


def norms_of(value):
    value = value.astype(jnp.float32)
    return jnp.sum(value * value, axis=1, keepdims=True)


def as_row(column):
    rows = column.shape[0]
    row = lax.broadcasted_iota(jnp.int32, (rows, rows), 0)
    same = row == lax.broadcasted_iota(jnp.int32, (rows, rows), 1)
    return jnp.sum(jnp.where(same, column, 0.0), axis=0, keepdims=True)


def with_ones(value):
    return jnp.concatenate([value, jnp.ones((value.shape[0], LANES), value.dtype)], axis=1)


def visiting(ref, t_width):
    t, s = ref[:, :t_width], ref[:, t_width:]
    return t, s, as_row(norms_of(t)), as_row(norms_of(s))


def pair_tile(c, v, inv_t, inv_s, own):
    (ct, cs, nct, ncs), (vt, vs, nvt, nvs) = c, v
    last = (((1,), (1,)), ((), ()))
    gram_t = lax.dot_general(ct, vt, last, preferred_element_type=jnp.float32)
    gram_s = lax.dot_general(cs, vs, last, preferred_element_type=jnp.float32)
    square_t = jnp.maximum(nct + nvt - 2.0 * gram_t, 0.0)
    square_s = jnp.maximum(ncs + nvs - 2.0 * gram_s, 0.0)
    under_t = square_t * inv_t + FLOOR
    under_s = square_s * inv_s + FLOOR
    inverse_s = lax.rsqrt(under_s)
    residue = under_s * inverse_s - under_t * lax.rsqrt(under_t)
    slope = jnp.clip(residue, -1.0, 1.0)
    huber = slope * (residue - 0.5 * slope)
    pull = slope * inverse_s
    if own:
        row = lax.broadcasted_iota(jnp.int32, pull.shape, 0)
        same = row == lax.broadcasted_iota(jnp.int32, pull.shape, 1)
        pull = jnp.where(same, 0.0, pull)
        huber = jnp.where(same, 0.0, huber)
    weights = (pull * inv_s).astype(jnp.bfloat16)
    return (
        weights,
        jnp.sum(huber, axis=0, keepdims=True),
        jnp.sum(pull * square_s, axis=0, keepdims=True),
    )


def direct_of(rows, summed):
    width = rows.shape[1]
    row_weight = jnp.concatenate([summed[:, width:]] * (width // LANES), axis=1)
    return rows.astype(jnp.float32) * row_weight - summed[:, :width]


def chunks_of(ref):
    for h in range(ref.shape[0]):
        for start in range(0, ref.shape[1], CHUNK):
            yield h, pl.ds(start, min(CHUNK, ref.shape[1] - start))


def early_kernel(n_blk, steps, t_width, total_rows, *refs):
    refs = list(refs)
    tiles = [refs.pop(0) for _ in range(n_blk)]
    line = [tiles[0]] + [refs.pop(0) for _ in range(steps - 1)]
    *stats_refs, own_ref = refs[: -4 - steps]
    back_refs = refs[-4 - steps : -5]
    acc_ref, norm_ref, total_ref, sums_ref, plane_ref = refs[-5:]
    rows = own_ref.shape[0]
    for d, ref in enumerate(tiles):
        start = d % (n_blk // 2) * rows
        plane_ref[d // (n_blk // 2), start : start + rows, :] = ref[...]
    s_width = own_ref.shape[1]
    stats = stats_refs[0][...]
    for ref in stats_refs[1:]:
        stats = stats + ref[...]
    total_ref[...] = stats
    spread_t, spread_s, _ = spreads_of(stats, t_width, s_width, total_rows)
    inv_t, inv_s = 1.0 / spread_t, 1.0 / spread_s
    loss = jnp.zeros((1, LANES), jnp.float32)
    spread = jnp.zeros((1, LANES), jnp.float32)
    if steps == 1:
        acc_ref[...] = jnp.zeros_like(acc_ref)
    for h, at in chunks_of(plane_ref):
        norm_ref[h, 0, at, :] = jnp.broadcast_to(norms_of(plane_ref[h, at, :t_width]), (at.size, LANES))
        norm_ref[h, 1, at, :] = jnp.broadcast_to(norms_of(plane_ref[h, at, t_width:]), (at.size, LANES))
    for k, ref in enumerate(line):
        v = visiting(ref, t_width)
        factor = 1.0 if k == 0 else 2.0
        summed = None
        for h, at in chunks_of(plane_ref):
            cs = plane_ref[h, at, t_width:]
            c = (plane_ref[h, at, :t_width], cs, norm_ref[h, 0, at, :], norm_ref[h, 1, at, :])
            own = k == 0 and h == 0 and at.start == 0
            weights, loss_part, spread_part = pair_tile(c, v, inv_t, inv_s, own)
            loss = loss + factor * loss_part
            spread = spread + factor * spread_part
            term = lax.dot_general(
                weights,
                with_ones(cs),
                (((0,), (0,)), ((), ())),
                preferred_element_type=jnp.float32,
            )
            summed = term if summed is None else summed + term
            if k > 0:
                back = jnp.dot(weights, with_ones(v[1]), preferred_element_type=jnp.float32)
                acc_ref[h, at, :] = back if k == 1 else acc_ref[h, at, :] + back
        to_ref = own_ref if k == 0 else back_refs[k - 1]
        to_ref[...] = direct_of(v[1], summed)
    sums_ref[0:1, :] = loss
    sums_ref[1:2, :] = spread


def late_kernel(t_width, total_rows, *refs):
    plane_ref, ref, stats_ref, acc_ref, norm_ref, early_sums, keep_ref, give_ref, sums_ref = refs
    s_width = keep_ref.shape[1]
    spread_t, spread_s, _ = spreads_of(stats_ref[...], t_width, s_width, total_rows)
    inv_t, inv_s = 1.0 / spread_t, 1.0 / spread_s
    loss = early_sums[0:1, :]
    spread = early_sums[1:2, :]
    v = visiting(ref, t_width)
    for h, at in chunks_of(plane_ref):
        cs = plane_ref[h, at, t_width:]
        c = (plane_ref[h, at, :t_width], cs, norm_ref[h, 0, at, :], norm_ref[h, 1, at, :])
        weights, loss_part, spread_part = pair_tile(c, v, inv_t, inv_s, False)
        loss = loss + loss_part
        spread = spread + spread_part
        back = jnp.dot(weights, with_ones(v[1]), preferred_element_type=jnp.float32)
        to_ref = (keep_ref, give_ref)[h]
        to_ref[at, :] = direct_of(cs, acc_ref[h, at, :] + back)
    for i in range(sums_ref.shape[0]):
        sums_ref[i, 0:1, :] = loss
        sums_ref[i, 1:2, :] = spread


def halve_kernel(rows, keep_ref, got_ref, *out_refs):
    out_refs[0][...] = keep_ref[:rows, :] + got_ref[:rows, :]
    out_refs[1][...] = keep_ref[rows : 2 * rows, :] + got_ref[rows : 2 * rows, :]


def final_kernel(t_width, total_rows, packed_ref, stats_ref, sums_ref, *refs):
    *parts, grad_ref, loss_ref = refs
    direct = parts[0][...]
    for part in parts[1:]:
        direct = direct + part[...]
    s_width = direct.shape[1]
    both = jnp.sum(jnp.sum(sums_ref[...], axis=0), axis=1, keepdims=True)
    loss_total, spread_total = both[0:1, :], -both[1:2, :]
    _, spread_s, centre = spreads_of(stats_ref[...], t_width, s_width, total_rows)
    pairs = total_rows * (total_rows - 1.0)
    correction = 2.0 * spread_total / (pairs * spread_s * spread_s)
    student = packed_ref[:, t_width:].astype(jnp.float32)
    grad_ref[...] = (2.0 / (total_rows - 1.0)) * direct + correction * (student - centre)
    loss_ref[...] = jnp.broadcast_to(loss_total / pairs, loss_ref.shape)


def call(kernel, out_shape, operands, flops, vmem=48, **more):
    nbytes = sum(x.size * x.dtype.itemsize for x in operands)
    in_specs = more.pop("in_specs", [WHOLE] * len(operands))
    out_specs = more.pop("out_specs", jax.tree.map(lambda _: WHOLE, out_shape))
    return pl.pallas_call(
        kernel,
        out_shape=out_shape,
        in_specs=in_specs,
        out_specs=out_specs,
        compiler_params=pltpu.CompilerParams(vmem_limit_bytes=vmem * 1024 * 1024),
        cost_estimate=pl.CostEstimate(flops=flops, bytes_accessed=nbytes, transcendentals=0),
        **more,
    )(*operands)


def gathered(value, axis):
    return [value] + [exchange(value, axis, d) for d in range(1, lax.axis_size(axis))]


def halvings(axis):
    size = lax.axis_size(axis)
    return [size >> i for i in range(1, size.bit_length())]


def to_all(value):
    return lax.all_to_all(value, ("blk", "sub"), 0, 0, tiled=True)


def per_device(teacher, student):
    rows, t_width = teacher.shape
    s_width = student.shape[1]
    n_blk = lax.axis_size("blk")
    n_sub = lax.axis_size("sub")
    total_rows = float(rows * n_blk * n_sub)
    half = n_sub // 2
    side = rows * n_blk // 2
    f32 = functools.partial(jax.ShapeDtypeStruct, dtype=jnp.float32)

    packed = jnp.concatenate([teacher, student], axis=1)
    stats = call(
        functools.partial(stats_kernel, t_width),
        f32((1, t_width + s_width + LANES)),
        (packed,),
        4 * packed.size,
    )
    line = [packed, shifted(packed, "sub", 1)]
    tz = [exchange(stats, "sub", d) for d in range(1, n_sub)]
    line[1], *tz = lax.optimization_barrier((line[1], *tz))
    for _ in range(half - 1):
        line.append(shifted(line[-1], "sub", 1))
    stats = functools.reduce(jnp.add, [stats] + tz)
    tiles = [packed]
    for distance in halvings("blk"):
        if distance == 1:
            *tiles, line[1] = lax.optimization_barrier((*tiles, line[1]))
        else:
            stats = stats + exchange(stats, "blk", distance)
        tiles = tiles + [exchange(x, "blk", distance) for x in tiles]
    stats = [stats, exchange(stats, "blk", 1)]

    pair_flops = 2 * rows * rows * n_blk * (t_width + 3 * s_width)
    out_shape = (
        [f32((rows, s_width))] * half
        + [f32((2, side, s_width + LANES)), f32((2, 2, side, LANES))]
        + [f32(stats[0].shape), f32((2, LANES))]
        + [jax.ShapeDtypeStruct((2, side, t_width + s_width), packed.dtype)]
    )
    *tiles, acc, norms, totals, early_sums, plane = call(
        functools.partial(early_kernel, n_blk, half, t_width, total_rows),
        out_shape,
        tiles + line[1:half] + stats,
        half * pair_flops,
    )
    own, backs = tiles[0], tiles[1:]
    returned = [shifted(x, "sub", -k) for k, x in enumerate(backs, 1)]
    keep, give, sums = call(
        functools.partial(late_kernel, t_width, total_rows),
        [f32((side, s_width))] * 2 + [f32((n_blk * n_sub, 2, LANES))],
        [plane, line[half], totals, acc, norms, early_sums],
        pair_flops,
    )
    got = exchange(give, "blk", 1)
    tiles, distance = n_blk // 2, 2
    while tiles > 1:
        tiles //= 2
        out_shape = [f32((rows * tiles, s_width))] * 2
        keep, give = call(
            functools.partial(halve_kernel, rows * tiles), out_shape, (keep, got), 2 * keep.size
        )
        got = exchange(give, "blk", distance)
        distance *= 2
    all_sums = to_all(sums)
    parts = [own, keep, got] + returned
    grad, loss = call(
        functools.partial(final_kernel, t_width, total_rows),
        [f32((rows, s_width)), f32((1, LANES))],
        [packed, totals, all_sums] + parts,
        8 * student.size,
    )
    return grad, loss[0, :1]


def solution(mesh):
    placed = P(("groups", "blk", "sub"), None)
    return jax.shard_map(
        per_device,
        mesh=mesh,
        in_specs=(placed, placed),
        out_specs=(placed, P("groups")),
        check_vma=False,
    )
```

```python
import functools

import jax
import jax.numpy as jnp
from jax import lax
from jax.experimental import pallas as pl
from jax.experimental.pallas import tpu as pltpu
from jax.sharding import PartitionSpec as P

FLOOR = 0.01
EPSILON = 1e-06
LANES = 128
CHUNK = 256
WHOLE = pl.BlockSpec(memory_space=pltpu.VMEM)


def exchange(value, axis, distance):
    size = lax.axis_size(axis)
    return lax.ppermute(value, axis, [(i, i ^ distance) for i in range(size)])


def shifted(value, axis, distance):
    size = lax.axis_size(axis)
    places = [*range(0, size, 2), *reversed(range(1, size, 2))]
    route = [(places[i], places[(i + distance) % size]) for i in range(size)]
    return lax.ppermute(value, axis, route)


def pack_kernel(t_hbm, s_hbm, packed_ref, sems):
    t_width = t_hbm.shape[1]
    copies = [
        pltpu.make_async_copy(t_hbm, packed_ref.at[:, :t_width], sems.at[0]),
        pltpu.make_async_copy(s_hbm, packed_ref.at[:, t_width:], sems.at[1]),
    ]
    for copy in copies:
        copy.start()
    for copy in copies:
        copy.wait()


def stats_kernel(t_width, packed_ref, stats_ref):
    value = packed_ref[...].astype(jnp.float32)
    squares = jnp.sum(value * value, axis=0, keepdims=True)
    square_t = jnp.sum(squares[:, :t_width], axis=1, keepdims=True)
    square_s = jnp.sum(squares[:, t_width:], axis=1, keepdims=True)
    lane = lax.broadcasted_iota(jnp.int32, (1, LANES), 1)
    width = value.shape[1]
    stats_ref[:, :width] = jnp.sum(value, axis=0, keepdims=True)
    stats_ref[:, width:] = jnp.where(lane == 0, square_t, jnp.where(lane == 1, square_s, 0.0))


def spreads_of(stats, t_width, s_width, total_rows):
    centre_t = stats[:, :t_width] / total_rows
    centre_s = stats[:, t_width : t_width + s_width] / total_rows
    square_t = stats[:, t_width + s_width : t_width + s_width + 1]
    square_s = stats[:, t_width + s_width + 1 : t_width + s_width + 2]
    spread_t = (
        2.0 * (square_t / total_rows - jnp.sum(centre_t * centre_t, axis=1, keepdims=True)) + EPSILON
    )
    spread_s = (
        2.0 * (square_s / total_rows - jnp.sum(centre_s * centre_s, axis=1, keepdims=True)) + EPSILON
    )
    return spread_t, spread_s, centre_s


def norms_of(value):
    value = value.astype(jnp.float32)
    return jnp.sum(value * value, axis=1, keepdims=True)


def as_row(column):
    rows = column.shape[0]
    row = lax.broadcasted_iota(jnp.int32, (rows, rows), 0)
    same = row == lax.broadcasted_iota(jnp.int32, (rows, rows), 1)
    return jnp.sum(jnp.where(same, column, 0.0), axis=0, keepdims=True)


def with_ones(value):
    return jnp.concatenate([value, jnp.ones((value.shape[0], LANES), value.dtype)], axis=1)


def visiting(ref, t_width):
    t, s = ref[:, :t_width], ref[:, t_width:]
    return t, s, as_row(norms_of(t)), as_row(norms_of(s))


def pair_tile(c, v, inv_t, inv_s, own):
    (ct, cs, nct, ncs), (vt, vs, nvt, nvs) = c, v
    last = (((1,), (1,)), ((), ()))
    gram_t = lax.dot_general(ct, vt, last, preferred_element_type=jnp.float32)
    gram_s = lax.dot_general(cs, vs, last, preferred_element_type=jnp.float32)
    square_t = jnp.maximum(nct + nvt - 2.0 * gram_t, 0.0)
    square_s = jnp.maximum(ncs + nvs - 2.0 * gram_s, 0.0)
    under_t = square_t * inv_t + FLOOR
    under_s = square_s * inv_s + FLOOR
    inverse_s = lax.rsqrt(under_s)
    residue = under_s * inverse_s - under_t * lax.rsqrt(under_t)
    slope = jnp.clip(residue, -1.0, 1.0)
    huber = slope * (residue - 0.5 * slope)
    pull = slope * inverse_s
    if own:
        row = lax.broadcasted_iota(jnp.int32, pull.shape, 0)
        same = row == lax.broadcasted_iota(jnp.int32, pull.shape, 1)
        pull = jnp.where(same, 0.0, pull)
        huber = jnp.where(same, 0.0, huber)
    weights = (pull * inv_s).astype(jnp.bfloat16)
    return (
        weights,
        jnp.sum(huber, axis=0, keepdims=True),
        jnp.sum(pull * square_s, axis=0, keepdims=True),
    )


def direct_of(rows, summed):
    width = rows.shape[1]
    row_weight = jnp.concatenate([summed[:, width:]] * (width // LANES), axis=1)
    return rows.astype(jnp.float32) * row_weight - summed[:, :width]


def chunks_of(ref):
    for h in range(ref.shape[0]):
        for start in range(0, ref.shape[1], CHUNK):
            yield h, pl.ds(start, min(CHUNK, ref.shape[1] - start))


def early_kernel(n_blk, steps, t_width, total_rows, *refs):
    refs = list(refs)
    tiles = [refs.pop(0) for _ in range(n_blk)]
    line = [tiles[0]] + [refs.pop(0) for _ in range(steps - 1)]
    *stats_refs, own_ref = refs[: -4 - steps]
    back_refs = refs[-4 - steps : -5]
    acc_ref, norm_ref, total_ref, sums_ref, plane_ref = refs[-5:]
    rows = own_ref.shape[0]
    for d, ref in enumerate(tiles):
        start = d % (n_blk // 2) * rows
        plane_ref[d // (n_blk // 2), start : start + rows, :] = ref[...]
    s_width = own_ref.shape[1]
    stats = stats_refs[0][...]
    for ref in stats_refs[1:]:
        stats = stats + ref[...]
    total_ref[...] = stats
    spread_t, spread_s, _ = spreads_of(stats, t_width, s_width, total_rows)
    inv_t, inv_s = 1.0 / spread_t, 1.0 / spread_s
    loss = jnp.zeros((1, LANES), jnp.float32)
    spread = jnp.zeros((1, LANES), jnp.float32)
    if steps == 1:
        acc_ref[...] = jnp.zeros_like(acc_ref)
    for h, at in chunks_of(plane_ref):
        norm_ref[h, 0, at, :] = jnp.broadcast_to(norms_of(plane_ref[h, at, :t_width]), (at.size, LANES))
        norm_ref[h, 1, at, :] = jnp.broadcast_to(norms_of(plane_ref[h, at, t_width:]), (at.size, LANES))
    for k, ref in enumerate(line):
        v = visiting(ref, t_width)
        factor = 1.0 if k == 0 else 2.0
        summed = None
        for h, at in chunks_of(plane_ref):
            cs = plane_ref[h, at, t_width:]
            c = (plane_ref[h, at, :t_width], cs, norm_ref[h, 0, at, :], norm_ref[h, 1, at, :])
            own = k == 0 and h == 0 and at.start == 0
            weights, loss_part, spread_part = pair_tile(c, v, inv_t, inv_s, own)
            loss = loss + factor * loss_part
            spread = spread + factor * spread_part
            term = lax.dot_general(
                weights,
                with_ones(cs),
                (((0,), (0,)), ((), ())),
                preferred_element_type=jnp.float32,
            )
            summed = term if summed is None else summed + term
            if k > 0:
                back = jnp.dot(weights, with_ones(v[1]), preferred_element_type=jnp.float32)
                acc_ref[h, at, :] = back if k == 1 else acc_ref[h, at, :] + back
        to_ref = own_ref if k == 0 else back_refs[k - 1]
        to_ref[...] = direct_of(v[1], summed)
    sums_ref[0:1, :] = loss
    sums_ref[1:2, :] = spread


def late_kernel(t_width, total_rows, *refs):
    plane_ref, ref, stats_ref, acc_ref, norm_ref, early_sums, keep_ref, give_ref, sums_ref = refs
    s_width = keep_ref.shape[1]
    spread_t, spread_s, _ = spreads_of(stats_ref[...], t_width, s_width, total_rows)
    inv_t, inv_s = 1.0 / spread_t, 1.0 / spread_s
    loss = early_sums[0:1, :]
    spread = early_sums[1:2, :]
    v = visiting(ref, t_width)
    for h, at in chunks_of(plane_ref):
        cs = plane_ref[h, at, t_width:]
        c = (plane_ref[h, at, :t_width], cs, norm_ref[h, 0, at, :], norm_ref[h, 1, at, :])
        weights, loss_part, spread_part = pair_tile(c, v, inv_t, inv_s, False)
        loss = loss + loss_part
        spread = spread + spread_part
        back = jnp.dot(weights, with_ones(v[1]), preferred_element_type=jnp.float32)
        to_ref = (keep_ref, give_ref)[h]
        to_ref[at, :] = direct_of(cs, acc_ref[h, at, :] + back)
    for i in range(sums_ref.shape[0]):
        sums_ref[i, 0:1, :] = loss
        sums_ref[i, 1:2, :] = spread


def halve_kernel(rows, keep_ref, got_ref, *out_refs):
    out_refs[0][...] = keep_ref[:rows, :] + got_ref[:rows, :]
    out_refs[1][...] = keep_ref[rows : 2 * rows, :] + got_ref[rows : 2 * rows, :]


def final_kernel(t_width, total_rows, packed_ref, stats_ref, sums_ref, *refs):
    *parts, grad_ref, loss_ref = refs
    direct = parts[0][...]
    for part in parts[1:]:
        direct = direct + part[...]
    s_width = direct.shape[1]
    both = jnp.sum(jnp.sum(sums_ref[...], axis=0), axis=1, keepdims=True)
    loss_total, spread_total = both[0:1, :], -both[1:2, :]
    _, spread_s, centre = spreads_of(stats_ref[...], t_width, s_width, total_rows)
    pairs = total_rows * (total_rows - 1.0)
    correction = 2.0 * spread_total / (pairs * spread_s * spread_s)
    student = packed_ref[:, t_width:].astype(jnp.float32)
    grad_ref[...] = (2.0 / (total_rows - 1.0)) * direct + correction * (student - centre)
    loss_ref[...] = jnp.broadcast_to(loss_total / pairs, loss_ref.shape)


def call(kernel, out_shape, operands, flops, vmem=48, **more):
    nbytes = sum(x.size * x.dtype.itemsize for x in operands)
    in_specs = more.pop("in_specs", [WHOLE] * len(operands))
    out_specs = more.pop("out_specs", jax.tree.map(lambda _: WHOLE, out_shape))
    return pl.pallas_call(
        kernel,
        out_shape=out_shape,
        in_specs=in_specs,
        out_specs=out_specs,
        compiler_params=pltpu.CompilerParams(vmem_limit_bytes=vmem * 1024 * 1024),
        cost_estimate=pl.CostEstimate(flops=flops, bytes_accessed=nbytes, transcendentals=0),
        **more,
    )(*operands)


def gathered(value, axis):
    return [value] + [exchange(value, axis, d) for d in range(1, lax.axis_size(axis))]


def halvings(axis):
    size = lax.axis_size(axis)
    return [size >> i for i in range(1, size.bit_length())]


def to_all(value):
    return lax.all_to_all(value, ("blk", "sub"), 0, 0, tiled=True)


def per_device(teacher, student):
    rows, t_width = teacher.shape
    s_width = student.shape[1]
    n_blk = lax.axis_size("blk")
    n_sub = lax.axis_size("sub")
    total_rows = float(rows * n_blk * n_sub)
    half = n_sub // 2
    side = rows * n_blk // 2
    f32 = functools.partial(jax.ShapeDtypeStruct, dtype=jnp.float32)

    teacher, student = (pltpu.with_memory_space_constraint(x, pltpu.HBM) for x in (teacher, student))
    packed = call(
        pack_kernel,
        jax.ShapeDtypeStruct((rows, t_width + s_width), teacher.dtype),
        (teacher, student),
        0,
        vmem=48,
        in_specs=[pl.BlockSpec(memory_space=pl.ANY)] * 2,
        scratch_shapes=[pltpu.SemaphoreType.DMA((2,))],
    )
    stats = call(
        functools.partial(stats_kernel, t_width),
        f32((1, t_width + s_width + LANES)),
        (packed,),
        4 * packed.size,
    )
    line = [packed, shifted(packed, "sub", 1)]
    tz = [exchange(stats, "sub", d) for d in range(1, n_sub)]
    line[1], *tz = lax.optimization_barrier((line[1], *tz))
    for _ in range(half - 1):
        line.append(shifted(line[-1], "sub", 1))
    stats = functools.reduce(jnp.add, [stats] + tz)
    tiles = [packed]
    for distance in halvings("blk"):
        if distance == 1:
            *tiles, line[1] = lax.optimization_barrier((*tiles, line[1]))
        else:
            stats = stats + exchange(stats, "blk", distance)
        tiles = tiles + [exchange(x, "blk", distance) for x in tiles]
    stats = [stats, exchange(stats, "blk", 1)]

    pair_flops = 2 * rows * rows * n_blk * (t_width + 3 * s_width)
    out_shape = (
        [f32((rows, s_width))] * half
        + [f32((2, side, s_width + LANES)), f32((2, 2, side, LANES))]
        + [f32(stats[0].shape), f32((2, LANES))]
        + [jax.ShapeDtypeStruct((2, side, t_width + s_width), packed.dtype)]
    )
    *tiles, acc, norms, totals, early_sums, plane = call(
        functools.partial(early_kernel, n_blk, half, t_width, total_rows),
        out_shape,
        tiles + line[1:half] + stats,
        half * pair_flops,
    )
    own, backs = tiles[0], tiles[1:]
    returned = [shifted(x, "sub", -k) for k, x in enumerate(backs, 1)]
    keep, give, sums = call(
        functools.partial(late_kernel, t_width, total_rows),
        [f32((side, s_width))] * 2 + [f32((n_blk * n_sub, 2, LANES))],
        [plane, line[half], totals, acc, norms, early_sums],
        pair_flops,
    )
    got = exchange(give, "blk", 1)
    tiles, distance = n_blk // 2, 2
    while tiles > 1:
        tiles //= 2
        out_shape = [f32((rows * tiles, s_width))] * 2
        keep, give = call(
            functools.partial(halve_kernel, rows * tiles), out_shape, (keep, got), 2 * keep.size
        )
        got = exchange(give, "blk", distance)
        distance *= 2
    all_sums = to_all(sums)
    parts = [own, keep, got] + returned
    grad, loss = call(
        functools.partial(final_kernel, t_width, total_rows),
        [f32((rows, s_width)), f32((1, LANES))],
        [packed, totals, all_sums] + parts,
        8 * student.size,
    )
    return grad, loss[0, :1]


def solution(mesh):
    placed = P(("groups", "blk", "sub"), None)
    return jax.shard_map(
        per_device,
        mesh=mesh,
        in_specs=(placed, placed),
        out_specs=(placed, P("groups")),
        check_vma=False,
    )
```

```python
import functools

import jax
import jax.numpy as jnp
from jax import lax
from jax.experimental import pallas as pl
from jax.experimental.pallas import tpu as pltpu
from jax.sharding import PartitionSpec as P

FLOOR = 0.01
EPSILON = 1e-06
LANES = 128
CHUNK = 256
WHOLE = pl.BlockSpec(memory_space=pltpu.VMEM)


def exchange(value, axis, distance):
    size = lax.axis_size(axis)
    return lax.ppermute(value, axis, [(i, i ^ distance) for i in range(size)])


def shifted(value, axis, distance):
    size = lax.axis_size(axis)
    places = [*range(0, size, 2), *reversed(range(1, size, 2))]
    route = [(places[i], places[(i + distance) % size]) for i in range(size)]
    return lax.ppermute(value, axis, route)


def pack_kernel(t_hbm, s_hbm, packed_ref, sems):
    t_width = t_hbm.shape[1]
    copies = [
        pltpu.make_async_copy(t_hbm, packed_ref.at[:, :t_width], sems.at[0]),
        pltpu.make_async_copy(s_hbm, packed_ref.at[:, t_width:], sems.at[1]),
    ]
    for copy in copies:
        copy.start()
    for copy in copies:
        copy.wait()


def stats_kernel(t_width, packed_ref, stats_ref):
    value = packed_ref[...].astype(jnp.float32)
    squares = jnp.sum(value * value, axis=0, keepdims=True)
    square_t = jnp.sum(squares[:, :t_width], axis=1, keepdims=True)
    square_s = jnp.sum(squares[:, t_width:], axis=1, keepdims=True)
    lane = lax.broadcasted_iota(jnp.int32, (1, LANES), 1)
    width = value.shape[1]
    stats_ref[:, :width] = jnp.sum(value, axis=0, keepdims=True)
    stats_ref[:, width:] = jnp.where(lane == 0, square_t, jnp.where(lane == 1, square_s, 0.0))


def spreads_of(stats, t_width, s_width, total_rows):
    centre_t = stats[:, :t_width] / total_rows
    centre_s = stats[:, t_width : t_width + s_width] / total_rows
    square_t = stats[:, t_width + s_width : t_width + s_width + 1]
    square_s = stats[:, t_width + s_width + 1 : t_width + s_width + 2]
    spread_t = (
        2.0 * (square_t / total_rows - jnp.sum(centre_t * centre_t, axis=1, keepdims=True)) + EPSILON
    )
    spread_s = (
        2.0 * (square_s / total_rows - jnp.sum(centre_s * centre_s, axis=1, keepdims=True)) + EPSILON
    )
    return spread_t, spread_s, centre_s


def norms_of(value):
    value = value.astype(jnp.float32)
    return jnp.sum(value * value, axis=1, keepdims=True)


def as_row(column):
    rows = column.shape[0]
    row = lax.broadcasted_iota(jnp.int32, (rows, rows), 0)
    same = row == lax.broadcasted_iota(jnp.int32, (rows, rows), 1)
    return jnp.sum(jnp.where(same, column, 0.0), axis=0, keepdims=True)


def with_ones(value):
    return jnp.concatenate([value, jnp.ones((value.shape[0], LANES), value.dtype)], axis=1)


def visiting(ref, t_width):
    t, s = ref[:, :t_width], ref[:, t_width:]
    return t, s, as_row(norms_of(t)), as_row(norms_of(s))


def pair_tile(c, v, inv_t, inv_s, own):
    (ct, cs, nct, ncs), (vt, vs, nvt, nvs) = c, v
    last = (((1,), (1,)), ((), ()))
    gram_t = lax.dot_general(ct, vt, last, preferred_element_type=jnp.float32)
    gram_s = lax.dot_general(cs, vs, last, preferred_element_type=jnp.float32)
    square_t = jnp.maximum(nct + nvt - 2.0 * gram_t, 0.0)
    square_s = jnp.maximum(ncs + nvs - 2.0 * gram_s, 0.0)
    under_t = square_t * inv_t + FLOOR
    under_s = square_s * inv_s + FLOOR
    inverse_s = lax.rsqrt(under_s)
    residue = under_s * inverse_s - under_t * lax.rsqrt(under_t)
    slope = jnp.clip(residue, -1.0, 1.0)
    huber = slope * (residue - 0.5 * slope)
    pull = slope * inverse_s
    if own:
        row = lax.broadcasted_iota(jnp.int32, pull.shape, 0)
        same = row == lax.broadcasted_iota(jnp.int32, pull.shape, 1)
        pull = jnp.where(same, 0.0, pull)
        huber = jnp.where(same, 0.0, huber)
    weights = (pull * inv_s).astype(jnp.bfloat16)
    return (
        weights,
        jnp.sum(huber, axis=0, keepdims=True),
        jnp.sum(pull * square_s, axis=0, keepdims=True),
    )


def direct_of(rows, summed):
    width = rows.shape[1]
    row_weight = jnp.concatenate([summed[:, width:]] * (width // LANES), axis=1)
    return rows.astype(jnp.float32) * row_weight - summed[:, :width]


def chunks_of(ref):
    for h in range(ref.shape[0]):
        for start in range(0, ref.shape[1], CHUNK):
            yield h, pl.ds(start, min(CHUNK, ref.shape[1] - start))


def early_kernel(n_blk, steps, t_width, total_rows, *refs):
    refs = list(refs)
    tiles = [refs.pop(0) for _ in range(n_blk)]
    line = [tiles[0]] + [refs.pop(0) for _ in range(steps - 1)]
    *stats_refs, own_ref = refs[: -4 - steps]
    back_refs = refs[-4 - steps : -5]
    acc_ref, norm_ref, total_ref, sums_ref, plane_ref = refs[-5:]
    rows = own_ref.shape[0]
    for d, ref in enumerate(tiles):
        start = d % (n_blk // 2) * rows
        plane_ref[d // (n_blk // 2), start : start + rows, :] = ref[...]
    s_width = own_ref.shape[1]
    stats = stats_refs[0][...]
    for ref in stats_refs[1:]:
        stats = stats + ref[...]
    total_ref[...] = stats
    spread_t, spread_s, _ = spreads_of(stats, t_width, s_width, total_rows)
    inv_t, inv_s = 1.0 / spread_t, 1.0 / spread_s
    loss = jnp.zeros((1, LANES), jnp.float32)
    spread = jnp.zeros((1, LANES), jnp.float32)
    if steps == 1:
        acc_ref[...] = jnp.zeros_like(acc_ref)
    for h, at in chunks_of(plane_ref):
        norm_ref[h, 0, at, :] = jnp.broadcast_to(norms_of(plane_ref[h, at, :t_width]), (at.size, LANES))
        norm_ref[h, 1, at, :] = jnp.broadcast_to(norms_of(plane_ref[h, at, t_width:]), (at.size, LANES))
    for k, ref in enumerate(line):
        v = visiting(ref, t_width)
        factor = 1.0 if k == 0 else 2.0
        summed = None
        for h, at in chunks_of(plane_ref):
            cs = plane_ref[h, at, t_width:]
            c = (plane_ref[h, at, :t_width], cs, norm_ref[h, 0, at, :], norm_ref[h, 1, at, :])
            own = k == 0 and h == 0 and at.start == 0
            weights, loss_part, spread_part = pair_tile(c, v, inv_t, inv_s, own)
            loss = loss + factor * loss_part
            spread = spread + factor * spread_part
            term = lax.dot_general(
                weights,
                with_ones(cs),
                (((0,), (0,)), ((), ())),
                preferred_element_type=jnp.float32,
            )
            summed = term if summed is None else summed + term
            if k > 0:
                back = jnp.dot(weights, with_ones(v[1]), preferred_element_type=jnp.float32)
                acc_ref[h, at, :] = back if k == 1 else acc_ref[h, at, :] + back
        to_ref = own_ref if k == 0 else back_refs[k - 1]
        to_ref[...] = direct_of(v[1], summed)
    sums_ref[0:1, :] = loss
    sums_ref[1:2, :] = spread


def late_kernel(t_width, total_rows, *refs):
    plane_ref, ref, stats_ref, acc_ref, norm_ref, early_sums, keep_ref, give_ref, sums_ref = refs
    s_width = keep_ref.shape[1]
    spread_t, spread_s, _ = spreads_of(stats_ref[...], t_width, s_width, total_rows)
    inv_t, inv_s = 1.0 / spread_t, 1.0 / spread_s
    loss = early_sums[0:1, :]
    spread = early_sums[1:2, :]
    v = visiting(ref, t_width)
    for h, at in chunks_of(plane_ref):
        cs = plane_ref[h, at, t_width:]
        c = (plane_ref[h, at, :t_width], cs, norm_ref[h, 0, at, :], norm_ref[h, 1, at, :])
        weights, loss_part, spread_part = pair_tile(c, v, inv_t, inv_s, False)
        loss = loss + loss_part
        spread = spread + spread_part
        back = jnp.dot(weights, with_ones(v[1]), preferred_element_type=jnp.float32)
        to_ref = (keep_ref, give_ref)[h]
        to_ref[at, :] = direct_of(cs, acc_ref[h, at, :] + back)
    for i in range(sums_ref.shape[0]):
        sums_ref[i, 0:1, :] = loss
        sums_ref[i, 1:2, :] = spread


def halve_kernel(rows, keep_ref, got_ref, *out_refs):
    out_refs[0][...] = keep_ref[:rows, :] + got_ref[:rows, :]
    out_refs[1][...] = keep_ref[rows : 2 * rows, :] + got_ref[rows : 2 * rows, :]


def final_kernel(t_width, total_rows, packed_ref, stats_ref, sums_ref, *refs):
    *parts, grad_ref, loss_ref = refs
    direct = parts[0][...]
    for part in parts[1:]:
        direct = direct + part[...]
    s_width = direct.shape[1]
    both = jnp.sum(jnp.sum(sums_ref[...], axis=0), axis=1, keepdims=True)
    loss_total, spread_total = both[0:1, :], -both[1:2, :]
    _, spread_s, centre = spreads_of(stats_ref[...], t_width, s_width, total_rows)
    pairs = total_rows * (total_rows - 1.0)
    correction = 2.0 * spread_total / (pairs * spread_s * spread_s)
    student = packed_ref[:, t_width:].astype(jnp.float32)
    grad_ref[...] = (2.0 / (total_rows - 1.0)) * direct + correction * (student - centre)
    loss_ref[...] = jnp.broadcast_to(loss_total / pairs, loss_ref.shape)


def call(kernel, out_shape, operands, flops, vmem=48, **more):
    nbytes = sum(x.size * x.dtype.itemsize for x in operands)
    in_specs = more.pop("in_specs", [WHOLE] * len(operands))
    out_specs = more.pop("out_specs", jax.tree.map(lambda _: WHOLE, out_shape))
    return pl.pallas_call(
        kernel,
        out_shape=out_shape,
        in_specs=in_specs,
        out_specs=out_specs,
        compiler_params=pltpu.CompilerParams(vmem_limit_bytes=vmem * 1024 * 1024),
        cost_estimate=pl.CostEstimate(flops=flops, bytes_accessed=nbytes, transcendentals=0),
        **more,
    )(*operands)


def gathered(value, axis):
    return [value] + [exchange(value, axis, d) for d in range(1, lax.axis_size(axis))]


def halvings(axis):
    size = lax.axis_size(axis)
    return [size >> i for i in range(1, size.bit_length())]


def to_all(value):
    return lax.all_to_all(value, ("blk", "sub"), 0, 0, tiled=True)


def per_device(teacher, student):
    rows, t_width = teacher.shape
    s_width = student.shape[1]
    n_blk = lax.axis_size("blk")
    n_sub = lax.axis_size("sub")
    total_rows = float(rows * n_blk * n_sub)
    half = n_sub // 2
    side = rows * n_blk // 2
    f32 = functools.partial(jax.ShapeDtypeStruct, dtype=jnp.float32)

    teacher, student = (pltpu.with_memory_space_constraint(x, pltpu.HBM) for x in (teacher, student))
    packed = call(
        pack_kernel,
        jax.ShapeDtypeStruct((rows, t_width + s_width), teacher.dtype),
        (teacher, student),
        0,
        vmem=48,
        in_specs=[pl.BlockSpec(memory_space=pl.ANY)] * 2,
        scratch_shapes=[pltpu.SemaphoreType.DMA((2,))],
    )
    stats = call(
        functools.partial(stats_kernel, t_width),
        f32((1, t_width + s_width + LANES)),
        (packed,),
        4 * packed.size,
    )
    line = [packed, shifted(packed, "sub", 1)]
    tz = [exchange(stats, "sub", d) for d in range(1, n_sub)]
    line[1], *tz = lax.optimization_barrier((line[1], *tz))
    for _ in range(half - 1):
        line.append(shifted(line[-1], "sub", 1))
    stats = functools.reduce(jnp.add, [stats] + tz)
    tiles = [packed]
    for distance in halvings("blk"):
        if distance == 1:
            *tiles, line[1] = lax.optimization_barrier((*tiles, line[1]))
        else:
            stats = stats + exchange(stats, "blk", distance)
        tiles = tiles + [exchange(x, "blk", distance) for x in tiles]
    stats = [stats, exchange(stats, "blk", 1)]

    pair_flops = 2 * rows * rows * n_blk * (t_width + 3 * s_width)
    out_shape = (
        [f32((rows, s_width))] * half
        + [f32((2, side, s_width + LANES)), f32((2, 2, side, LANES))]
        + [f32(stats[0].shape), f32((2, LANES))]
        + [jax.ShapeDtypeStruct((2, side, t_width + s_width), packed.dtype)]
    )
    *tiles, acc, norms, totals, early_sums, plane = call(
        functools.partial(early_kernel, n_blk, half, t_width, total_rows),
        out_shape,
        tiles + line[1:half] + stats,
        half * pair_flops,
    )
    own, backs = tiles[0], tiles[1:]
    keep, give, sums = call(
        functools.partial(late_kernel, t_width, total_rows),
        [f32((side, s_width))] * 2 + [f32((n_blk * n_sub, 2, LANES))],
        [plane, line[half], totals, acc, norms, early_sums],
        pair_flops,
    )
    got = exchange(give, "blk", 1)
    all_sums = to_all(sums)
    got, all_sums, backs = lax.optimization_barrier((got, all_sums, backs))
    returned = [shifted(x, "sub", -k) for k, x in enumerate(backs, 1)]
    tiles, distance = n_blk // 2, 2
    while tiles > 1:
        tiles //= 2
        out_shape = [f32((rows * tiles, s_width))] * 2
        keep, give = call(
            functools.partial(halve_kernel, rows * tiles), out_shape, (keep, got), 2 * keep.size
        )
        got = exchange(give, "blk", distance)
        distance *= 2
    parts = [own, keep, got] + returned
    grad, loss = call(
        functools.partial(final_kernel, t_width, total_rows),
        [f32((rows, s_width)), f32((1, LANES))],
        [packed, totals, all_sums] + parts,
        8 * student.size,
    )
    return grad, loss[0, :1]


def solution(mesh):
    placed = P(("groups", "blk", "sub"), None)
    return jax.shard_map(
        per_device,
        mesh=mesh,
        in_specs=(placed, placed),
        out_specs=(placed, P("groups")),
        check_vma=False,
    )
```

```python
import functools

import jax
import jax.numpy as jnp
from jax import lax
from jax.experimental import pallas as pl
from jax.experimental.pallas import tpu as pltpu
from jax.sharding import PartitionSpec as P

FLOOR = 0.01
EPSILON = 1e-06
LANES = 128
CHUNK = 256
WHOLE = pl.BlockSpec(memory_space=pltpu.VMEM)


def exchange(value, axis, distance):
    size = lax.axis_size(axis)
    return lax.ppermute(value, axis, [(i, i ^ distance) for i in range(size)])


def shifted(value, axis, distance):
    size = lax.axis_size(axis)
    places = [*range(0, size, 2), *reversed(range(1, size, 2))]
    route = [(places[i], places[(i + distance) % size]) for i in range(size)]
    return lax.ppermute(value, axis, route)


def pack_kernel(t_hbm, s_hbm, packed_ref, sems):
    t_width = t_hbm.shape[1]
    copies = [
        pltpu.make_async_copy(t_hbm, packed_ref.at[:, :t_width], sems.at[0]),
        pltpu.make_async_copy(s_hbm, packed_ref.at[:, t_width:], sems.at[1]),
    ]
    for copy in copies:
        copy.start()
    for copy in copies:
        copy.wait()


def stats_kernel(t_width, packed_ref, stats_ref):
    value = packed_ref[...].astype(jnp.float32)
    squares = jnp.sum(value * value, axis=0, keepdims=True)
    square_t = jnp.sum(squares[:, :t_width], axis=1, keepdims=True)
    square_s = jnp.sum(squares[:, t_width:], axis=1, keepdims=True)
    lane = lax.broadcasted_iota(jnp.int32, (1, LANES), 1)
    width = value.shape[1]
    stats_ref[:, :width] = jnp.sum(value, axis=0, keepdims=True)
    stats_ref[:, width:] = jnp.where(lane == 0, square_t, jnp.where(lane == 1, square_s, 0.0))


def spreads_of(stats, t_width, s_width, total_rows):
    centre_t = stats[:, :t_width] / total_rows
    centre_s = stats[:, t_width : t_width + s_width] / total_rows
    square_t = stats[:, t_width + s_width : t_width + s_width + 1]
    square_s = stats[:, t_width + s_width + 1 : t_width + s_width + 2]
    spread_t = (
        2.0 * (square_t / total_rows - jnp.sum(centre_t * centre_t, axis=1, keepdims=True)) + EPSILON
    )
    spread_s = (
        2.0 * (square_s / total_rows - jnp.sum(centre_s * centre_s, axis=1, keepdims=True)) + EPSILON
    )
    return spread_t, spread_s, centre_s


def norms_of(value):
    value = value.astype(jnp.float32)
    return jnp.sum(value * value, axis=1, keepdims=True)


def as_row(column):
    rows = column.shape[0]
    row = lax.broadcasted_iota(jnp.int32, (rows, rows), 0)
    same = row == lax.broadcasted_iota(jnp.int32, (rows, rows), 1)
    return jnp.sum(jnp.where(same, column, 0.0), axis=0, keepdims=True)


def with_ones(value):
    return jnp.concatenate([value, jnp.ones((value.shape[0], LANES), value.dtype)], axis=1)


def visiting(ref, t_width):
    t, s = ref[:, :t_width], ref[:, t_width:]
    return t, s, as_row(norms_of(t)), as_row(norms_of(s))


def pair_tile(c, v, inv_t, inv_s, own):
    (ct, cs, nct, ncs), (vt, vs, nvt, nvs) = c, v
    last = (((1,), (1,)), ((), ()))
    gram_t = lax.dot_general(ct, vt, last, preferred_element_type=jnp.float32)
    gram_s = lax.dot_general(cs, vs, last, preferred_element_type=jnp.float32)
    square_t = jnp.maximum(nct + nvt - 2.0 * gram_t, 0.0)
    square_s = jnp.maximum(ncs + nvs - 2.0 * gram_s, 0.0)
    under_t = square_t * inv_t + FLOOR
    under_s = square_s * inv_s + FLOOR
    inverse_s = lax.rsqrt(under_s)
    residue = under_s * inverse_s - under_t * lax.rsqrt(under_t)
    slope = jnp.clip(residue, -1.0, 1.0)
    huber = slope * (residue - 0.5 * slope)
    pull = slope * inverse_s
    if own:
        row = lax.broadcasted_iota(jnp.int32, pull.shape, 0)
        same = row == lax.broadcasted_iota(jnp.int32, pull.shape, 1)
        pull = jnp.where(same, 0.0, pull)
        huber = jnp.where(same, 0.0, huber)
    weights = (pull * inv_s).astype(jnp.bfloat16)
    return (
        weights,
        jnp.sum(huber, axis=0, keepdims=True),
        jnp.sum(pull * square_s, axis=0, keepdims=True),
    )


def direct_of(rows, summed):
    width = rows.shape[1]
    row_weight = jnp.concatenate([summed[:, width:]] * (width // LANES), axis=1)
    return rows.astype(jnp.float32) * row_weight - summed[:, :width]


def chunks_of(ref):
    for h in range(ref.shape[0]):
        for start in range(0, ref.shape[1], CHUNK):
            yield h, pl.ds(start, min(CHUNK, ref.shape[1] - start))


def early_kernel(n_blk, steps, t_width, total_rows, *refs):
    refs = list(refs)
    tiles = [refs.pop(0) for _ in range(n_blk)]
    line = [tiles[0]] + [refs.pop(0) for _ in range(steps - 1)]
    *stats_refs, own_ref = refs[: -4 - steps]
    back_refs = refs[-4 - steps : -5]
    acc_ref, norm_ref, total_ref, sums_ref, plane_ref = refs[-5:]
    rows = own_ref.shape[0]
    for d, ref in enumerate(tiles):
        start = d % (n_blk // 2) * rows
        plane_ref[d // (n_blk // 2), start : start + rows, :] = ref[...]
    s_width = own_ref.shape[1]
    stats = stats_refs[0][...]
    for ref in stats_refs[1:]:
        stats = stats + ref[...]
    total_ref[...] = stats
    spread_t, spread_s, _ = spreads_of(stats, t_width, s_width, total_rows)
    inv_t, inv_s = 1.0 / spread_t, 1.0 / spread_s
    loss = jnp.zeros((1, LANES), jnp.float32)
    spread = jnp.zeros((1, LANES), jnp.float32)
    if steps == 1:
        acc_ref[...] = jnp.zeros_like(acc_ref)
    for h, at in chunks_of(plane_ref):
        norm_ref[h, 0, at, :] = jnp.broadcast_to(norms_of(plane_ref[h, at, :t_width]), (at.size, LANES))
        norm_ref[h, 1, at, :] = jnp.broadcast_to(norms_of(plane_ref[h, at, t_width:]), (at.size, LANES))
    for k, ref in enumerate(line):
        v = visiting(ref, t_width)
        factor = 1.0 if k == 0 else 2.0
        summed = None
        for h, at in chunks_of(plane_ref):
            cs = plane_ref[h, at, t_width:]
            c = (plane_ref[h, at, :t_width], cs, norm_ref[h, 0, at, :], norm_ref[h, 1, at, :])
            own = k == 0 and h == 0 and at.start == 0
            weights, loss_part, spread_part = pair_tile(c, v, inv_t, inv_s, own)
            loss = loss + factor * loss_part
            spread = spread + factor * spread_part
            term = lax.dot_general(
                weights,
                with_ones(cs),
                (((0,), (0,)), ((), ())),
                preferred_element_type=jnp.float32,
            )
            summed = term if summed is None else summed + term
            if k > 0:
                back = jnp.dot(weights, with_ones(v[1]), preferred_element_type=jnp.float32)
                acc_ref[h, at, :] = back if k == 1 else acc_ref[h, at, :] + back
        to_ref = own_ref if k == 0 else back_refs[k - 1]
        to_ref[...] = direct_of(v[1], summed)
    sums_ref[0:1, :] = loss
    sums_ref[1:2, :] = spread


def late_kernel(t_width, total_rows, *refs):
    plane_ref, ref, stats_ref, acc_ref, norm_ref, early_sums, keep_ref, give_ref, sums_ref = refs
    s_width = keep_ref.shape[1]
    spread_t, spread_s, _ = spreads_of(stats_ref[...], t_width, s_width, total_rows)
    inv_t, inv_s = 1.0 / spread_t, 1.0 / spread_s
    loss = early_sums[0:1, :]
    spread = early_sums[1:2, :]
    v = visiting(ref, t_width)
    for h, at in chunks_of(plane_ref):
        cs = plane_ref[h, at, t_width:]
        c = (plane_ref[h, at, :t_width], cs, norm_ref[h, 0, at, :], norm_ref[h, 1, at, :])
        weights, loss_part, spread_part = pair_tile(c, v, inv_t, inv_s, False)
        loss = loss + loss_part
        spread = spread + spread_part
        back = jnp.dot(weights, with_ones(v[1]), preferred_element_type=jnp.float32)
        to_ref = (keep_ref, give_ref)[h]
        to_ref[at, :] = direct_of(cs, acc_ref[h, at, :] + back)
    sums_ref[0:1, :] = loss
    sums_ref[1:2, :] = spread


def halve_kernel(rows, keep_ref, got_ref, *out_refs):
    out_refs[0][...] = keep_ref[:rows, :] + got_ref[:rows, :]
    out_refs[1][...] = keep_ref[rows : 2 * rows, :] + got_ref[rows : 2 * rows, :]


def final_kernel(n_parts, t_width, total_rows, packed_ref, stats_ref, *refs):
    *inputs, grad_ref, loss_ref = refs
    direct = inputs[0][...]
    for part in inputs[1:n_parts]:
        direct = direct + part[...]
    both = inputs[n_parts][...]
    for sums in inputs[n_parts + 1 :]:
        both = both + sums[...]
    s_width = direct.shape[1]
    both = jnp.sum(both, axis=1, keepdims=True)
    loss_total, spread_total = both[0:1, :], -both[1:2, :]
    _, spread_s, centre = spreads_of(stats_ref[...], t_width, s_width, total_rows)
    pairs = total_rows * (total_rows - 1.0)
    correction = 2.0 * spread_total / (pairs * spread_s * spread_s)
    student = packed_ref[:, t_width:].astype(jnp.float32)
    grad_ref[...] = (2.0 / (total_rows - 1.0)) * direct + correction * (student - centre)
    loss_ref[...] = jnp.broadcast_to(loss_total / pairs, loss_ref.shape)


def call(kernel, out_shape, operands, flops, vmem=48, **more):
    nbytes = sum(x.size * x.dtype.itemsize for x in operands)
    in_specs = more.pop("in_specs", [WHOLE] * len(operands))
    out_specs = more.pop("out_specs", jax.tree.map(lambda _: WHOLE, out_shape))
    return pl.pallas_call(
        kernel,
        out_shape=out_shape,
        in_specs=in_specs,
        out_specs=out_specs,
        compiler_params=pltpu.CompilerParams(vmem_limit_bytes=vmem * 1024 * 1024),
        cost_estimate=pl.CostEstimate(flops=flops, bytes_accessed=nbytes, transcendentals=0),
        **more,
    )(*operands)


def gathered(value, axis):
    return [value] + [exchange(value, axis, d) for d in range(1, lax.axis_size(axis))]


def halvings(axis):
    size = lax.axis_size(axis)
    return [size >> i for i in range(1, size.bit_length())]


def per_device(teacher, student):
    rows, t_width = teacher.shape
    s_width = student.shape[1]
    n_blk = lax.axis_size("blk")
    n_sub = lax.axis_size("sub")
    total_rows = float(rows * n_blk * n_sub)
    half = n_sub // 2
    side = rows * n_blk // 2
    f32 = functools.partial(jax.ShapeDtypeStruct, dtype=jnp.float32)

    teacher, student = (pltpu.with_memory_space_constraint(x, pltpu.HBM) for x in (teacher, student))
    packed = call(
        pack_kernel,
        jax.ShapeDtypeStruct((rows, t_width + s_width), teacher.dtype),
        (teacher, student),
        0,
        vmem=48,
        in_specs=[pl.BlockSpec(memory_space=pl.ANY)] * 2,
        scratch_shapes=[pltpu.SemaphoreType.DMA((2,))],
    )
    stats = call(
        functools.partial(stats_kernel, t_width),
        f32((1, t_width + s_width + LANES)),
        (packed,),
        4 * packed.size,
    )
    line = [packed, shifted(packed, "sub", 1)]
    tz = [exchange(stats, "sub", d) for d in range(1, n_sub)]
    line[1], *tz = lax.optimization_barrier((line[1], *tz))
    for _ in range(half - 1):
        line.append(shifted(line[-1], "sub", 1))
    stats = functools.reduce(jnp.add, [stats] + tz)
    tiles = [packed]
    for distance in halvings("blk"):
        if distance == 1:
            *tiles, line[1] = lax.optimization_barrier((*tiles, line[1]))
        else:
            stats = stats + exchange(stats, "blk", distance)
        tiles = tiles + [exchange(x, "blk", distance) for x in tiles]
    stats = [stats, exchange(stats, "blk", 1)]

    pair_flops = 2 * rows * rows * n_blk * (t_width + 3 * s_width)
    out_shape = (
        [f32((rows, s_width))] * half
        + [f32((2, side, s_width + LANES)), f32((2, 2, side, LANES))]
        + [f32(stats[0].shape), f32((2, LANES))]
        + [jax.ShapeDtypeStruct((2, side, t_width + s_width), packed.dtype)]
    )
    *tiles, acc, norms, totals, early_sums, plane = call(
        functools.partial(early_kernel, n_blk, half, t_width, total_rows),
        out_shape,
        tiles + line[1:half] + stats,
        half * pair_flops,
    )
    own, backs = tiles[0], tiles[1:]
    returned = [shifted(x, "sub", -k) for k, x in enumerate(backs, 1)]
    keep, give, sums = call(
        functools.partial(late_kernel, t_width, total_rows),
        [f32((side, s_width))] * 2 + [f32((2, LANES))],
        [plane, line[half], totals, acc, norms, early_sums],
        pair_flops,
    )
    got = exchange(give, "blk", 1)
    for distance in halvings("blk")[:-1]:
        sums = sums + exchange(sums, "blk", distance)
    got, sums = lax.optimization_barrier((got, sums))
    sums = sums + exchange(sums, "blk", 1)
    all_sums = gathered(sums, "sub")
    tiles, distance = n_blk // 2, 2
    while tiles > 1:
        tiles //= 2
        out_shape = [f32((rows * tiles, s_width))] * 2
        keep, give = call(
            functools.partial(halve_kernel, rows * tiles), out_shape, (keep, got), 2 * keep.size
        )
        got = exchange(give, "blk", distance)
        distance *= 2
    parts = [own, keep, got] + returned
    grad, loss = call(
        functools.partial(final_kernel, len(parts), t_width, total_rows),
        [f32((rows, s_width)), f32((1, LANES))],
        [packed, totals] + parts + all_sums,
        8 * student.size,
    )
    return grad, loss[0, :1]


def solution(mesh):
    placed = P(("groups", "blk", "sub"), None)
    return jax.shard_map(
        per_device,
        mesh=mesh,
        in_specs=(placed, placed),
        out_specs=(placed, P("groups")),
        check_vma=False,
    )
```

```python
import functools

import jax
import jax.numpy as jnp
from jax import lax
from jax.experimental import pallas as pl
from jax.experimental.pallas import tpu as pltpu
from jax.sharding import PartitionSpec as P

FLOOR = 0.01
EPSILON = 1e-06
LANES = 128
CHUNK = 256
WHOLE = pl.BlockSpec(memory_space=pltpu.VMEM)


def exchange(value, axis, distance):
    size = lax.axis_size(axis)
    return lax.ppermute(value, axis, [(i, i ^ distance) for i in range(size)])


def shifted(value, axis, distance):
    size = lax.axis_size(axis)
    places = [*range(0, size, 2), *reversed(range(1, size, 2))]
    route = [(places[i], places[(i + distance) % size]) for i in range(size)]
    return lax.ppermute(value, axis, route)


def pack_kernel(t_hbm, s_hbm, packed_ref, sems):
    t_width = t_hbm.shape[1]
    copies = [
        pltpu.make_async_copy(t_hbm, packed_ref.at[:, :t_width], sems.at[0]),
        pltpu.make_async_copy(s_hbm, packed_ref.at[:, t_width:], sems.at[1]),
    ]
    for copy in copies:
        copy.start()
    for copy in copies:
        copy.wait()


def stats_kernel(t_width, packed_ref, stats_ref):
    value = packed_ref[...].astype(jnp.float32)
    squares = jnp.sum(value * value, axis=0, keepdims=True)
    square_t = jnp.sum(squares[:, :t_width], axis=1, keepdims=True)
    square_s = jnp.sum(squares[:, t_width:], axis=1, keepdims=True)
    lane = lax.broadcasted_iota(jnp.int32, (1, LANES), 1)
    width = value.shape[1]
    stats_ref[:, :width] = jnp.sum(value, axis=0, keepdims=True)
    stats_ref[:, width:] = jnp.where(lane == 0, square_t, jnp.where(lane == 1, square_s, 0.0))


def spreads_of(stats, t_width, s_width, total_rows):
    centre_t = stats[:, :t_width] / total_rows
    centre_s = stats[:, t_width : t_width + s_width] / total_rows
    square_t = stats[:, t_width + s_width : t_width + s_width + 1]
    square_s = stats[:, t_width + s_width + 1 : t_width + s_width + 2]
    spread_t = (
        2.0 * (square_t / total_rows - jnp.sum(centre_t * centre_t, axis=1, keepdims=True)) + EPSILON
    )
    spread_s = (
        2.0 * (square_s / total_rows - jnp.sum(centre_s * centre_s, axis=1, keepdims=True)) + EPSILON
    )
    return spread_t, spread_s, centre_s


def norms_of(value):
    value = value.astype(jnp.float32)
    return jnp.sum(value * value, axis=1, keepdims=True)


def as_row(column):
    rows = column.shape[0]
    row = lax.broadcasted_iota(jnp.int32, (rows, rows), 0)
    same = row == lax.broadcasted_iota(jnp.int32, (rows, rows), 1)
    return jnp.sum(jnp.where(same, column, 0.0), axis=0, keepdims=True)


def with_ones(value):
    return jnp.concatenate([value, jnp.ones((value.shape[0], LANES), value.dtype)], axis=1)


def visiting(ref, t_width):
    t, s = ref[:, :t_width], ref[:, t_width:]
    return t, s, as_row(norms_of(t)), as_row(norms_of(s))


def pair_tile(c, v, inv_t, inv_s, own):
    (ct, cs, nct, ncs), (vt, vs, nvt, nvs) = c, v
    last = (((1,), (1,)), ((), ()))
    gram_t = lax.dot_general(ct, vt, last, preferred_element_type=jnp.float32)
    gram_s = lax.dot_general(cs, vs, last, preferred_element_type=jnp.float32)
    square_t = jnp.maximum(nct + nvt - 2.0 * gram_t, 0.0)
    square_s = jnp.maximum(ncs + nvs - 2.0 * gram_s, 0.0)
    under_t = square_t * inv_t + FLOOR
    under_s = square_s * inv_s + FLOOR
    inverse_s = lax.rsqrt(under_s)
    residue = under_s * inverse_s - under_t * lax.rsqrt(under_t)
    slope = jnp.clip(residue, -1.0, 1.0)
    huber = slope * (residue - 0.5 * slope)
    pull = slope * inverse_s
    if own:
        row = lax.broadcasted_iota(jnp.int32, pull.shape, 0)
        same = row == lax.broadcasted_iota(jnp.int32, pull.shape, 1)
        pull = jnp.where(same, 0.0, pull)
        huber = jnp.where(same, 0.0, huber)
    weights = (pull * inv_s).astype(jnp.bfloat16)
    return (
        weights,
        jnp.sum(huber, axis=0, keepdims=True),
        jnp.sum(pull * square_s, axis=0, keepdims=True),
    )


def direct_of(rows, summed):
    width = rows.shape[1]
    row_weight = jnp.concatenate([summed[:, width:]] * (width // LANES), axis=1)
    return rows.astype(jnp.float32) * row_weight - summed[:, :width]


def chunks_of(ref):
    for h in range(ref.shape[0]):
        for start in range(0, ref.shape[1], CHUNK):
            yield h, pl.ds(start, min(CHUNK, ref.shape[1] - start))


def early_kernel(n_blk, steps, t_width, total_rows, *refs):
    refs = list(refs)
    tiles = [refs.pop(0) for _ in range(n_blk)]
    line = [tiles[0]] + [refs.pop(0) for _ in range(steps - 1)]
    *stats_refs, own_ref = refs[: -4 - steps]
    back_refs = refs[-4 - steps : -5]
    acc_ref, norm_ref, total_ref, sums_ref, plane_ref = refs[-5:]
    rows = own_ref.shape[0]
    for d, ref in enumerate(tiles):
        start = d % (n_blk // 2) * rows
        plane_ref[d // (n_blk // 2), start : start + rows, :] = ref[...]
    s_width = own_ref.shape[1]
    stats = stats_refs[0][...]
    for ref in stats_refs[1:]:
        stats = stats + ref[...]
    total_ref[...] = stats
    spread_t, spread_s, _ = spreads_of(stats, t_width, s_width, total_rows)
    inv_t, inv_s = 1.0 / spread_t, 1.0 / spread_s
    loss = jnp.zeros((1, LANES), jnp.float32)
    spread = jnp.zeros((1, LANES), jnp.float32)
    if steps == 1:
        acc_ref[...] = jnp.zeros_like(acc_ref)
    for h, at in chunks_of(plane_ref):
        norm_ref[h, 0, at, :] = jnp.broadcast_to(norms_of(plane_ref[h, at, :t_width]), (at.size, LANES))
        norm_ref[h, 1, at, :] = jnp.broadcast_to(norms_of(plane_ref[h, at, t_width:]), (at.size, LANES))
    for k, ref in enumerate(line):
        v = visiting(ref, t_width)
        factor = 1.0 if k == 0 else 2.0
        summed = None
        for h, at in chunks_of(plane_ref):
            cs = plane_ref[h, at, t_width:]
            c = (plane_ref[h, at, :t_width], cs, norm_ref[h, 0, at, :], norm_ref[h, 1, at, :])
            own = k == 0 and h == 0 and at.start == 0
            weights, loss_part, spread_part = pair_tile(c, v, inv_t, inv_s, own)
            loss = loss + factor * loss_part
            spread = spread + factor * spread_part
            term = lax.dot_general(
                weights,
                with_ones(cs),
                (((0,), (0,)), ((), ())),
                preferred_element_type=jnp.float32,
            )
            summed = term if summed is None else summed + term
            if k > 0:
                back = jnp.dot(weights, with_ones(v[1]), preferred_element_type=jnp.float32)
                acc_ref[h, at, :] = back if k == 1 else acc_ref[h, at, :] + back
        to_ref = own_ref if k == 0 else back_refs[k - 1]
        to_ref[...] = direct_of(v[1], summed)
    sums_ref[0:1, :] = loss
    sums_ref[1:2, :] = spread


def late_kernel(t_width, total_rows, *refs):
    plane_ref, ref, stats_ref, acc_ref, norm_ref, early_sums, keep_ref, give_ref, sums_ref = refs
    s_width = keep_ref.shape[1]
    spread_t, spread_s, _ = spreads_of(stats_ref[...], t_width, s_width, total_rows)
    inv_t, inv_s = 1.0 / spread_t, 1.0 / spread_s
    loss = early_sums[0:1, :]
    spread = early_sums[1:2, :]
    v = visiting(ref, t_width)
    for h, at in chunks_of(plane_ref):
        cs = plane_ref[h, at, t_width:]
        c = (plane_ref[h, at, :t_width], cs, norm_ref[h, 0, at, :], norm_ref[h, 1, at, :])
        weights, loss_part, spread_part = pair_tile(c, v, inv_t, inv_s, False)
        loss = loss + loss_part
        spread = spread + spread_part
        back = jnp.dot(weights, with_ones(v[1]), preferred_element_type=jnp.float32)
        to_ref = (keep_ref, give_ref)[h]
        to_ref[at, :] = direct_of(cs, acc_ref[h, at, :] + back)
    for i in range(sums_ref.shape[0]):
        sums_ref[i, 0:1, :] = loss
        sums_ref[i, 1:2, :] = spread


def halve_kernel(rows, keep_ref, got_ref, *out_refs):
    out_refs[0][...] = keep_ref[:rows, :] + got_ref[:rows, :]
    out_refs[1][...] = keep_ref[rows : 2 * rows, :] + got_ref[rows : 2 * rows, :]


def final_kernel(t_width, total_rows, packed_ref, stats_ref, sums_ref, *refs):
    *parts, grad_ref, loss_ref = refs
    direct = parts[0][...]
    for part in parts[1:]:
        direct = direct + part[...]
    s_width = direct.shape[1]
    both = jnp.sum(jnp.sum(sums_ref[...], axis=0), axis=1, keepdims=True)
    loss_total, spread_total = both[0:1, :], -both[1:2, :]
    _, spread_s, centre = spreads_of(stats_ref[...], t_width, s_width, total_rows)
    pairs = total_rows * (total_rows - 1.0)
    correction = 2.0 * spread_total / (pairs * spread_s * spread_s)
    student = packed_ref[:, t_width:].astype(jnp.float32)
    grad_ref[...] = (2.0 / (total_rows - 1.0)) * direct + correction * (student - centre)
    loss_ref[...] = jnp.broadcast_to(loss_total / pairs, loss_ref.shape)


def call(kernel, out_shape, operands, flops, vmem=48, **more):
    nbytes = sum(x.size * x.dtype.itemsize for x in operands)
    in_specs = more.pop("in_specs", [WHOLE] * len(operands))
    out_specs = more.pop("out_specs", jax.tree.map(lambda _: WHOLE, out_shape))
    return pl.pallas_call(
        kernel,
        out_shape=out_shape,
        in_specs=in_specs,
        out_specs=out_specs,
        compiler_params=pltpu.CompilerParams(vmem_limit_bytes=vmem * 1024 * 1024),
        cost_estimate=pl.CostEstimate(flops=flops, bytes_accessed=nbytes, transcendentals=0),
        **more,
    )(*operands)


def gathered(value, axis):
    return [value] + [exchange(value, axis, d) for d in range(1, lax.axis_size(axis))]


def halvings(axis):
    size = lax.axis_size(axis)
    return [size >> i for i in range(1, size.bit_length())]


def to_all(value, axis):
    return lax.all_to_all(value, axis, 0, 0, tiled=True)


def per_device(teacher, student):
    rows, t_width = teacher.shape
    s_width = student.shape[1]
    n_blk = lax.axis_size("blk")
    n_sub = lax.axis_size("sub")
    total_rows = float(rows * n_blk * n_sub)
    half = n_sub // 2
    side = rows * n_blk // 2
    f32 = functools.partial(jax.ShapeDtypeStruct, dtype=jnp.float32)

    teacher, student = (pltpu.with_memory_space_constraint(x, pltpu.HBM) for x in (teacher, student))
    packed = call(
        pack_kernel,
        jax.ShapeDtypeStruct((rows, t_width + s_width), teacher.dtype),
        (teacher, student),
        0,
        vmem=48,
        in_specs=[pl.BlockSpec(memory_space=pl.ANY)] * 2,
        scratch_shapes=[pltpu.SemaphoreType.DMA((2,))],
    )
    stats = call(
        functools.partial(stats_kernel, t_width),
        f32((1, t_width + s_width + LANES)),
        (packed,),
        4 * packed.size,
    )
    line = [packed, shifted(packed, "sub", 1)]
    tz = [exchange(stats, "sub", d) for d in range(1, n_sub)]
    line[1], *tz = lax.optimization_barrier((line[1], *tz))
    for _ in range(half - 1):
        line.append(shifted(line[-1], "sub", 1))
    stats = functools.reduce(jnp.add, [stats] + tz)
    tiles = [packed]
    for distance in halvings("blk"):
        if distance == 1:
            *tiles, line[1] = lax.optimization_barrier((*tiles, line[1]))
        else:
            stats = stats + exchange(stats, "blk", distance)
        tiles = tiles + [exchange(x, "blk", distance) for x in tiles]
    stats = [stats, exchange(stats, "blk", 1)]

    pair_flops = 2 * rows * rows * n_blk * (t_width + 3 * s_width)
    out_shape = (
        [f32((rows, s_width))] * half
        + [f32((2, side, s_width + LANES)), f32((2, 2, side, LANES))]
        + [f32(stats[0].shape), f32((2, LANES))]
        + [jax.ShapeDtypeStruct((2, side, t_width + s_width), packed.dtype)]
    )
    *tiles, acc, norms, totals, early_sums, plane = call(
        functools.partial(early_kernel, n_blk, half, t_width, total_rows),
        out_shape,
        tiles + line[1:half] + stats,
        half * pair_flops,
    )
    own, backs = tiles[0], tiles[1:]
    returned = [shifted(x, "sub", -k) for k, x in enumerate(backs, 1)]
    keep, give, sums = call(
        functools.partial(late_kernel, t_width, total_rows),
        [f32((side, s_width))] * 2 + [f32((n_blk, 2, LANES))],
        [plane, line[half], totals, acc, norms, early_sums],
        pair_flops,
    )
    got = exchange(give, "blk", 1)
    sums = jnp.sum(to_all(sums, "blk"), axis=0)
    got, sums = lax.optimization_barrier((got, sums))
    all_sums = to_all(jnp.broadcast_to(sums[None], (n_sub, *sums.shape)), "sub")
    tiles, distance = n_blk // 2, 2
    while tiles > 1:
        tiles //= 2
        out_shape = [f32((rows * tiles, s_width))] * 2
        keep, give = call(
            functools.partial(halve_kernel, rows * tiles), out_shape, (keep, got), 2 * keep.size
        )
        got = exchange(give, "blk", distance)
        distance *= 2
    parts = [own, keep, got] + returned
    grad, loss = call(
        functools.partial(final_kernel, t_width, total_rows),
        [f32((rows, s_width)), f32((1, LANES))],
        [packed, totals, all_sums] + parts,
        8 * student.size,
    )
    return grad, loss[0, :1]


def solution(mesh):
    placed = P(("groups", "blk", "sub"), None)
    return jax.shard_map(
        per_device,
        mesh=mesh,
        in_specs=(placed, placed),
        out_specs=(placed, P("groups")),
        check_vma=False,
    )
```

```python
import functools

import jax
import jax.numpy as jnp
from jax import lax
from jax.experimental import pallas as pl
from jax.experimental.pallas import tpu as pltpu
from jax.sharding import PartitionSpec as P

FLOOR = 0.01
EPSILON = 1e-06
LANES = 128
SUBLANES = 8
CHUNK = 256
WHOLE = pl.BlockSpec(memory_space=pltpu.VMEM)


BLK = ("y", "core")
PART = ("y", "core", "sub")


def exchange(value, distance, axis=BLK):
    size = lax.axis_size(axis)
    return lax.ppermute(value, axis, [(i, i ^ distance) for i in range(size)])


def shifted(value, axis, distance):
    size = lax.axis_size(axis)
    places = [*range(0, size, 2), *reversed(range(1, size, 2))]
    route = [(places[i], places[(i + distance) % size]) for i in range(size)]
    return lax.ppermute(value, axis, route)


def pack_kernel(t_hbm, s_hbm, packed_ref, sems):
    t_width = t_hbm.shape[1]
    copies = [
        pltpu.make_async_copy(t_hbm, packed_ref.at[:, :t_width], sems.at[0]),
        pltpu.make_async_copy(s_hbm, packed_ref.at[:, t_width:], sems.at[1]),
    ]
    for copy in copies:
        copy.start()
    for copy in copies:
        copy.wait()


def stats_kernel(t_width, packed_ref, stats_ref):
    value = packed_ref[...].astype(jnp.float32)
    squares = jnp.sum(value * value, axis=0, keepdims=True)
    square_t = jnp.sum(squares[:, :t_width], axis=1, keepdims=True)
    square_s = jnp.sum(squares[:, t_width:], axis=1, keepdims=True)
    lane = lax.broadcasted_iota(jnp.int32, (1, LANES), 1)
    width = value.shape[1]
    stats_ref[:, :width] = jnp.sum(value, axis=0, keepdims=True)
    stats_ref[:, width:] = jnp.where(lane == 0, square_t, jnp.where(lane == 1, square_s, 0.0))


def spreads_of(stats, t_width, s_width, total_rows):
    centre_t = stats[:, :t_width] / total_rows
    centre_s = stats[:, t_width : t_width + s_width] / total_rows
    square_t = stats[:, t_width + s_width : t_width + s_width + 1]
    square_s = stats[:, t_width + s_width + 1 : t_width + s_width + 2]
    spread_t = (
        2.0 * (square_t / total_rows - jnp.sum(centre_t * centre_t, axis=1, keepdims=True)) + EPSILON
    )
    spread_s = (
        2.0 * (square_s / total_rows - jnp.sum(centre_s * centre_s, axis=1, keepdims=True)) + EPSILON
    )
    return spread_t, spread_s, centre_s


def norms_of(value):
    value = value.astype(jnp.float32)
    return jnp.sum(value * value, axis=1, keepdims=True)


def as_row(column):
    rows = column.shape[0]
    row = lax.broadcasted_iota(jnp.int32, (rows, rows), 0)
    same = row == lax.broadcasted_iota(jnp.int32, (rows, rows), 1)
    return jnp.sum(jnp.where(same, column, 0.0), axis=0, keepdims=True)


def with_ones(value):
    return jnp.concatenate([value, jnp.ones((value.shape[0], LANES), value.dtype)], axis=1)


def visiting(ref, t_width):
    t, s = ref[:, :t_width], ref[:, t_width:]
    return t, s, as_row(norms_of(t)), as_row(norms_of(s))


def pair_tile(c, v, inv_t, inv_s, own):
    (ct, cs, nct, ncs), (vt, vs, nvt, nvs) = c, v
    last = (((1,), (1,)), ((), ()))
    gram_t = lax.dot_general(ct, vt, last, preferred_element_type=jnp.float32)
    gram_s = lax.dot_general(cs, vs, last, preferred_element_type=jnp.float32)
    square_t = jnp.maximum(nct + nvt - 2.0 * gram_t, 0.0)
    square_s = jnp.maximum(ncs + nvs - 2.0 * gram_s, 0.0)
    under_t = square_t * inv_t + FLOOR
    under_s = square_s * inv_s + FLOOR
    inverse_s = lax.rsqrt(under_s)
    residue = under_s * inverse_s - under_t * lax.rsqrt(under_t)
    slope = jnp.clip(residue, -1.0, 1.0)
    huber = slope * (residue - 0.5 * slope)
    pull = slope * inverse_s
    if own:
        row = lax.broadcasted_iota(jnp.int32, pull.shape, 0)
        same = row == lax.broadcasted_iota(jnp.int32, pull.shape, 1)
        pull = jnp.where(same, 0.0, pull)
        huber = jnp.where(same, 0.0, huber)
    weights = (pull * inv_s).astype(jnp.bfloat16)
    return (
        weights,
        jnp.sum(huber, axis=0, keepdims=True),
        jnp.sum(pull * square_s, axis=0, keepdims=True),
    )


def direct_of(rows, summed):
    width = rows.shape[1]
    row_weight = jnp.concatenate([summed[:, width:]] * (width // LANES), axis=1)
    return rows.astype(jnp.float32) * row_weight - summed[:, :width]


def chunks_of(ref):
    for h in range(ref.shape[0]):
        for start in range(0, ref.shape[1], CHUNK):
            yield h, pl.ds(start, min(CHUNK, ref.shape[1] - start))


def early_kernel(n_blk, steps, t_width, total_rows, *refs):
    refs = list(refs)
    tiles = [refs.pop(0) for _ in range(n_blk)]
    line = [tiles[0]] + [refs.pop(0) for _ in range(steps - 1)]
    *stats_refs, own_ref = refs[: -4 - steps]
    back_refs = refs[-4 - steps : -5]
    acc_ref, norm_ref, total_ref, sums_ref, plane_ref = refs[-5:]
    rows = own_ref.shape[0]
    for d, ref in enumerate(tiles):
        start = d % (n_blk // 2) * rows
        plane_ref[d // (n_blk // 2), start : start + rows, :] = ref[...]
    s_width = own_ref.shape[1]
    stats = stats_refs[0][...]
    for ref in stats_refs[1:]:
        stats = stats + ref[...]
    total_ref[...] = stats
    spread_t, spread_s, _ = spreads_of(stats, t_width, s_width, total_rows)
    inv_t, inv_s = 1.0 / spread_t, 1.0 / spread_s
    loss = jnp.zeros((1, LANES), jnp.float32)
    spread = jnp.zeros((1, LANES), jnp.float32)
    if steps == 1:
        acc_ref[...] = jnp.zeros_like(acc_ref)
    for h, at in chunks_of(plane_ref):
        norm_ref[h, 0, at, :] = jnp.broadcast_to(norms_of(plane_ref[h, at, :t_width]), (at.size, LANES))
        norm_ref[h, 1, at, :] = jnp.broadcast_to(norms_of(plane_ref[h, at, t_width:]), (at.size, LANES))
    for k, ref in enumerate(line):
        v = visiting(ref, t_width)
        factor = 1.0 if k == 0 else 2.0
        summed = None
        for h, at in chunks_of(plane_ref):
            cs = plane_ref[h, at, t_width:]
            c = (plane_ref[h, at, :t_width], cs, norm_ref[h, 0, at, :], norm_ref[h, 1, at, :])
            own = k == 0 and h == 0 and at.start == 0
            weights, loss_part, spread_part = pair_tile(c, v, inv_t, inv_s, own)
            loss = loss + factor * loss_part
            spread = spread + factor * spread_part
            term = lax.dot_general(
                weights,
                with_ones(cs),
                (((0,), (0,)), ((), ())),
                preferred_element_type=jnp.float32,
            )
            summed = term if summed is None else summed + term
            if k > 0:
                back = jnp.dot(weights, with_ones(v[1]), preferred_element_type=jnp.float32)
                acc_ref[h, at, :] = back if k == 1 else acc_ref[h, at, :] + back
        to_ref = own_ref if k == 0 else back_refs[k - 1]
        to_ref[...] = direct_of(v[1], summed)
    sums_ref[0:1, :] = loss
    sums_ref[1:2, :] = spread


def late_kernel(t_width, total_rows, *refs):
    plane_ref, ref, stats_ref, acc_ref, norm_ref, early_sums, keep_ref, give_ref = refs
    s_width = keep_ref.shape[1]
    spread_t, spread_s, _ = spreads_of(stats_ref[...], t_width, s_width, total_rows)
    inv_t, inv_s = 1.0 / spread_t, 1.0 / spread_s
    loss = early_sums[0:1, :]
    spread = early_sums[1:2, :]
    v = visiting(ref, t_width)
    for h, at in chunks_of(plane_ref):
        cs = plane_ref[h, at, t_width:]
        c = (plane_ref[h, at, :t_width], cs, norm_ref[h, 0, at, :], norm_ref[h, 1, at, :])
        weights, loss_part, spread_part = pair_tile(c, v, inv_t, inv_s, False)
        loss = loss + loss_part
        spread = spread + spread_part
        back = jnp.dot(weights, with_ones(v[1]), preferred_element_type=jnp.float32)
        to_ref = (keep_ref, give_ref)[h]
        to_ref[at, :] = direct_of(cs, acc_ref[h, at, :] + back)
    for ref in (keep_ref, give_ref):
        ref[-SUBLANES:, :] = jnp.zeros((SUBLANES, s_width), jnp.float32)
        ref[-SUBLANES : 1 - SUBLANES, :LANES] = loss
        ref[1 - SUBLANES : 2 - SUBLANES, :LANES] = spread


def halve_kernel(rows, keep_ref, got_ref, *out_refs):
    for ref in out_refs[2:]:
        sums = keep_ref[-SUBLANES:, :LANES] + got_ref[-SUBLANES:, :LANES]
        for i in range(ref.shape[0]):
            ref[i] = sums[: ref.shape[1]]
    out_refs[0][...] = keep_ref[:rows, :] + got_ref[:rows, :]
    out_refs[1][...] = keep_ref[rows : 2 * rows, :] + got_ref[rows : 2 * rows, :]


def final_kernel(t_width, total_rows, packed_ref, stats_ref, sums_ref, *refs):
    *parts, grad_ref, loss_ref = refs
    direct = parts[0][...]
    for part in parts[1:]:
        direct = direct + part[...]
    s_width = direct.shape[1]
    both = jnp.sum(jnp.sum(sums_ref[...], axis=0), axis=1, keepdims=True)
    loss_total, spread_total = both[0:1, :], -both[1:2, :]
    _, spread_s, centre = spreads_of(stats_ref[...], t_width, s_width, total_rows)
    pairs = total_rows * (total_rows - 1.0)
    correction = 2.0 * spread_total / (pairs * spread_s * spread_s)
    student = packed_ref[:, t_width:].astype(jnp.float32)
    grad_ref[...] = (2.0 / (total_rows - 1.0)) * direct + correction * (student - centre)
    loss_ref[...] = jnp.broadcast_to(loss_total / pairs, loss_ref.shape)


def call(kernel, out_shape, operands, flops, vmem=48, **more):
    nbytes = sum(x.size * x.dtype.itemsize for x in operands)
    in_specs = more.pop("in_specs", [WHOLE] * len(operands))
    out_specs = more.pop("out_specs", jax.tree.map(lambda _: WHOLE, out_shape))
    return pl.pallas_call(
        kernel,
        out_shape=out_shape,
        in_specs=in_specs,
        out_specs=out_specs,
        compiler_params=pltpu.CompilerParams(vmem_limit_bytes=vmem * 1024 * 1024),
        cost_estimate=pl.CostEstimate(flops=flops, bytes_accessed=nbytes, transcendentals=0),
        **more,
    )(*operands)


def gathered(value, axis):
    return [value] + [exchange(value, d, axis) for d in range(1, lax.axis_size(axis))]


def halvings(axis):
    size = lax.axis_size(axis)
    return [size >> i for i in range(1, size.bit_length())]


def to_all(value):
    return lax.all_to_all(value, ("y", "sub"), 0, 0, tiled=True)


def per_device(teacher, student):
    rows, t_width = teacher.shape
    s_width = student.shape[1]
    n_blk = lax.axis_size(BLK)
    n_sub = lax.axis_size("sub")
    total_rows = float(rows * n_blk * n_sub)
    half = n_sub // 2
    side = rows * n_blk // 2
    f32 = functools.partial(jax.ShapeDtypeStruct, dtype=jnp.float32)

    teacher, student = (pltpu.with_memory_space_constraint(x, pltpu.HBM) for x in (teacher, student))
    packed = call(
        pack_kernel,
        jax.ShapeDtypeStruct((rows, t_width + s_width), teacher.dtype),
        (teacher, student),
        0,
        vmem=48,
        in_specs=[pl.BlockSpec(memory_space=pl.ANY)] * 2,
        scratch_shapes=[pltpu.SemaphoreType.DMA((2,))],
    )
    stats = call(
        functools.partial(stats_kernel, t_width),
        f32((1, t_width + s_width + LANES)),
        (packed,),
        4 * packed.size,
    )
    line = [packed, shifted(packed, "sub", 1)]
    tz = [exchange(stats, d, "sub") for d in range(1, n_sub)]
    line[1], *tz = lax.optimization_barrier((line[1], *tz))
    for _ in range(half - 1):
        line.append(shifted(line[-1], "sub", 1))
    stats = functools.reduce(jnp.add, [stats] + tz)
    tiles = [packed]
    for distance in halvings(BLK):
        if distance == 1:
            *tiles, line[1] = lax.optimization_barrier((*tiles, line[1]))
        else:
            stats = stats + exchange(stats, distance)
        tiles = tiles + [exchange(x, distance) for x in tiles]
    stats = [stats, exchange(stats, 1)]

    pair_flops = 2 * rows * rows * n_blk * (t_width + 3 * s_width)
    out_shape = (
        [f32((rows, s_width))] * half
        + [f32((2, side, s_width + LANES)), f32((2, 2, side, LANES))]
        + [f32(stats[0].shape), f32((2, LANES))]
        + [jax.ShapeDtypeStruct((2, side, t_width + s_width), packed.dtype)]
    )
    *tiles, acc, norms, totals, early_sums, plane = call(
        functools.partial(early_kernel, n_blk, half, t_width, total_rows),
        out_shape,
        tiles + line[1:half] + stats,
        half * pair_flops,
    )
    own, backs = tiles[0], tiles[1:]
    returned = [shifted(x, "sub", -k) for k, x in enumerate(backs, 1)]
    keep, give = call(
        functools.partial(late_kernel, t_width, total_rows),
        [f32((side + SUBLANES, s_width))] * 2,
        [plane, line[half], totals, acc, norms, early_sums],
        pair_flops,
    )
    got = exchange(give, 1)
    tiles, distance, all_sums = n_blk // 2, 2, None
    while tiles > 1:
        tiles //= 2
        out_shape = [f32((rows * tiles, s_width))] * 2
        if all_sums is None:
            out_shape = out_shape + [f32((n_blk // 2 * n_sub, 2, LANES))]
        keep, give, *sums = call(
            functools.partial(halve_kernel, rows * tiles), out_shape, (keep, got), 2 * keep.size
        )
        got = exchange(give, distance)
        if all_sums is None:
            all_sums = to_all(sums[0])
        distance *= 2
    parts = [own, keep, got] + returned
    grad, loss = call(
        functools.partial(final_kernel, t_width, total_rows),
        [f32((rows, s_width)), f32((1, LANES))],
        [packed, totals, all_sums] + parts,
        8 * student.size,
    )
    return grad, loss[0, :1]


def solution(mesh):
    groups, blk, sub = (mesh.shape[name] for name in ("groups", "blk", "sub"))
    devices = mesh.devices.reshape(groups, blk // 2, 2, sub)
    split = jax.sharding.Mesh(devices, ("groups", *PART))
    placed = P(("groups", *PART), None)
    return jax.shard_map(
        per_device,
        mesh=split,
        in_specs=(placed, placed),
        out_specs=(placed, P("groups")),
        check_vma=False,
    )
```

```python
import functools

import jax
import jax.numpy as jnp
from jax import lax
from jax.experimental import pallas as pl
from jax.experimental.pallas import tpu as pltpu
from jax.sharding import PartitionSpec as P

FLOOR = 0.01
EPSILON = 1e-06
LANES = 128
CHUNK = 256
WHOLE = pl.BlockSpec(memory_space=pltpu.VMEM)


BLK = ("y", "core")
PART = ("y", "core", "sub")


def exchange(value, distance, axis=BLK):
    size = lax.axis_size(axis)
    return lax.ppermute(value, axis, [(i, i ^ distance) for i in range(size)])


def shifted(value, axis, distance):
    size = lax.axis_size(axis)
    places = [*range(0, size, 2), *reversed(range(1, size, 2))]
    route = [(places[i], places[(i + distance) % size]) for i in range(size)]
    return lax.ppermute(value, axis, route)


def pack_kernel(t_hbm, s_hbm, packed_ref, sems):
    t_width = t_hbm.shape[1]
    copies = [
        pltpu.make_async_copy(t_hbm, packed_ref.at[:, :t_width], sems.at[0]),
        pltpu.make_async_copy(s_hbm, packed_ref.at[:, t_width:], sems.at[1]),
    ]
    for copy in copies:
        copy.start()
    for copy in copies:
        copy.wait()


def stats_kernel(t_width, packed_ref, stats_ref):
    value = packed_ref[...].astype(jnp.float32)
    squares = jnp.sum(value * value, axis=0, keepdims=True)
    square_t = jnp.sum(squares[:, :t_width], axis=1, keepdims=True)
    square_s = jnp.sum(squares[:, t_width:], axis=1, keepdims=True)
    lane = lax.broadcasted_iota(jnp.int32, (1, LANES), 1)
    width = value.shape[1]
    stats_ref[:, :width] = jnp.sum(value, axis=0, keepdims=True)
    stats_ref[:, width:] = jnp.where(lane == 0, square_t, jnp.where(lane == 1, square_s, 0.0))


def spreads_of(stats, t_width, s_width, total_rows):
    centre_t = stats[:, :t_width] / total_rows
    centre_s = stats[:, t_width : t_width + s_width] / total_rows
    square_t = stats[:, t_width + s_width : t_width + s_width + 1]
    square_s = stats[:, t_width + s_width + 1 : t_width + s_width + 2]
    spread_t = (
        2.0 * (square_t / total_rows - jnp.sum(centre_t * centre_t, axis=1, keepdims=True)) + EPSILON
    )
    spread_s = (
        2.0 * (square_s / total_rows - jnp.sum(centre_s * centre_s, axis=1, keepdims=True)) + EPSILON
    )
    return spread_t, spread_s, centre_s


def norms_of(value):
    value = value.astype(jnp.float32)
    return jnp.sum(value * value, axis=1, keepdims=True)


def as_row(column):
    rows = column.shape[0]
    row = lax.broadcasted_iota(jnp.int32, (rows, rows), 0)
    same = row == lax.broadcasted_iota(jnp.int32, (rows, rows), 1)
    return jnp.sum(jnp.where(same, column, 0.0), axis=0, keepdims=True)


def with_ones(value):
    return jnp.concatenate([value, jnp.ones((value.shape[0], LANES), value.dtype)], axis=1)


def visiting(ref, t_width):
    t, s = ref[:, :t_width], ref[:, t_width:]
    return t, s, as_row(norms_of(t)), as_row(norms_of(s))


def pair_tile(c, v, inv_t, inv_s, own):
    (ct, cs, nct, ncs), (vt, vs, nvt, nvs) = c, v
    last = (((1,), (1,)), ((), ()))
    gram_t = lax.dot_general(ct, vt, last, preferred_element_type=jnp.float32)
    gram_s = lax.dot_general(cs, vs, last, preferred_element_type=jnp.float32)
    square_t = jnp.maximum(nct + nvt - 2.0 * gram_t, 0.0)
    square_s = jnp.maximum(ncs + nvs - 2.0 * gram_s, 0.0)
    under_t = square_t * inv_t + FLOOR
    under_s = square_s * inv_s + FLOOR
    inverse_s = lax.rsqrt(under_s)
    residue = under_s * inverse_s - under_t * lax.rsqrt(under_t)
    slope = jnp.clip(residue, -1.0, 1.0)
    huber = slope * (residue - 0.5 * slope)
    pull = slope * inverse_s
    if own:
        row = lax.broadcasted_iota(jnp.int32, pull.shape, 0)
        same = row == lax.broadcasted_iota(jnp.int32, pull.shape, 1)
        pull = jnp.where(same, 0.0, pull)
        huber = jnp.where(same, 0.0, huber)
    weights = (pull * inv_s).astype(jnp.bfloat16)
    return (
        weights,
        jnp.sum(huber, axis=0, keepdims=True),
        jnp.sum(pull * square_s, axis=0, keepdims=True),
    )


def direct_of(rows, summed):
    width = rows.shape[1]
    row_weight = jnp.concatenate([summed[:, width:]] * (width // LANES), axis=1)
    return rows.astype(jnp.float32) * row_weight - summed[:, :width]


def chunks_of(ref):
    for h in range(ref.shape[0]):
        for start in range(0, ref.shape[1], CHUNK):
            yield h, pl.ds(start, min(CHUNK, ref.shape[1] - start))


def early_kernel(n_blk, steps, t_width, total_rows, *refs):
    refs = list(refs)
    tiles = [refs.pop(0) for _ in range(n_blk)]
    line = [tiles[0]] + [refs.pop(0) for _ in range(steps - 1)]
    *stats_refs, own_ref = refs[: -4 - steps]
    back_refs = refs[-4 - steps : -5]
    acc_ref, norm_ref, total_ref, sums_ref, plane_ref = refs[-5:]
    rows = own_ref.shape[0]
    for d, ref in enumerate(tiles):
        start = d % (n_blk // 2) * rows
        plane_ref[d // (n_blk // 2), start : start + rows, :] = ref[...]
    s_width = own_ref.shape[1]
    stats = stats_refs[0][...]
    for ref in stats_refs[1:]:
        stats = stats + ref[...]
    total_ref[...] = stats
    spread_t, spread_s, _ = spreads_of(stats, t_width, s_width, total_rows)
    inv_t, inv_s = 1.0 / spread_t, 1.0 / spread_s
    loss = jnp.zeros((1, LANES), jnp.float32)
    spread = jnp.zeros((1, LANES), jnp.float32)
    if steps == 1:
        acc_ref[...] = jnp.zeros_like(acc_ref)
    for h, at in chunks_of(plane_ref):
        norm_ref[h, 0, at, :] = jnp.broadcast_to(norms_of(plane_ref[h, at, :t_width]), (at.size, LANES))
        norm_ref[h, 1, at, :] = jnp.broadcast_to(norms_of(plane_ref[h, at, t_width:]), (at.size, LANES))
    for k, ref in enumerate(line):
        v = visiting(ref, t_width)
        factor = 1.0 if k == 0 else 2.0
        summed = None
        for h, at in chunks_of(plane_ref):
            cs = plane_ref[h, at, t_width:]
            c = (plane_ref[h, at, :t_width], cs, norm_ref[h, 0, at, :], norm_ref[h, 1, at, :])
            own = k == 0 and h == 0 and at.start == 0
            weights, loss_part, spread_part = pair_tile(c, v, inv_t, inv_s, own)
            loss = loss + factor * loss_part
            spread = spread + factor * spread_part
            term = lax.dot_general(
                weights,
                with_ones(cs),
                (((0,), (0,)), ((), ())),
                preferred_element_type=jnp.float32,
            )
            summed = term if summed is None else summed + term
            if k > 0:
                back = jnp.dot(weights, with_ones(v[1]), preferred_element_type=jnp.float32)
                acc_ref[h, at, :] = back if k == 1 else acc_ref[h, at, :] + back
        to_ref = own_ref if k == 0 else back_refs[k - 1]
        to_ref[...] = direct_of(v[1], summed)
    sums_ref[0:1, :] = loss
    sums_ref[1:2, :] = spread


def late_kernel(t_width, total_rows, *refs):
    plane_ref, ref, stats_ref, acc_ref, norm_ref, early_sums, keep_ref, give_ref, sums_ref = refs
    s_width = keep_ref.shape[1]
    spread_t, spread_s, _ = spreads_of(stats_ref[...], t_width, s_width, total_rows)
    inv_t, inv_s = 1.0 / spread_t, 1.0 / spread_s
    loss = early_sums[0:1, :]
    spread = early_sums[1:2, :]
    v = visiting(ref, t_width)
    for h, at in chunks_of(plane_ref):
        cs = plane_ref[h, at, t_width:]
        c = (plane_ref[h, at, :t_width], cs, norm_ref[h, 0, at, :], norm_ref[h, 1, at, :])
        weights, loss_part, spread_part = pair_tile(c, v, inv_t, inv_s, False)
        loss = loss + loss_part
        spread = spread + spread_part
        back = jnp.dot(weights, with_ones(v[1]), preferred_element_type=jnp.float32)
        to_ref = (keep_ref, give_ref)[h]
        to_ref[at, :] = direct_of(cs, acc_ref[h, at, :] + back)
    for i in range(sums_ref.shape[0]):
        sums_ref[i, 0:1, :] = loss
        sums_ref[i, 1:2, :] = spread


def halve_kernel(rows, keep_ref, got_ref, *out_refs):
    out_refs[0][...] = keep_ref[:rows, :] + got_ref[:rows, :]
    out_refs[1][...] = keep_ref[rows : 2 * rows, :] + got_ref[rows : 2 * rows, :]


def final_kernel(t_width, total_rows, packed_ref, stats_ref, sums_ref, other_ref, *refs):
    *parts, grad_ref, loss_ref = refs
    direct = parts[0][...]
    for part in parts[1:]:
        direct = direct + part[...]
    s_width = direct.shape[1]
    both = jnp.sum(sums_ref[...] + other_ref[...], axis=1, keepdims=True)
    loss_total, spread_total = both[0:1, :], -both[1:2, :]
    _, spread_s, centre = spreads_of(stats_ref[...], t_width, s_width, total_rows)
    pairs = total_rows * (total_rows - 1.0)
    correction = 2.0 * spread_total / (pairs * spread_s * spread_s)
    student = packed_ref[:, t_width:].astype(jnp.float32)
    grad_ref[...] = (2.0 / (total_rows - 1.0)) * direct + correction * (student - centre)
    loss_ref[...] = jnp.broadcast_to(loss_total / pairs, loss_ref.shape)


def call(kernel, out_shape, operands, flops, vmem=48, **more):
    nbytes = sum(x.size * x.dtype.itemsize for x in operands)
    in_specs = more.pop("in_specs", [WHOLE] * len(operands))
    out_specs = more.pop("out_specs", jax.tree.map(lambda _: WHOLE, out_shape))
    return pl.pallas_call(
        kernel,
        out_shape=out_shape,
        in_specs=in_specs,
        out_specs=out_specs,
        compiler_params=pltpu.CompilerParams(vmem_limit_bytes=vmem * 1024 * 1024),
        cost_estimate=pl.CostEstimate(flops=flops, bytes_accessed=nbytes, transcendentals=0),
        **more,
    )(*operands)


def gathered(value, axis):
    return [value] + [exchange(value, d, axis) for d in range(1, lax.axis_size(axis))]


def halvings(axis):
    size = lax.axis_size(axis)
    return [size >> i for i in range(1, size.bit_length())]


def to_all(value):
    return lax.all_to_all(value, ("y", "sub"), 0, 0, tiled=True)


def per_device(teacher, student):
    rows, t_width = teacher.shape
    s_width = student.shape[1]
    n_blk = lax.axis_size(BLK)
    n_sub = lax.axis_size("sub")
    total_rows = float(rows * n_blk * n_sub)
    half = n_sub // 2
    side = rows * n_blk // 2
    f32 = functools.partial(jax.ShapeDtypeStruct, dtype=jnp.float32)

    teacher, student = (pltpu.with_memory_space_constraint(x, pltpu.HBM) for x in (teacher, student))
    packed = call(
        pack_kernel,
        jax.ShapeDtypeStruct((rows, t_width + s_width), teacher.dtype),
        (teacher, student),
        0,
        vmem=48,
        in_specs=[pl.BlockSpec(memory_space=pl.ANY)] * 2,
        scratch_shapes=[pltpu.SemaphoreType.DMA((2,))],
    )
    stats = call(
        functools.partial(stats_kernel, t_width),
        f32((1, t_width + s_width + LANES)),
        (packed,),
        4 * packed.size,
    )
    line = [packed, shifted(packed, "sub", 1)]
    tz = [exchange(stats, d, "sub") for d in range(1, n_sub)]
    line[1], *tz = lax.optimization_barrier((line[1], *tz))
    for _ in range(half - 1):
        line.append(shifted(line[-1], "sub", 1))
    stats = functools.reduce(jnp.add, [stats] + tz)
    tiles = [packed]
    for distance in halvings(BLK):
        if distance == 1:
            *tiles, line[1] = lax.optimization_barrier((*tiles, line[1]))
        else:
            stats = stats + exchange(stats, distance)
        tiles = tiles + [exchange(x, distance) for x in tiles]
    stats = [stats, exchange(stats, 1)]

    pair_flops = 2 * rows * rows * n_blk * (t_width + 3 * s_width)
    out_shape = (
        [f32((rows, s_width))] * half
        + [f32((2, side, s_width + LANES)), f32((2, 2, side, LANES))]
        + [f32(stats[0].shape), f32((2, LANES))]
        + [jax.ShapeDtypeStruct((2, side, t_width + s_width), packed.dtype)]
    )
    *tiles, acc, norms, totals, early_sums, plane = call(
        functools.partial(early_kernel, n_blk, half, t_width, total_rows),
        out_shape,
        tiles + line[1:half] + stats,
        half * pair_flops,
    )
    own, backs = tiles[0], tiles[1:]
    returned = [shifted(x, "sub", -k) for k, x in enumerate(backs, 1)]
    keep, give, sums = call(
        functools.partial(late_kernel, t_width, total_rows),
        [f32((side, s_width))] * 2 + [f32((n_blk // 2 * n_sub, 2, LANES))],
        [plane, line[half], totals, acc, norms, early_sums],
        pair_flops,
    )
    got = exchange(give, 1)
    sums = jnp.sum(to_all(sums), axis=0)
    got, sums = lax.optimization_barrier((got, sums))
    tiles, distance = n_blk // 2, 2
    while tiles > 1:
        tiles //= 2
        out_shape = [f32((rows * tiles, s_width))] * 2
        keep, give = call(
            functools.partial(halve_kernel, rows * tiles), out_shape, (keep, got), 2 * keep.size
        )
        got = exchange(give, distance)
        distance *= 2
    all_sums = [sums, exchange(sums, 1)]
    parts = [own, keep, got] + returned
    grad, loss = call(
        functools.partial(final_kernel, t_width, total_rows),
        [f32((rows, s_width)), f32((1, LANES))],
        [packed, totals, *all_sums] + parts,
        8 * student.size,
    )
    return grad, loss[0, :1]


def solution(mesh):
    groups, blk, sub = (mesh.shape[name] for name in ("groups", "blk", "sub"))
    devices = mesh.devices.reshape(groups, blk // 2, 2, sub)
    split = jax.sharding.Mesh(devices, ("groups", *PART))
    placed = P(("groups", *PART), None)
    return jax.shard_map(
        per_device,
        mesh=split,
        in_specs=(placed, placed),
        out_specs=(placed, P("groups")),
        check_vma=False,
    )
```

```python
import functools

import jax
import jax.numpy as jnp
from jax import lax
from jax.experimental import pallas as pl
from jax.experimental.pallas import tpu as pltpu
from jax.sharding import PartitionSpec as P

FLOOR = 0.01
EPSILON = 1e-06
LANES = 128
CHUNK = 256
WHOLE = pl.BlockSpec(memory_space=pltpu.VMEM)


def exchange(value, axis, distance):
    size = lax.axis_size(axis)
    return lax.ppermute(value, axis, [(i, i ^ distance) for i in range(size)])


def shifted(value, axis, distance):
    size = lax.axis_size(axis)
    places = [*range(0, size, 2), *reversed(range(1, size, 2))]
    route = [(places[i], places[(i + distance) % size]) for i in range(size)]
    return lax.ppermute(value, axis, route)


def pack_kernel(t_hbm, s_hbm, packed_ref, sems):
    t_width = t_hbm.shape[1]
    copies = [
        pltpu.make_async_copy(t_hbm, packed_ref.at[:, :t_width], sems.at[0]),
        pltpu.make_async_copy(s_hbm, packed_ref.at[:, t_width:], sems.at[1]),
    ]
    for copy in copies:
        copy.start()
    for copy in copies:
        copy.wait()


def stats_kernel(t_width, packed_ref, stats_ref):
    value = packed_ref[...].astype(jnp.float32)
    squares = jnp.sum(value * value, axis=0, keepdims=True)
    square_t = jnp.sum(squares[:, :t_width], axis=1, keepdims=True)
    square_s = jnp.sum(squares[:, t_width:], axis=1, keepdims=True)
    lane = lax.broadcasted_iota(jnp.int32, (1, LANES), 1)
    width = value.shape[1]
    stats_ref[:, :width] = jnp.sum(value, axis=0, keepdims=True)
    stats_ref[:, width:] = jnp.where(lane == 0, square_t, jnp.where(lane == 1, square_s, 0.0))


def spreads_of(stats, t_width, s_width, total_rows):
    centre_t = stats[:, :t_width] / total_rows
    centre_s = stats[:, t_width : t_width + s_width] / total_rows
    square_t = stats[:, t_width + s_width : t_width + s_width + 1]
    square_s = stats[:, t_width + s_width + 1 : t_width + s_width + 2]
    spread_t = (
        2.0 * (square_t / total_rows - jnp.sum(centre_t * centre_t, axis=1, keepdims=True)) + EPSILON
    )
    spread_s = (
        2.0 * (square_s / total_rows - jnp.sum(centre_s * centre_s, axis=1, keepdims=True)) + EPSILON
    )
    return spread_t, spread_s, centre_s


def norms_of(value):
    value = value.astype(jnp.float32)
    return jnp.sum(value * value, axis=1, keepdims=True)


def as_row(column):
    rows = column.shape[0]
    row = lax.broadcasted_iota(jnp.int32, (rows, rows), 0)
    same = row == lax.broadcasted_iota(jnp.int32, (rows, rows), 1)
    return jnp.sum(jnp.where(same, column, 0.0), axis=0, keepdims=True)


def with_ones(value):
    return jnp.concatenate([value, jnp.ones((value.shape[0], LANES), value.dtype)], axis=1)


def visiting(ref, t_width):
    t, s = ref[:, :t_width], ref[:, t_width:]
    return t, s, as_row(norms_of(t)), as_row(norms_of(s))


def pair_tile(c, v, inv_t, inv_s, own):
    (ct, cs, nct, ncs), (vt, vs, nvt, nvs) = c, v
    last = (((1,), (1,)), ((), ()))
    gram_t = lax.dot_general(ct, vt, last, preferred_element_type=jnp.float32)
    gram_s = lax.dot_general(cs, vs, last, preferred_element_type=jnp.float32)
    square_t = jnp.maximum(nct + nvt - 2.0 * gram_t, 0.0)
    square_s = jnp.maximum(ncs + nvs - 2.0 * gram_s, 0.0)
    under_t = square_t * inv_t + FLOOR
    under_s = square_s * inv_s + FLOOR
    inverse_s = lax.rsqrt(under_s)
    residue = under_s * inverse_s - under_t * lax.rsqrt(under_t)
    slope = jnp.clip(residue, -1.0, 1.0)
    huber = slope * (residue - 0.5 * slope)
    pull = slope * inverse_s
    if own:
        row = lax.broadcasted_iota(jnp.int32, pull.shape, 0)
        same = row == lax.broadcasted_iota(jnp.int32, pull.shape, 1)
        pull = jnp.where(same, 0.0, pull)
        huber = jnp.where(same, 0.0, huber)
    weights = (pull * inv_s).astype(jnp.bfloat16)
    return (
        weights,
        jnp.sum(huber, axis=0, keepdims=True),
        jnp.sum(pull * square_s, axis=0, keepdims=True),
    )


def direct_of(rows, summed):
    width = rows.shape[1]
    row_weight = jnp.concatenate([summed[:, width:]] * (width // LANES), axis=1)
    return rows.astype(jnp.float32) * row_weight - summed[:, :width]


def chunks_of(ref):
    for h in range(ref.shape[0]):
        for start in range(0, ref.shape[1], CHUNK):
            yield h, pl.ds(start, min(CHUNK, ref.shape[1] - start))


def early_kernel(n_blk, steps, t_width, total_rows, *refs):
    refs = list(refs)
    tiles = [refs.pop(0) for _ in range(n_blk)]
    line = [tiles[0]] + [refs.pop(0) for _ in range(steps - 1)]
    *stats_refs, own_ref = refs[: -4 - steps]
    back_refs = refs[-4 - steps : -5]
    acc_ref, norm_ref, total_ref, sums_ref, plane_ref = refs[-5:]
    rows = own_ref.shape[0]
    for d, ref in enumerate(tiles):
        start = d % (n_blk // 2) * rows
        plane_ref[d // (n_blk // 2), start : start + rows, :] = ref[...]
    s_width = own_ref.shape[1]
    stats = stats_refs[0][...]
    for ref in stats_refs[1:]:
        stats = stats + ref[...]
    total_ref[...] = stats
    spread_t, spread_s, _ = spreads_of(stats, t_width, s_width, total_rows)
    inv_t, inv_s = 1.0 / spread_t, 1.0 / spread_s
    loss = jnp.zeros((1, LANES), jnp.float32)
    spread = jnp.zeros((1, LANES), jnp.float32)
    if steps == 1:
        acc_ref[...] = jnp.zeros_like(acc_ref)
    for h, at in chunks_of(plane_ref):
        norm_ref[h, 0, at, :] = jnp.broadcast_to(norms_of(plane_ref[h, at, :t_width]), (at.size, LANES))
        norm_ref[h, 1, at, :] = jnp.broadcast_to(norms_of(plane_ref[h, at, t_width:]), (at.size, LANES))
    for k, ref in enumerate(line):
        v = visiting(ref, t_width)
        factor = 1.0 if k == 0 else 2.0
        summed = None
        for h, at in chunks_of(plane_ref):
            cs = plane_ref[h, at, t_width:]
            c = (plane_ref[h, at, :t_width], cs, norm_ref[h, 0, at, :], norm_ref[h, 1, at, :])
            own = k == 0 and h == 0 and at.start == 0
            weights, loss_part, spread_part = pair_tile(c, v, inv_t, inv_s, own)
            loss = loss + factor * loss_part
            spread = spread + factor * spread_part
            term = lax.dot_general(
                weights,
                with_ones(cs),
                (((0,), (0,)), ((), ())),
                preferred_element_type=jnp.float32,
            )
            summed = term if summed is None else summed + term
            if k > 0:
                back = jnp.dot(weights, with_ones(v[1]), preferred_element_type=jnp.float32)
                acc_ref[h, at, :] = back if k == 1 else acc_ref[h, at, :] + back
        to_ref = own_ref if k == 0 else back_refs[k - 1]
        to_ref[...] = direct_of(v[1], summed)
    sums_ref[0:1, :] = loss
    sums_ref[1:2, :] = spread


def late_kernel(t_width, total_rows, *refs):
    plane_ref, ref, stats_ref, acc_ref, norm_ref, early_sums, keep_ref, give_ref, sums_ref = refs
    s_width = keep_ref.shape[1]
    spread_t, spread_s, _ = spreads_of(stats_ref[...], t_width, s_width, total_rows)
    inv_t, inv_s = 1.0 / spread_t, 1.0 / spread_s
    loss = early_sums[0:1, :]
    spread = early_sums[1:2, :]
    v = visiting(ref, t_width)
    for h, at in chunks_of(plane_ref):
        cs = plane_ref[h, at, t_width:]
        c = (plane_ref[h, at, :t_width], cs, norm_ref[h, 0, at, :], norm_ref[h, 1, at, :])
        weights, loss_part, spread_part = pair_tile(c, v, inv_t, inv_s, False)
        loss = loss + loss_part
        spread = spread + spread_part
        back = jnp.dot(weights, with_ones(v[1]), preferred_element_type=jnp.float32)
        to_ref = (keep_ref, give_ref)[h]
        to_ref[at, :] = direct_of(cs, acc_ref[h, at, :] + back)
    sums_ref[0:1, :] = loss
    sums_ref[1:2, :] = spread


def halve_kernel(rows, keep_ref, got_ref, *out_refs):
    out_refs[0][...] = keep_ref[:rows, :] + got_ref[:rows, :]
    out_refs[1][...] = keep_ref[rows : 2 * rows, :] + got_ref[rows : 2 * rows, :]


def final_kernel(n_parts, t_width, total_rows, packed_ref, stats_ref, *refs):
    *inputs, grad_ref, loss_ref = refs
    direct = inputs[0][...]
    for part in inputs[1:n_parts]:
        direct = direct + part[...]
    both = inputs[n_parts][...]
    for sums in inputs[n_parts + 1 :]:
        both = both + sums[...]
    s_width = direct.shape[1]
    both = jnp.sum(both, axis=1, keepdims=True)
    loss_total, spread_total = both[0:1, :], -both[1:2, :]
    _, spread_s, centre = spreads_of(stats_ref[...], t_width, s_width, total_rows)
    pairs = total_rows * (total_rows - 1.0)
    correction = 2.0 * spread_total / (pairs * spread_s * spread_s)
    student = packed_ref[:, t_width:].astype(jnp.float32)
    grad_ref[...] = (2.0 / (total_rows - 1.0)) * direct + correction * (student - centre)
    loss_ref[...] = jnp.broadcast_to(loss_total / pairs, loss_ref.shape)


def call(kernel, out_shape, operands, flops, vmem=48, **more):
    nbytes = sum(x.size * x.dtype.itemsize for x in operands)
    in_specs = more.pop("in_specs", [WHOLE] * len(operands))
    out_specs = more.pop("out_specs", jax.tree.map(lambda _: WHOLE, out_shape))
    return pl.pallas_call(
        kernel,
        out_shape=out_shape,
        in_specs=in_specs,
        out_specs=out_specs,
        compiler_params=pltpu.CompilerParams(vmem_limit_bytes=vmem * 1024 * 1024),
        cost_estimate=pl.CostEstimate(flops=flops, bytes_accessed=nbytes, transcendentals=0),
        **more,
    )(*operands)


def gathered(value, axis):
    return [value] + [exchange(value, axis, d) for d in range(1, lax.axis_size(axis))]


def halvings(axis):
    size = lax.axis_size(axis)
    return [size >> i for i in range(1, size.bit_length())]


def per_device(teacher, student):
    rows, t_width = teacher.shape
    s_width = student.shape[1]
    n_blk = lax.axis_size("blk")
    n_sub = lax.axis_size("sub")
    total_rows = float(rows * n_blk * n_sub)
    half = n_sub // 2
    side = rows * n_blk // 2
    f32 = functools.partial(jax.ShapeDtypeStruct, dtype=jnp.float32)

    teacher, student = (pltpu.with_memory_space_constraint(x, pltpu.HBM) for x in (teacher, student))
    packed = call(
        pack_kernel,
        jax.ShapeDtypeStruct((rows, t_width + s_width), teacher.dtype),
        (teacher, student),
        0,
        vmem=48,
        in_specs=[pl.BlockSpec(memory_space=pl.ANY)] * 2,
        scratch_shapes=[pltpu.SemaphoreType.DMA((2,))],
    )
    stats = call(
        functools.partial(stats_kernel, t_width),
        f32((1, t_width + s_width + LANES)),
        (packed,),
        4 * packed.size,
    )
    line = [packed, shifted(packed, "sub", 1)]
    tz = [exchange(stats, "sub", d) for d in range(1, n_sub)]
    line[1], *tz = lax.optimization_barrier((line[1], *tz))
    for _ in range(half - 1):
        line.append(shifted(line[-1], "sub", 1))
    stats = functools.reduce(jnp.add, [stats] + tz)
    tiles = [packed]
    for distance in halvings("blk"):
        if distance == 1:
            *tiles, line[1] = lax.optimization_barrier((*tiles, line[1]))
        else:
            stats = stats + exchange(stats, "blk", distance)
        tiles = tiles + [exchange(x, "blk", distance) for x in tiles]
    stats = [stats, exchange(stats, "blk", 1)]

    pair_flops = 2 * rows * rows * n_blk * (t_width + 3 * s_width)
    out_shape = (
        [f32((rows, s_width))] * half
        + [f32((2, side, s_width + LANES)), f32((2, 2, side, LANES))]
        + [f32(stats[0].shape), f32((2, LANES))]
        + [jax.ShapeDtypeStruct((2, side, t_width + s_width), packed.dtype)]
    )
    *tiles, acc, norms, totals, early_sums, plane = call(
        functools.partial(early_kernel, n_blk, half, t_width, total_rows),
        out_shape,
        tiles + line[1:half] + stats,
        half * pair_flops,
    )
    own, backs = tiles[0], tiles[1:]
    returned = [shifted(x, "sub", -k) for k, x in enumerate(backs, 1)]
    keep, give, sums = call(
        functools.partial(late_kernel, t_width, total_rows),
        [f32((side, s_width))] * 2 + [f32((2, LANES))],
        [plane, line[half], totals, acc, norms, early_sums],
        pair_flops,
    )
    got = exchange(give, "blk", 1)
    for distance in halvings("blk")[:-1]:
        sums = sums + exchange(sums, "blk", distance)
    got, sums = lax.optimization_barrier((got, sums))
    sums = sums + exchange(sums, "blk", 1)
    for distance in reversed(halvings("sub")):
        all_sums = [sums, exchange(sums, "sub", distance)]
        sums = sum(all_sums[1:], all_sums[0])
    tiles, distance = n_blk // 2, 2
    while tiles > 1:
        tiles //= 2
        out_shape = [f32((rows * tiles, s_width))] * 2
        keep, give = call(
            functools.partial(halve_kernel, rows * tiles), out_shape, (keep, got), 2 * keep.size
        )
        got = exchange(give, "blk", distance)
        distance *= 2
    parts = [own, keep, got] + returned
    grad, loss = call(
        functools.partial(final_kernel, len(parts), t_width, total_rows),
        [f32((rows, s_width)), f32((1, LANES))],
        [packed, totals] + parts + all_sums,
        8 * student.size,
    )
    return grad, loss[0, :1]


def solution(mesh):
    placed = P(("groups", "blk", "sub"), None)
    return jax.shard_map(
        per_device,
        mesh=mesh,
        in_specs=(placed, placed),
        out_specs=(placed, P("groups")),
        check_vma=False,
    )
```

```python
import functools

import jax
import jax.numpy as jnp
from jax import lax
from jax.experimental import pallas as pl
from jax.experimental.pallas import tpu as pltpu
from jax.sharding import PartitionSpec as P

FLOOR = 0.01
EPSILON = 1e-06
LANES = 128
CHUNK = 256
WHOLE = pl.BlockSpec(memory_space=pltpu.VMEM)


def exchange(value, axis, distance):
    size = lax.axis_size(axis)
    return lax.ppermute(value, axis, [(i, i ^ distance) for i in range(size)])


def shifted(value, axis, distance):
    size = lax.axis_size(axis)
    places = [*range(0, size, 2), *reversed(range(1, size, 2))]
    route = [(places[i], places[(i + distance) % size]) for i in range(size)]
    return lax.ppermute(value, axis, route)


def pack_kernel(t_hbm, s_hbm, packed_ref, sems):
    t_width = t_hbm.shape[1]
    copies = [
        pltpu.make_async_copy(t_hbm, packed_ref.at[:, :t_width], sems.at[0]),
        pltpu.make_async_copy(s_hbm, packed_ref.at[:, t_width:], sems.at[1]),
    ]
    for copy in copies:
        copy.start()
    for copy in copies:
        copy.wait()


def stats_kernel(t_width, packed_ref, stats_ref):
    value = packed_ref[...].astype(jnp.float32)
    squares = jnp.sum(value * value, axis=0, keepdims=True)
    square_t = jnp.sum(squares[:, :t_width], axis=1, keepdims=True)
    square_s = jnp.sum(squares[:, t_width:], axis=1, keepdims=True)
    lane = lax.broadcasted_iota(jnp.int32, (1, LANES), 1)
    width = value.shape[1]
    stats_ref[:, :width] = jnp.sum(value, axis=0, keepdims=True)
    stats_ref[:, width:] = jnp.where(lane == 0, square_t, jnp.where(lane == 1, square_s, 0.0))


def spreads_of(stats, t_width, s_width, total_rows):
    centre_t = stats[:, :t_width] / total_rows
    centre_s = stats[:, t_width : t_width + s_width] / total_rows
    square_t = stats[:, t_width + s_width : t_width + s_width + 1]
    square_s = stats[:, t_width + s_width + 1 : t_width + s_width + 2]
    spread_t = (
        2.0 * (square_t / total_rows - jnp.sum(centre_t * centre_t, axis=1, keepdims=True)) + EPSILON
    )
    spread_s = (
        2.0 * (square_s / total_rows - jnp.sum(centre_s * centre_s, axis=1, keepdims=True)) + EPSILON
    )
    return spread_t, spread_s, centre_s


def norms_of(value):
    value = value.astype(jnp.float32)
    return jnp.sum(value * value, axis=1, keepdims=True)


def as_row(column):
    rows = column.shape[0]
    row = lax.broadcasted_iota(jnp.int32, (rows, rows), 0)
    same = row == lax.broadcasted_iota(jnp.int32, (rows, rows), 1)
    return jnp.sum(jnp.where(same, column, 0.0), axis=0, keepdims=True)


def with_ones(value):
    return jnp.concatenate([value, jnp.ones((value.shape[0], LANES), value.dtype)], axis=1)


def visiting(ref, t_width):
    t, s = ref[:, :t_width], ref[:, t_width:]
    return t, s, as_row(norms_of(t)), as_row(norms_of(s))


def pair_tile(c, v, inv_t, inv_s, own):
    (ct, cs, nct, ncs), (vt, vs, nvt, nvs) = c, v
    last = (((1,), (1,)), ((), ()))
    gram_t = lax.dot_general(ct, vt, last, preferred_element_type=jnp.float32)
    gram_s = lax.dot_general(cs, vs, last, preferred_element_type=jnp.float32)
    square_t = jnp.maximum(nct + nvt - 2.0 * gram_t, 0.0)
    square_s = jnp.maximum(ncs + nvs - 2.0 * gram_s, 0.0)
    under_t = square_t * inv_t + FLOOR
    under_s = square_s * inv_s + FLOOR
    inverse_s = lax.rsqrt(under_s)
    residue = under_s * inverse_s - under_t * lax.rsqrt(under_t)
    slope = jnp.clip(residue, -1.0, 1.0)
    huber = slope * (residue - 0.5 * slope)
    pull = slope * inverse_s
    if own:
        row = lax.broadcasted_iota(jnp.int32, pull.shape, 0)
        same = row == lax.broadcasted_iota(jnp.int32, pull.shape, 1)
        pull = jnp.where(same, 0.0, pull)
        huber = jnp.where(same, 0.0, huber)
    weights = (pull * inv_s).astype(jnp.bfloat16)
    return (
        weights,
        jnp.sum(huber, axis=0, keepdims=True),
        jnp.sum(pull * square_s, axis=0, keepdims=True),
    )


def direct_of(rows, summed):
    width = rows.shape[1]
    row_weight = jnp.concatenate([summed[:, width:]] * (width // LANES), axis=1)
    return rows.astype(jnp.float32) * row_weight - summed[:, :width]


def chunks_of(ref):
    for h in range(ref.shape[0]):
        for start in range(0, ref.shape[1], CHUNK):
            yield h, pl.ds(start, min(CHUNK, ref.shape[1] - start))


def early_kernel(n_blk, steps, t_width, total_rows, *refs):
    refs = list(refs)
    tiles = [refs.pop(0) for _ in range(n_blk)]
    line = [tiles[0]] + [refs.pop(0) for _ in range(steps - 1)]
    *stats_refs, own_ref = refs[: -4 - steps]
    back_refs = refs[-4 - steps : -5]
    acc_ref, norm_ref, total_ref, sums_ref, plane_ref = refs[-5:]
    rows = own_ref.shape[0]
    for d, ref in enumerate(tiles):
        start = d % (n_blk // 2) * rows
        plane_ref[d // (n_blk // 2), start : start + rows, :] = ref[...]
    s_width = own_ref.shape[1]
    stats = stats_refs[0][...]
    for ref in stats_refs[1:]:
        stats = stats + ref[...]
    total_ref[...] = stats
    spread_t, spread_s, _ = spreads_of(stats, t_width, s_width, total_rows)
    inv_t, inv_s = 1.0 / spread_t, 1.0 / spread_s
    loss = jnp.zeros((1, LANES), jnp.float32)
    spread = jnp.zeros((1, LANES), jnp.float32)
    if steps == 1:
        acc_ref[...] = jnp.zeros_like(acc_ref)
    for h, at in chunks_of(plane_ref):
        norm_ref[h, 0, at, :] = jnp.broadcast_to(norms_of(plane_ref[h, at, :t_width]), (at.size, LANES))
        norm_ref[h, 1, at, :] = jnp.broadcast_to(norms_of(plane_ref[h, at, t_width:]), (at.size, LANES))
    for k, ref in enumerate(line):
        v = visiting(ref, t_width)
        factor = 1.0 if k == 0 else 2.0
        summed = None
        for h, at in chunks_of(plane_ref):
            cs = plane_ref[h, at, t_width:]
            c = (plane_ref[h, at, :t_width], cs, norm_ref[h, 0, at, :], norm_ref[h, 1, at, :])
            own = k == 0 and h == 0 and at.start == 0
            weights, loss_part, spread_part = pair_tile(c, v, inv_t, inv_s, own)
            loss = loss + factor * loss_part
            spread = spread + factor * spread_part
            term = lax.dot_general(
                weights,
                with_ones(cs),
                (((0,), (0,)), ((), ())),
                preferred_element_type=jnp.float32,
            )
            summed = term if summed is None else summed + term
            if k > 0:
                back = jnp.dot(weights, with_ones(v[1]), preferred_element_type=jnp.float32)
                acc_ref[h, at, :] = back if k == 1 else acc_ref[h, at, :] + back
        to_ref = own_ref if k == 0 else back_refs[k - 1]
        to_ref[...] = direct_of(v[1], summed)
    sums_ref[0:1, :] = loss
    sums_ref[1:2, :] = spread


def late_kernel(t_width, total_rows, *refs):
    plane_ref, ref, stats_ref, acc_ref, norm_ref, early_sums, keep_ref, give_ref, sums_ref = refs
    s_width = keep_ref.shape[1]
    spread_t, spread_s, _ = spreads_of(stats_ref[...], t_width, s_width, total_rows)
    inv_t, inv_s = 1.0 / spread_t, 1.0 / spread_s
    loss = early_sums[0:1, :]
    spread = early_sums[1:2, :]
    v = visiting(ref, t_width)
    for h, at in chunks_of(plane_ref):
        cs = plane_ref[h, at, t_width:]
        c = (plane_ref[h, at, :t_width], cs, norm_ref[h, 0, at, :], norm_ref[h, 1, at, :])
        weights, loss_part, spread_part = pair_tile(c, v, inv_t, inv_s, False)
        loss = loss + loss_part
        spread = spread + spread_part
        back = jnp.dot(weights, with_ones(v[1]), preferred_element_type=jnp.float32)
        to_ref = (keep_ref, give_ref)[h]
        to_ref[at, :] = direct_of(cs, acc_ref[h, at, :] + back)
    sums_ref[0:1, :] = loss
    sums_ref[1:2, :] = spread


def halve_kernel(rows, keep_ref, got_ref, *out_refs):
    out_refs[0][...] = keep_ref[:rows, :] + got_ref[:rows, :]
    out_refs[1][...] = keep_ref[rows : 2 * rows, :] + got_ref[rows : 2 * rows, :]


def final_kernel(t_width, total_rows, packed_ref, stats_ref, sums_ref, *refs):
    *parts, grad_ref, loss_ref = refs
    direct = parts[0][...]
    for part in parts[1:]:
        direct = direct + part[...]
    s_width = direct.shape[1]
    both = jnp.sum(sums_ref[...], axis=1, keepdims=True)
    loss_total, spread_total = both[0:1, :], -both[1:2, :]
    _, spread_s, centre = spreads_of(stats_ref[...], t_width, s_width, total_rows)
    pairs = total_rows * (total_rows - 1.0)
    correction = 2.0 * spread_total / (pairs * spread_s * spread_s)
    student = packed_ref[:, t_width:].astype(jnp.float32)
    grad_ref[...] = (2.0 / (total_rows - 1.0)) * direct + correction * (student - centre)
    loss_ref[...] = jnp.broadcast_to(loss_total / pairs, loss_ref.shape)


def call(kernel, out_shape, operands, flops, vmem=48, **more):
    nbytes = sum(x.size * x.dtype.itemsize for x in operands)
    in_specs = more.pop("in_specs", [WHOLE] * len(operands))
    out_specs = more.pop("out_specs", jax.tree.map(lambda _: WHOLE, out_shape))
    return pl.pallas_call(
        kernel,
        out_shape=out_shape,
        in_specs=in_specs,
        out_specs=out_specs,
        compiler_params=pltpu.CompilerParams(vmem_limit_bytes=vmem * 1024 * 1024),
        cost_estimate=pl.CostEstimate(flops=flops, bytes_accessed=nbytes, transcendentals=0),
        **more,
    )(*operands)


def gathered(value, axis):
    return [value] + [exchange(value, axis, d) for d in range(1, lax.axis_size(axis))]


def halvings(axis):
    size = lax.axis_size(axis)
    return [size >> i for i in range(1, size.bit_length())]


def per_device(teacher, student):
    rows, t_width = teacher.shape
    s_width = student.shape[1]
    n_blk = lax.axis_size("blk")
    n_sub = lax.axis_size("sub")
    total_rows = float(rows * n_blk * n_sub)
    half = n_sub // 2
    side = rows * n_blk // 2
    f32 = functools.partial(jax.ShapeDtypeStruct, dtype=jnp.float32)

    teacher, student = (pltpu.with_memory_space_constraint(x, pltpu.HBM) for x in (teacher, student))
    packed = call(
        pack_kernel,
        jax.ShapeDtypeStruct((rows, t_width + s_width), teacher.dtype),
        (teacher, student),
        0,
        vmem=48,
        in_specs=[pl.BlockSpec(memory_space=pl.ANY)] * 2,
        scratch_shapes=[pltpu.SemaphoreType.DMA((2,))],
    )
    stats = call(
        functools.partial(stats_kernel, t_width),
        f32((1, t_width + s_width + LANES)),
        (packed,),
        4 * packed.size,
    )
    line = [packed, shifted(packed, "sub", 1)]
    tz = [exchange(stats, "sub", d) for d in range(1, n_sub)]
    line[1], *tz = lax.optimization_barrier((line[1], *tz))
    for _ in range(half - 1):
        line.append(shifted(line[-1], "sub", 1))
    stats = functools.reduce(jnp.add, [stats] + tz)
    tiles = [packed]
    for distance in halvings("blk"):
        if distance == 1:
            *tiles, line[1] = lax.optimization_barrier((*tiles, line[1]))
        else:
            stats = stats + exchange(stats, "blk", distance)
        tiles = tiles + [exchange(x, "blk", distance) for x in tiles]
    stats = [stats, exchange(stats, "blk", 1)]

    pair_flops = 2 * rows * rows * n_blk * (t_width + 3 * s_width)
    out_shape = (
        [f32((rows, s_width))] * half
        + [f32((2, side, s_width + LANES)), f32((2, 2, side, LANES))]
        + [f32(stats[0].shape), f32((2, LANES))]
        + [jax.ShapeDtypeStruct((2, side, t_width + s_width), packed.dtype)]
    )
    *tiles, acc, norms, totals, early_sums, plane = call(
        functools.partial(early_kernel, n_blk, half, t_width, total_rows),
        out_shape,
        tiles + line[1:half] + stats,
        half * pair_flops,
    )
    own, backs = tiles[0], tiles[1:]
    returned = [shifted(x, "sub", -k) for k, x in enumerate(backs, 1)]
    keep, give, sums = call(
        functools.partial(late_kernel, t_width, total_rows),
        [f32((side, s_width))] * 2 + [f32((2, LANES))],
        [plane, line[half], totals, acc, norms, early_sums],
        pair_flops,
    )
    got = exchange(give, "blk", 1)
    tiles, distance = n_blk // 2, 2
    while tiles > 1:
        tiles //= 2
        out_shape = [f32((rows * tiles, s_width))] * 2
        keep, give = call(
            functools.partial(halve_kernel, rows * tiles), out_shape, (keep, got), 2 * keep.size
        )
        got = exchange(give, "blk", distance)
        distance *= 2
    all_sums = lax.psum(sums, ("blk", "sub"))
    parts = [own, keep, got] + returned
    grad, loss = call(
        functools.partial(final_kernel, t_width, total_rows),
        [f32((rows, s_width)), f32((1, LANES))],
        [packed, totals, all_sums] + parts,
        8 * student.size,
    )
    return grad, loss[0, :1]


def solution(mesh):
    placed = P(("groups", "blk", "sub"), None)
    return jax.shard_map(
        per_device,
        mesh=mesh,
        in_specs=(placed, placed),
        out_specs=(placed, P("groups")),
        check_vma=False,
    )
```

```python
import functools

import jax
import jax.numpy as jnp
from jax import lax
from jax.experimental import pallas as pl
from jax.experimental.pallas import tpu as pltpu
from jax.sharding import PartitionSpec as P

FLOOR = 0.01
EPSILON = 1e-06
LANES = 128
CHUNK = 256
WHOLE = pl.BlockSpec(memory_space=pltpu.VMEM)


def exchange(value, axis, distance):
    size = lax.axis_size(axis)
    return lax.ppermute(value, axis, [(i, i ^ distance) for i in range(size)])


def shifted(value, axis, distance):
    size = lax.axis_size(axis)
    places = [*range(0, size, 2), *reversed(range(1, size, 2))]
    route = [(places[i], places[(i + distance) % size]) for i in range(size)]
    return lax.ppermute(value, axis, route)


def pack_kernel(t_hbm, s_hbm, packed_ref, sems):
    t_width = t_hbm.shape[1]
    copies = [
        pltpu.make_async_copy(t_hbm, packed_ref.at[:, :t_width], sems.at[0]),
        pltpu.make_async_copy(s_hbm, packed_ref.at[:, t_width:], sems.at[1]),
    ]
    for copy in copies:
        copy.start()
    for copy in copies:
        copy.wait()


def stats_kernel(t_width, packed_ref, stats_ref):
    value = packed_ref[...].astype(jnp.float32)
    squares = jnp.sum(value * value, axis=0, keepdims=True)
    square_t = jnp.sum(squares[:, :t_width], axis=1, keepdims=True)
    square_s = jnp.sum(squares[:, t_width:], axis=1, keepdims=True)
    lane = lax.broadcasted_iota(jnp.int32, (1, LANES), 1)
    width = value.shape[1]
    stats_ref[:, :width] = jnp.sum(value, axis=0, keepdims=True)
    stats_ref[:, width:] = jnp.where(lane == 0, square_t, jnp.where(lane == 1, square_s, 0.0))


def spreads_of(stats, t_width, s_width, total_rows):
    centre_t = stats[:, :t_width] / total_rows
    centre_s = stats[:, t_width : t_width + s_width] / total_rows
    square_t = stats[:, t_width + s_width : t_width + s_width + 1]
    square_s = stats[:, t_width + s_width + 1 : t_width + s_width + 2]
    spread_t = (
        2.0 * (square_t / total_rows - jnp.sum(centre_t * centre_t, axis=1, keepdims=True)) + EPSILON
    )
    spread_s = (
        2.0 * (square_s / total_rows - jnp.sum(centre_s * centre_s, axis=1, keepdims=True)) + EPSILON
    )
    return spread_t, spread_s, centre_s


def norms_of(value):
    value = value.astype(jnp.float32)
    return jnp.sum(value * value, axis=1, keepdims=True)


def as_row(column):
    rows = column.shape[0]
    row = lax.broadcasted_iota(jnp.int32, (rows, rows), 0)
    same = row == lax.broadcasted_iota(jnp.int32, (rows, rows), 1)
    return jnp.sum(jnp.where(same, column, 0.0), axis=0, keepdims=True)


def with_ones(value):
    return jnp.concatenate([value, jnp.ones((value.shape[0], LANES), value.dtype)], axis=1)


def visiting(ref, t_width):
    t, s = ref[:, :t_width], ref[:, t_width:]
    return t, s, as_row(norms_of(t)), as_row(norms_of(s))


def pair_tile(c, v, inv_t, inv_s, own):
    (ct, cs, nct, ncs), (vt, vs, nvt, nvs) = c, v
    last = (((1,), (1,)), ((), ()))
    gram_t = lax.dot_general(ct, vt, last, preferred_element_type=jnp.float32)
    gram_s = lax.dot_general(cs, vs, last, preferred_element_type=jnp.float32)
    square_t = jnp.maximum(nct + nvt - 2.0 * gram_t, 0.0)
    square_s = jnp.maximum(ncs + nvs - 2.0 * gram_s, 0.0)
    under_t = square_t * inv_t + FLOOR
    under_s = square_s * inv_s + FLOOR
    inverse_s = lax.rsqrt(under_s)
    residue = under_s * inverse_s - under_t * lax.rsqrt(under_t)
    slope = jnp.clip(residue, -1.0, 1.0)
    huber = slope * (residue - 0.5 * slope)
    pull = slope * inverse_s
    if own:
        row = lax.broadcasted_iota(jnp.int32, pull.shape, 0)
        same = row == lax.broadcasted_iota(jnp.int32, pull.shape, 1)
        pull = jnp.where(same, 0.0, pull)
        huber = jnp.where(same, 0.0, huber)
    weights = (pull * inv_s).astype(jnp.bfloat16)
    return (
        weights,
        jnp.sum(huber, axis=0, keepdims=True),
        jnp.sum(pull * square_s, axis=0, keepdims=True),
    )


def direct_of(rows, summed):
    width = rows.shape[1]
    row_weight = jnp.concatenate([summed[:, width:]] * (width // LANES), axis=1)
    return rows.astype(jnp.float32) * row_weight - summed[:, :width]


def chunks_of(ref):
    for h in range(ref.shape[0]):
        for start in range(0, ref.shape[1], CHUNK):
            yield h, pl.ds(start, min(CHUNK, ref.shape[1] - start))


def early_kernel(n_blk, steps, t_width, total_rows, *refs):
    refs = list(refs)
    tiles = [refs.pop(0) for _ in range(n_blk)]
    line = [tiles[0]] + [refs.pop(0) for _ in range(steps - 1)]
    *stats_refs, own_ref = refs[: -4 - steps]
    back_refs = refs[-4 - steps : -5]
    acc_ref, norm_ref, total_ref, sums_ref, plane_ref = refs[-5:]
    rows = own_ref.shape[0]
    for d, ref in enumerate(tiles):
        start = d % (n_blk // 2) * rows
        plane_ref[d // (n_blk // 2), start : start + rows, :] = ref[...]
    s_width = own_ref.shape[1]
    stats = stats_refs[0][...]
    for ref in stats_refs[1:]:
        stats = stats + ref[...]
    total_ref[...] = stats
    spread_t, spread_s, _ = spreads_of(stats, t_width, s_width, total_rows)
    inv_t, inv_s = 1.0 / spread_t, 1.0 / spread_s
    loss = jnp.zeros((1, LANES), jnp.float32)
    spread = jnp.zeros((1, LANES), jnp.float32)
    if steps == 1:
        acc_ref[...] = jnp.zeros_like(acc_ref)
    for h, at in chunks_of(plane_ref):
        norm_ref[h, 0, at, :] = jnp.broadcast_to(norms_of(plane_ref[h, at, :t_width]), (at.size, LANES))
        norm_ref[h, 1, at, :] = jnp.broadcast_to(norms_of(plane_ref[h, at, t_width:]), (at.size, LANES))
    for k, ref in enumerate(line):
        v = visiting(ref, t_width)
        factor = 1.0 if k == 0 else 2.0
        summed = None
        for h, at in chunks_of(plane_ref):
            cs = plane_ref[h, at, t_width:]
            c = (plane_ref[h, at, :t_width], cs, norm_ref[h, 0, at, :], norm_ref[h, 1, at, :])
            own = k == 0 and h == 0 and at.start == 0
            weights, loss_part, spread_part = pair_tile(c, v, inv_t, inv_s, own)
            loss = loss + factor * loss_part
            spread = spread + factor * spread_part
            term = lax.dot_general(
                weights,
                with_ones(cs),
                (((0,), (0,)), ((), ())),
                preferred_element_type=jnp.float32,
            )
            summed = term if summed is None else summed + term
            if k > 0:
                back = jnp.dot(weights, with_ones(v[1]), preferred_element_type=jnp.float32)
                acc_ref[h, at, :] = back if k == 1 else acc_ref[h, at, :] + back
        to_ref = own_ref if k == 0 else back_refs[k - 1]
        to_ref[...] = direct_of(v[1], summed)
    sums_ref[0:1, :] = loss
    sums_ref[1:2, :] = spread


def late_kernel(side, t_width, total_rows, *refs):
    if side:
        plane_ref, ref, stats_ref, acc_ref, norm_ref, sums_in, out_ref, sums_ref, visit_ref = refs
        v = visiting(ref, t_width)
        visit_ref[0:1, :], visit_ref[1:2, :] = v[2:]
    else:
        plane_ref, ref, stats_ref, acc_ref, norm_ref, sums_in, visit_ref, out_ref, sums_ref = refs
        v = (ref[:, :t_width], ref[:, t_width:], visit_ref[0:1, :], visit_ref[1:2, :])
    s_width = out_ref.shape[1]
    spread_t, spread_s, _ = spreads_of(stats_ref[...], t_width, s_width, total_rows)
    inv_t, inv_s = 1.0 / spread_t, 1.0 / spread_s
    loss = sums_in[0:1, :]
    spread = sums_in[1:2, :]
    for h, at in chunks_of(plane_ref):
        if h != side:
            continue
        cs = plane_ref[h, at, t_width:]
        c = (plane_ref[h, at, :t_width], cs, norm_ref[h, 0, at, :], norm_ref[h, 1, at, :])
        weights, loss_part, spread_part = pair_tile(c, v, inv_t, inv_s, False)
        loss = loss + loss_part
        spread = spread + spread_part
        back = jnp.dot(weights, with_ones(v[1]), preferred_element_type=jnp.float32)
        out_ref[at, :] = direct_of(cs, acc_ref[h, at, :] + back)
    for i in range(1 if side else sums_ref.shape[0]):
        at = sums_ref if side else sums_ref.at[i]
        at[0:1, :] = loss
        at[1:2, :] = spread


def halve_kernel(rows, keep_ref, got_ref, *out_refs):
    out_refs[0][...] = keep_ref[:rows, :] + got_ref[:rows, :]
    out_refs[1][...] = keep_ref[rows : 2 * rows, :] + got_ref[rows : 2 * rows, :]


def final_kernel(t_width, total_rows, packed_ref, stats_ref, sums_ref, *refs):
    *parts, grad_ref, loss_ref = refs
    direct = parts[0][...]
    for part in parts[1:]:
        direct = direct + part[...]
    s_width = direct.shape[1]
    both = jnp.sum(jnp.sum(sums_ref[...], axis=0), axis=1, keepdims=True)
    loss_total, spread_total = both[0:1, :], -both[1:2, :]
    _, spread_s, centre = spreads_of(stats_ref[...], t_width, s_width, total_rows)
    pairs = total_rows * (total_rows - 1.0)
    correction = 2.0 * spread_total / (pairs * spread_s * spread_s)
    student = packed_ref[:, t_width:].astype(jnp.float32)
    grad_ref[...] = (2.0 / (total_rows - 1.0)) * direct + correction * (student - centre)
    loss_ref[...] = jnp.broadcast_to(loss_total / pairs, loss_ref.shape)


def call(kernel, out_shape, operands, flops, vmem=48, **more):
    nbytes = sum(x.size * x.dtype.itemsize for x in operands)
    in_specs = more.pop("in_specs", [WHOLE] * len(operands))
    out_specs = more.pop("out_specs", jax.tree.map(lambda _: WHOLE, out_shape))
    return pl.pallas_call(
        kernel,
        out_shape=out_shape,
        in_specs=in_specs,
        out_specs=out_specs,
        compiler_params=pltpu.CompilerParams(vmem_limit_bytes=vmem * 1024 * 1024),
        cost_estimate=pl.CostEstimate(flops=flops, bytes_accessed=nbytes, transcendentals=0),
        **more,
    )(*operands)


def gathered(value, axis):
    return [value] + [exchange(value, axis, d) for d in range(1, lax.axis_size(axis))]


def halvings(axis):
    size = lax.axis_size(axis)
    return [size >> i for i in range(1, size.bit_length())]


def to_all(value):
    return lax.all_to_all(value, ("blk", "sub"), 0, 0, tiled=True)


def per_device(teacher, student):
    rows, t_width = teacher.shape
    s_width = student.shape[1]
    n_blk = lax.axis_size("blk")
    n_sub = lax.axis_size("sub")
    total_rows = float(rows * n_blk * n_sub)
    half = n_sub // 2
    side = rows * n_blk // 2
    f32 = functools.partial(jax.ShapeDtypeStruct, dtype=jnp.float32)

    teacher, student = (pltpu.with_memory_space_constraint(x, pltpu.HBM) for x in (teacher, student))
    packed = call(
        pack_kernel,
        jax.ShapeDtypeStruct((rows, t_width + s_width), teacher.dtype),
        (teacher, student),
        0,
        vmem=48,
        in_specs=[pl.BlockSpec(memory_space=pl.ANY)] * 2,
        scratch_shapes=[pltpu.SemaphoreType.DMA((2,))],
    )
    stats = call(
        functools.partial(stats_kernel, t_width),
        f32((1, t_width + s_width + LANES)),
        (packed,),
        4 * packed.size,
    )
    line = [packed, shifted(packed, "sub", 1)]
    tz = [exchange(stats, "sub", d) for d in range(1, n_sub)]
    line[1], *tz = lax.optimization_barrier((line[1], *tz))
    for _ in range(half - 1):
        line.append(shifted(line[-1], "sub", 1))
    stats = functools.reduce(jnp.add, [stats] + tz)
    tiles = [packed]
    for distance in halvings("blk"):
        if distance == 1:
            *tiles, line[1] = lax.optimization_barrier((*tiles, line[1]))
        else:
            stats = stats + exchange(stats, "blk", distance)
        tiles = tiles + [exchange(x, "blk", distance) for x in tiles]
    stats = [stats, exchange(stats, "blk", 1)]

    pair_flops = 2 * rows * rows * n_blk * (t_width + 3 * s_width)
    out_shape = (
        [f32((rows, s_width))] * half
        + [f32((2, side, s_width + LANES)), f32((2, 2, side, LANES))]
        + [f32(stats[0].shape), f32((2, LANES))]
        + [jax.ShapeDtypeStruct((2, side, t_width + s_width), packed.dtype)]
    )
    *tiles, acc, norms, totals, early_sums, plane = call(
        functools.partial(early_kernel, n_blk, half, t_width, total_rows),
        out_shape,
        tiles + line[1:half] + stats,
        half * pair_flops,
    )
    own, backs = tiles[0], tiles[1:]
    returned = [shifted(x, "sub", -k) for k, x in enumerate(backs, 1)]
    given = [plane, line[half], totals, acc, norms]
    give, late_sums, visit_norms = call(
        functools.partial(late_kernel, 1, t_width, total_rows),
        [f32((side, s_width)), f32((2, LANES)), f32((2, rows))],
        [*given, early_sums],
        pair_flops // 2,
    )
    keep, sums = call(
        functools.partial(late_kernel, 0, t_width, total_rows),
        [f32((side, s_width)), f32((n_blk * n_sub, 2, LANES))],
        [*given, late_sums, visit_norms],
        pair_flops // 2,
    )
    got = exchange(give, "blk", 1)
    tiles, distance = n_blk // 2, 2
    while tiles > 1:
        tiles //= 2
        out_shape = [f32((rows * tiles, s_width))] * 2
        keep, give = call(
            functools.partial(halve_kernel, rows * tiles), out_shape, (keep, got), 2 * keep.size
        )
        got = exchange(give, "blk", distance)
        distance *= 2
    all_sums = to_all(sums)
    parts = [own, keep, got] + returned
    grad, loss = call(
        functools.partial(final_kernel, t_width, total_rows),
        [f32((rows, s_width)), f32((1, LANES))],
        [packed, totals, all_sums] + parts,
        8 * student.size,
    )
    return grad, loss[0, :1]


def solution(mesh):
    placed = P(("groups", "blk", "sub"), None)
    return jax.shard_map(
        per_device,
        mesh=mesh,
        in_specs=(placed, placed),
        out_specs=(placed, P("groups")),
        check_vma=False,
    )
```

```python
import functools

import jax
import jax.numpy as jnp
from jax import lax
from jax.experimental import pallas as pl
from jax.experimental.pallas import tpu as pltpu
from jax.sharding import PartitionSpec as P

FLOOR = 0.01
EPSILON = 1e-06
LANES = 128
CHUNK = 256
PIECES = 4
WHOLE = pl.BlockSpec(memory_space=pltpu.VMEM)


def exchange(value, axis, distance):
    size = lax.axis_size(axis)
    return lax.ppermute(value, axis, [(i, i ^ distance) for i in range(size)])


def shifted(value, axis, distance):
    size = lax.axis_size(axis)
    places = [*range(0, size, 2), *reversed(range(1, size, 2))]
    route = [(places[i], places[(i + distance) % size]) for i in range(size)]
    return lax.ppermute(value, axis, route)


def pack_kernel(t_hbm, s_hbm, packed_ref, sems):
    t_width = t_hbm.shape[1]
    rows = t_hbm.shape[0] // PIECES
    copies = []
    for i in range(PIECES):
        at = pl.ds(i * rows, rows)
        to_t, to_s = packed_ref.at[at, :t_width], packed_ref.at[at, t_width:]
        copies.append(pltpu.make_async_copy(t_hbm.at[at, :], to_t, sems.at[0, i]))
        copies.append(pltpu.make_async_copy(s_hbm.at[at, :], to_s, sems.at[1, i]))
    for copy in copies:
        copy.start()
    for copy in copies:
        copy.wait()


def stats_kernel(t_width, packed_ref, stats_ref):
    value = packed_ref[...].astype(jnp.float32)
    squares = jnp.sum(value * value, axis=0, keepdims=True)
    square_t = jnp.sum(squares[:, :t_width], axis=1, keepdims=True)
    square_s = jnp.sum(squares[:, t_width:], axis=1, keepdims=True)
    lane = lax.broadcasted_iota(jnp.int32, (1, LANES), 1)
    width = value.shape[1]
    stats_ref[:, :width] = jnp.sum(value, axis=0, keepdims=True)
    stats_ref[:, width:] = jnp.where(lane == 0, square_t, jnp.where(lane == 1, square_s, 0.0))


def spreads_of(stats, t_width, s_width, total_rows):
    centre_t = stats[:, :t_width] / total_rows
    centre_s = stats[:, t_width : t_width + s_width] / total_rows
    square_t = stats[:, t_width + s_width : t_width + s_width + 1]
    square_s = stats[:, t_width + s_width + 1 : t_width + s_width + 2]
    spread_t = (
        2.0 * (square_t / total_rows - jnp.sum(centre_t * centre_t, axis=1, keepdims=True)) + EPSILON
    )
    spread_s = (
        2.0 * (square_s / total_rows - jnp.sum(centre_s * centre_s, axis=1, keepdims=True)) + EPSILON
    )
    return spread_t, spread_s, centre_s


def norms_of(value):
    value = value.astype(jnp.float32)
    return jnp.sum(value * value, axis=1, keepdims=True)


def as_row(column):
    rows = column.shape[0]
    row = lax.broadcasted_iota(jnp.int32, (rows, rows), 0)
    same = row == lax.broadcasted_iota(jnp.int32, (rows, rows), 1)
    return jnp.sum(jnp.where(same, column, 0.0), axis=0, keepdims=True)


def with_ones(value):
    return jnp.concatenate([value, jnp.ones((value.shape[0], LANES), value.dtype)], axis=1)


def visiting(ref, t_width):
    t, s = ref[:, :t_width], ref[:, t_width:]
    return t, s, as_row(norms_of(t)), as_row(norms_of(s))


def pair_tile(c, v, inv_t, inv_s, own):
    (ct, cs, nct, ncs), (vt, vs, nvt, nvs) = c, v
    last = (((1,), (1,)), ((), ()))
    gram_t = lax.dot_general(ct, vt, last, preferred_element_type=jnp.float32)
    gram_s = lax.dot_general(cs, vs, last, preferred_element_type=jnp.float32)
    square_t = jnp.maximum(nct + nvt - 2.0 * gram_t, 0.0)
    square_s = jnp.maximum(ncs + nvs - 2.0 * gram_s, 0.0)
    under_t = square_t * inv_t + FLOOR
    under_s = square_s * inv_s + FLOOR
    inverse_s = lax.rsqrt(under_s)
    residue = under_s * inverse_s - under_t * lax.rsqrt(under_t)
    slope = jnp.clip(residue, -1.0, 1.0)
    huber = slope * (residue - 0.5 * slope)
    pull = slope * inverse_s
    if own:
        row = lax.broadcasted_iota(jnp.int32, pull.shape, 0)
        same = row == lax.broadcasted_iota(jnp.int32, pull.shape, 1)
        pull = jnp.where(same, 0.0, pull)
        huber = jnp.where(same, 0.0, huber)
    weights = (pull * inv_s).astype(jnp.bfloat16)
    return (
        weights,
        jnp.sum(huber, axis=0, keepdims=True),
        jnp.sum(pull * square_s, axis=0, keepdims=True),
    )


def direct_of(rows, summed):
    width = rows.shape[1]
    row_weight = jnp.concatenate([summed[:, width:]] * (width // LANES), axis=1)
    return rows.astype(jnp.float32) * row_weight - summed[:, :width]


def chunks_of(ref):
    for h in range(ref.shape[0]):
        for start in range(0, ref.shape[1], CHUNK):
            yield h, pl.ds(start, min(CHUNK, ref.shape[1] - start))


def early_kernel(n_blk, steps, t_width, total_rows, *refs):
    refs = list(refs)
    tiles = [refs.pop(0) for _ in range(n_blk)]
    line = [tiles[0]] + [refs.pop(0) for _ in range(steps - 1)]
    *stats_refs, own_ref = refs[: -4 - steps]
    back_refs = refs[-4 - steps : -5]
    acc_ref, norm_ref, total_ref, sums_ref, plane_ref = refs[-5:]
    rows = own_ref.shape[0]
    for d, ref in enumerate(tiles):
        start = d % (n_blk // 2) * rows
        plane_ref[d // (n_blk // 2), start : start + rows, :] = ref[...]
    s_width = own_ref.shape[1]
    stats = stats_refs[0][...]
    for ref in stats_refs[1:]:
        stats = stats + ref[...]
    spread_t, spread_s, centre_s = spreads_of(stats, t_width, s_width, total_rows)
    inv_t, inv_s = 1.0 / spread_t, 1.0 / spread_s
    for row, value in enumerate((inv_t, inv_s, spread_s)):
        total_ref[row : row + 1, :] = jnp.broadcast_to(value, (1, s_width))
    total_ref[3:4, :] = centre_s
    loss = jnp.zeros((1, LANES), jnp.float32)
    spread = jnp.zeros((1, LANES), jnp.float32)
    if steps == 1:
        acc_ref[...] = jnp.zeros_like(acc_ref)
    for h, at in chunks_of(plane_ref):
        norm_ref[h, 0, at, :] = jnp.broadcast_to(norms_of(plane_ref[h, at, :t_width]), (at.size, LANES))
        norm_ref[h, 1, at, :] = jnp.broadcast_to(norms_of(plane_ref[h, at, t_width:]), (at.size, LANES))
    for k, ref in enumerate(line):
        v = visiting(ref, t_width)
        factor = 1.0 if k == 0 else 2.0
        summed = None
        for h, at in chunks_of(plane_ref):
            cs = plane_ref[h, at, t_width:]
            c = (plane_ref[h, at, :t_width], cs, norm_ref[h, 0, at, :], norm_ref[h, 1, at, :])
            own = k == 0 and h == 0 and at.start == 0
            weights, loss_part, spread_part = pair_tile(c, v, inv_t, inv_s, own)
            loss = loss + factor * loss_part
            spread = spread + factor * spread_part
            term = lax.dot_general(
                weights,
                with_ones(cs),
                (((0,), (0,)), ((), ())),
                preferred_element_type=jnp.float32,
            )
            summed = term if summed is None else summed + term
            if k > 0:
                back = jnp.dot(weights, with_ones(v[1]), preferred_element_type=jnp.float32)
                acc_ref[h, at, :] = back if k == 1 else acc_ref[h, at, :] + back
        to_ref = own_ref if k == 0 else back_refs[k - 1]
        to_ref[...] = direct_of(v[1], summed)
    sums_ref[0:1, :] = loss
    sums_ref[1:2, :] = spread


def late_kernel(side, t_width, *refs):
    if side:
        plane_ref, ref, stats_ref, acc_ref, norm_ref, sums_in, out_ref, sums_ref, visit_ref = refs
        v = visiting(ref, t_width)
        visit_ref[0:1, :], visit_ref[1:2, :] = v[2:]
    else:
        plane_ref, ref, stats_ref, acc_ref, norm_ref, sums_in, visit_ref, out_ref, sums_ref = refs
        v = (ref[:, :t_width], ref[:, t_width:], visit_ref[0:1, :], visit_ref[1:2, :])
    inv_t, inv_s = stats_ref[0:1, :LANES], stats_ref[1:2, :LANES]
    loss = sums_in[0:1, :]
    spread = sums_in[1:2, :]
    for h, at in chunks_of(plane_ref):
        if h != side:
            continue
        cs = plane_ref[h, at, t_width:]
        c = (plane_ref[h, at, :t_width], cs, norm_ref[h, 0, at, :], norm_ref[h, 1, at, :])
        weights, loss_part, spread_part = pair_tile(c, v, inv_t, inv_s, False)
        loss = loss + loss_part
        spread = spread + spread_part
        back = jnp.dot(weights, with_ones(v[1]), preferred_element_type=jnp.float32)
        out_ref[at, :] = direct_of(cs, acc_ref[h, at, :] + back)
    for i in range(1 if side else sums_ref.shape[0]):
        at = sums_ref if side else sums_ref.at[i]
        at[0:1, :] = loss
        at[1:2, :] = spread


def halve_kernel(rows, keep_ref, got_ref, *out_refs):
    out_refs[0][...] = keep_ref[:rows, :] + got_ref[:rows, :]
    out_refs[1][...] = keep_ref[rows : 2 * rows, :] + got_ref[rows : 2 * rows, :]


def final_kernel(t_width, total_rows, packed_ref, stats_ref, sums_ref, *refs):
    *parts, grad_hbm, loss_ref, grad_ref, sems = refs
    both = jnp.sum(jnp.sum(sums_ref[...], axis=0), axis=1, keepdims=True)
    loss_total, spread_total = both[0:1, :], -both[1:2, :]
    spread_s, centre = stats_ref[2:3, :], stats_ref[3:4, :]
    pairs = total_rows * (total_rows - 1.0)
    correction = 2.0 * spread_total / (pairs * spread_s * spread_s)
    copies = []
    rows = grad_ref.shape[0] // PIECES
    for i in range(PIECES):
        at = pl.ds(i * rows, rows)
        direct = parts[0][at, :]
        for part in parts[1:]:
            direct = direct + part[at, :]
        student = packed_ref[at, t_width:].astype(jnp.float32)
        grad_ref[at, :] = (2.0 / (total_rows - 1.0)) * direct + correction * (student - centre)
        copies.append(pltpu.make_async_copy(grad_ref.at[at, :], grad_hbm.at[at, :], sems.at[i]))
        copies[-1].start()
    loss_ref[...] = jnp.broadcast_to(loss_total / pairs, loss_ref.shape)
    for copy in copies:
        copy.wait()


def call(kernel, out_shape, operands, flops, vmem=48, **more):
    nbytes = sum(x.size * x.dtype.itemsize for x in operands)
    in_specs = more.pop("in_specs", [WHOLE] * len(operands))
    out_specs = more.pop("out_specs", jax.tree.map(lambda _: WHOLE, out_shape))
    return pl.pallas_call(
        kernel,
        out_shape=out_shape,
        in_specs=in_specs,
        out_specs=out_specs,
        compiler_params=pltpu.CompilerParams(vmem_limit_bytes=vmem * 1024 * 1024),
        cost_estimate=pl.CostEstimate(flops=flops, bytes_accessed=nbytes, transcendentals=0),
        **more,
    )(*operands)


def gathered(value, axis):
    return [value] + [exchange(value, axis, d) for d in range(1, lax.axis_size(axis))]


def halvings(axis):
    size = lax.axis_size(axis)
    return [size >> i for i in range(1, size.bit_length())]


def to_all(value):
    return lax.all_to_all(value, ("blk", "sub"), 0, 0, tiled=True)


def per_device(teacher, student):
    rows, t_width = teacher.shape
    s_width = student.shape[1]
    n_blk = lax.axis_size("blk")
    n_sub = lax.axis_size("sub")
    total_rows = float(rows * n_blk * n_sub)
    half = n_sub // 2
    side = rows * n_blk // 2
    f32 = functools.partial(jax.ShapeDtypeStruct, dtype=jnp.float32)

    teacher, student = (pltpu.with_memory_space_constraint(x, pltpu.HBM) for x in (teacher, student))
    packed = call(
        pack_kernel,
        jax.ShapeDtypeStruct((rows, t_width + s_width), teacher.dtype),
        (teacher, student),
        0,
        vmem=48,
        in_specs=[pl.BlockSpec(memory_space=pl.ANY)] * 2,
        scratch_shapes=[pltpu.SemaphoreType.DMA((2, PIECES))],
    )
    stats = call(
        functools.partial(stats_kernel, t_width),
        f32((1, t_width + s_width + LANES)),
        (packed,),
        4 * packed.size,
    )
    line = [packed, shifted(packed, "sub", 1)]
    tz = [exchange(stats, "sub", d) for d in range(1, n_sub)]
    line[1], *tz = lax.optimization_barrier((line[1], *tz))
    for _ in range(half - 1):
        line.append(shifted(line[-1], "sub", 1))
    stats = functools.reduce(jnp.add, [stats] + tz)
    tiles = [packed]
    for distance in halvings("blk"):
        if distance == 1:
            *tiles, line[1] = lax.optimization_barrier((*tiles, line[1]))
        else:
            stats = stats + exchange(stats, "blk", distance)
        tiles = tiles + [exchange(x, "blk", distance) for x in tiles]
    stats = [stats, exchange(stats, "blk", 1)]

    pair_flops = 2 * rows * rows * n_blk * (t_width + 3 * s_width)
    out_shape = (
        [f32((rows, s_width))] * half
        + [f32((2, side, s_width + LANES)), f32((2, 2, side, LANES))]
        + [f32((4, s_width)), f32((2, LANES))]
        + [jax.ShapeDtypeStruct((2, side, t_width + s_width), packed.dtype)]
    )
    *tiles, acc, norms, totals, early_sums, plane = call(
        functools.partial(early_kernel, n_blk, half, t_width, total_rows),
        out_shape,
        tiles + line[1:half] + stats,
        half * pair_flops,
    )
    own, backs = tiles[0], tiles[1:]
    returned = [shifted(x, "sub", -k) for k, x in enumerate(backs, 1)]
    given = [plane, line[half], totals, acc, norms]
    give, late_sums, visit_norms = call(
        functools.partial(late_kernel, 1, t_width),
        [f32((side, s_width)), f32((2, LANES)), f32((2, rows))],
        [*given, early_sums],
        pair_flops // 2,
    )
    keep, sums = call(
        functools.partial(late_kernel, 0, t_width),
        [f32((side, s_width)), f32((n_blk * n_sub, 2, LANES))],
        [*given, late_sums, visit_norms],
        pair_flops // 2,
    )
    got = exchange(give, "blk", 1)
    tiles, distance = n_blk // 2, 2
    while tiles > 1:
        tiles //= 2
        out_shape = [f32((rows * tiles, s_width))] * 2
        keep, give = call(
            functools.partial(halve_kernel, rows * tiles), out_shape, (keep, got), 2 * keep.size
        )
        got = exchange(give, "blk", distance)
        distance *= 2
    all_sums = to_all(sums)
    parts = [own, keep, got] + returned
    grad, loss = call(
        functools.partial(final_kernel, t_width, total_rows),
        [f32((rows, s_width)), f32((1, LANES))],
        [packed, totals, all_sums] + parts,
        8 * student.size,
        out_specs=[pl.BlockSpec(memory_space=pl.ANY), WHOLE],
        scratch_shapes=[
            pltpu.VMEM((rows, s_width), jnp.float32),
            pltpu.SemaphoreType.DMA((PIECES,)),
        ],
    )
    return grad, loss[0, :1]


def solution(mesh):
    placed = P(("groups", "blk", "sub"), None)
    return jax.shard_map(
        per_device,
        mesh=mesh,
        in_specs=(placed, placed),
        out_specs=(placed, P("groups")),
        check_vma=False,
    )
```

```python
import functools

import jax
import jax.numpy as jnp
from jax import lax
from jax.experimental import pallas as pl
from jax.experimental.pallas import tpu as pltpu
from jax.sharding import PartitionSpec as P

FLOOR = 0.01
EPSILON = 1e-06
LANES = 128
CHUNK = 256
WHOLE = pl.BlockSpec(memory_space=pltpu.VMEM)


def exchange(value, axis, distance):
    size = lax.axis_size(axis)
    return lax.ppermute(value, axis, [(i, i ^ distance) for i in range(size)])


def shifted(value, axis, distance):
    size = lax.axis_size(axis)
    return lax.ppermute(value, axis, [(i, (i + distance) % size) for i in range(size)])


def pack_kernel(t_hbm, s_hbm, packed_ref, sems):
    t_width = t_hbm.shape[1]
    copies = [
        pltpu.make_async_copy(t_hbm, packed_ref.at[:, :t_width], sems.at[0]),
        pltpu.make_async_copy(s_hbm, packed_ref.at[:, t_width:], sems.at[1]),
    ]
    for copy in copies:
        copy.start()
    for copy in copies:
        copy.wait()


def stats_kernel(t_width, packed_ref, stats_ref):
    value = packed_ref[...].astype(jnp.float32)
    squares = jnp.sum(value * value, axis=0, keepdims=True)
    square_t = jnp.sum(squares[:, :t_width], axis=1, keepdims=True)
    square_s = jnp.sum(squares[:, t_width:], axis=1, keepdims=True)
    lane = lax.broadcasted_iota(jnp.int32, (1, LANES), 1)
    width = value.shape[1]
    stats_ref[:, :width] = jnp.sum(value, axis=0, keepdims=True)
    stats_ref[:, width:] = jnp.where(lane == 0, square_t, jnp.where(lane == 1, square_s, 0.0))


def spreads_of(stats, t_width, s_width, total_rows):
    centre_t = stats[:, :t_width] / total_rows
    centre_s = stats[:, t_width : t_width + s_width] / total_rows
    square_t = stats[:, t_width + s_width : t_width + s_width + 1]
    square_s = stats[:, t_width + s_width + 1 : t_width + s_width + 2]
    spread_t = (
        2.0 * (square_t / total_rows - jnp.sum(centre_t * centre_t, axis=1, keepdims=True)) + EPSILON
    )
    spread_s = (
        2.0 * (square_s / total_rows - jnp.sum(centre_s * centre_s, axis=1, keepdims=True)) + EPSILON
    )
    return spread_t, spread_s, centre_s


def norms_of(value):
    value = value.astype(jnp.float32)
    return jnp.sum(value * value, axis=1, keepdims=True)


def as_row(column):
    rows = column.shape[0]
    row = lax.broadcasted_iota(jnp.int32, (rows, rows), 0)
    same = row == lax.broadcasted_iota(jnp.int32, (rows, rows), 1)
    return jnp.sum(jnp.where(same, column, 0.0), axis=0, keepdims=True)


def with_ones(value):
    return jnp.concatenate([value, jnp.ones((value.shape[0], LANES), value.dtype)], axis=1)


def visiting(ref, t_width):
    t, s = ref[:, :t_width], ref[:, t_width:]
    return t, s, as_row(norms_of(t)), as_row(norms_of(s))


def pair_tile(c, v, inv_t, inv_s, own):
    (ct, cs, nct, ncs), (vt, vs, nvt, nvs) = c, v
    last = (((1,), (1,)), ((), ()))
    gram_t = lax.dot_general(ct, vt, last, preferred_element_type=jnp.float32)
    gram_s = lax.dot_general(cs, vs, last, preferred_element_type=jnp.float32)
    square_t = jnp.maximum(nct + nvt - 2.0 * gram_t, 0.0)
    square_s = jnp.maximum(ncs + nvs - 2.0 * gram_s, 0.0)
    under_t = square_t * inv_t + FLOOR
    under_s = square_s * inv_s + FLOOR
    inverse_s = lax.rsqrt(under_s)
    residue = under_s * inverse_s - under_t * lax.rsqrt(under_t)
    slope = jnp.clip(residue, -1.0, 1.0)
    huber = slope * (residue - 0.5 * slope)
    pull = slope * inverse_s
    if own:
        row = lax.broadcasted_iota(jnp.int32, pull.shape, 0)
        same = row == lax.broadcasted_iota(jnp.int32, pull.shape, 1)
        pull = jnp.where(same, 0.0, pull)
        huber = jnp.where(same, 0.0, huber)
    weights = (pull * inv_s).astype(jnp.bfloat16)
    return (
        weights,
        jnp.sum(huber, axis=0, keepdims=True),
        jnp.sum(pull * square_s, axis=0, keepdims=True),
    )


def direct_of(rows, summed):
    width = rows.shape[1]
    row_weight = jnp.concatenate([summed[:, width:]] * (width // LANES), axis=1)
    return rows.astype(jnp.float32) * row_weight - summed[:, :width]


def chunks_of(ref):
    for h in range(ref.shape[0]):
        for start in range(0, ref.shape[1], CHUNK):
            yield h, pl.ds(start, min(CHUNK, ref.shape[1] - start))


def early_kernel(n_blk, steps, t_width, total_rows, *refs):
    refs = list(refs)
    tiles = [refs.pop(0) for _ in range(n_blk)]
    line = [tiles[0]] + [refs.pop(0) for _ in range(steps - 1)]
    *stats_refs, own_ref = refs[: -4 - steps]
    back_refs = refs[-4 - steps : -5]
    acc_ref, norm_ref, total_ref, sums_ref, plane_ref = refs[-5:]
    rows = own_ref.shape[0]
    for d, ref in enumerate(tiles):
        start = d % (n_blk // 2) * rows
        plane_ref[d // (n_blk // 2), start : start + rows, :] = ref[...]
    s_width = own_ref.shape[1]
    stats = stats_refs[0][...]
    for ref in stats_refs[1:]:
        stats = stats + ref[...]
    spread_t, spread_s, centre_s = spreads_of(stats, t_width, s_width, total_rows)
    inv_t, inv_s = 1.0 / spread_t, 1.0 / spread_s
    for row, value in enumerate((inv_t, inv_s, spread_s)):
        total_ref[row : row + 1, :] = jnp.broadcast_to(value, (1, s_width))
    total_ref[3:4, :] = centre_s
    loss = jnp.zeros((1, LANES), jnp.float32)
    spread = jnp.zeros((1, LANES), jnp.float32)
    if steps == 1:
        acc_ref[...] = jnp.zeros_like(acc_ref)
    for h, at in chunks_of(plane_ref):
        norm_ref[h, 0, at, :] = jnp.broadcast_to(norms_of(plane_ref[h, at, :t_width]), (at.size, LANES))
        norm_ref[h, 1, at, :] = jnp.broadcast_to(norms_of(plane_ref[h, at, t_width:]), (at.size, LANES))
    for k, ref in enumerate(line):
        v = visiting(ref, t_width)
        factor = 1.0 if k == 0 else 2.0
        summed = None
        for h, at in chunks_of(plane_ref):
            cs = plane_ref[h, at, t_width:]
            c = (plane_ref[h, at, :t_width], cs, norm_ref[h, 0, at, :], norm_ref[h, 1, at, :])
            own = k == 0 and h == 0 and at.start == 0
            weights, loss_part, spread_part = pair_tile(c, v, inv_t, inv_s, own)
            loss = loss + factor * loss_part
            spread = spread + factor * spread_part
            term = lax.dot_general(
                weights,
                with_ones(cs),
                (((0,), (0,)), ((), ())),
                preferred_element_type=jnp.float32,
            )
            summed = term if summed is None else summed + term
            if k > 0:
                back = jnp.dot(weights, with_ones(v[1]), preferred_element_type=jnp.float32)
                acc_ref[h, at, :] = back if k == 1 else acc_ref[h, at, :] + back
        to_ref = own_ref if k == 0 else back_refs[k - 1]
        to_ref[...] = direct_of(v[1], summed)
    sums_ref[0:1, :] = loss
    sums_ref[1:2, :] = spread


def late_kernel(side, t_width, *refs):
    if side:
        plane_ref, ref, stats_ref, acc_ref, norm_ref, sums_in, out_ref, sums_ref, visit_ref = refs
        v = visiting(ref, t_width)
        visit_ref[0:1, :], visit_ref[1:2, :] = v[2:]
    else:
        plane_ref, ref, stats_ref, acc_ref, norm_ref, sums_in, visit_ref, out_ref, sums_ref = refs
        v = (ref[:, :t_width], ref[:, t_width:], visit_ref[0:1, :], visit_ref[1:2, :])
    inv_t, inv_s = stats_ref[0:1, :LANES], stats_ref[1:2, :LANES]
    loss = sums_in[0:1, :]
    spread = sums_in[1:2, :]
    for h, at in chunks_of(plane_ref):
        if h != side:
            continue
        cs = plane_ref[h, at, t_width:]
        c = (plane_ref[h, at, :t_width], cs, norm_ref[h, 0, at, :], norm_ref[h, 1, at, :])
        weights, loss_part, spread_part = pair_tile(c, v, inv_t, inv_s, False)
        loss = loss + loss_part
        spread = spread + spread_part
        back = jnp.dot(weights, with_ones(v[1]), preferred_element_type=jnp.float32)
        out_ref[at, :] = direct_of(cs, acc_ref[h, at, :] + back)
    for i in range(1 if side else sums_ref.shape[0]):
        at = sums_ref if side else sums_ref.at[i]
        at[0:1, :] = loss
        at[1:2, :] = spread


def halve_kernel(rows, keep_ref, got_ref, *out_refs):
    out_refs[0][...] = keep_ref[:rows, :] + got_ref[:rows, :]
    out_refs[1][...] = keep_ref[rows : 2 * rows, :] + got_ref[rows : 2 * rows, :]


def final_kernel(t_width, total_rows, packed_ref, stats_ref, sums_ref, *refs):
    *parts, grad_ref, loss_ref = refs
    direct = parts[0][...]
    for part in parts[1:]:
        direct = direct + part[...]
    both = jnp.sum(jnp.sum(sums_ref[...], axis=0), axis=1, keepdims=True)
    loss_total, spread_total = both[0:1, :], -both[1:2, :]
    spread_s, centre = stats_ref[2:3, :], stats_ref[3:4, :]
    pairs = total_rows * (total_rows - 1.0)
    correction = 2.0 * spread_total / (pairs * spread_s * spread_s)
    student = packed_ref[:, t_width:].astype(jnp.float32)
    grad_ref[...] = (2.0 / (total_rows - 1.0)) * direct + correction * (student - centre)
    loss_ref[...] = jnp.broadcast_to(loss_total / pairs, loss_ref.shape)


def call(kernel, out_shape, operands, flops, vmem=48, **more):
    nbytes = sum(x.size * x.dtype.itemsize for x in operands)
    in_specs = more.pop("in_specs", [WHOLE] * len(operands))
    out_specs = more.pop("out_specs", jax.tree.map(lambda _: WHOLE, out_shape))
    return pl.pallas_call(
        kernel,
        out_shape=out_shape,
        in_specs=in_specs,
        out_specs=out_specs,
        compiler_params=pltpu.CompilerParams(vmem_limit_bytes=vmem * 1024 * 1024),
        cost_estimate=pl.CostEstimate(flops=flops, bytes_accessed=nbytes, transcendentals=0),
        **more,
    )(*operands)


def gathered(value, axis):
    return [value] + [exchange(value, axis, d) for d in range(1, lax.axis_size(axis))]


def halvings(axis):
    size = lax.axis_size(axis)
    return [size >> i for i in range(1, size.bit_length())]


def to_all(value):
    return lax.all_to_all(value, ("blk", "sub"), 0, 0, tiled=True)


def per_device(teacher, student):
    rows, t_width = teacher.shape
    s_width = student.shape[1]
    n_blk = lax.axis_size("blk")
    n_sub = lax.axis_size("sub")
    total_rows = float(rows * n_blk * n_sub)
    half = n_sub // 2
    side = rows * n_blk // 2
    f32 = functools.partial(jax.ShapeDtypeStruct, dtype=jnp.float32)

    teacher, student = (pltpu.with_memory_space_constraint(x, pltpu.HBM) for x in (teacher, student))
    packed = call(
        pack_kernel,
        jax.ShapeDtypeStruct((rows, t_width + s_width), teacher.dtype),
        (teacher, student),
        0,
        vmem=48,
        in_specs=[pl.BlockSpec(memory_space=pl.ANY)] * 2,
        scratch_shapes=[pltpu.SemaphoreType.DMA((2,))],
    )
    stats = call(
        functools.partial(stats_kernel, t_width),
        f32((1, t_width + s_width + LANES)),
        (packed,),
        4 * packed.size,
    )
    line = [packed, shifted(packed, "sub", 1)]
    tz = [exchange(stats, "sub", d) for d in range(1, n_sub)]
    line[1], *tz = lax.optimization_barrier((line[1], *tz))
    for _ in range(half - 1):
        line.append(shifted(line[-1], "sub", 1))
    stats = functools.reduce(jnp.add, [stats] + tz)
    tiles = [packed]
    for distance in halvings("blk"):
        if distance == 1:
            *tiles, line[1] = lax.optimization_barrier((*tiles, line[1]))
        else:
            stats = stats + exchange(stats, "blk", distance)
        tiles = tiles + [exchange(x, "blk", distance) for x in tiles]
    stats = [stats, exchange(stats, "blk", 1)]

    pair_flops = 2 * rows * rows * n_blk * (t_width + 3 * s_width)
    out_shape = (
        [f32((rows, s_width))] * half
        + [f32((2, side, s_width + LANES)), f32((2, 2, side, LANES))]
        + [f32((4, s_width)), f32((2, LANES))]
        + [jax.ShapeDtypeStruct((2, side, t_width + s_width), packed.dtype)]
    )
    *tiles, acc, norms, totals, early_sums, plane = call(
        functools.partial(early_kernel, n_blk, half, t_width, total_rows),
        out_shape,
        tiles + line[1:half] + stats,
        half * pair_flops,
    )
    own, backs = tiles[0], tiles[1:]
    returned = [shifted(x, "sub", -k) for k, x in enumerate(backs, 1)]
    given = [plane, line[half], totals, acc, norms]
    give, late_sums, visit_norms = call(
        functools.partial(late_kernel, 1, t_width),
        [f32((side, s_width)), f32((2, LANES)), f32((2, rows))],
        [*given, early_sums],
        pair_flops // 2,
    )
    keep, sums = call(
        functools.partial(late_kernel, 0, t_width),
        [f32((side, s_width)), f32((n_blk * n_sub, 2, LANES))],
        [*given, late_sums, visit_norms],
        pair_flops // 2,
    )
    got = exchange(give, "blk", 1)
    tiles, distance = n_blk // 2, 2
    while tiles > 1:
        tiles //= 2
        out_shape = [f32((rows * tiles, s_width))] * 2
        keep, give = call(
            functools.partial(halve_kernel, rows * tiles), out_shape, (keep, got), 2 * keep.size
        )
        got = exchange(give, "blk", distance)
        distance *= 2
    all_sums = to_all(sums)
    parts = [own, keep, got] + returned
    grad, loss = call(
        functools.partial(final_kernel, t_width, total_rows),
        [f32((rows, s_width)), f32((1, LANES))],
        [packed, totals, all_sums] + parts,
        8 * student.size,
    )
    return grad, loss[0, :1]


def solution(mesh):
    placed = P(("groups", "blk", "sub"), None)
    return jax.shard_map(
        per_device,
        mesh=mesh,
        in_specs=(placed, placed),
        out_specs=(placed, P("groups")),
        check_vma=False,
    )
```

```python
import functools

import jax
import jax.numpy as jnp
from jax import lax
from jax.experimental import pallas as pl
from jax.experimental.pallas import tpu as pltpu
from jax.sharding import PartitionSpec as P

FLOOR = 0.01
EPSILON = 1e-06
LANES = 128
CHUNK = 256
WHOLE = pl.BlockSpec(memory_space=pltpu.VMEM)


def exchange(value, axis, distance):
    size = lax.axis_size(axis)
    return lax.ppermute(value, axis, [(i, i ^ distance) for i in range(size)])


def shifted(value, axis, distance):
    size = lax.axis_size(axis)
    return lax.ppermute(value, axis, [(i, (i - distance) % size) for i in range(size)])


def pack_kernel(t_hbm, s_hbm, packed_ref, sems):
    t_width = t_hbm.shape[1]
    copies = [
        pltpu.make_async_copy(t_hbm, packed_ref.at[:, :t_width], sems.at[0]),
        pltpu.make_async_copy(s_hbm, packed_ref.at[:, t_width:], sems.at[1]),
    ]
    for copy in copies:
        copy.start()
    for copy in copies:
        copy.wait()


def stats_kernel(t_width, packed_ref, stats_ref):
    value = packed_ref[...].astype(jnp.float32)
    squares = jnp.sum(value * value, axis=0, keepdims=True)
    square_t = jnp.sum(squares[:, :t_width], axis=1, keepdims=True)
    square_s = jnp.sum(squares[:, t_width:], axis=1, keepdims=True)
    lane = lax.broadcasted_iota(jnp.int32, (1, LANES), 1)
    width = value.shape[1]
    stats_ref[:, :width] = jnp.sum(value, axis=0, keepdims=True)
    stats_ref[:, width:] = jnp.where(lane == 0, square_t, jnp.where(lane == 1, square_s, 0.0))


def spreads_of(stats, t_width, s_width, total_rows):
    centre_t = stats[:, :t_width] / total_rows
    centre_s = stats[:, t_width : t_width + s_width] / total_rows
    square_t = stats[:, t_width + s_width : t_width + s_width + 1]
    square_s = stats[:, t_width + s_width + 1 : t_width + s_width + 2]
    spread_t = (
        2.0 * (square_t / total_rows - jnp.sum(centre_t * centre_t, axis=1, keepdims=True)) + EPSILON
    )
    spread_s = (
        2.0 * (square_s / total_rows - jnp.sum(centre_s * centre_s, axis=1, keepdims=True)) + EPSILON
    )
    return spread_t, spread_s, centre_s


def norms_of(value):
    value = value.astype(jnp.float32)
    return jnp.sum(value * value, axis=1, keepdims=True)


def as_row(column):
    rows = column.shape[0]
    row = lax.broadcasted_iota(jnp.int32, (rows, rows), 0)
    same = row == lax.broadcasted_iota(jnp.int32, (rows, rows), 1)
    return jnp.sum(jnp.where(same, column, 0.0), axis=0, keepdims=True)


def with_ones(value):
    return jnp.concatenate([value, jnp.ones((value.shape[0], LANES), value.dtype)], axis=1)


def visiting(ref, t_width):
    t, s = ref[:, :t_width], ref[:, t_width:]
    return t, s, as_row(norms_of(t)), as_row(norms_of(s))


def pair_tile(c, v, inv_t, inv_s, own):
    (ct, cs, nct, ncs), (vt, vs, nvt, nvs) = c, v
    last = (((1,), (1,)), ((), ()))
    gram_t = lax.dot_general(ct, vt, last, preferred_element_type=jnp.float32)
    gram_s = lax.dot_general(cs, vs, last, preferred_element_type=jnp.float32)
    square_t = jnp.maximum(nct + nvt - 2.0 * gram_t, 0.0)
    square_s = jnp.maximum(ncs + nvs - 2.0 * gram_s, 0.0)
    under_t = square_t * inv_t + FLOOR
    under_s = square_s * inv_s + FLOOR
    inverse_s = lax.rsqrt(under_s)
    residue = under_s * inverse_s - under_t * lax.rsqrt(under_t)
    slope = jnp.clip(residue, -1.0, 1.0)
    huber = slope * (residue - 0.5 * slope)
    pull = slope * inverse_s
    if own:
        row = lax.broadcasted_iota(jnp.int32, pull.shape, 0)
        same = row == lax.broadcasted_iota(jnp.int32, pull.shape, 1)
        pull = jnp.where(same, 0.0, pull)
        huber = jnp.where(same, 0.0, huber)
    weights = (pull * inv_s).astype(jnp.bfloat16)
    return (
        weights,
        jnp.sum(huber, axis=0, keepdims=True),
        jnp.sum(pull * square_s, axis=0, keepdims=True),
    )


def direct_of(rows, summed):
    width = rows.shape[1]
    row_weight = jnp.concatenate([summed[:, width:]] * (width // LANES), axis=1)
    return rows.astype(jnp.float32) * row_weight - summed[:, :width]


def chunks_of(ref):
    for h in range(ref.shape[0]):
        for start in range(0, ref.shape[1], CHUNK):
            yield h, pl.ds(start, min(CHUNK, ref.shape[1] - start))


def early_kernel(n_blk, steps, t_width, total_rows, *refs):
    refs = list(refs)
    tiles = [refs.pop(0) for _ in range(n_blk)]
    line = [tiles[0]] + [refs.pop(0) for _ in range(steps - 1)]
    *stats_refs, own_ref = refs[: -4 - steps]
    back_refs = refs[-4 - steps : -5]
    acc_ref, norm_ref, total_ref, sums_ref, plane_ref = refs[-5:]
    rows = own_ref.shape[0]
    for d, ref in enumerate(tiles):
        start = d % (n_blk // 2) * rows
        plane_ref[d // (n_blk // 2), start : start + rows, :] = ref[...]
    s_width = own_ref.shape[1]
    stats = stats_refs[0][...]
    for ref in stats_refs[1:]:
        stats = stats + ref[...]
    spread_t, spread_s, centre_s = spreads_of(stats, t_width, s_width, total_rows)
    inv_t, inv_s = 1.0 / spread_t, 1.0 / spread_s
    for row, value in enumerate((inv_t, inv_s, spread_s)):
        total_ref[row : row + 1, :] = jnp.broadcast_to(value, (1, s_width))
    total_ref[3:4, :] = centre_s
    loss = jnp.zeros((1, LANES), jnp.float32)
    spread = jnp.zeros((1, LANES), jnp.float32)
    if steps == 1:
        acc_ref[...] = jnp.zeros_like(acc_ref)
    for h, at in chunks_of(plane_ref):
        norm_ref[h, 0, at, :] = jnp.broadcast_to(norms_of(plane_ref[h, at, :t_width]), (at.size, LANES))
        norm_ref[h, 1, at, :] = jnp.broadcast_to(norms_of(plane_ref[h, at, t_width:]), (at.size, LANES))
    for k, ref in enumerate(line):
        v = visiting(ref, t_width)
        factor = 1.0 if k == 0 else 2.0
        summed = None
        for h, at in chunks_of(plane_ref):
            cs = plane_ref[h, at, t_width:]
            c = (plane_ref[h, at, :t_width], cs, norm_ref[h, 0, at, :], norm_ref[h, 1, at, :])
            own = k == 0 and h == 0 and at.start == 0
            weights, loss_part, spread_part = pair_tile(c, v, inv_t, inv_s, own)
            loss = loss + factor * loss_part
            spread = spread + factor * spread_part
            term = lax.dot_general(
                weights,
                with_ones(cs),
                (((0,), (0,)), ((), ())),
                preferred_element_type=jnp.float32,
            )
            summed = term if summed is None else summed + term
            if k > 0:
                back = jnp.dot(weights, with_ones(v[1]), preferred_element_type=jnp.float32)
                acc_ref[h, at, :] = back if k == 1 else acc_ref[h, at, :] + back
        to_ref = own_ref if k == 0 else back_refs[k - 1]
        to_ref[...] = direct_of(v[1], summed)
    sums_ref[0:1, :] = loss
    sums_ref[1:2, :] = spread


def late_kernel(side, t_width, *refs):
    if side:
        plane_ref, ref, stats_ref, acc_ref, norm_ref, sums_in, out_ref, sums_ref, visit_ref = refs
        v = visiting(ref, t_width)
        visit_ref[0:1, :], visit_ref[1:2, :] = v[2:]
    else:
        plane_ref, ref, stats_ref, acc_ref, norm_ref, sums_in, visit_ref, out_ref, sums_ref = refs
        v = (ref[:, :t_width], ref[:, t_width:], visit_ref[0:1, :], visit_ref[1:2, :])
    inv_t, inv_s = stats_ref[0:1, :LANES], stats_ref[1:2, :LANES]
    loss = sums_in[0:1, :]
    spread = sums_in[1:2, :]
    for h, at in chunks_of(plane_ref):
        if h != side:
            continue
        cs = plane_ref[h, at, t_width:]
        c = (plane_ref[h, at, :t_width], cs, norm_ref[h, 0, at, :], norm_ref[h, 1, at, :])
        weights, loss_part, spread_part = pair_tile(c, v, inv_t, inv_s, False)
        loss = loss + loss_part
        spread = spread + spread_part
        back = jnp.dot(weights, with_ones(v[1]), preferred_element_type=jnp.float32)
        out_ref[at, :] = direct_of(cs, acc_ref[h, at, :] + back)
    for i in range(1 if side else sums_ref.shape[0]):
        at = sums_ref if side else sums_ref.at[i]
        at[0:1, :] = loss
        at[1:2, :] = spread


def halve_kernel(rows, keep_ref, got_ref, *out_refs):
    out_refs[0][...] = keep_ref[:rows, :] + got_ref[:rows, :]
    out_refs[1][...] = keep_ref[rows : 2 * rows, :] + got_ref[rows : 2 * rows, :]


def final_kernel(t_width, total_rows, packed_ref, stats_ref, sums_ref, *refs):
    *parts, grad_ref, loss_ref = refs
    direct = parts[0][...]
    for part in parts[1:]:
        direct = direct + part[...]
    both = jnp.sum(jnp.sum(sums_ref[...], axis=0), axis=1, keepdims=True)
    loss_total, spread_total = both[0:1, :], -both[1:2, :]
    spread_s, centre = stats_ref[2:3, :], stats_ref[3:4, :]
    pairs = total_rows * (total_rows - 1.0)
    correction = 2.0 * spread_total / (pairs * spread_s * spread_s)
    student = packed_ref[:, t_width:].astype(jnp.float32)
    grad_ref[...] = (2.0 / (total_rows - 1.0)) * direct + correction * (student - centre)
    loss_ref[...] = jnp.broadcast_to(loss_total / pairs, loss_ref.shape)


def call(kernel, out_shape, operands, flops, vmem=48, **more):
    nbytes = sum(x.size * x.dtype.itemsize for x in operands)
    in_specs = more.pop("in_specs", [WHOLE] * len(operands))
    out_specs = more.pop("out_specs", jax.tree.map(lambda _: WHOLE, out_shape))
    return pl.pallas_call(
        kernel,
        out_shape=out_shape,
        in_specs=in_specs,
        out_specs=out_specs,
        compiler_params=pltpu.CompilerParams(vmem_limit_bytes=vmem * 1024 * 1024),
        cost_estimate=pl.CostEstimate(flops=flops, bytes_accessed=nbytes, transcendentals=0),
        **more,
    )(*operands)


def gathered(value, axis):
    return [value] + [exchange(value, axis, d) for d in range(1, lax.axis_size(axis))]


def halvings(axis):
    size = lax.axis_size(axis)
    return [size >> i for i in range(1, size.bit_length())]


def to_all(value):
    return lax.all_to_all(value, ("blk", "sub"), 0, 0, tiled=True)


def per_device(teacher, student):
    rows, t_width = teacher.shape
    s_width = student.shape[1]
    n_blk = lax.axis_size("blk")
    n_sub = lax.axis_size("sub")
    total_rows = float(rows * n_blk * n_sub)
    half = n_sub // 2
    side = rows * n_blk // 2
    f32 = functools.partial(jax.ShapeDtypeStruct, dtype=jnp.float32)

    teacher, student = (pltpu.with_memory_space_constraint(x, pltpu.HBM) for x in (teacher, student))
    packed = call(
        pack_kernel,
        jax.ShapeDtypeStruct((rows, t_width + s_width), teacher.dtype),
        (teacher, student),
        0,
        vmem=48,
        in_specs=[pl.BlockSpec(memory_space=pl.ANY)] * 2,
        scratch_shapes=[pltpu.SemaphoreType.DMA((2,))],
    )
    stats = call(
        functools.partial(stats_kernel, t_width),
        f32((1, t_width + s_width + LANES)),
        (packed,),
        4 * packed.size,
    )
    line = [packed, shifted(packed, "sub", 1)]
    tz = [exchange(stats, "sub", d) for d in range(1, n_sub)]
    line[1], *tz = lax.optimization_barrier((line[1], *tz))
    for _ in range(half - 1):
        line.append(shifted(line[-1], "sub", 1))
    stats = functools.reduce(jnp.add, [stats] + tz)
    tiles = [packed]
    for distance in halvings("blk"):
        if distance == 1:
            *tiles, line[1] = lax.optimization_barrier((*tiles, line[1]))
        else:
            stats = stats + exchange(stats, "blk", distance)
        tiles = tiles + [exchange(x, "blk", distance) for x in tiles]
    stats = [stats, exchange(stats, "blk", 1)]

    pair_flops = 2 * rows * rows * n_blk * (t_width + 3 * s_width)
    out_shape = (
        [f32((rows, s_width))] * half
        + [f32((2, side, s_width + LANES)), f32((2, 2, side, LANES))]
        + [f32((4, s_width)), f32((2, LANES))]
        + [jax.ShapeDtypeStruct((2, side, t_width + s_width), packed.dtype)]
    )
    *tiles, acc, norms, totals, early_sums, plane = call(
        functools.partial(early_kernel, n_blk, half, t_width, total_rows),
        out_shape,
        tiles + line[1:half] + stats,
        half * pair_flops,
    )
    own, backs = tiles[0], tiles[1:]
    returned = [shifted(x, "sub", -k) for k, x in enumerate(backs, 1)]
    given = [plane, line[half], totals, acc, norms]
    give, late_sums, visit_norms = call(
        functools.partial(late_kernel, 1, t_width),
        [f32((side, s_width)), f32((2, LANES)), f32((2, rows))],
        [*given, early_sums],
        pair_flops // 2,
    )
    keep, sums = call(
        functools.partial(late_kernel, 0, t_width),
        [f32((side, s_width)), f32((n_blk * n_sub, 2, LANES))],
        [*given, late_sums, visit_norms],
        pair_flops // 2,
    )
    got = exchange(give, "blk", 1)
    tiles, distance = n_blk // 2, 2
    while tiles > 1:
        tiles //= 2
        out_shape = [f32((rows * tiles, s_width))] * 2
        keep, give = call(
            functools.partial(halve_kernel, rows * tiles), out_shape, (keep, got), 2 * keep.size
        )
        got = exchange(give, "blk", distance)
        distance *= 2
    all_sums = to_all(sums)
    parts = [own, keep, got] + returned
    grad, loss = call(
        functools.partial(final_kernel, t_width, total_rows),
        [f32((rows, s_width)), f32((1, LANES))],
        [packed, totals, all_sums] + parts,
        8 * student.size,
    )
    return grad, loss[0, :1]


def solution(mesh):
    placed = P(("groups", "blk", "sub"), None)
    return jax.shard_map(
        per_device,
        mesh=mesh,
        in_specs=(placed, placed),
        out_specs=(placed, P("groups")),
        check_vma=False,
    )
```

```python
import functools

import jax
import jax.numpy as jnp
from jax import lax
from jax.experimental import pallas as pl
from jax.experimental.pallas import tpu as pltpu
from jax.sharding import PartitionSpec as P

FLOOR = 0.01
EPSILON = 1e-06
LANES = 128
CHUNK = 256
WHOLE = pl.BlockSpec(memory_space=pltpu.VMEM)


def exchange(value, axis, distance):
    size = lax.axis_size(axis)
    return lax.ppermute(value, axis, [(i, i ^ distance) for i in range(size)])


def shifted(value, axis, distance):
    size = lax.axis_size(axis)
    places = [0, *range(1, size, 2), *reversed(range(2, size, 2))]
    route = [(places[i], places[(i + distance) % size]) for i in range(size)]
    return lax.ppermute(value, axis, route)


def pack_kernel(t_hbm, s_hbm, packed_ref, sems):
    t_width = t_hbm.shape[1]
    copies = [
        pltpu.make_async_copy(t_hbm, packed_ref.at[:, :t_width], sems.at[0]),
        pltpu.make_async_copy(s_hbm, packed_ref.at[:, t_width:], sems.at[1]),
    ]
    for copy in copies:
        copy.start()
    for copy in copies:
        copy.wait()


def stats_kernel(t_width, packed_ref, stats_ref):
    value = packed_ref[...].astype(jnp.float32)
    squares = jnp.sum(value * value, axis=0, keepdims=True)
    square_t = jnp.sum(squares[:, :t_width], axis=1, keepdims=True)
    square_s = jnp.sum(squares[:, t_width:], axis=1, keepdims=True)
    lane = lax.broadcasted_iota(jnp.int32, (1, LANES), 1)
    width = value.shape[1]
    stats_ref[:, :width] = jnp.sum(value, axis=0, keepdims=True)
    stats_ref[:, width:] = jnp.where(lane == 0, square_t, jnp.where(lane == 1, square_s, 0.0))


def spreads_of(stats, t_width, s_width, total_rows):
    centre_t = stats[:, :t_width] / total_rows
    centre_s = stats[:, t_width : t_width + s_width] / total_rows
    square_t = stats[:, t_width + s_width : t_width + s_width + 1]
    square_s = stats[:, t_width + s_width + 1 : t_width + s_width + 2]
    spread_t = (
        2.0 * (square_t / total_rows - jnp.sum(centre_t * centre_t, axis=1, keepdims=True)) + EPSILON
    )
    spread_s = (
        2.0 * (square_s / total_rows - jnp.sum(centre_s * centre_s, axis=1, keepdims=True)) + EPSILON
    )
    return spread_t, spread_s, centre_s


def norms_of(value):
    value = value.astype(jnp.float32)
    return jnp.sum(value * value, axis=1, keepdims=True)


def as_row(column):
    rows = column.shape[0]
    row = lax.broadcasted_iota(jnp.int32, (rows, rows), 0)
    same = row == lax.broadcasted_iota(jnp.int32, (rows, rows), 1)
    return jnp.sum(jnp.where(same, column, 0.0), axis=0, keepdims=True)


def with_ones(value):
    return jnp.concatenate([value, jnp.ones((value.shape[0], LANES), value.dtype)], axis=1)


def visiting(ref, t_width):
    t, s = ref[:, :t_width], ref[:, t_width:]
    return t, s, as_row(norms_of(t)), as_row(norms_of(s))


def pair_tile(c, v, inv_t, inv_s, own):
    (ct, cs, nct, ncs), (vt, vs, nvt, nvs) = c, v
    last = (((1,), (1,)), ((), ()))
    gram_t = lax.dot_general(ct, vt, last, preferred_element_type=jnp.float32)
    gram_s = lax.dot_general(cs, vs, last, preferred_element_type=jnp.float32)
    square_t = jnp.maximum(nct + nvt - 2.0 * gram_t, 0.0)
    square_s = jnp.maximum(ncs + nvs - 2.0 * gram_s, 0.0)
    under_t = square_t * inv_t + FLOOR
    under_s = square_s * inv_s + FLOOR
    inverse_s = lax.rsqrt(under_s)
    residue = under_s * inverse_s - under_t * lax.rsqrt(under_t)
    slope = jnp.clip(residue, -1.0, 1.0)
    huber = slope * (residue - 0.5 * slope)
    pull = slope * inverse_s
    if own:
        row = lax.broadcasted_iota(jnp.int32, pull.shape, 0)
        same = row == lax.broadcasted_iota(jnp.int32, pull.shape, 1)
        pull = jnp.where(same, 0.0, pull)
        huber = jnp.where(same, 0.0, huber)
    weights = (pull * inv_s).astype(jnp.bfloat16)
    return (
        weights,
        jnp.sum(huber, axis=0, keepdims=True),
        jnp.sum(pull * square_s, axis=0, keepdims=True),
    )


def direct_of(rows, summed):
    width = rows.shape[1]
    row_weight = jnp.concatenate([summed[:, width:]] * (width // LANES), axis=1)
    return rows.astype(jnp.float32) * row_weight - summed[:, :width]


def chunks_of(ref):
    for h in range(ref.shape[0]):
        for start in range(0, ref.shape[1], CHUNK):
            yield h, pl.ds(start, min(CHUNK, ref.shape[1] - start))


def early_kernel(n_blk, steps, t_width, total_rows, *refs):
    refs = list(refs)
    tiles = [refs.pop(0) for _ in range(n_blk)]
    line = [tiles[0]] + [refs.pop(0) for _ in range(steps - 1)]
    *stats_refs, own_ref = refs[: -4 - steps]
    back_refs = refs[-4 - steps : -5]
    acc_ref, norm_ref, total_ref, sums_ref, plane_ref = refs[-5:]
    rows = own_ref.shape[0]
    for d, ref in enumerate(tiles):
        start = d % (n_blk // 2) * rows
        plane_ref[d // (n_blk // 2), start : start + rows, :] = ref[...]
    s_width = own_ref.shape[1]
    stats = stats_refs[0][...]
    for ref in stats_refs[1:]:
        stats = stats + ref[...]
    spread_t, spread_s, centre_s = spreads_of(stats, t_width, s_width, total_rows)
    inv_t, inv_s = 1.0 / spread_t, 1.0 / spread_s
    for row, value in enumerate((inv_t, inv_s, spread_s)):
        total_ref[row : row + 1, :] = jnp.broadcast_to(value, (1, s_width))
    total_ref[3:4, :] = centre_s
    loss = jnp.zeros((1, LANES), jnp.float32)
    spread = jnp.zeros((1, LANES), jnp.float32)
    if steps == 1:
        acc_ref[...] = jnp.zeros_like(acc_ref)
    for h, at in chunks_of(plane_ref):
        norm_ref[h, 0, at, :] = jnp.broadcast_to(norms_of(plane_ref[h, at, :t_width]), (at.size, LANES))
        norm_ref[h, 1, at, :] = jnp.broadcast_to(norms_of(plane_ref[h, at, t_width:]), (at.size, LANES))
    for k, ref in enumerate(line):
        v = visiting(ref, t_width)
        factor = 1.0 if k == 0 else 2.0
        summed = None
        for h, at in chunks_of(plane_ref):
            cs = plane_ref[h, at, t_width:]
            c = (plane_ref[h, at, :t_width], cs, norm_ref[h, 0, at, :], norm_ref[h, 1, at, :])
            own = k == 0 and h == 0 and at.start == 0
            weights, loss_part, spread_part = pair_tile(c, v, inv_t, inv_s, own)
            loss = loss + factor * loss_part
            spread = spread + factor * spread_part
            term = lax.dot_general(
                weights,
                with_ones(cs),
                (((0,), (0,)), ((), ())),
                preferred_element_type=jnp.float32,
            )
            summed = term if summed is None else summed + term
            if k > 0:
                back = jnp.dot(weights, with_ones(v[1]), preferred_element_type=jnp.float32)
                acc_ref[h, at, :] = back if k == 1 else acc_ref[h, at, :] + back
        to_ref = own_ref if k == 0 else back_refs[k - 1]
        to_ref[...] = direct_of(v[1], summed)
    sums_ref[0:1, :] = loss
    sums_ref[1:2, :] = spread


def late_kernel(side, t_width, *refs):
    if side:
        plane_ref, ref, stats_ref, acc_ref, norm_ref, sums_in, out_ref, sums_ref, visit_ref = refs
        v = visiting(ref, t_width)
        visit_ref[0:1, :], visit_ref[1:2, :] = v[2:]
    else:
        plane_ref, ref, stats_ref, acc_ref, norm_ref, sums_in, visit_ref, out_ref, sums_ref = refs
        v = (ref[:, :t_width], ref[:, t_width:], visit_ref[0:1, :], visit_ref[1:2, :])
    inv_t, inv_s = stats_ref[0:1, :LANES], stats_ref[1:2, :LANES]
    loss = sums_in[0:1, :]
    spread = sums_in[1:2, :]
    for h, at in chunks_of(plane_ref):
        if h != side:
            continue
        cs = plane_ref[h, at, t_width:]
        c = (plane_ref[h, at, :t_width], cs, norm_ref[h, 0, at, :], norm_ref[h, 1, at, :])
        weights, loss_part, spread_part = pair_tile(c, v, inv_t, inv_s, False)
        loss = loss + loss_part
        spread = spread + spread_part
        back = jnp.dot(weights, with_ones(v[1]), preferred_element_type=jnp.float32)
        out_ref[at, :] = direct_of(cs, acc_ref[h, at, :] + back)
    for i in range(1 if side else sums_ref.shape[0]):
        at = sums_ref if side else sums_ref.at[i]
        at[0:1, :] = loss
        at[1:2, :] = spread


def halve_kernel(rows, keep_ref, got_ref, *out_refs):
    out_refs[0][...] = keep_ref[:rows, :] + got_ref[:rows, :]
    out_refs[1][...] = keep_ref[rows : 2 * rows, :] + got_ref[rows : 2 * rows, :]


def final_kernel(t_width, total_rows, packed_ref, stats_ref, sums_ref, *refs):
    *parts, grad_ref, loss_ref = refs
    direct = parts[0][...]
    for part in parts[1:]:
        direct = direct + part[...]
    both = jnp.sum(jnp.sum(sums_ref[...], axis=0), axis=1, keepdims=True)
    loss_total, spread_total = both[0:1, :], -both[1:2, :]
    spread_s, centre = stats_ref[2:3, :], stats_ref[3:4, :]
    pairs = total_rows * (total_rows - 1.0)
    correction = 2.0 * spread_total / (pairs * spread_s * spread_s)
    student = packed_ref[:, t_width:].astype(jnp.float32)
    grad_ref[...] = (2.0 / (total_rows - 1.0)) * direct + correction * (student - centre)
    loss_ref[...] = jnp.broadcast_to(loss_total / pairs, loss_ref.shape)


def call(kernel, out_shape, operands, flops, vmem=48, **more):
    nbytes = sum(x.size * x.dtype.itemsize for x in operands)
    in_specs = more.pop("in_specs", [WHOLE] * len(operands))
    out_specs = more.pop("out_specs", jax.tree.map(lambda _: WHOLE, out_shape))
    return pl.pallas_call(
        kernel,
        out_shape=out_shape,
        in_specs=in_specs,
        out_specs=out_specs,
        compiler_params=pltpu.CompilerParams(vmem_limit_bytes=vmem * 1024 * 1024),
        cost_estimate=pl.CostEstimate(flops=flops, bytes_accessed=nbytes, transcendentals=0),
        **more,
    )(*operands)


def gathered(value, axis):
    return [value] + [exchange(value, axis, d) for d in range(1, lax.axis_size(axis))]


def halvings(axis):
    size = lax.axis_size(axis)
    return [size >> i for i in range(1, size.bit_length())]


def to_all(value):
    return lax.all_to_all(value, ("blk", "sub"), 0, 0, tiled=True)


def per_device(teacher, student):
    rows, t_width = teacher.shape
    s_width = student.shape[1]
    n_blk = lax.axis_size("blk")
    n_sub = lax.axis_size("sub")
    total_rows = float(rows * n_blk * n_sub)
    half = n_sub // 2
    side = rows * n_blk // 2
    f32 = functools.partial(jax.ShapeDtypeStruct, dtype=jnp.float32)

    teacher, student = (pltpu.with_memory_space_constraint(x, pltpu.HBM) for x in (teacher, student))
    packed = call(
        pack_kernel,
        jax.ShapeDtypeStruct((rows, t_width + s_width), teacher.dtype),
        (teacher, student),
        0,
        vmem=48,
        in_specs=[pl.BlockSpec(memory_space=pl.ANY)] * 2,
        scratch_shapes=[pltpu.SemaphoreType.DMA((2,))],
    )
    stats = call(
        functools.partial(stats_kernel, t_width),
        f32((1, t_width + s_width + LANES)),
        (packed,),
        4 * packed.size,
    )
    line = [packed, shifted(packed, "sub", 1)]
    tz = [exchange(stats, "sub", d) for d in range(1, n_sub)]
    line[1], *tz = lax.optimization_barrier((line[1], *tz))
    for _ in range(half - 1):
        line.append(shifted(line[-1], "sub", 1))
    stats = functools.reduce(jnp.add, [stats] + tz)
    tiles = [packed]
    for distance in halvings("blk"):
        if distance == 1:
            *tiles, line[1] = lax.optimization_barrier((*tiles, line[1]))
        else:
            stats = stats + exchange(stats, "blk", distance)
        tiles = tiles + [exchange(x, "blk", distance) for x in tiles]
    stats = [stats, exchange(stats, "blk", 1)]

    pair_flops = 2 * rows * rows * n_blk * (t_width + 3 * s_width)
    out_shape = (
        [f32((rows, s_width))] * half
        + [f32((2, side, s_width + LANES)), f32((2, 2, side, LANES))]
        + [f32((4, s_width)), f32((2, LANES))]
        + [jax.ShapeDtypeStruct((2, side, t_width + s_width), packed.dtype)]
    )
    *tiles, acc, norms, totals, early_sums, plane = call(
        functools.partial(early_kernel, n_blk, half, t_width, total_rows),
        out_shape,
        tiles + line[1:half] + stats,
        half * pair_flops,
    )
    own, backs = tiles[0], tiles[1:]
    returned = [shifted(x, "sub", -k) for k, x in enumerate(backs, 1)]
    given = [plane, line[half], totals, acc, norms]
    give, late_sums, visit_norms = call(
        functools.partial(late_kernel, 1, t_width),
        [f32((side, s_width)), f32((2, LANES)), f32((2, rows))],
        [*given, early_sums],
        pair_flops // 2,
    )
    keep, sums = call(
        functools.partial(late_kernel, 0, t_width),
        [f32((side, s_width)), f32((n_blk * n_sub, 2, LANES))],
        [*given, late_sums, visit_norms],
        pair_flops // 2,
    )
    got = exchange(give, "blk", 1)
    tiles, distance = n_blk // 2, 2
    while tiles > 1:
        tiles //= 2
        out_shape = [f32((rows * tiles, s_width))] * 2
        keep, give = call(
            functools.partial(halve_kernel, rows * tiles), out_shape, (keep, got), 2 * keep.size
        )
        got = exchange(give, "blk", distance)
        distance *= 2
    all_sums = to_all(sums)
    parts = [own, keep, got] + returned
    grad, loss = call(
        functools.partial(final_kernel, t_width, total_rows),
        [f32((rows, s_width)), f32((1, LANES))],
        [packed, totals, all_sums] + parts,
        8 * student.size,
    )
    return grad, loss[0, :1]


def solution(mesh):
    placed = P(("groups", "blk", "sub"), None)
    return jax.shard_map(
        per_device,
        mesh=mesh,
        in_specs=(placed, placed),
        out_specs=(placed, P("groups")),
        check_vma=False,
    )
```

```python
import functools

import jax
import jax.numpy as jnp
from jax import lax
from jax.experimental import pallas as pl
from jax.experimental.pallas import tpu as pltpu
from jax.sharding import PartitionSpec as P

FLOOR = 0.01
EPSILON = 1e-06
LANES = 128
CHUNK = 128
WHOLE = pl.BlockSpec(memory_space=pltpu.VMEM)


def exchange(value, axis, distance):
    size = lax.axis_size(axis)
    return lax.ppermute(value, axis, [(i, i ^ distance) for i in range(size)])


def shifted(value, axis, distance):
    size = lax.axis_size(axis)
    return lax.ppermute(value, axis, [(i, (i + distance) % size) for i in range(size)])


def pack_kernel(t_hbm, s_hbm, packed_ref, sems):
    t_width = t_hbm.shape[1]
    copies = [
        pltpu.make_async_copy(t_hbm, packed_ref.at[:, :t_width], sems.at[0]),
        pltpu.make_async_copy(s_hbm, packed_ref.at[:, t_width:], sems.at[1]),
    ]
    for copy in copies:
        copy.start()
    for copy in copies:
        copy.wait()


def stats_kernel(t_width, packed_ref, stats_ref):
    value = packed_ref[...].astype(jnp.float32)
    squares = jnp.sum(value * value, axis=0, keepdims=True)
    square_t = jnp.sum(squares[:, :t_width], axis=1, keepdims=True)
    square_s = jnp.sum(squares[:, t_width:], axis=1, keepdims=True)
    lane = lax.broadcasted_iota(jnp.int32, (1, LANES), 1)
    width = value.shape[1]
    stats_ref[:, :width] = jnp.sum(value, axis=0, keepdims=True)
    stats_ref[:, width:] = jnp.where(lane == 0, square_t, jnp.where(lane == 1, square_s, 0.0))


def spreads_of(stats, t_width, s_width, total_rows):
    centre_t = stats[:, :t_width] / total_rows
    centre_s = stats[:, t_width : t_width + s_width] / total_rows
    square_t = stats[:, t_width + s_width : t_width + s_width + 1]
    square_s = stats[:, t_width + s_width + 1 : t_width + s_width + 2]
    spread_t = (
        2.0 * (square_t / total_rows - jnp.sum(centre_t * centre_t, axis=1, keepdims=True)) + EPSILON
    )
    spread_s = (
        2.0 * (square_s / total_rows - jnp.sum(centre_s * centre_s, axis=1, keepdims=True)) + EPSILON
    )
    return spread_t, spread_s, centre_s


def norms_of(value):
    value = value.astype(jnp.float32)
    return jnp.sum(value * value, axis=1, keepdims=True)


def as_row(column):
    rows = column.shape[0]
    row = lax.broadcasted_iota(jnp.int32, (rows, rows), 0)
    same = row == lax.broadcasted_iota(jnp.int32, (rows, rows), 1)
    return jnp.sum(jnp.where(same, column, 0.0), axis=0, keepdims=True)


def with_ones(value):
    return jnp.concatenate([value, jnp.ones((value.shape[0], LANES), value.dtype)], axis=1)


def visiting(ref, t_width):
    t, s = ref[:, :t_width], ref[:, t_width:]
    return t, s, as_row(norms_of(t)), as_row(norms_of(s))


def pair_tile(c, v, inv_t, inv_s, own):
    (ct, cs, nct, ncs), (vt, vs, nvt, nvs) = c, v
    last = (((1,), (1,)), ((), ()))
    gram_t = lax.dot_general(ct, vt, last, preferred_element_type=jnp.float32)
    gram_s = lax.dot_general(cs, vs, last, preferred_element_type=jnp.float32)
    square_t = jnp.maximum(nct + nvt - 2.0 * gram_t, 0.0)
    square_s = jnp.maximum(ncs + nvs - 2.0 * gram_s, 0.0)
    under_t = square_t * inv_t + FLOOR
    under_s = square_s * inv_s + FLOOR
    inverse_s = lax.rsqrt(under_s)
    residue = under_s * inverse_s - under_t * lax.rsqrt(under_t)
    slope = jnp.clip(residue, -1.0, 1.0)
    huber = slope * (residue - 0.5 * slope)
    pull = slope * inverse_s
    if own:
        row = lax.broadcasted_iota(jnp.int32, pull.shape, 0)
        same = row == lax.broadcasted_iota(jnp.int32, pull.shape, 1)
        pull = jnp.where(same, 0.0, pull)
        huber = jnp.where(same, 0.0, huber)
    weights = (pull * inv_s).astype(jnp.bfloat16)
    return (
        weights,
        jnp.sum(huber, axis=0, keepdims=True),
        jnp.sum(pull * square_s, axis=0, keepdims=True),
    )


def direct_of(rows, summed):
    width = rows.shape[1]
    row_weight = jnp.concatenate([summed[:, width:]] * (width // LANES), axis=1)
    return rows.astype(jnp.float32) * row_weight - summed[:, :width]


def chunks_of(ref):
    for h in range(ref.shape[0]):
        for start in range(0, ref.shape[1], CHUNK):
            yield h, pl.ds(start, min(CHUNK, ref.shape[1] - start))


def early_kernel(n_blk, steps, t_width, total_rows, *refs):
    refs = list(refs)
    tiles = [refs.pop(0) for _ in range(n_blk)]
    line = [tiles[0]] + [refs.pop(0) for _ in range(steps - 1)]
    *stats_refs, own_ref = refs[: -4 - steps]
    back_refs = refs[-4 - steps : -5]
    acc_ref, norm_ref, total_ref, sums_ref, plane_ref = refs[-5:]
    rows = own_ref.shape[0]
    for d, ref in enumerate(tiles):
        start = d % (n_blk // 2) * rows
        plane_ref[d // (n_blk // 2), start : start + rows, :] = ref[...]
    s_width = own_ref.shape[1]
    stats = stats_refs[0][...]
    for ref in stats_refs[1:]:
        stats = stats + ref[...]
    spread_t, spread_s, centre_s = spreads_of(stats, t_width, s_width, total_rows)
    inv_t, inv_s = 1.0 / spread_t, 1.0 / spread_s
    for row, value in enumerate((inv_t, inv_s, spread_s)):
        total_ref[row : row + 1, :] = jnp.broadcast_to(value, (1, s_width))
    total_ref[3:4, :] = centre_s
    loss = jnp.zeros((1, LANES), jnp.float32)
    spread = jnp.zeros((1, LANES), jnp.float32)
    if steps == 1:
        acc_ref[...] = jnp.zeros_like(acc_ref)
    for h, at in chunks_of(plane_ref):
        norm_ref[h, 0, at, :] = jnp.broadcast_to(norms_of(plane_ref[h, at, :t_width]), (at.size, LANES))
        norm_ref[h, 1, at, :] = jnp.broadcast_to(norms_of(plane_ref[h, at, t_width:]), (at.size, LANES))
    for k, ref in enumerate(line):
        v = visiting(ref, t_width)
        factor = 1.0 if k == 0 else 2.0
        summed = None
        for h, at in chunks_of(plane_ref):
            cs = plane_ref[h, at, t_width:]
            c = (plane_ref[h, at, :t_width], cs, norm_ref[h, 0, at, :], norm_ref[h, 1, at, :])
            own = k == 0 and h == 0 and at.start == 0
            weights, loss_part, spread_part = pair_tile(c, v, inv_t, inv_s, own)
            loss = loss + factor * loss_part
            spread = spread + factor * spread_part
            term = lax.dot_general(
                weights,
                with_ones(cs),
                (((0,), (0,)), ((), ())),
                preferred_element_type=jnp.float32,
            )
            summed = term if summed is None else summed + term
            if k > 0:
                back = jnp.dot(weights, with_ones(v[1]), preferred_element_type=jnp.float32)
                acc_ref[h, at, :] = back if k == 1 else acc_ref[h, at, :] + back
        to_ref = own_ref if k == 0 else back_refs[k - 1]
        to_ref[...] = direct_of(v[1], summed)
    sums_ref[0:1, :] = loss
    sums_ref[1:2, :] = spread


def late_kernel(side, t_width, *refs):
    if side:
        plane_ref, ref, stats_ref, acc_ref, norm_ref, sums_in, out_ref, sums_ref, visit_ref = refs
        v = visiting(ref, t_width)
        visit_ref[0:1, :], visit_ref[1:2, :] = v[2:]
    else:
        plane_ref, ref, stats_ref, acc_ref, norm_ref, sums_in, visit_ref, out_ref, sums_ref = refs
        v = (ref[:, :t_width], ref[:, t_width:], visit_ref[0:1, :], visit_ref[1:2, :])
    inv_t, inv_s = stats_ref[0:1, :LANES], stats_ref[1:2, :LANES]
    loss = sums_in[0:1, :]
    spread = sums_in[1:2, :]
    for h, at in chunks_of(plane_ref):
        if h != side:
            continue
        cs = plane_ref[h, at, t_width:]
        c = (plane_ref[h, at, :t_width], cs, norm_ref[h, 0, at, :], norm_ref[h, 1, at, :])
        weights, loss_part, spread_part = pair_tile(c, v, inv_t, inv_s, False)
        loss = loss + loss_part
        spread = spread + spread_part
        back = jnp.dot(weights, with_ones(v[1]), preferred_element_type=jnp.float32)
        out_ref[at, :] = direct_of(cs, acc_ref[h, at, :] + back)
    for i in range(1 if side else sums_ref.shape[0]):
        at = sums_ref if side else sums_ref.at[i]
        at[0:1, :] = loss
        at[1:2, :] = spread


def halve_kernel(rows, keep_ref, got_ref, *out_refs):
    out_refs[0][...] = keep_ref[:rows, :] + got_ref[:rows, :]
    out_refs[1][...] = keep_ref[rows : 2 * rows, :] + got_ref[rows : 2 * rows, :]


def final_kernel(t_width, total_rows, packed_ref, stats_ref, sums_ref, *refs):
    *parts, grad_ref, loss_ref = refs
    direct = parts[0][...]
    for part in parts[1:]:
        direct = direct + part[...]
    both = jnp.sum(jnp.sum(sums_ref[...], axis=0), axis=1, keepdims=True)
    loss_total, spread_total = both[0:1, :], -both[1:2, :]
    spread_s, centre = stats_ref[2:3, :], stats_ref[3:4, :]
    pairs = total_rows * (total_rows - 1.0)
    correction = 2.0 * spread_total / (pairs * spread_s * spread_s)
    student = packed_ref[:, t_width:].astype(jnp.float32)
    grad_ref[...] = (2.0 / (total_rows - 1.0)) * direct + correction * (student - centre)
    loss_ref[...] = jnp.broadcast_to(loss_total / pairs, loss_ref.shape)


def call(kernel, out_shape, operands, flops, vmem=48, **more):
    nbytes = sum(x.size * x.dtype.itemsize for x in operands)
    in_specs = more.pop("in_specs", [WHOLE] * len(operands))
    out_specs = more.pop("out_specs", jax.tree.map(lambda _: WHOLE, out_shape))
    return pl.pallas_call(
        kernel,
        out_shape=out_shape,
        in_specs=in_specs,
        out_specs=out_specs,
        compiler_params=pltpu.CompilerParams(vmem_limit_bytes=vmem * 1024 * 1024),
        cost_estimate=pl.CostEstimate(flops=flops, bytes_accessed=nbytes, transcendentals=0),
        **more,
    )(*operands)


def gathered(value, axis):
    return [value] + [exchange(value, axis, d) for d in range(1, lax.axis_size(axis))]


def halvings(axis):
    size = lax.axis_size(axis)
    return [size >> i for i in range(1, size.bit_length())]


def to_all(value):
    return lax.all_to_all(value, ("blk", "sub"), 0, 0, tiled=True)


def per_device(teacher, student):
    rows, t_width = teacher.shape
    s_width = student.shape[1]
    n_blk = lax.axis_size("blk")
    n_sub = lax.axis_size("sub")
    total_rows = float(rows * n_blk * n_sub)
    half = n_sub // 2
    side = rows * n_blk // 2
    f32 = functools.partial(jax.ShapeDtypeStruct, dtype=jnp.float32)

    teacher, student = (pltpu.with_memory_space_constraint(x, pltpu.HBM) for x in (teacher, student))
    packed = call(
        pack_kernel,
        jax.ShapeDtypeStruct((rows, t_width + s_width), teacher.dtype),
        (teacher, student),
        0,
        vmem=48,
        in_specs=[pl.BlockSpec(memory_space=pl.ANY)] * 2,
        scratch_shapes=[pltpu.SemaphoreType.DMA((2,))],
    )
    stats = call(
        functools.partial(stats_kernel, t_width),
        f32((1, t_width + s_width + LANES)),
        (packed,),
        4 * packed.size,
    )
    line = [packed, shifted(packed, "sub", 1)]
    tz = [exchange(stats, "sub", d) for d in range(1, n_sub)]
    line[1], *tz = lax.optimization_barrier((line[1], *tz))
    for _ in range(half - 1):
        line.append(shifted(line[-1], "sub", 1))
    stats = functools.reduce(jnp.add, [stats] + tz)
    tiles = [packed]
    for distance in halvings("blk"):
        if distance == 1:
            *tiles, line[1] = lax.optimization_barrier((*tiles, line[1]))
        else:
            stats = stats + exchange(stats, "blk", distance)
        tiles = tiles + [exchange(x, "blk", distance) for x in tiles]
    stats = [stats, exchange(stats, "blk", 1)]

    pair_flops = 2 * rows * rows * n_blk * (t_width + 3 * s_width)
    out_shape = (
        [f32((rows, s_width))] * half
        + [f32((2, side, s_width + LANES)), f32((2, 2, side, LANES))]
        + [f32((4, s_width)), f32((2, LANES))]
        + [jax.ShapeDtypeStruct((2, side, t_width + s_width), packed.dtype)]
    )
    *tiles, acc, norms, totals, early_sums, plane = call(
        functools.partial(early_kernel, n_blk, half, t_width, total_rows),
        out_shape,
        tiles + line[1:half] + stats,
        half * pair_flops,
    )
    own, backs = tiles[0], tiles[1:]
    returned = [shifted(x, "sub", -k) for k, x in enumerate(backs, 1)]
    given = [plane, line[half], totals, acc, norms]
    give, late_sums, visit_norms = call(
        functools.partial(late_kernel, 1, t_width),
        [f32((side, s_width)), f32((2, LANES)), f32((2, rows))],
        [*given, early_sums],
        pair_flops // 2,
    )
    keep, sums = call(
        functools.partial(late_kernel, 0, t_width),
        [f32((side, s_width)), f32((n_blk * n_sub, 2, LANES))],
        [*given, late_sums, visit_norms],
        pair_flops // 2,
    )
    got = exchange(give, "blk", 1)
    tiles, distance = n_blk // 2, 2
    while tiles > 1:
        tiles //= 2
        out_shape = [f32((rows * tiles, s_width))] * 2
        keep, give = call(
            functools.partial(halve_kernel, rows * tiles), out_shape, (keep, got), 2 * keep.size
        )
        got = exchange(give, "blk", distance)
        distance *= 2
    all_sums = to_all(sums)
    parts = [own, keep, got] + returned
    grad, loss = call(
        functools.partial(final_kernel, t_width, total_rows),
        [f32((rows, s_width)), f32((1, LANES))],
        [packed, totals, all_sums] + parts,
        8 * student.size,
    )
    return grad, loss[0, :1]


def solution(mesh):
    placed = P(("groups", "blk", "sub"), None)
    return jax.shard_map(
        per_device,
        mesh=mesh,
        in_specs=(placed, placed),
        out_specs=(placed, P("groups")),
        check_vma=False,
    )
```

```python
import functools

import jax
import jax.numpy as jnp
from jax import lax
from jax.experimental import pallas as pl
from jax.experimental.pallas import tpu as pltpu
from jax.sharding import PartitionSpec as P

FLOOR = 0.01
EPSILON = 1e-06
LANES = 128
CHUNK = 256
WHOLE = pl.BlockSpec(memory_space=pltpu.VMEM)


def exchange(value, axis, distance):
    size = lax.axis_size(axis)
    return lax.ppermute(value, axis, [(i, i ^ distance) for i in range(size)])


def shifted(value, axis, distance):
    size = lax.axis_size(axis)
    return lax.ppermute(value, axis, [(i, (i + distance) % size) for i in range(size)])


def pack_kernel(t_hbm, s_hbm, packed_ref, sems):
    t_width = t_hbm.shape[1]
    copies = [
        pltpu.make_async_copy(t_hbm, packed_ref.at[:, :t_width], sems.at[0]),
        pltpu.make_async_copy(s_hbm, packed_ref.at[:, t_width:], sems.at[1]),
    ]
    for copy in copies:
        copy.start()
    for copy in copies:
        copy.wait()


def stats_kernel(t_width, packed_ref, stats_ref):
    value = packed_ref[...].astype(jnp.float32)
    squares = jnp.sum(value * value, axis=0, keepdims=True)
    square_t = jnp.sum(squares[:, :t_width], axis=1, keepdims=True)
    square_s = jnp.sum(squares[:, t_width:], axis=1, keepdims=True)
    lane = lax.broadcasted_iota(jnp.int32, (1, LANES), 1)
    width = value.shape[1]
    stats_ref[:, :width] = jnp.sum(value, axis=0, keepdims=True)
    stats_ref[:, width:] = jnp.where(lane == 0, square_t, jnp.where(lane == 1, square_s, 0.0))


def spreads_of(stats, t_width, s_width, total_rows):
    centre_t = stats[:, :t_width] / total_rows
    centre_s = stats[:, t_width : t_width + s_width] / total_rows
    square_t = stats[:, t_width + s_width : t_width + s_width + 1]
    square_s = stats[:, t_width + s_width + 1 : t_width + s_width + 2]
    spread_t = (
        2.0 * (square_t / total_rows - jnp.sum(centre_t * centre_t, axis=1, keepdims=True)) + EPSILON
    )
    spread_s = (
        2.0 * (square_s / total_rows - jnp.sum(centre_s * centre_s, axis=1, keepdims=True)) + EPSILON
    )
    return spread_t, spread_s, centre_s


def norms_of(value):
    value = value.astype(jnp.float32)
    return jnp.sum(value * value, axis=1, keepdims=True)


def as_row(column):
    rows = column.shape[0]
    row = lax.broadcasted_iota(jnp.int32, (rows, rows), 0)
    same = row == lax.broadcasted_iota(jnp.int32, (rows, rows), 1)
    return jnp.sum(jnp.where(same, column, 0.0), axis=0, keepdims=True)


def with_ones(value):
    return jnp.concatenate([value, jnp.ones((value.shape[0], LANES), value.dtype)], axis=1)


def visiting(ref, t_width):
    t, s = ref[:, :t_width], ref[:, t_width:]
    return t, s, as_row(norms_of(t)), as_row(norms_of(s))


def pair_tile(c, v, inv_t, inv_s, own):
    (ct, cs, nct, ncs), (vt, vs, nvt, nvs) = c, v
    last = (((1,), (1,)), ((), ()))
    gram_t = lax.dot_general(ct, vt, last, preferred_element_type=jnp.float32)
    gram_s = lax.dot_general(cs, vs, last, preferred_element_type=jnp.float32)
    square_t = jnp.maximum(nct + nvt - 2.0 * gram_t, 0.0)
    square_s = jnp.maximum(ncs + nvs - 2.0 * gram_s, 0.0)
    under_t = square_t * inv_t + FLOOR
    under_s = square_s * inv_s + FLOOR
    inverse_s = lax.rsqrt(under_s)
    residue = under_s * inverse_s - under_t * lax.rsqrt(under_t)
    slope = jnp.clip(residue, -1.0, 1.0)
    huber = slope * (residue - 0.5 * slope)
    pull = slope * inverse_s
    if own:
        row = lax.broadcasted_iota(jnp.int32, pull.shape, 0)
        same = row == lax.broadcasted_iota(jnp.int32, pull.shape, 1)
        pull = jnp.where(same, 0.0, pull)
        huber = jnp.where(same, 0.0, huber)
    weights = (pull * inv_s).astype(jnp.bfloat16)
    return (
        weights,
        jnp.sum(huber, axis=0, keepdims=True),
        jnp.sum(pull * square_s, axis=0, keepdims=True),
    )


def direct_of(rows, summed):
    width = rows.shape[1]
    row_weight = jnp.concatenate([summed[:, width:]] * (width // LANES), axis=1)
    return rows.astype(jnp.float32) * row_weight - summed[:, :width]


def chunks_of(ref):
    for h in range(ref.shape[0]):
        for start in range(0, ref.shape[1], CHUNK):
            yield h, pl.ds(start, min(CHUNK, ref.shape[1] - start))


def early_kernel(n_blk, steps, t_width, total_rows, *refs):
    refs = list(refs)
    tiles = [refs.pop(0) for _ in range(n_blk)]
    line = [tiles[0]] + [refs.pop(0) for _ in range(steps - 1)]
    *stats_refs, own_ref = refs[: -4 - steps]
    back_refs = refs[-4 - steps : -5]
    acc_ref, norm_ref, total_ref, sums_ref, plane_ref = refs[-5:]
    rows = own_ref.shape[0]
    for d, ref in enumerate(tiles):
        start = d % (n_blk // 2) * rows
        plane_ref[d // (n_blk // 2), start : start + rows, :] = ref[...]
    s_width = own_ref.shape[1]
    stats = stats_refs[0][...]
    for ref in stats_refs[1:]:
        stats = stats + ref[...]
    spread_t, spread_s, centre_s = spreads_of(stats, t_width, s_width, total_rows)
    inv_t, inv_s = 1.0 / spread_t, 1.0 / spread_s
    for row, value in enumerate((inv_t, inv_s, spread_s)):
        total_ref[row : row + 1, :] = jnp.broadcast_to(value, (1, s_width))
    total_ref[3:4, :] = centre_s
    loss = jnp.zeros((1, LANES), jnp.float32)
    spread = jnp.zeros((1, LANES), jnp.float32)
    if steps == 1:
        acc_ref[...] = jnp.zeros_like(acc_ref)
    for h, at in chunks_of(plane_ref):
        norm_ref[h, 0, at, :] = jnp.broadcast_to(norms_of(plane_ref[h, at, :t_width]), (at.size, LANES))
        norm_ref[h, 1, at, :] = jnp.broadcast_to(norms_of(plane_ref[h, at, t_width:]), (at.size, LANES))
    for k, ref in enumerate(line):
        v = visiting(ref, t_width)
        factor = 1.0 if k == 0 else 2.0
        summed = None
        for h, at in chunks_of(plane_ref):
            cs = plane_ref[h, at, t_width:]
            c = (plane_ref[h, at, :t_width], cs, norm_ref[h, 0, at, :], norm_ref[h, 1, at, :])
            own = k == 0 and h == 0 and at.start == 0
            weights, loss_part, spread_part = pair_tile(c, v, inv_t, inv_s, own)
            loss = loss + factor * loss_part
            spread = spread + factor * spread_part
            term = lax.dot_general(
                weights,
                with_ones(cs),
                (((0,), (0,)), ((), ())),
                preferred_element_type=jnp.float32,
            )
            summed = term if summed is None else summed + term
            if k > 0:
                back = jnp.dot(weights, with_ones(v[1]), preferred_element_type=jnp.float32)
                acc_ref[h, at, :] = back if k == 1 else acc_ref[h, at, :] + back
        to_ref = own_ref if k == 0 else back_refs[k - 1]
        to_ref[...] = direct_of(v[1], summed)
    sums_ref[0:1, :] = loss
    sums_ref[1:2, :] = spread


def late_kernel(side, t_width, *refs):
    if side:
        plane_ref, ref, stats_ref, acc_ref, norm_ref, sums_in, out_ref, sums_ref, visit_ref = refs
        v = visiting(ref, t_width)
        visit_ref[0:1, :], visit_ref[1:2, :] = v[2:]
    else:
        plane_ref, ref, stats_ref, acc_ref, norm_ref, sums_in, visit_ref, out_ref, sums_ref = refs
        v = (ref[:, :t_width], ref[:, t_width:], visit_ref[0:1, :], visit_ref[1:2, :])
    inv_t, inv_s = stats_ref[0:1, :LANES], stats_ref[1:2, :LANES]
    loss = sums_in[0:1, :]
    spread = sums_in[1:2, :]
    for h, at in chunks_of(plane_ref):
        if h != side:
            continue
        cs = plane_ref[h, at, t_width:]
        c = (plane_ref[h, at, :t_width], cs, norm_ref[h, 0, at, :], norm_ref[h, 1, at, :])
        weights, loss_part, spread_part = pair_tile(c, v, inv_t, inv_s, False)
        loss = loss + loss_part
        spread = spread + spread_part
        back = jnp.dot(weights, with_ones(v[1]), preferred_element_type=jnp.float32)
        out_ref[at, :] = direct_of(cs, acc_ref[h, at, :] + back)
    for i in range(1 if side else sums_ref.shape[0]):
        at = sums_ref if side else sums_ref.at[i]
        at[0:1, :] = loss
        at[1:2, :] = spread


def halve_kernel(rows, keep_ref, got_ref, *out_refs):
    out_refs[0][...] = keep_ref[:rows, :] + got_ref[:rows, :]
    out_refs[1][...] = keep_ref[rows : 2 * rows, :] + got_ref[rows : 2 * rows, :]


def final_kernel(total_rows, stats_ref, sums_ref, factor_ref, loss_ref):
    both = jnp.sum(jnp.sum(sums_ref[...], axis=0), axis=1, keepdims=True)
    loss_total, spread_total = both[0:1, :], -both[1:2, :]
    spread_s = stats_ref[2:3, :]
    pairs = total_rows * (total_rows - 1.0)
    factor_ref[...] = 2.0 * spread_total / (pairs * spread_s * spread_s)
    loss_ref[...] = jnp.broadcast_to(loss_total / pairs, loss_ref.shape)


def call(kernel, out_shape, operands, flops, vmem=48, **more):
    nbytes = sum(x.size * x.dtype.itemsize for x in operands)
    in_specs = more.pop("in_specs", [WHOLE] * len(operands))
    out_specs = more.pop("out_specs", jax.tree.map(lambda _: WHOLE, out_shape))
    return pl.pallas_call(
        kernel,
        out_shape=out_shape,
        in_specs=in_specs,
        out_specs=out_specs,
        compiler_params=pltpu.CompilerParams(vmem_limit_bytes=vmem * 1024 * 1024),
        cost_estimate=pl.CostEstimate(flops=flops, bytes_accessed=nbytes, transcendentals=0),
        **more,
    )(*operands)


def gathered(value, axis):
    return [value] + [exchange(value, axis, d) for d in range(1, lax.axis_size(axis))]


def halvings(axis):
    size = lax.axis_size(axis)
    return [size >> i for i in range(1, size.bit_length())]


def to_all(value):
    return lax.all_to_all(value, ("blk", "sub"), 0, 0, tiled=True)


def per_device(teacher, student):
    rows, t_width = teacher.shape
    s_width = student.shape[1]
    n_blk = lax.axis_size("blk")
    n_sub = lax.axis_size("sub")
    total_rows = float(rows * n_blk * n_sub)
    half = n_sub // 2
    side = rows * n_blk // 2
    f32 = functools.partial(jax.ShapeDtypeStruct, dtype=jnp.float32)

    teacher, student = (pltpu.with_memory_space_constraint(x, pltpu.HBM) for x in (teacher, student))
    packed = call(
        pack_kernel,
        jax.ShapeDtypeStruct((rows, t_width + s_width), teacher.dtype),
        (teacher, student),
        0,
        vmem=48,
        in_specs=[pl.BlockSpec(memory_space=pl.ANY)] * 2,
        scratch_shapes=[pltpu.SemaphoreType.DMA((2,))],
    )
    stats = call(
        functools.partial(stats_kernel, t_width),
        f32((1, t_width + s_width + LANES)),
        (packed,),
        4 * packed.size,
    )
    line = [packed, shifted(packed, "sub", 1)]
    tz = [exchange(stats, "sub", d) for d in range(1, n_sub)]
    line[1], *tz = lax.optimization_barrier((line[1], *tz))
    for _ in range(half - 1):
        line.append(shifted(line[-1], "sub", 1))
    stats = functools.reduce(jnp.add, [stats] + tz)
    tiles = [packed]
    for distance in halvings("blk"):
        if distance == 1:
            *tiles, line[1] = lax.optimization_barrier((*tiles, line[1]))
        else:
            stats = stats + exchange(stats, "blk", distance)
        tiles = tiles + [exchange(x, "blk", distance) for x in tiles]
    stats = [stats, exchange(stats, "blk", 1)]

    pair_flops = 2 * rows * rows * n_blk * (t_width + 3 * s_width)
    out_shape = (
        [f32((rows, s_width))] * half
        + [f32((2, side, s_width + LANES)), f32((2, 2, side, LANES))]
        + [f32((4, s_width)), f32((2, LANES))]
        + [jax.ShapeDtypeStruct((2, side, t_width + s_width), packed.dtype)]
    )
    *tiles, acc, norms, totals, early_sums, plane = call(
        functools.partial(early_kernel, n_blk, half, t_width, total_rows),
        out_shape,
        tiles + line[1:half] + stats,
        half * pair_flops,
    )
    own, backs = tiles[0], tiles[1:]
    returned = [shifted(x, "sub", -k) for k, x in enumerate(backs, 1)]
    given = [plane, line[half], totals, acc, norms]
    give, late_sums, visit_norms = call(
        functools.partial(late_kernel, 1, t_width),
        [f32((side, s_width)), f32((2, LANES)), f32((2, rows))],
        [*given, early_sums],
        pair_flops // 2,
    )
    keep, sums = call(
        functools.partial(late_kernel, 0, t_width),
        [f32((side, s_width)), f32((n_blk * n_sub, 2, LANES))],
        [*given, late_sums, visit_norms],
        pair_flops // 2,
    )
    got = exchange(give, "blk", 1)
    tiles, distance = n_blk // 2, 2
    while tiles > 1:
        tiles //= 2
        out_shape = [f32((rows * tiles, s_width))] * 2
        keep, give = call(
            functools.partial(halve_kernel, rows * tiles), out_shape, (keep, got), 2 * keep.size
        )
        got = exchange(give, "blk", distance)
        distance *= 2
    all_sums = to_all(sums)
    parts = [own, keep, got] + returned
    factor, loss = call(
        functools.partial(final_kernel, total_rows),
        [f32((1, s_width)), f32((1, LANES))],
        [totals, all_sums],
        8 * student.size,
    )
    direct = functools.reduce(jnp.add, parts)
    from_centre = packed[:, t_width:].astype(jnp.float32) - totals[3:4, :]
    grad = (2.0 / (total_rows - 1.0)) * direct + factor * from_centre
    return grad, loss[0, :1]


def solution(mesh):
    placed = P(("groups", "blk", "sub"), None)
    return jax.shard_map(
        per_device,
        mesh=mesh,
        in_specs=(placed, placed),
        out_specs=(placed, P("groups")),
        check_vma=False,
    )
```

```python
import functools

import jax
import jax.numpy as jnp
from jax import lax
from jax.experimental import pallas as pl
from jax.experimental.pallas import tpu as pltpu
from jax.sharding import PartitionSpec as P

FLOOR = 0.01
EPSILON = 1e-06
LANES = 128
CHUNK = 256
WHOLE = pl.BlockSpec(memory_space=pltpu.VMEM)


def exchange(value, axis, distance):
    size = lax.axis_size(axis)
    return lax.ppermute(value, axis, [(i, i ^ distance) for i in range(size)])


def shifted(value, axis, distance):
    size = lax.axis_size(axis)
    return lax.ppermute(value, axis, [(i, (i + distance) % size) for i in range(size)])


def pack_kernel(t_hbm, s_hbm, packed_ref, sems):
    t_width = t_hbm.shape[1]
    copies = [
        pltpu.make_async_copy(t_hbm, packed_ref.at[:, :t_width], sems.at[0]),
        pltpu.make_async_copy(s_hbm, packed_ref.at[:, t_width:], sems.at[1]),
    ]
    for copy in copies:
        copy.start()
    for copy in copies:
        copy.wait()


def stats_kernel(t_width, packed_ref, stats_ref):
    value = packed_ref[...].astype(jnp.float32)
    squares = jnp.sum(value * value, axis=0, keepdims=True)
    square_t = jnp.sum(squares[:, :t_width], axis=1, keepdims=True)
    square_s = jnp.sum(squares[:, t_width:], axis=1, keepdims=True)
    lane = lax.broadcasted_iota(jnp.int32, (1, LANES), 1)
    width = value.shape[1]
    stats_ref[:, :width] = jnp.sum(value, axis=0, keepdims=True)
    stats_ref[:, width:] = jnp.where(lane == 0, square_t, jnp.where(lane == 1, square_s, 0.0))


def spreads_of(stats, t_width, s_width, total_rows):
    centre_t = stats[:, :t_width] / total_rows
    centre_s = stats[:, t_width : t_width + s_width] / total_rows
    square_t = stats[:, t_width + s_width : t_width + s_width + 1]
    square_s = stats[:, t_width + s_width + 1 : t_width + s_width + 2]
    spread_t = (
        2.0 * (square_t / total_rows - jnp.sum(centre_t * centre_t, axis=1, keepdims=True)) + EPSILON
    )
    spread_s = (
        2.0 * (square_s / total_rows - jnp.sum(centre_s * centre_s, axis=1, keepdims=True)) + EPSILON
    )
    return spread_t, spread_s, centre_s


def norms_of(value):
    value = value.astype(jnp.float32)
    return jnp.sum(value * value, axis=1, keepdims=True)


def as_row(column):
    rows = column.shape[0]
    row = lax.broadcasted_iota(jnp.int32, (rows, rows), 0)
    same = row == lax.broadcasted_iota(jnp.int32, (rows, rows), 1)
    return jnp.sum(jnp.where(same, column, 0.0), axis=0, keepdims=True)


def with_ones(value):
    return jnp.concatenate([value, jnp.ones((value.shape[0], LANES), value.dtype)], axis=1)


def visiting(ref, t_width):
    t, s = ref[:, :t_width], ref[:, t_width:]
    return t, s, as_row(norms_of(t)), as_row(norms_of(s))


def pair_tile(c, v, inv_t, inv_s, own):
    (ct, cs, nct, ncs), (vt, vs, nvt, nvs) = c, v
    last = (((1,), (1,)), ((), ()))
    gram_t = lax.dot_general(ct, vt, last, preferred_element_type=jnp.float32)
    gram_s = lax.dot_general(cs, vs, last, preferred_element_type=jnp.float32)
    square_t = jnp.maximum(nct + nvt - 2.0 * gram_t, 0.0)
    square_s = jnp.maximum(ncs + nvs - 2.0 * gram_s, 0.0)
    under_t = square_t * inv_t + FLOOR
    under_s = square_s * inv_s + FLOOR
    inverse_s = lax.rsqrt(under_s)
    residue = under_s * inverse_s - under_t * lax.rsqrt(under_t)
    slope = jnp.clip(residue, -1.0, 1.0)
    huber = slope * (residue - 0.5 * slope)
    pull = slope * inverse_s
    if own:
        row = lax.broadcasted_iota(jnp.int32, pull.shape, 0)
        same = row == lax.broadcasted_iota(jnp.int32, pull.shape, 1)
        pull = jnp.where(same, 0.0, pull)
        huber = jnp.where(same, 0.0, huber)
    weights = (pull * inv_s).astype(jnp.bfloat16)
    return (
        weights,
        jnp.sum(huber, axis=0, keepdims=True),
        jnp.sum(pull * square_s, axis=0, keepdims=True),
    )


def direct_of(rows, summed):
    width = rows.shape[1]
    row_weight = jnp.concatenate([summed[:, width:]] * (width // LANES), axis=1)
    return rows.astype(jnp.float32) * row_weight - summed[:, :width]


def chunks_of(ref):
    for h in range(ref.shape[0]):
        for start in range(0, ref.shape[1], CHUNK):
            yield h, pl.ds(start, min(CHUNK, ref.shape[1] - start))


def early_kernel(n_blk, steps, t_width, total_rows, *refs):
    refs = list(refs)
    tiles = [refs.pop(0) for _ in range(n_blk)]
    line = [tiles[0]] + [refs.pop(0) for _ in range(steps - 1)]
    *stats_refs, own_ref = refs[: -4 - steps]
    back_refs = refs[-4 - steps : -5]
    acc_ref, norm_ref, total_ref, sums_ref, plane_ref = refs[-5:]
    rows = own_ref.shape[0]
    for d, ref in enumerate(tiles):
        start = d % (n_blk // 2) * rows
        plane_ref[d // (n_blk // 2), start : start + rows, :] = ref[...]
    s_width = own_ref.shape[1]
    stats = stats_refs[0][...]
    for ref in stats_refs[1:]:
        stats = stats + ref[...]
    spread_t, spread_s, centre_s = spreads_of(stats, t_width, s_width, total_rows)
    inv_t, inv_s = 1.0 / spread_t, 1.0 / spread_s
    for row, value in enumerate((inv_t, inv_s, spread_s)):
        total_ref[row : row + 1, :] = jnp.broadcast_to(value, (1, s_width))
    total_ref[3:4, :] = centre_s
    loss = jnp.zeros((1, LANES), jnp.float32)
    spread = jnp.zeros((1, LANES), jnp.float32)
    if steps == 1:
        acc_ref[...] = jnp.zeros_like(acc_ref)
    for h, at in chunks_of(plane_ref):
        norm_ref[h, 0, at, :] = jnp.broadcast_to(norms_of(plane_ref[h, at, :t_width]), (at.size, LANES))
        norm_ref[h, 1, at, :] = jnp.broadcast_to(norms_of(plane_ref[h, at, t_width:]), (at.size, LANES))
    for k, ref in enumerate(line):
        v = visiting(ref, t_width)
        factor = 1.0 if k == 0 else 2.0
        summed = None
        for h, at in chunks_of(plane_ref):
            cs = plane_ref[h, at, t_width:]
            c = (plane_ref[h, at, :t_width], cs, norm_ref[h, 0, at, :], norm_ref[h, 1, at, :])
            own = k == 0 and h == 0 and at.start == 0
            weights, loss_part, spread_part = pair_tile(c, v, inv_t, inv_s, own)
            loss = loss + factor * loss_part
            spread = spread + factor * spread_part
            term = lax.dot_general(
                weights,
                with_ones(cs),
                (((0,), (0,)), ((), ())),
                preferred_element_type=jnp.float32,
            )
            summed = term if summed is None else summed + term
            if k > 0:
                back = jnp.dot(weights, with_ones(v[1]), preferred_element_type=jnp.float32)
                acc_ref[h, at, :] = back if k == 1 else acc_ref[h, at, :] + back
        to_ref = own_ref if k == 0 else back_refs[k - 1]
        to_ref[...] = direct_of(v[1], summed)
    sums_ref[0:1, :] = loss
    sums_ref[1:2, :] = spread


def late_kernel(side, t_width, *refs):
    if side:
        plane_ref, ref, stats_ref, acc_ref, norm_ref, sums_in, out_ref, sums_ref, visit_ref = refs
        v = visiting(ref, t_width)
        visit_ref[0:1, :], visit_ref[1:2, :] = v[2:]
    else:
        plane_ref, ref, stats_ref, acc_ref, norm_ref, sums_in, visit_ref, out_ref, sums_ref = refs
        v = (ref[:, :t_width], ref[:, t_width:], visit_ref[0:1, :], visit_ref[1:2, :])
    inv_t, inv_s = stats_ref[0:1, :LANES], stats_ref[1:2, :LANES]
    loss = sums_in[0:1, :]
    spread = sums_in[1:2, :]
    for h, at in chunks_of(plane_ref):
        if h != side:
            continue
        cs = plane_ref[h, at, t_width:]
        c = (plane_ref[h, at, :t_width], cs, norm_ref[h, 0, at, :], norm_ref[h, 1, at, :])
        weights, loss_part, spread_part = pair_tile(c, v, inv_t, inv_s, False)
        loss = loss + loss_part
        spread = spread + spread_part
        back = jnp.dot(weights, with_ones(v[1]), preferred_element_type=jnp.float32)
        out_ref[at, :] = direct_of(cs, acc_ref[h, at, :] + back)
    for i in range(1 if side else sums_ref.shape[0]):
        at = sums_ref if side else sums_ref.at[i]
        at[0:1, :] = loss
        at[1:2, :] = spread


def halve_kernel(rows, keep_ref, got_ref, *out_refs):
    out_refs[0][...] = keep_ref[:rows, :] + got_ref[:rows, :]
    out_refs[1][...] = keep_ref[rows : 2 * rows, :] + got_ref[rows : 2 * rows, :]


def final_kernel(t_width, total_rows, packed_ref, stats_ref, sums_ref, *refs):
    *parts, grad_ref, loss_ref = refs
    direct = parts[0][...]
    for part in parts[1:]:
        direct = direct + part[...]
    both = jnp.sum(jnp.sum(sums_ref[...], axis=0), axis=1, keepdims=True)
    loss_total, spread_total = both[0:1, :], -both[1:2, :]
    spread_s, centre = stats_ref[2:3, :], stats_ref[3:4, :]
    pairs = total_rows * (total_rows - 1.0)
    correction = 2.0 * spread_total / (pairs * spread_s * spread_s)
    student = packed_ref[:, t_width:].astype(jnp.float32)
    grad_ref[...] = (2.0 / (total_rows - 1.0)) * direct + correction * (student - centre)
    loss_ref[...] = jnp.broadcast_to(loss_total / pairs, loss_ref.shape)


def call(kernel, out_shape, operands, flops, vmem=48, **more):
    nbytes = sum(x.size * x.dtype.itemsize for x in operands)
    in_specs = more.pop("in_specs", [WHOLE] * len(operands))
    out_specs = more.pop("out_specs", jax.tree.map(lambda _: WHOLE, out_shape))
    return pl.pallas_call(
        kernel,
        out_shape=out_shape,
        in_specs=in_specs,
        out_specs=out_specs,
        compiler_params=pltpu.CompilerParams(vmem_limit_bytes=vmem * 1024 * 1024),
        cost_estimate=pl.CostEstimate(flops=flops, bytes_accessed=nbytes, transcendentals=0),
        **more,
    )(*operands)


def gathered(value, axis):
    return [value] + [exchange(value, axis, d) for d in range(1, lax.axis_size(axis))]


def halvings(axis):
    size = lax.axis_size(axis)
    return [size >> i for i in range(1, size.bit_length())]


def to_all(value):
    return lax.all_to_all(value, ("blk", "sub"), 0, 0, tiled=True)


def per_device(teacher, student):
    rows, t_width = teacher.shape
    s_width = student.shape[1]
    n_blk = lax.axis_size("blk")
    n_sub = lax.axis_size("sub")
    total_rows = float(rows * n_blk * n_sub)
    half = n_sub // 2
    side = rows * n_blk // 2
    f32 = functools.partial(jax.ShapeDtypeStruct, dtype=jnp.float32)

    teacher, student = (pltpu.with_memory_space_constraint(x, pltpu.HBM) for x in (teacher, student))
    packed = call(
        pack_kernel,
        jax.ShapeDtypeStruct((rows, t_width + s_width), teacher.dtype),
        (teacher, student),
        0,
        vmem=48,
        in_specs=[pl.BlockSpec(memory_space=pl.ANY)] * 2,
        scratch_shapes=[pltpu.SemaphoreType.DMA((2,))],
    )
    stats = call(
        functools.partial(stats_kernel, t_width),
        f32((1, t_width + s_width + LANES)),
        (packed,),
        4 * packed.size,
    )
    line = [packed, shifted(packed, "sub", 1)]
    other_stats = exchange(stats, "blk", 1)
    packed, other_stats = lax.optimization_barrier((packed, other_stats))
    stats = stats + other_stats
    tz = [exchange(stats, "sub", d) for d in range(1, n_sub)]
    line[1], *tz = lax.optimization_barrier((line[1], *tz))
    for _ in range(half - 1):
        line.append(shifted(line[-1], "sub", 1))
    stats = functools.reduce(jnp.add, [stats] + tz)
    tiles = [packed]
    distances = halvings("blk")
    for distance in distances:
        if distance == 1:
            *tiles, line[1] = lax.optimization_barrier((*tiles, line[1]))
        elif distance == 2:
            stats = [stats, exchange(stats, "blk", distance)]
        else:
            stats = stats + exchange(stats, "blk", distance)
        tiles = tiles + [exchange(x, "blk", distance) for x in tiles]

    pair_flops = 2 * rows * rows * n_blk * (t_width + 3 * s_width)
    out_shape = (
        [f32((rows, s_width))] * half
        + [f32((2, side, s_width + LANES)), f32((2, 2, side, LANES))]
        + [f32((4, s_width)), f32((2, LANES))]
        + [jax.ShapeDtypeStruct((2, side, t_width + s_width), packed.dtype)]
    )
    *tiles, acc, norms, totals, early_sums, plane = call(
        functools.partial(early_kernel, n_blk, half, t_width, total_rows),
        out_shape,
        tiles + line[1:half] + stats,
        half * pair_flops,
    )
    own, backs = tiles[0], tiles[1:]
    returned = [shifted(x, "sub", -k) for k, x in enumerate(backs, 1)]
    given = [plane, line[half], totals, acc, norms]
    give, late_sums, visit_norms = call(
        functools.partial(late_kernel, 1, t_width),
        [f32((side, s_width)), f32((2, LANES)), f32((2, rows))],
        [*given, early_sums],
        pair_flops // 2,
    )
    keep, sums = call(
        functools.partial(late_kernel, 0, t_width),
        [f32((side, s_width)), f32((n_blk * n_sub, 2, LANES))],
        [*given, late_sums, visit_norms],
        pair_flops // 2,
    )
    got = exchange(give, "blk", 1)
    tiles, distance = n_blk // 2, 2
    while tiles > 1:
        tiles //= 2
        out_shape = [f32((rows * tiles, s_width))] * 2
        keep, give = call(
            functools.partial(halve_kernel, rows * tiles), out_shape, (keep, got), 2 * keep.size
        )
        got = exchange(give, "blk", distance)
        distance *= 2
    all_sums = to_all(sums)
    parts = [own, keep, got] + returned
    grad, loss = call(
        functools.partial(final_kernel, t_width, total_rows),
        [f32((rows, s_width)), f32((1, LANES))],
        [packed, totals, all_sums] + parts,
        8 * student.size,
    )
    return grad, loss[0, :1]


def solution(mesh):
    placed = P(("groups", "blk", "sub"), None)
    return jax.shard_map(
        per_device,
        mesh=mesh,
        in_specs=(placed, placed),
        out_specs=(placed, P("groups")),
        check_vma=False,
    )
```

```python
import functools

import jax
import jax.numpy as jnp
from jax import lax
from jax.experimental import pallas as pl
from jax.experimental.pallas import tpu as pltpu
from jax.sharding import PartitionSpec as P

FLOOR = 0.01
EPSILON = 1e-06
LANES = 128
CHUNK = 256
WHOLE = pl.BlockSpec(memory_space=pltpu.VMEM)


def exchange(value, axis, distance):
    size = lax.axis_size(axis)
    return lax.ppermute(value, axis, [(i, i ^ distance) for i in range(size)])


def shifted(value, axis, distance):
    size = lax.axis_size(axis)
    return lax.ppermute(value, axis, [(i, (i + distance) % size) for i in range(size)])


def pack_kernel(t_hbm, s_hbm, packed_ref, sems):
    t_width = t_hbm.shape[1]
    copies = [
        pltpu.make_async_copy(t_hbm, packed_ref.at[:, :t_width], sems.at[0]),
        pltpu.make_async_copy(s_hbm, packed_ref.at[:, t_width:], sems.at[1]),
    ]
    for copy in copies:
        copy.start()
    for copy in copies:
        copy.wait()


def stats_kernel(t_width, packed_ref, stats_ref):
    value = packed_ref[...].astype(jnp.float32)
    squares = jnp.sum(value * value, axis=0, keepdims=True)
    square_t = jnp.sum(squares[:, :t_width], axis=1, keepdims=True)
    square_s = jnp.sum(squares[:, t_width:], axis=1, keepdims=True)
    lane = lax.broadcasted_iota(jnp.int32, (1, LANES), 1)
    width = value.shape[1]
    stats_ref[:, :width] = jnp.sum(value, axis=0, keepdims=True)
    stats_ref[:, width:] = jnp.where(lane == 0, square_t, jnp.where(lane == 1, square_s, 0.0))


def spreads_of(stats, t_width, s_width, total_rows):
    centre_t = stats[:, :t_width] / total_rows
    centre_s = stats[:, t_width : t_width + s_width] / total_rows
    square_t = stats[:, t_width + s_width : t_width + s_width + 1]
    square_s = stats[:, t_width + s_width + 1 : t_width + s_width + 2]
    spread_t = (
        2.0 * (square_t / total_rows - jnp.sum(centre_t * centre_t, axis=1, keepdims=True)) + EPSILON
    )
    spread_s = (
        2.0 * (square_s / total_rows - jnp.sum(centre_s * centre_s, axis=1, keepdims=True)) + EPSILON
    )
    return spread_t, spread_s, centre_s


def norms_of(value):
    value = value.astype(jnp.float32)
    return jnp.sum(value * value, axis=1, keepdims=True)


def as_row(column):
    rows = column.shape[0]
    row = lax.broadcasted_iota(jnp.int32, (rows, rows), 0)
    same = row == lax.broadcasted_iota(jnp.int32, (rows, rows), 1)
    return jnp.sum(jnp.where(same, column, 0.0), axis=0, keepdims=True)


def with_ones(value):
    return jnp.concatenate([value, jnp.ones((value.shape[0], LANES), value.dtype)], axis=1)


def visiting(ref, t_width):
    t, s = ref[:, :t_width], ref[:, t_width:]
    return t, s, as_row(norms_of(t)), as_row(norms_of(s))


def pair_tile(c, v, inv_t, inv_s, own):
    (ct, cs, nct, ncs), (vt, vs, nvt, nvs) = c, v
    last = (((1,), (1,)), ((), ()))
    gram_t = lax.dot_general(ct, vt, last, preferred_element_type=jnp.float32)
    gram_s = lax.dot_general(cs, vs, last, preferred_element_type=jnp.float32)
    square_t = jnp.maximum(nct + nvt - 2.0 * gram_t, 0.0)
    square_s = jnp.maximum(ncs + nvs - 2.0 * gram_s, 0.0)
    under_t = square_t * inv_t + FLOOR
    under_s = square_s * inv_s + FLOOR
    inverse_s = lax.rsqrt(under_s)
    residue = under_s * inverse_s - under_t * lax.rsqrt(under_t)
    slope = jnp.clip(residue, -1.0, 1.0)
    huber = slope * (residue - 0.5 * slope)
    pull = slope * inverse_s
    if own:
        row = lax.broadcasted_iota(jnp.int32, pull.shape, 0)
        same = row == lax.broadcasted_iota(jnp.int32, pull.shape, 1)
        pull = jnp.where(same, 0.0, pull)
        huber = jnp.where(same, 0.0, huber)
    weights = (pull * inv_s).astype(jnp.bfloat16)
    return (
        weights,
        jnp.sum(huber, axis=0, keepdims=True),
        jnp.sum(pull * square_s, axis=0, keepdims=True),
    )


def direct_of(rows, summed):
    width = rows.shape[1]
    row_weight = jnp.concatenate([summed[:, width:]] * (width // LANES), axis=1)
    return rows.astype(jnp.float32) * row_weight - summed[:, :width]


def chunks_of(ref):
    for h in range(ref.shape[0]):
        for start in range(0, ref.shape[1], CHUNK):
            yield h, pl.ds(start, min(CHUNK, ref.shape[1] - start))


def early_kernel(n_blk, steps, t_width, total_rows, *refs):
    refs = list(refs)
    tiles = [refs.pop(0) for _ in range(n_blk)]
    line = [tiles[0]] + [refs.pop(0) for _ in range(steps - 1)]
    *stats_refs, own_ref = refs[: -4 - steps]
    back_refs = refs[-4 - steps : -5]
    acc_ref, norm_ref, total_ref, sums_ref, plane_ref = refs[-5:]
    rows = own_ref.shape[0]
    for d, ref in enumerate(tiles):
        start = d % (n_blk // 2) * rows
        plane_ref[d // (n_blk // 2), start : start + rows, :] = ref[...]
    s_width = own_ref.shape[1]
    stats = stats_refs[0][...]
    for ref in stats_refs[1:]:
        stats = stats + ref[...]
    spread_t, spread_s, centre_s = spreads_of(stats, t_width, s_width, total_rows)
    inv_t, inv_s = 1.0 / spread_t, 1.0 / spread_s
    for row, value in enumerate((inv_t, inv_s, spread_s)):
        total_ref[row : row + 1, :] = jnp.broadcast_to(value, (1, s_width))
    total_ref[3:4, :] = centre_s
    loss = jnp.zeros((1, LANES), jnp.float32)
    spread = jnp.zeros((1, LANES), jnp.float32)
    if steps == 1:
        acc_ref[...] = jnp.zeros_like(acc_ref)
    for h, at in chunks_of(plane_ref):
        norm_ref[h, 0, at, :] = jnp.broadcast_to(norms_of(plane_ref[h, at, :t_width]), (at.size, LANES))
        norm_ref[h, 1, at, :] = jnp.broadcast_to(norms_of(plane_ref[h, at, t_width:]), (at.size, LANES))
    for k, ref in enumerate(line):
        v = visiting(ref, t_width)
        factor = 1.0 if k == 0 else 2.0
        summed = None
        for h, at in chunks_of(plane_ref):
            cs = plane_ref[h, at, t_width:]
            c = (plane_ref[h, at, :t_width], cs, norm_ref[h, 0, at, :], norm_ref[h, 1, at, :])
            own = k == 0 and h == 0 and at.start == 0
            weights, loss_part, spread_part = pair_tile(c, v, inv_t, inv_s, own)
            loss = loss + factor * loss_part
            spread = spread + factor * spread_part
            term = lax.dot_general(
                weights,
                with_ones(cs),
                (((0,), (0,)), ((), ())),
                preferred_element_type=jnp.float32,
            )
            summed = term if summed is None else summed + term
            if k > 0:
                back = jnp.dot(weights, with_ones(v[1]), preferred_element_type=jnp.float32)
                acc_ref[h, at, :] = back if k == 1 else acc_ref[h, at, :] + back
        to_ref = own_ref if k == 0 else back_refs[k - 1]
        to_ref[...] = direct_of(v[1], summed)
    sums_ref[0:1, :] = loss
    sums_ref[1:2, :] = spread


def late_kernel(side, t_width, *refs):
    if side:
        plane_ref, ref, stats_ref, acc_ref, norm_ref, sums_in, out_ref, sums_ref, visit_ref = refs
        v = visiting(ref, t_width)
        visit_ref[0:1, :], visit_ref[1:2, :] = v[2:]
    else:
        plane_ref, ref, stats_ref, acc_ref, norm_ref, sums_in, visit_ref, out_ref, sums_ref = refs
        v = (ref[:, :t_width], ref[:, t_width:], visit_ref[0:1, :], visit_ref[1:2, :])
    inv_t, inv_s = stats_ref[0:1, :LANES], stats_ref[1:2, :LANES]
    loss = sums_in[0:1, :]
    spread = sums_in[1:2, :]
    for h, at in chunks_of(plane_ref):
        if h != side:
            continue
        cs = plane_ref[h, at, t_width:]
        c = (plane_ref[h, at, :t_width], cs, norm_ref[h, 0, at, :], norm_ref[h, 1, at, :])
        weights, loss_part, spread_part = pair_tile(c, v, inv_t, inv_s, False)
        loss = loss + loss_part
        spread = spread + spread_part
        back = jnp.dot(weights, with_ones(v[1]), preferred_element_type=jnp.float32)
        out_ref[at, :] = direct_of(cs, acc_ref[h, at, :] + back)
    for i in range(1 if side else sums_ref.shape[0]):
        at = sums_ref if side else sums_ref.at[i]
        at[0:1, :] = loss
        at[1:2, :] = spread


def halve_kernel(rows, keep_ref, got_ref, *out_refs):
    out_refs[0][...] = keep_ref[:rows, :] + got_ref[:rows, :]
    out_refs[1][...] = keep_ref[rows : 2 * rows, :] + got_ref[rows : 2 * rows, :]


def final_kernel(t_width, total_rows, packed_ref, stats_ref, sums_ref, *refs):
    *parts, grad_ref, loss_ref = refs
    direct = parts[0][...]
    for part in parts[1:]:
        direct = direct + part[...]
    both = jnp.sum(jnp.sum(sums_ref[...], axis=0), axis=1, keepdims=True)
    loss_total, spread_total = both[0:1, :], -both[1:2, :]
    spread_s, centre = stats_ref[2:3, :], stats_ref[3:4, :]
    pairs = total_rows * (total_rows - 1.0)
    correction = 2.0 * spread_total / (pairs * spread_s * spread_s)
    student = packed_ref[:, t_width:].astype(jnp.float32)
    grad_ref[...] = (2.0 / (total_rows - 1.0)) * direct + correction * (student - centre)
    loss_ref[...] = jnp.broadcast_to(loss_total / pairs, loss_ref.shape)


def call(kernel, out_shape, operands, flops, vmem=48, **more):
    nbytes = sum(x.size * x.dtype.itemsize for x in operands)
    in_specs = more.pop("in_specs", [WHOLE] * len(operands))
    out_specs = more.pop("out_specs", jax.tree.map(lambda _: WHOLE, out_shape))
    return pl.pallas_call(
        kernel,
        out_shape=out_shape,
        in_specs=in_specs,
        out_specs=out_specs,
        compiler_params=pltpu.CompilerParams(vmem_limit_bytes=vmem * 1024 * 1024),
        cost_estimate=pl.CostEstimate(flops=flops, bytes_accessed=nbytes, transcendentals=0),
        **more,
    )(*operands)


def gathered(value, axis):
    return [value] + [exchange(value, axis, d) for d in range(1, lax.axis_size(axis))]


def halvings(axis):
    size = lax.axis_size(axis)
    return [size >> i for i in range(1, size.bit_length())]


def to_all(value):
    return lax.all_to_all(value, ("sub", "blk"), 0, 0, tiled=True)


def per_device(teacher, student):
    rows, t_width = teacher.shape
    s_width = student.shape[1]
    n_blk = lax.axis_size("blk")
    n_sub = lax.axis_size("sub")
    total_rows = float(rows * n_blk * n_sub)
    half = n_sub // 2
    side = rows * n_blk // 2
    f32 = functools.partial(jax.ShapeDtypeStruct, dtype=jnp.float32)

    teacher, student = (pltpu.with_memory_space_constraint(x, pltpu.HBM) for x in (teacher, student))
    packed = call(
        pack_kernel,
        jax.ShapeDtypeStruct((rows, t_width + s_width), teacher.dtype),
        (teacher, student),
        0,
        vmem=48,
        in_specs=[pl.BlockSpec(memory_space=pl.ANY)] * 2,
        scratch_shapes=[pltpu.SemaphoreType.DMA((2,))],
    )
    stats = call(
        functools.partial(stats_kernel, t_width),
        f32((1, t_width + s_width + LANES)),
        (packed,),
        4 * packed.size,
    )
    line = [packed, shifted(packed, "sub", 1)]
    tz = [exchange(stats, "sub", d) for d in range(1, n_sub)]
    line[1], *tz = lax.optimization_barrier((line[1], *tz))
    for _ in range(half - 1):
        line.append(shifted(line[-1], "sub", 1))
    stats = functools.reduce(jnp.add, [stats] + tz)
    tiles = [packed]
    for distance in halvings("blk"):
        if distance == 1:
            *tiles, line[1] = lax.optimization_barrier((*tiles, line[1]))
        else:
            stats = stats + exchange(stats, "blk", distance)
        tiles = tiles + [exchange(x, "blk", distance) for x in tiles]
    stats = [stats, exchange(stats, "blk", 1)]

    pair_flops = 2 * rows * rows * n_blk * (t_width + 3 * s_width)
    out_shape = (
        [f32((rows, s_width))] * half
        + [f32((2, side, s_width + LANES)), f32((2, 2, side, LANES))]
        + [f32((4, s_width)), f32((2, LANES))]
        + [jax.ShapeDtypeStruct((2, side, t_width + s_width), packed.dtype)]
    )
    *tiles, acc, norms, totals, early_sums, plane = call(
        functools.partial(early_kernel, n_blk, half, t_width, total_rows),
        out_shape,
        tiles + line[1:half] + stats,
        half * pair_flops,
    )
    own, backs = tiles[0], tiles[1:]
    returned = [shifted(x, "sub", -k) for k, x in enumerate(backs, 1)]
    given = [plane, line[half], totals, acc, norms]
    give, late_sums, visit_norms = call(
        functools.partial(late_kernel, 1, t_width),
        [f32((side, s_width)), f32((2, LANES)), f32((2, rows))],
        [*given, early_sums],
        pair_flops // 2,
    )
    keep, sums = call(
        functools.partial(late_kernel, 0, t_width),
        [f32((side, s_width)), f32((n_blk * n_sub, 2, LANES))],
        [*given, late_sums, visit_norms],
        pair_flops // 2,
    )
    got = exchange(give, "blk", 1)
    tiles, distance = n_blk // 2, 2
    while tiles > 1:
        tiles //= 2
        out_shape = [f32((rows * tiles, s_width))] * 2
        keep, give = call(
            functools.partial(halve_kernel, rows * tiles), out_shape, (keep, got), 2 * keep.size
        )
        got = exchange(give, "blk", distance)
        distance *= 2
    all_sums = to_all(sums)
    parts = [own, keep, got] + returned
    grad, loss = call(
        functools.partial(final_kernel, t_width, total_rows),
        [f32((rows, s_width)), f32((1, LANES))],
        [packed, totals, all_sums] + parts,
        8 * student.size,
    )
    return grad, loss[0, :1]


def solution(mesh):
    placed = P(("groups", "blk", "sub"), None)
    return jax.shard_map(
        per_device,
        mesh=mesh,
        in_specs=(placed, placed),
        out_specs=(placed, P("groups")),
        check_vma=False,
    )
```

```python
import functools

import jax
import jax.numpy as jnp
from jax import lax
from jax.experimental import pallas as pl
from jax.experimental.pallas import tpu as pltpu
from jax.sharding import PartitionSpec as P

FLOOR = 0.01
EPSILON = 1e-06
LANES = 128
CHUNK = 256
WHOLE = pl.BlockSpec(memory_space=pltpu.VMEM)


def exchange(value, axis, distance):
    size = lax.axis_size(axis)
    return lax.ppermute(value, axis, [(i, i ^ distance) for i in range(size)])


def shifted(value, axis, distance):
    size = lax.axis_size(axis)
    return lax.ppermute(value, axis, [(i, (i + distance) % size) for i in range(size)])


def pack_kernel(t_hbm, s_hbm, packed_ref, sems):
    t_width = t_hbm.shape[1]
    copies = [
        pltpu.make_async_copy(t_hbm, packed_ref.at[:, :t_width], sems.at[0]),
        pltpu.make_async_copy(s_hbm, packed_ref.at[:, t_width:], sems.at[1]),
    ]
    for copy in copies:
        copy.start()
    for copy in copies:
        copy.wait()


def stats_kernel(t_width, packed_ref, stats_ref):
    value = packed_ref[...].astype(jnp.float32)
    squares = jnp.sum(value * value, axis=0, keepdims=True)
    square_t = jnp.sum(squares[:, :t_width], axis=1, keepdims=True)
    square_s = jnp.sum(squares[:, t_width:], axis=1, keepdims=True)
    lane = lax.broadcasted_iota(jnp.int32, (1, LANES), 1)
    width = value.shape[1]
    stats_ref[:, :width] = jnp.sum(value, axis=0, keepdims=True)
    stats_ref[:, width:] = jnp.where(lane == 0, square_t, jnp.where(lane == 1, square_s, 0.0))


def spreads_of(stats, t_width, s_width, total_rows):
    centre_t = stats[:, :t_width] / total_rows
    centre_s = stats[:, t_width : t_width + s_width] / total_rows
    square_t = stats[:, t_width + s_width : t_width + s_width + 1]
    square_s = stats[:, t_width + s_width + 1 : t_width + s_width + 2]
    spread_t = (
        2.0 * (square_t / total_rows - jnp.sum(centre_t * centre_t, axis=1, keepdims=True)) + EPSILON
    )
    spread_s = (
        2.0 * (square_s / total_rows - jnp.sum(centre_s * centre_s, axis=1, keepdims=True)) + EPSILON
    )
    return spread_t, spread_s, centre_s


def norms_of(value):
    value = value.astype(jnp.float32)
    return jnp.sum(value * value, axis=1, keepdims=True)


def as_row(column):
    rows = column.shape[0]
    row = lax.broadcasted_iota(jnp.int32, (rows, rows), 0)
    same = row == lax.broadcasted_iota(jnp.int32, (rows, rows), 1)
    return jnp.sum(jnp.where(same, column, 0.0), axis=0, keepdims=True)


def with_ones(value):
    return jnp.concatenate([value, jnp.ones((value.shape[0], LANES), value.dtype)], axis=1)


def visiting(ref, t_width):
    t, s = ref[:, :t_width], ref[:, t_width:]
    return t, s, as_row(norms_of(t)), as_row(norms_of(s))


def pair_tile(c, v, inv_t, inv_s, own):
    (ct, cs, nct, ncs), (vt, vs, nvt, nvs) = c, v
    last = (((1,), (1,)), ((), ()))
    gram_t = lax.dot_general(ct, vt, last, preferred_element_type=jnp.float32)
    gram_s = lax.dot_general(cs, vs, last, preferred_element_type=jnp.float32)
    square_t = jnp.maximum(nct + nvt - 2.0 * gram_t, 0.0)
    square_s = jnp.maximum(ncs + nvs - 2.0 * gram_s, 0.0)
    under_t = square_t * inv_t + FLOOR
    under_s = square_s * inv_s + FLOOR
    inverse_s = lax.rsqrt(under_s)
    residue = under_s * inverse_s - under_t * lax.rsqrt(under_t)
    slope = jnp.clip(residue, -1.0, 1.0)
    huber = slope * (residue - 0.5 * slope)
    pull = slope * inverse_s
    if own:
        row = lax.broadcasted_iota(jnp.int32, pull.shape, 0)
        same = row == lax.broadcasted_iota(jnp.int32, pull.shape, 1)
        pull = jnp.where(same, 0.0, pull)
        huber = jnp.where(same, 0.0, huber)
    weights = (pull * inv_s).astype(jnp.bfloat16)
    return (
        weights,
        jnp.sum(huber, axis=0, keepdims=True),
        jnp.sum(pull * square_s, axis=0, keepdims=True),
    )


def direct_of(rows, summed):
    width = rows.shape[1]
    row_weight = jnp.concatenate([summed[:, width:]] * (width // LANES), axis=1)
    return rows.astype(jnp.float32) * row_weight - summed[:, :width]


def chunks_of(ref):
    for h in range(ref.shape[0]):
        for start in range(0, ref.shape[1], CHUNK):
            yield h, pl.ds(start, min(CHUNK, ref.shape[1] - start))


def early_kernel(n_blk, steps, t_width, total_rows, *refs):
    refs = list(refs)
    tiles = [refs.pop(0) for _ in range(n_blk)]
    line = [tiles[0]] + [refs.pop(0) for _ in range(steps - 1)]
    *stats_refs, own_ref = refs[: -4 - steps]
    back_refs = refs[-4 - steps : -5]
    acc_ref, norm_ref, total_ref, sums_ref, plane_ref = refs[-5:]
    rows = own_ref.shape[0]
    for d, ref in enumerate(tiles):
        start = d % (n_blk // 2) * rows
        plane_ref[d // (n_blk // 2), start : start + rows, :] = ref[...]
    s_width = own_ref.shape[1]
    stats = stats_refs[0][...]
    for ref in stats_refs[1:]:
        stats = stats + ref[...]
    spread_t, spread_s, centre_s = spreads_of(stats, t_width, s_width, total_rows)
    inv_t, inv_s = 1.0 / spread_t, 1.0 / spread_s
    for row, value in enumerate((inv_t, inv_s, spread_s)):
        total_ref[row : row + 1, :] = jnp.broadcast_to(value, (1, s_width))
    total_ref[3:4, :] = centre_s
    loss = jnp.zeros((1, LANES), jnp.float32)
    spread = jnp.zeros((1, LANES), jnp.float32)
    if steps == 1:
        acc_ref[...] = jnp.zeros_like(acc_ref)
    for h, at in chunks_of(plane_ref):
        norm_ref[h, 0, at, :] = jnp.broadcast_to(norms_of(plane_ref[h, at, :t_width]), (at.size, LANES))
        norm_ref[h, 1, at, :] = jnp.broadcast_to(norms_of(plane_ref[h, at, t_width:]), (at.size, LANES))
    for k, ref in enumerate(line):
        v = visiting(ref, t_width)
        factor = 1.0 if k == 0 else 2.0
        summed = None
        for h, at in chunks_of(plane_ref):
            cs = plane_ref[h, at, t_width:]
            c = (plane_ref[h, at, :t_width], cs, norm_ref[h, 0, at, :], norm_ref[h, 1, at, :])
            own = k == 0 and h == 0 and at.start == 0
            weights, loss_part, spread_part = pair_tile(c, v, inv_t, inv_s, own)
            loss = loss + factor * loss_part
            spread = spread + factor * spread_part
            term = lax.dot_general(
                weights,
                with_ones(cs),
                (((0,), (0,)), ((), ())),
                preferred_element_type=jnp.float32,
            )
            summed = term if summed is None else summed + term
            if k > 0:
                back = jnp.dot(weights, with_ones(v[1]), preferred_element_type=jnp.float32)
                acc_ref[h, at, :] = back if k == 1 else acc_ref[h, at, :] + back
        to_ref = own_ref if k == 0 else back_refs[k - 1]
        to_ref[...] = direct_of(v[1], summed)
    sums_ref[0:1, :] = loss
    sums_ref[1:2, :] = spread


def late_kernel(side, t_width, *refs):
    if side:
        plane_ref, ref, stats_ref, acc_ref, norm_ref, sums_in, *out_refs, sums_ref, visit_ref = refs
        v = visiting(ref, t_width)
        visit_ref[0:1, :], visit_ref[1:2, :] = v[2:]
    else:
        plane_ref, ref, stats_ref, acc_ref, norm_ref, sums_in, visit_ref, *out_refs, sums_ref = refs
        v = (ref[:, :t_width], ref[:, t_width:], visit_ref[0:1, :], visit_ref[1:2, :])
    inv_t, inv_s = stats_ref[0:1, :LANES], stats_ref[1:2, :LANES]
    loss = sums_in[0:1, :]
    spread = sums_in[1:2, :]
    for h, at in chunks_of(plane_ref):
        if h != side:
            continue
        cs = plane_ref[h, at, t_width:]
        c = (plane_ref[h, at, :t_width], cs, norm_ref[h, 0, at, :], norm_ref[h, 1, at, :])
        weights, loss_part, spread_part = pair_tile(c, v, inv_t, inv_s, False)
        loss = loss + loss_part
        spread = spread + spread_part
        back = jnp.dot(weights, with_ones(v[1]), preferred_element_type=jnp.float32)
        direct = direct_of(cs, acc_ref[h, at, :] + back)
        share = out_refs[0].shape[0]
        step = min(share, at.size)
        for begin in range(at.start, at.start + at.size, step):
            to_ref, to = out_refs[begin // share], begin % share
            to_ref[to : to + step, :] = direct[begin - at.start : begin - at.start + step]
    for i in range(1 if side else sums_ref.shape[0]):
        at = sums_ref if side else sums_ref.at[i]
        at[0:1, :] = loss
        at[1:2, :] = spread


def halve_kernel(keep_ref, *refs):
    *got_refs, first_ref, second_ref = refs
    rows = first_ref.shape[0]
    if len(got_refs) == 1:
        got_refs = [got_refs[0].at[:rows, :], got_refs[0].at[rows:, :]]
    first_ref[...] = keep_ref[:rows, :] + got_refs[0][...]
    second_ref[...] = keep_ref[rows:, :] + got_refs[1][...]


def final_kernel(t_width, total_rows, packed_ref, stats_ref, sums_ref, *refs):
    *parts, grad_ref, loss_ref = refs
    direct = parts[0][...]
    for part in parts[1:]:
        direct = direct + part[...]
    both = jnp.sum(jnp.sum(sums_ref[...], axis=0), axis=1, keepdims=True)
    loss_total, spread_total = both[0:1, :], -both[1:2, :]
    spread_s, centre = stats_ref[2:3, :], stats_ref[3:4, :]
    pairs = total_rows * (total_rows - 1.0)
    correction = 2.0 * spread_total / (pairs * spread_s * spread_s)
    student = packed_ref[:, t_width:].astype(jnp.float32)
    grad_ref[...] = (2.0 / (total_rows - 1.0)) * direct + correction * (student - centre)
    loss_ref[...] = jnp.broadcast_to(loss_total / pairs, loss_ref.shape)


def call(kernel, out_shape, operands, flops, vmem=48, **more):
    nbytes = sum(x.size * x.dtype.itemsize for x in operands)
    in_specs = more.pop("in_specs", [WHOLE] * len(operands))
    out_specs = more.pop("out_specs", jax.tree.map(lambda _: WHOLE, out_shape))
    return pl.pallas_call(
        kernel,
        out_shape=out_shape,
        in_specs=in_specs,
        out_specs=out_specs,
        compiler_params=pltpu.CompilerParams(vmem_limit_bytes=vmem * 1024 * 1024),
        cost_estimate=pl.CostEstimate(flops=flops, bytes_accessed=nbytes, transcendentals=0),
        **more,
    )(*operands)


def gathered(value, axis):
    return [value] + [exchange(value, axis, d) for d in range(1, lax.axis_size(axis))]


def halvings(axis):
    size = lax.axis_size(axis)
    return [size >> i for i in range(1, size.bit_length())]


def to_all(value):
    return lax.all_to_all(value, ("blk", "sub"), 0, 0, tiled=True)


def per_device(teacher, student):
    rows, t_width = teacher.shape
    s_width = student.shape[1]
    n_blk = lax.axis_size("blk")
    n_sub = lax.axis_size("sub")
    total_rows = float(rows * n_blk * n_sub)
    half = n_sub // 2
    side = rows * n_blk // 2
    f32 = functools.partial(jax.ShapeDtypeStruct, dtype=jnp.float32)

    teacher, student = (pltpu.with_memory_space_constraint(x, pltpu.HBM) for x in (teacher, student))
    packed = call(
        pack_kernel,
        jax.ShapeDtypeStruct((rows, t_width + s_width), teacher.dtype),
        (teacher, student),
        0,
        vmem=48,
        in_specs=[pl.BlockSpec(memory_space=pl.ANY)] * 2,
        scratch_shapes=[pltpu.SemaphoreType.DMA((2,))],
    )
    stats = call(
        functools.partial(stats_kernel, t_width),
        f32((1, t_width + s_width + LANES)),
        (packed,),
        4 * packed.size,
    )
    line = [packed, shifted(packed, "sub", 1)]
    tz = [exchange(stats, "sub", d) for d in range(1, n_sub)]
    line[1], *tz = lax.optimization_barrier((line[1], *tz))
    for _ in range(half - 1):
        line.append(shifted(line[-1], "sub", 1))
    stats = functools.reduce(jnp.add, [stats] + tz)
    tiles = [packed]
    for distance in halvings("blk"):
        if distance == 1:
            *tiles, line[1] = lax.optimization_barrier((*tiles, line[1]))
        else:
            stats = stats + exchange(stats, "blk", distance)
        tiles = tiles + [exchange(x, "blk", distance) for x in tiles]
    stats = [stats, exchange(stats, "blk", 1)]

    pair_flops = 2 * rows * rows * n_blk * (t_width + 3 * s_width)
    out_shape = (
        [f32((rows, s_width))] * half
        + [f32((2, side, s_width + LANES)), f32((2, 2, side, LANES))]
        + [f32((4, s_width)), f32((2, LANES))]
        + [jax.ShapeDtypeStruct((2, side, t_width + s_width), packed.dtype)]
    )
    *tiles, acc, norms, totals, early_sums, plane = call(
        functools.partial(early_kernel, n_blk, half, t_width, total_rows),
        out_shape,
        tiles + line[1:half] + stats,
        half * pair_flops,
    )
    own, backs = tiles[0], tiles[1:]
    returned = [shifted(x, "sub", -k) for k, x in enumerate(backs, 1)]
    given = [plane, line[half], totals, acc, norms]
    *give, late_sums, visit_norms = call(
        functools.partial(late_kernel, 1, t_width),
        [f32((side // 2, s_width))] * 2 + [f32((2, LANES)), f32((2, rows))],
        [*given, early_sums],
        pair_flops // 2,
    )
    keep, sums = call(
        functools.partial(late_kernel, 0, t_width),
        [f32((side, s_width)), f32((n_blk * n_sub, 2, LANES))],
        [*given, late_sums, visit_norms],
        pair_flops // 2,
    )
    got = [exchange(x, "blk", 1) for x in give]
    tiles, distance = n_blk // 2, 2
    while tiles > 1:
        tiles //= 2
        out_shape = [f32((rows * tiles, s_width))] * 2
        keep, give = call(halve_kernel, out_shape, (keep, *got), 2 * keep.size)
        got = [exchange(give, "blk", distance)]
        distance *= 2
    all_sums = to_all(sums)
    parts = [own, keep] + got + returned
    grad, loss = call(
        functools.partial(final_kernel, t_width, total_rows),
        [f32((rows, s_width)), f32((1, LANES))],
        [packed, totals, all_sums] + parts,
        8 * student.size,
    )
    return grad, loss[0, :1]


def solution(mesh):
    placed = P(("groups", "blk", "sub"), None)
    return jax.shard_map(
        per_device,
        mesh=mesh,
        in_specs=(placed, placed),
        out_specs=(placed, P("groups")),
        check_vma=False,
    )
```

```python
import functools

import jax
import jax.numpy as jnp
from jax import lax
from jax.experimental import pallas as pl
from jax.experimental.pallas import tpu as pltpu
from jax.sharding import PartitionSpec as P

FLOOR = 0.01
EPSILON = 1e-06
LANES = 128
CHUNK = 256
WHOLE = pl.BlockSpec(memory_space=pltpu.VMEM)


def exchange(value, axis, distance):
    size = lax.axis_size(axis)
    return lax.ppermute(value, axis, [(i, i ^ distance) for i in range(size)])


def shifted(value, axis, distance):
    size = lax.axis_size(axis)
    return lax.ppermute(value, axis, [(i, (i + distance) % size) for i in range(size)])


def pack_kernel(t_hbm, s_hbm, packed_ref, sems):
    t_width = t_hbm.shape[1]
    copies = [
        pltpu.make_async_copy(t_hbm, packed_ref.at[:, :t_width], sems.at[0]),
        pltpu.make_async_copy(s_hbm, packed_ref.at[:, t_width:], sems.at[1]),
    ]
    for copy in copies:
        copy.start()
    for copy in copies:
        copy.wait()


def stats_kernel(t_width, packed_ref, stats_ref):
    value = packed_ref[...].astype(jnp.float32)
    squares = jnp.sum(value * value, axis=0, keepdims=True)
    square_t = jnp.sum(squares[:, :t_width], axis=1, keepdims=True)
    square_s = jnp.sum(squares[:, t_width:], axis=1, keepdims=True)
    lane = lax.broadcasted_iota(jnp.int32, (1, LANES), 1)
    width = value.shape[1]
    stats_ref[:, :width] = jnp.sum(value, axis=0, keepdims=True)
    stats_ref[:, width:] = jnp.where(lane == 0, square_t, jnp.where(lane == 1, square_s, 0.0))


def spreads_of(stats, t_width, s_width, total_rows):
    centre_t = stats[:, :t_width] / total_rows
    centre_s = stats[:, t_width : t_width + s_width] / total_rows
    square_t = stats[:, t_width + s_width : t_width + s_width + 1]
    square_s = stats[:, t_width + s_width + 1 : t_width + s_width + 2]
    spread_t = (
        2.0 * (square_t / total_rows - jnp.sum(centre_t * centre_t, axis=1, keepdims=True)) + EPSILON
    )
    spread_s = (
        2.0 * (square_s / total_rows - jnp.sum(centre_s * centre_s, axis=1, keepdims=True)) + EPSILON
    )
    return spread_t, spread_s, centre_s


def norms_of(value):
    value = value.astype(jnp.float32)
    return jnp.sum(value * value, axis=1, keepdims=True)


def as_row(column):
    rows = column.shape[0]
    row = lax.broadcasted_iota(jnp.int32, (rows, rows), 0)
    same = row == lax.broadcasted_iota(jnp.int32, (rows, rows), 1)
    return jnp.sum(jnp.where(same, column, 0.0), axis=0, keepdims=True)


def with_ones(value):
    return jnp.concatenate([value, jnp.ones((value.shape[0], LANES), value.dtype)], axis=1)


def visiting(ref, t_width):
    t, s = ref[:, :t_width], ref[:, t_width:]
    return t, s, as_row(norms_of(t)), as_row(norms_of(s))


def pair_tile(c, v, inv_t, inv_s, own):
    (ct, cs, nct, ncs), (vt, vs, nvt, nvs) = c, v
    last = (((1,), (1,)), ((), ()))
    gram_t = lax.dot_general(ct, vt, last, preferred_element_type=jnp.float32)
    gram_s = lax.dot_general(cs, vs, last, preferred_element_type=jnp.float32)
    square_t = jnp.maximum(nct + nvt - 2.0 * gram_t, 0.0)
    square_s = jnp.maximum(ncs + nvs - 2.0 * gram_s, 0.0)
    under_t = square_t * inv_t + FLOOR
    under_s = square_s * inv_s + FLOOR
    inverse_s = lax.rsqrt(under_s)
    residue = under_s * inverse_s - under_t * lax.rsqrt(under_t)
    slope = jnp.clip(residue, -1.0, 1.0)
    huber = slope * (residue - 0.5 * slope)
    pull = slope * inverse_s
    if own:
        row = lax.broadcasted_iota(jnp.int32, pull.shape, 0)
        same = row == lax.broadcasted_iota(jnp.int32, pull.shape, 1)
        pull = jnp.where(same, 0.0, pull)
        huber = jnp.where(same, 0.0, huber)
    weights = (pull * inv_s).astype(jnp.bfloat16)
    return (
        weights,
        jnp.sum(huber, axis=0, keepdims=True),
        jnp.sum(pull * square_s, axis=0, keepdims=True),
    )


def direct_of(rows, summed):
    width = rows.shape[1]
    row_weight = jnp.concatenate([summed[:, width:]] * (width // LANES), axis=1)
    return rows.astype(jnp.float32) * row_weight - summed[:, :width]


def chunks_of(ref):
    for h in range(ref.shape[0]):
        for start in range(0, ref.shape[1], CHUNK):
            yield h, pl.ds(start, min(CHUNK, ref.shape[1] - start))


def early_kernel(n_blk, steps, t_width, total_rows, *refs):
    refs = list(refs)
    tiles = [refs.pop(0) for _ in range(n_blk)]
    line = [tiles[0]] + [refs.pop(0) for _ in range(steps - 1)]
    *stats_refs, own_ref = refs[: -4 - steps]
    back_refs = refs[-4 - steps : -5]
    acc_ref, norm_ref, total_ref, sums_ref, plane_ref = refs[-5:]
    rows = own_ref.shape[0]
    for d, ref in enumerate(tiles):
        start = d % (n_blk // 2) * rows
        plane_ref[d // (n_blk // 2), start : start + rows, :] = ref[...]
    s_width = own_ref.shape[1]
    stats = stats_refs[0][...]
    for ref in stats_refs[1:]:
        stats = stats + ref[...]
    spread_t, spread_s, centre_s = spreads_of(stats, t_width, s_width, total_rows)
    inv_t, inv_s = 1.0 / spread_t, 1.0 / spread_s
    for row, value in enumerate((inv_t, inv_s, spread_s)):
        total_ref[row : row + 1, :] = jnp.broadcast_to(value, (1, s_width))
    total_ref[3:4, :] = centre_s
    loss = jnp.zeros((1, LANES), jnp.float32)
    spread = jnp.zeros((1, LANES), jnp.float32)
    if steps == 1:
        acc_ref[...] = jnp.zeros_like(acc_ref)
    for h, at in chunks_of(plane_ref):
        norm_ref[h, 0, at, :] = jnp.broadcast_to(norms_of(plane_ref[h, at, :t_width]), (at.size, LANES))
        norm_ref[h, 1, at, :] = jnp.broadcast_to(norms_of(plane_ref[h, at, t_width:]), (at.size, LANES))
    for k, ref in enumerate(line):
        v = visiting(ref, t_width)
        factor = 1.0 if k == 0 else 2.0
        summed = None
        for h, at in chunks_of(plane_ref):
            cs = plane_ref[h, at, t_width:]
            c = (plane_ref[h, at, :t_width], cs, norm_ref[h, 0, at, :], norm_ref[h, 1, at, :])
            own = k == 0 and h == 0 and at.start == 0
            weights, loss_part, spread_part = pair_tile(c, v, inv_t, inv_s, own)
            loss = loss + factor * loss_part
            spread = spread + factor * spread_part
            term = lax.dot_general(
                weights,
                with_ones(cs),
                (((0,), (0,)), ((), ())),
                preferred_element_type=jnp.float32,
            )
            summed = term if summed is None else summed + term
            if k > 0:
                back = jnp.dot(weights, with_ones(v[1]), preferred_element_type=jnp.float32)
                acc_ref[h, at, :] = back if k == 1 else acc_ref[h, at, :] + back
        to_ref = own_ref if k == 0 else back_refs[k - 1]
        to_ref[...] = direct_of(v[1], summed)
    sums_ref[0:1, :] = loss
    sums_ref[1:2, :] = spread


def late_kernel(side, t_width, *refs):
    if side:
        plane_ref, ref, stats_ref, acc_ref, norm_ref, sums_in, out_ref, sums_ref, visit_ref = refs
        v = visiting(ref, t_width)
        visit_ref[0:1, :], visit_ref[1:2, :] = v[2:]
    else:
        plane_ref, ref, stats_ref, acc_ref, norm_ref, sums_in, visit_ref, out_ref, sums_ref = refs
        v = (ref[:, :t_width], ref[:, t_width:], visit_ref[0:1, :], visit_ref[1:2, :])
    inv_t, inv_s = stats_ref[0:1, :LANES], stats_ref[1:2, :LANES]
    loss = sums_in[0:1, :]
    spread = sums_in[1:2, :]
    for h, at in chunks_of(plane_ref):
        if h != side:
            continue
        cs = plane_ref[h, at, t_width:]
        c = (plane_ref[h, at, :t_width], cs, norm_ref[h, 0, at, :], norm_ref[h, 1, at, :])
        weights, loss_part, spread_part = pair_tile(c, v, inv_t, inv_s, False)
        loss = loss + loss_part
        spread = spread + spread_part
        back = jnp.dot(weights, with_ones(v[1]), preferred_element_type=jnp.float32)
        out_ref[at, :] = direct_of(cs, acc_ref[h, at, :] + back)
    if side:
        sums_ref[0:1, :] = loss
        sums_ref[1:2, :] = spread
    else:
        middle = LANES // 2
        folded = [row[:, :middle] + row[:, middle:] for row in (loss, spread)]
        row = jnp.concatenate(folded, axis=1)
        sums_ref[...] = jnp.broadcast_to(row[None], sums_ref.shape)


def halve_kernel(rows, keep_ref, got_ref, *out_refs):
    out_refs[0][...] = keep_ref[:rows, :] + got_ref[:rows, :]
    out_refs[1][...] = keep_ref[rows : 2 * rows, :] + got_ref[rows : 2 * rows, :]


def final_kernel(t_width, total_rows, packed_ref, stats_ref, sums_ref, *refs):
    *parts, grad_ref, loss_ref = refs
    direct = parts[0][...]
    for part in parts[1:]:
        direct = direct + part[...]
    both = jnp.sum(sums_ref[...], axis=0)
    loss_total = jnp.sum(both[:, : LANES // 2], axis=1, keepdims=True)
    spread_total = -jnp.sum(both[:, LANES // 2 :], axis=1, keepdims=True)
    spread_s, centre = stats_ref[2:3, :], stats_ref[3:4, :]
    pairs = total_rows * (total_rows - 1.0)
    correction = 2.0 * spread_total / (pairs * spread_s * spread_s)
    student = packed_ref[:, t_width:].astype(jnp.float32)
    grad_ref[...] = (2.0 / (total_rows - 1.0)) * direct + correction * (student - centre)
    loss_ref[...] = jnp.broadcast_to(loss_total / pairs, loss_ref.shape)


def call(kernel, out_shape, operands, flops, vmem=48, **more):
    nbytes = sum(x.size * x.dtype.itemsize for x in operands)
    in_specs = more.pop("in_specs", [WHOLE] * len(operands))
    out_specs = more.pop("out_specs", jax.tree.map(lambda _: WHOLE, out_shape))
    return pl.pallas_call(
        kernel,
        out_shape=out_shape,
        in_specs=in_specs,
        out_specs=out_specs,
        compiler_params=pltpu.CompilerParams(vmem_limit_bytes=vmem * 1024 * 1024),
        cost_estimate=pl.CostEstimate(flops=flops, bytes_accessed=nbytes, transcendentals=0),
        **more,
    )(*operands)


def gathered(value, axis):
    return [value] + [exchange(value, axis, d) for d in range(1, lax.axis_size(axis))]


def halvings(axis):
    size = lax.axis_size(axis)
    return [size >> i for i in range(1, size.bit_length())]


def to_all(value):
    return lax.all_to_all(value, ("blk", "sub"), 0, 0, tiled=True)


def per_device(teacher, student):
    rows, t_width = teacher.shape
    s_width = student.shape[1]
    n_blk = lax.axis_size("blk")
    n_sub = lax.axis_size("sub")
    total_rows = float(rows * n_blk * n_sub)
    half = n_sub // 2
    side = rows * n_blk // 2
    f32 = functools.partial(jax.ShapeDtypeStruct, dtype=jnp.float32)

    teacher, student = (pltpu.with_memory_space_constraint(x, pltpu.HBM) for x in (teacher, student))
    packed = call(
        pack_kernel,
        jax.ShapeDtypeStruct((rows, t_width + s_width), teacher.dtype),
        (teacher, student),
        0,
        vmem=48,
        in_specs=[pl.BlockSpec(memory_space=pl.ANY)] * 2,
        scratch_shapes=[pltpu.SemaphoreType.DMA((2,))],
    )
    stats = call(
        functools.partial(stats_kernel, t_width),
        f32((1, t_width + s_width + LANES)),
        (packed,),
        4 * packed.size,
    )
    line = [packed, shifted(packed, "sub", 1)]
    tz = [exchange(stats, "sub", d) for d in range(1, n_sub)]
    line[1], *tz = lax.optimization_barrier((line[1], *tz))
    for _ in range(half - 1):
        line.append(shifted(line[-1], "sub", 1))
    stats = functools.reduce(jnp.add, [stats] + tz)
    tiles = [packed]
    for distance in halvings("blk"):
        if distance == 1:
            *tiles, line[1] = lax.optimization_barrier((*tiles, line[1]))
        else:
            stats = stats + exchange(stats, "blk", distance)
        tiles = tiles + [exchange(x, "blk", distance) for x in tiles]
    stats = [stats, exchange(stats, "blk", 1)]

    pair_flops = 2 * rows * rows * n_blk * (t_width + 3 * s_width)
    out_shape = (
        [f32((rows, s_width))] * half
        + [f32((2, side, s_width + LANES)), f32((2, 2, side, LANES))]
        + [f32((4, s_width)), f32((2, LANES))]
        + [jax.ShapeDtypeStruct((2, side, t_width + s_width), packed.dtype)]
    )
    *tiles, acc, norms, totals, early_sums, plane = call(
        functools.partial(early_kernel, n_blk, half, t_width, total_rows),
        out_shape,
        tiles + line[1:half] + stats,
        half * pair_flops,
    )
    own, backs = tiles[0], tiles[1:]
    returned = [shifted(x, "sub", -k) for k, x in enumerate(backs, 1)]
    given = [plane, line[half], totals, acc, norms]
    give, late_sums, visit_norms = call(
        functools.partial(late_kernel, 1, t_width),
        [f32((side, s_width)), f32((2, LANES)), f32((2, rows))],
        [*given, early_sums],
        pair_flops // 2,
    )
    keep, sums = call(
        functools.partial(late_kernel, 0, t_width),
        [f32((side, s_width)), f32((n_blk * n_sub, 1, LANES))],
        [*given, late_sums, visit_norms],
        pair_flops // 2,
    )
    got = exchange(give, "blk", 1)
    tiles, distance = n_blk // 2, 2
    while tiles > 1:
        tiles //= 2
        out_shape = [f32((rows * tiles, s_width))] * 2
        keep, give = call(
            functools.partial(halve_kernel, rows * tiles), out_shape, (keep, got), 2 * keep.size
        )
        got = exchange(give, "blk", distance)
        distance *= 2
    all_sums = to_all(sums)
    parts = [own, keep, got] + returned
    grad, loss = call(
        functools.partial(final_kernel, t_width, total_rows),
        [f32((rows, s_width)), f32((1, LANES))],
        [packed, totals, all_sums] + parts,
        8 * student.size,
    )
    return grad, loss[0, :1]


def solution(mesh):
    placed = P(("groups", "blk", "sub"), None)
    return jax.shard_map(
        per_device,
        mesh=mesh,
        in_specs=(placed, placed),
        out_specs=(placed, P("groups")),
        check_vma=False,
    )
```

```python
import functools

import jax
import jax.numpy as jnp
from jax import lax
from jax.experimental import pallas as pl
from jax.experimental.pallas import tpu as pltpu
from jax.sharding import PartitionSpec as P

FLOOR = 0.01
EPSILON = 1e-06
LANES = 128
CHUNK = 256
WHOLE = pl.BlockSpec(memory_space=pltpu.VMEM)


def exchange(value, axis, distance):
    size = lax.axis_size(axis)
    return lax.ppermute(value, axis, [(i, i ^ distance) for i in range(size)])


def shifted(value, axis, distance):
    size = lax.axis_size(axis)
    places = [0, *range(1, size, 2), *reversed(range(2, size, 2))]
    route = [(places[i], places[(i + distance) % size]) for i in range(size)]
    return lax.ppermute(value, axis, route)


def pack_kernel(t_hbm, s_hbm, packed_ref, sems):
    t_width = t_hbm.shape[1]
    copies = [
        pltpu.make_async_copy(t_hbm, packed_ref.at[:, :t_width], sems.at[0]),
        pltpu.make_async_copy(s_hbm, packed_ref.at[:, t_width:], sems.at[1]),
    ]
    for copy in copies:
        copy.start()
    for copy in copies:
        copy.wait()


def stats_kernel(t_width, packed_ref, stats_ref):
    value = packed_ref[...].astype(jnp.float32)
    squares = jnp.sum(value * value, axis=0, keepdims=True)
    square_t = jnp.sum(squares[:, :t_width], axis=1, keepdims=True)
    square_s = jnp.sum(squares[:, t_width:], axis=1, keepdims=True)
    lane = lax.broadcasted_iota(jnp.int32, (1, LANES), 1)
    width = value.shape[1]
    stats_ref[:, :width] = jnp.sum(value, axis=0, keepdims=True)
    stats_ref[:, width:] = jnp.where(lane == 0, square_t, jnp.where(lane == 1, square_s, 0.0))


def spreads_of(stats, t_width, s_width, total_rows):
    centre_t = stats[:, :t_width] / total_rows
    centre_s = stats[:, t_width : t_width + s_width] / total_rows
    square_t = stats[:, t_width + s_width : t_width + s_width + 1]
    square_s = stats[:, t_width + s_width + 1 : t_width + s_width + 2]
    spread_t = (
        2.0 * (square_t / total_rows - jnp.sum(centre_t * centre_t, axis=1, keepdims=True)) + EPSILON
    )
    spread_s = (
        2.0 * (square_s / total_rows - jnp.sum(centre_s * centre_s, axis=1, keepdims=True)) + EPSILON
    )
    return spread_t, spread_s, centre_s


def norms_of(value):
    value = value.astype(jnp.float32)
    return jnp.sum(value * value, axis=1, keepdims=True)


def as_row(column):
    rows = column.shape[0]
    row = lax.broadcasted_iota(jnp.int32, (rows, rows), 0)
    same = row == lax.broadcasted_iota(jnp.int32, (rows, rows), 1)
    return jnp.sum(jnp.where(same, column, 0.0), axis=0, keepdims=True)


def with_ones(value):
    return jnp.concatenate([value, jnp.ones((value.shape[0], LANES), value.dtype)], axis=1)


def visiting(ref, t_width):
    t, s = ref[:, :t_width], ref[:, t_width:]
    return t, s, as_row(norms_of(t)), as_row(norms_of(s))


def pair_tile(c, v, inv_t, inv_s, own):
    (ct, cs, nct, ncs), (vt, vs, nvt, nvs) = c, v
    last = (((1,), (1,)), ((), ()))
    gram_t = lax.dot_general(ct, vt, last, preferred_element_type=jnp.float32)
    gram_s = lax.dot_general(cs, vs, last, preferred_element_type=jnp.float32)
    square_t = jnp.maximum(nct + nvt - 2.0 * gram_t, 0.0)
    square_s = jnp.maximum(ncs + nvs - 2.0 * gram_s, 0.0)
    under_t = square_t * inv_t + FLOOR
    under_s = square_s * inv_s + FLOOR
    inverse_s = lax.rsqrt(under_s)
    residue = under_s * inverse_s - under_t * lax.rsqrt(under_t)
    slope = jnp.clip(residue, -1.0, 1.0)
    huber = slope * (residue - 0.5 * slope)
    pull = slope * inverse_s
    if own:
        row = lax.broadcasted_iota(jnp.int32, pull.shape, 0)
        same = row == lax.broadcasted_iota(jnp.int32, pull.shape, 1)
        pull = jnp.where(same, 0.0, pull)
        huber = jnp.where(same, 0.0, huber)
    weights = (pull * inv_s).astype(jnp.bfloat16)
    return (
        weights,
        jnp.sum(huber, axis=0, keepdims=True),
        jnp.sum(pull * square_s, axis=0, keepdims=True),
    )


def direct_of(rows, summed):
    width = rows.shape[1]
    row_weight = jnp.concatenate([summed[:, width:]] * (width // LANES), axis=1)
    return rows.astype(jnp.float32) * row_weight - summed[:, :width]


def chunks_of(ref):
    for h in range(ref.shape[0]):
        for start in range(0, ref.shape[1], CHUNK):
            yield h, pl.ds(start, min(CHUNK, ref.shape[1] - start))


def early_kernel(n_blk, steps, t_width, total_rows, *refs):
    refs = list(refs)
    tiles = [refs.pop(0) for _ in range(n_blk)]
    line = [tiles[0]] + [refs.pop(0) for _ in range(steps - 1)]
    *stats_refs, own_ref = refs[: -4 - steps]
    back_refs = refs[-4 - steps : -5]
    acc_ref, norm_ref, total_ref, sums_ref, plane_ref = refs[-5:]
    rows = own_ref.shape[0]
    for d, ref in enumerate(tiles):
        start = d % (n_blk // 2) * rows
        plane_ref[d // (n_blk // 2), start : start + rows, :] = ref[...]
    s_width = own_ref.shape[1]
    stats = stats_refs[0][...]
    for ref in stats_refs[1:]:
        stats = stats + ref[...]
    spread_t, spread_s, centre_s = spreads_of(stats, t_width, s_width, total_rows)
    inv_t, inv_s = 1.0 / spread_t, 1.0 / spread_s
    for row, value in enumerate((inv_t, inv_s, spread_s)):
        total_ref[row : row + 1, :] = jnp.broadcast_to(value, (1, s_width))
    total_ref[3:4, :] = centre_s
    loss = jnp.zeros((1, LANES), jnp.float32)
    spread = jnp.zeros((1, LANES), jnp.float32)
    if steps == 1:
        acc_ref[...] = jnp.zeros_like(acc_ref)
    for h, at in chunks_of(plane_ref):
        norm_ref[h, 0, at, :] = jnp.broadcast_to(norms_of(plane_ref[h, at, :t_width]), (at.size, LANES))
        norm_ref[h, 1, at, :] = jnp.broadcast_to(norms_of(plane_ref[h, at, t_width:]), (at.size, LANES))
    for k, ref in enumerate(line):
        v = visiting(ref, t_width)
        factor = 1.0 if k == 0 else 2.0
        summed = None
        for h, at in chunks_of(plane_ref):
            cs = plane_ref[h, at, t_width:]
            c = (plane_ref[h, at, :t_width], cs, norm_ref[h, 0, at, :], norm_ref[h, 1, at, :])
            own = k == 0 and h == 0 and at.start == 0
            weights, loss_part, spread_part = pair_tile(c, v, inv_t, inv_s, own)
            loss = loss + factor * loss_part
            spread = spread + factor * spread_part
            term = lax.dot_general(
                weights,
                with_ones(cs),
                (((0,), (0,)), ((), ())),
                preferred_element_type=jnp.float32,
            )
            summed = term if summed is None else summed + term
            if k > 0:
                back = jnp.dot(weights, with_ones(v[1]), preferred_element_type=jnp.float32)
                acc_ref[h, at, :] = back if k == 1 else acc_ref[h, at, :] + back
        to_ref = own_ref if k == 0 else back_refs[k - 1]
        to_ref[...] = direct_of(v[1], summed)
    sums_ref[0:1, :] = loss
    sums_ref[1:2, :] = spread


def late_kernel(side, t_width, *refs):
    if side:
        plane_ref, ref, stats_ref, acc_ref, norm_ref, sums_in, out_ref, sums_ref, visit_ref = refs
        v = visiting(ref, t_width)
        visit_ref[0:1, :], visit_ref[1:2, :] = v[2:]
    else:
        plane_ref, ref, stats_ref, acc_ref, norm_ref, sums_in, visit_ref, out_ref, sums_ref = refs
        v = (ref[:, :t_width], ref[:, t_width:], visit_ref[0:1, :], visit_ref[1:2, :])
    inv_t, inv_s = stats_ref[0:1, :LANES], stats_ref[1:2, :LANES]
    loss = sums_in[0:1, :]
    spread = sums_in[1:2, :]
    for h, at in chunks_of(plane_ref):
        if h != side:
            continue
        cs = plane_ref[h, at, t_width:]
        c = (plane_ref[h, at, :t_width], cs, norm_ref[h, 0, at, :], norm_ref[h, 1, at, :])
        weights, loss_part, spread_part = pair_tile(c, v, inv_t, inv_s, False)
        loss = loss + loss_part
        spread = spread + spread_part
        back = jnp.dot(weights, with_ones(v[1]), preferred_element_type=jnp.float32)
        out_ref[at, :] = direct_of(cs, acc_ref[h, at, :] + back)
    if side:
        sums_ref[0:1, :] = loss
        sums_ref[1:2, :] = spread
    else:
        middle = LANES // 2
        folded = [row[:, :middle] + row[:, middle:] for row in (loss, spread)]
        row = jnp.concatenate(folded, axis=1)
        sums_ref[...] = jnp.broadcast_to(row[None], sums_ref.shape)


def halve_kernel(rows, keep_ref, got_ref, *out_refs):
    out_refs[0][...] = keep_ref[:rows, :] + got_ref[:rows, :]
    out_refs[1][...] = keep_ref[rows : 2 * rows, :] + got_ref[rows : 2 * rows, :]


def final_kernel(t_width, total_rows, packed_ref, stats_ref, sums_ref, *refs):
    *parts, grad_ref, loss_ref = refs
    direct = parts[0][...]
    for part in parts[1:]:
        direct = direct + part[...]
    both = jnp.sum(sums_ref[...], axis=0)
    loss_total = jnp.sum(both[:, : LANES // 2], axis=1, keepdims=True)
    spread_total = -jnp.sum(both[:, LANES // 2 :], axis=1, keepdims=True)
    spread_s, centre = stats_ref[2:3, :], stats_ref[3:4, :]
    pairs = total_rows * (total_rows - 1.0)
    correction = 2.0 * spread_total / (pairs * spread_s * spread_s)
    student = packed_ref[:, t_width:].astype(jnp.float32)
    grad_ref[...] = (2.0 / (total_rows - 1.0)) * direct + correction * (student - centre)
    loss_ref[...] = jnp.broadcast_to(loss_total / pairs, loss_ref.shape)


def call(kernel, out_shape, operands, flops, vmem=48, **more):
    nbytes = sum(x.size * x.dtype.itemsize for x in operands)
    in_specs = more.pop("in_specs", [WHOLE] * len(operands))
    out_specs = more.pop("out_specs", jax.tree.map(lambda _: WHOLE, out_shape))
    return pl.pallas_call(
        kernel,
        out_shape=out_shape,
        in_specs=in_specs,
        out_specs=out_specs,
        compiler_params=pltpu.CompilerParams(vmem_limit_bytes=vmem * 1024 * 1024),
        cost_estimate=pl.CostEstimate(flops=flops, bytes_accessed=nbytes, transcendentals=0),
        **more,
    )(*operands)


def gathered(value, axis):
    return [value] + [exchange(value, axis, d) for d in range(1, lax.axis_size(axis))]


def halvings(axis):
    size = lax.axis_size(axis)
    return [size >> i for i in range(1, size.bit_length())]


def to_all(value):
    return lax.all_to_all(value, ("blk", "sub"), 0, 0, tiled=True)


def per_device(teacher, student):
    rows, t_width = teacher.shape
    s_width = student.shape[1]
    n_blk = lax.axis_size("blk")
    n_sub = lax.axis_size("sub")
    total_rows = float(rows * n_blk * n_sub)
    half = n_sub // 2
    side = rows * n_blk // 2
    f32 = functools.partial(jax.ShapeDtypeStruct, dtype=jnp.float32)

    teacher, student = (pltpu.with_memory_space_constraint(x, pltpu.HBM) for x in (teacher, student))
    packed = call(
        pack_kernel,
        jax.ShapeDtypeStruct((rows, t_width + s_width), teacher.dtype),
        (teacher, student),
        0,
        vmem=48,
        in_specs=[pl.BlockSpec(memory_space=pl.ANY)] * 2,
        scratch_shapes=[pltpu.SemaphoreType.DMA((2,))],
    )
    stats = call(
        functools.partial(stats_kernel, t_width),
        f32((1, t_width + s_width + LANES)),
        (packed,),
        4 * packed.size,
    )
    line = [packed, shifted(packed, "sub", 1)]
    tz = [exchange(stats, "sub", d) for d in range(1, n_sub)]
    line[1], *tz = lax.optimization_barrier((line[1], *tz))
    for _ in range(half - 1):
        line.append(shifted(line[-1], "sub", 1))
    stats = functools.reduce(jnp.add, [stats] + tz)
    tiles = [packed]
    for distance in halvings("blk"):
        if distance == 1:
            *tiles, line[1] = lax.optimization_barrier((*tiles, line[1]))
        else:
            stats = stats + exchange(stats, "blk", distance)
        tiles = tiles + [exchange(x, "blk", distance) for x in tiles]
    stats = [stats, exchange(stats, "blk", 1)]

    pair_flops = 2 * rows * rows * n_blk * (t_width + 3 * s_width)
    out_shape = (
        [f32((rows, s_width))] * half
        + [f32((2, side, s_width + LANES)), f32((2, 2, side, LANES))]
        + [f32((4, s_width)), f32((2, LANES))]
        + [jax.ShapeDtypeStruct((2, side, t_width + s_width), packed.dtype)]
    )
    *tiles, acc, norms, totals, early_sums, plane = call(
        functools.partial(early_kernel, n_blk, half, t_width, total_rows),
        out_shape,
        tiles + line[1:half] + stats,
        half * pair_flops,
    )
    own, backs = tiles[0], tiles[1:]
    returned = [shifted(x, "sub", -k) for k, x in enumerate(backs, 1)]
    given = [plane, line[half], totals, acc, norms]
    give, late_sums, visit_norms = call(
        functools.partial(late_kernel, 1, t_width),
        [f32((side, s_width)), f32((2, LANES)), f32((2, rows))],
        [*given, early_sums],
        pair_flops // 2,
    )
    keep, sums = call(
        functools.partial(late_kernel, 0, t_width),
        [f32((side, s_width)), f32((n_blk * n_sub, 1, LANES))],
        [*given, late_sums, visit_norms],
        pair_flops // 2,
    )
    got = exchange(give, "blk", 1)
    tiles, distance = n_blk // 2, 2
    while tiles > 1:
        tiles //= 2
        out_shape = [f32((rows * tiles, s_width))] * 2
        keep, give = call(
            functools.partial(halve_kernel, rows * tiles), out_shape, (keep, got), 2 * keep.size
        )
        got = exchange(give, "blk", distance)
        distance *= 2
    all_sums = to_all(sums)
    parts = [own, keep, got] + returned
    grad, loss = call(
        functools.partial(final_kernel, t_width, total_rows),
        [f32((rows, s_width)), f32((1, LANES))],
        [packed, totals, all_sums] + parts,
        8 * student.size,
    )
    return grad, loss[0, :1]


def solution(mesh):
    placed = P(("groups", "blk", "sub"), None)
    return jax.shard_map(
        per_device,
        mesh=mesh,
        in_specs=(placed, placed),
        out_specs=(placed, P("groups")),
        check_vma=False,
    )
```

```python
import functools

import jax
import jax.numpy as jnp
from jax import lax
from jax.experimental import pallas as pl
from jax.experimental.pallas import tpu as pltpu
from jax.sharding import PartitionSpec as P

FLOOR = 0.01
EPSILON = 1e-06
LANES = 128
CHUNK = 256
WHOLE = pl.BlockSpec(memory_space=pltpu.VMEM)


def exchange(value, axis, distance):
    size = lax.axis_size(axis)
    return lax.ppermute(value, axis, [(i, i ^ distance) for i in range(size)])


def shifted(value, axis, distance):
    size = lax.axis_size(axis)
    return lax.ppermute(value, axis, [(i, (i + distance) % size) for i in range(size)])


def pack_kernel(t_hbm, s_hbm, packed_ref, sems):
    t_width = t_hbm.shape[1]
    copies = [
        pltpu.make_async_copy(t_hbm, packed_ref.at[:, :t_width], sems.at[0]),
        pltpu.make_async_copy(s_hbm, packed_ref.at[:, t_width:], sems.at[1]),
    ]
    for copy in copies:
        copy.start()
    for copy in copies:
        copy.wait()


def stats_kernel(t_width, packed_ref, *refs):
    *given, stats_ref = refs
    value = packed_ref[...].astype(jnp.float32)
    squares = jnp.sum(value * value, axis=0, keepdims=True)
    square_t = jnp.sum(squares[:, :t_width], axis=1, keepdims=True)
    square_s = jnp.sum(squares[:, t_width:], axis=1, keepdims=True)
    lane = lax.broadcasted_iota(jnp.int32, (1, LANES), 1)
    width = value.shape[1]
    stats_ref[:, :width] = jnp.sum(value, axis=0, keepdims=True)
    stats_ref[:, width:] = jnp.where(lane == 0, square_t, jnp.where(lane == 1, square_s, 0.0))
    for ref in given:
        stats_ref[...] = stats_ref[...] + ref[...]


def spreads_of(stats, t_width, s_width, total_rows):
    centre_t = stats[:, :t_width] / total_rows
    centre_s = stats[:, t_width : t_width + s_width] / total_rows
    square_t = stats[:, t_width + s_width : t_width + s_width + 1]
    square_s = stats[:, t_width + s_width + 1 : t_width + s_width + 2]
    spread_t = (
        2.0 * (square_t / total_rows - jnp.sum(centre_t * centre_t, axis=1, keepdims=True)) + EPSILON
    )
    spread_s = (
        2.0 * (square_s / total_rows - jnp.sum(centre_s * centre_s, axis=1, keepdims=True)) + EPSILON
    )
    return spread_t, spread_s, centre_s


def norms_of(value):
    value = value.astype(jnp.float32)
    return jnp.sum(value * value, axis=1, keepdims=True)


def as_row(column):
    rows = column.shape[0]
    row = lax.broadcasted_iota(jnp.int32, (rows, rows), 0)
    same = row == lax.broadcasted_iota(jnp.int32, (rows, rows), 1)
    return jnp.sum(jnp.where(same, column, 0.0), axis=0, keepdims=True)


def with_ones(value):
    return jnp.concatenate([value, jnp.ones((value.shape[0], LANES), value.dtype)], axis=1)


def visiting(ref, t_width):
    t, s = ref[:, :t_width], ref[:, t_width:]
    return t, s, as_row(norms_of(t)), as_row(norms_of(s))


def pair_tile(c, v, inv_t, inv_s, own):
    (ct, cs, nct, ncs), (vt, vs, nvt, nvs) = c, v
    last = (((1,), (1,)), ((), ()))
    gram_t = lax.dot_general(ct, vt, last, preferred_element_type=jnp.float32)
    gram_s = lax.dot_general(cs, vs, last, preferred_element_type=jnp.float32)
    square_t = jnp.maximum(nct + nvt - 2.0 * gram_t, 0.0)
    square_s = jnp.maximum(ncs + nvs - 2.0 * gram_s, 0.0)
    under_t = square_t * inv_t + FLOOR
    under_s = square_s * inv_s + FLOOR
    inverse_s = lax.rsqrt(under_s)
    residue = under_s * inverse_s - under_t * lax.rsqrt(under_t)
    slope = jnp.clip(residue, -1.0, 1.0)
    huber = slope * (residue - 0.5 * slope)
    pull = slope * inverse_s
    if own:
        row = lax.broadcasted_iota(jnp.int32, pull.shape, 0)
        same = row == lax.broadcasted_iota(jnp.int32, pull.shape, 1)
        pull = jnp.where(same, 0.0, pull)
        huber = jnp.where(same, 0.0, huber)
    weights = (pull * inv_s).astype(jnp.bfloat16)
    return (
        weights,
        jnp.sum(huber, axis=0, keepdims=True),
        jnp.sum(pull * square_s, axis=0, keepdims=True),
    )


def direct_of(rows, summed):
    width = rows.shape[1]
    row_weight = jnp.concatenate([summed[:, width:]] * (width // LANES), axis=1)
    return rows.astype(jnp.float32) * row_weight - summed[:, :width]


def chunks_of(ref):
    for h in range(ref.shape[0]):
        for start in range(0, ref.shape[1], CHUNK):
            yield h, pl.ds(start, min(CHUNK, ref.shape[1] - start))


def early_kernel(n_blk, steps, t_width, total_rows, *refs):
    refs = list(refs)
    tiles = [refs.pop(0) for _ in range(n_blk)]
    line = [tiles[0]] + [refs.pop(0) for _ in range(steps - 1)]
    *stats_refs, own_ref = refs[: -4 - steps]
    back_refs = refs[-4 - steps : -5]
    acc_ref, norm_ref, total_ref, sums_ref, plane_ref = refs[-5:]
    rows = own_ref.shape[0]
    for d, ref in enumerate(tiles):
        start = d % (n_blk // 2) * rows
        plane_ref[d // (n_blk // 2), start : start + rows, :] = ref[...]
    s_width = own_ref.shape[1]
    stats = stats_refs[0][...]
    for ref in stats_refs[1:]:
        stats = stats + ref[...]
    spread_t, spread_s, centre_s = spreads_of(stats, t_width, s_width, total_rows)
    inv_t, inv_s = 1.0 / spread_t, 1.0 / spread_s
    for row, value in enumerate((inv_t, inv_s, spread_s)):
        total_ref[row : row + 1, :] = jnp.broadcast_to(value, (1, s_width))
    total_ref[3:4, :] = centre_s
    loss = jnp.zeros((1, LANES), jnp.float32)
    spread = jnp.zeros((1, LANES), jnp.float32)
    if steps == 1:
        acc_ref[...] = jnp.zeros_like(acc_ref)
    for h, at in chunks_of(plane_ref):
        norm_ref[h, 0, at, :] = jnp.broadcast_to(norms_of(plane_ref[h, at, :t_width]), (at.size, LANES))
        norm_ref[h, 1, at, :] = jnp.broadcast_to(norms_of(plane_ref[h, at, t_width:]), (at.size, LANES))
    for k, ref in enumerate(line):
        v = visiting(ref, t_width)
        factor = 1.0 if k == 0 else 2.0
        summed = None
        for h, at in chunks_of(plane_ref):
            cs = plane_ref[h, at, t_width:]
            c = (plane_ref[h, at, :t_width], cs, norm_ref[h, 0, at, :], norm_ref[h, 1, at, :])
            own = k == 0 and h == 0 and at.start == 0
            weights, loss_part, spread_part = pair_tile(c, v, inv_t, inv_s, own)
            loss = loss + factor * loss_part
            spread = spread + factor * spread_part
            term = lax.dot_general(
                weights,
                with_ones(cs),
                (((0,), (0,)), ((), ())),
                preferred_element_type=jnp.float32,
            )
            summed = term if summed is None else summed + term
            if k > 0:
                back = jnp.dot(weights, with_ones(v[1]), preferred_element_type=jnp.float32)
                acc_ref[h, at, :] = back if k == 1 else acc_ref[h, at, :] + back
        to_ref = own_ref if k == 0 else back_refs[k - 1]
        to_ref[...] = direct_of(v[1], summed)
    sums_ref[0:1, :] = loss
    sums_ref[1:2, :] = spread


def late_kernel(side, t_width, *refs):
    if side:
        plane_ref, ref, stats_ref, acc_ref, norm_ref, sums_in, out_ref, sums_ref, visit_ref = refs
        v = visiting(ref, t_width)
        visit_ref[0:1, :], visit_ref[1:2, :] = v[2:]
    else:
        plane_ref, ref, stats_ref, acc_ref, norm_ref, sums_in, visit_ref, out_ref, sums_ref = refs
        v = (ref[:, :t_width], ref[:, t_width:], visit_ref[0:1, :], visit_ref[1:2, :])
    inv_t, inv_s = stats_ref[0:1, :LANES], stats_ref[1:2, :LANES]
    loss = sums_in[0:1, :]
    spread = sums_in[1:2, :]
    for h, at in chunks_of(plane_ref):
        if h != side:
            continue
        cs = plane_ref[h, at, t_width:]
        c = (plane_ref[h, at, :t_width], cs, norm_ref[h, 0, at, :], norm_ref[h, 1, at, :])
        weights, loss_part, spread_part = pair_tile(c, v, inv_t, inv_s, False)
        loss = loss + loss_part
        spread = spread + spread_part
        back = jnp.dot(weights, with_ones(v[1]), preferred_element_type=jnp.float32)
        out_ref[at, :] = direct_of(cs, acc_ref[h, at, :] + back)
    if side:
        sums_ref[0:1, :] = loss
        sums_ref[1:2, :] = spread
    else:
        middle = LANES // 2
        folded = [row[:, :middle] + row[:, middle:] for row in (loss, spread)]
        row = jnp.concatenate(folded, axis=1)
        sums_ref[...] = jnp.broadcast_to(row[None], sums_ref.shape)


def halve_kernel(rows, keep_ref, got_ref, *out_refs):
    out_refs[0][...] = keep_ref[:rows, :] + got_ref[:rows, :]
    out_refs[1][...] = keep_ref[rows : 2 * rows, :] + got_ref[rows : 2 * rows, :]


def final_kernel(t_width, total_rows, packed_ref, stats_ref, sums_ref, *refs):
    *parts, grad_ref, loss_ref = refs
    direct = parts[0][...]
    for part in parts[1:]:
        direct = direct + part[...]
    both = jnp.sum(sums_ref[...], axis=0)
    loss_total = jnp.sum(both[:, : LANES // 2], axis=1, keepdims=True)
    spread_total = -jnp.sum(both[:, LANES // 2 :], axis=1, keepdims=True)
    spread_s, centre = stats_ref[2:3, :], stats_ref[3:4, :]
    pairs = total_rows * (total_rows - 1.0)
    correction = 2.0 * spread_total / (pairs * spread_s * spread_s)
    student = packed_ref[:, t_width:].astype(jnp.float32)
    grad_ref[...] = (2.0 / (total_rows - 1.0)) * direct + correction * (student - centre)
    loss_ref[...] = jnp.broadcast_to(loss_total / pairs, loss_ref.shape)


def call(kernel, out_shape, operands, flops, vmem=48, **more):
    nbytes = sum(x.size * x.dtype.itemsize for x in operands)
    in_specs = more.pop("in_specs", [WHOLE] * len(operands))
    out_specs = more.pop("out_specs", jax.tree.map(lambda _: WHOLE, out_shape))
    return pl.pallas_call(
        kernel,
        out_shape=out_shape,
        in_specs=in_specs,
        out_specs=out_specs,
        compiler_params=pltpu.CompilerParams(vmem_limit_bytes=vmem * 1024 * 1024),
        cost_estimate=pl.CostEstimate(flops=flops, bytes_accessed=nbytes, transcendentals=0),
        **more,
    )(*operands)


def gathered(value, axis):
    return [value] + [exchange(value, axis, d) for d in range(1, lax.axis_size(axis))]


def halvings(axis):
    size = lax.axis_size(axis)
    return [size >> i for i in range(1, size.bit_length())]


def to_all(value):
    return lax.all_to_all(value, ("blk", "sub"), 0, 0, tiled=True)


def per_device(teacher, student):
    rows, t_width = teacher.shape
    s_width = student.shape[1]
    n_blk = lax.axis_size("blk")
    n_sub = lax.axis_size("sub")
    total_rows = float(rows * n_blk * n_sub)
    half = n_sub // 2
    side = rows * n_blk // 2
    f32 = functools.partial(jax.ShapeDtypeStruct, dtype=jnp.float32)

    teacher, student = (pltpu.with_memory_space_constraint(x, pltpu.HBM) for x in (teacher, student))
    packed = call(
        pack_kernel,
        jax.ShapeDtypeStruct((rows, t_width + s_width), teacher.dtype),
        (teacher, student),
        0,
        vmem=48,
        in_specs=[pl.BlockSpec(memory_space=pl.ANY)] * 2,
        scratch_shapes=[pltpu.SemaphoreType.DMA((2,))],
    )
    stats = call(
        functools.partial(stats_kernel, t_width),
        f32((1, t_width + s_width + LANES)),
        (packed,),
        4 * packed.size,
    )
    line = [packed, shifted(packed, "sub", 1)]
    tz = [shifted(stats, "sub", d) for d in range(2, n_sub)]
    line[1], *tz = lax.optimization_barrier((line[1], *tz))
    for _ in range(half - 1):
        line.append(shifted(line[-1], "sub", 1))
    stats = call(
        functools.partial(stats_kernel, t_width),
        f32(stats.shape),
        (line[1], stats, *tz),
        4 * packed.size,
    )
    tiles = [packed]
    for distance in halvings("blk"):
        if distance == 1:
            *tiles, line[1] = lax.optimization_barrier((*tiles, line[1]))
        else:
            stats = stats + exchange(stats, "blk", distance)
        tiles = tiles + [exchange(x, "blk", distance) for x in tiles]
    stats = [stats, exchange(stats, "blk", 1)]

    pair_flops = 2 * rows * rows * n_blk * (t_width + 3 * s_width)
    out_shape = (
        [f32((rows, s_width))] * half
        + [f32((2, side, s_width + LANES)), f32((2, 2, side, LANES))]
        + [f32((4, s_width)), f32((2, LANES))]
        + [jax.ShapeDtypeStruct((2, side, t_width + s_width), packed.dtype)]
    )
    *tiles, acc, norms, totals, early_sums, plane = call(
        functools.partial(early_kernel, n_blk, half, t_width, total_rows),
        out_shape,
        tiles + line[1:half] + stats,
        half * pair_flops,
    )
    own, backs = tiles[0], tiles[1:]
    returned = [shifted(x, "sub", -k) for k, x in enumerate(backs, 1)]
    given = [plane, line[half], totals, acc, norms]
    give, late_sums, visit_norms = call(
        functools.partial(late_kernel, 1, t_width),
        [f32((side, s_width)), f32((2, LANES)), f32((2, rows))],
        [*given, early_sums],
        pair_flops // 2,
    )
    keep, sums = call(
        functools.partial(late_kernel, 0, t_width),
        [f32((side, s_width)), f32((n_blk * n_sub, 1, LANES))],
        [*given, late_sums, visit_norms],
        pair_flops // 2,
    )
    got = exchange(give, "blk", 1)
    tiles, distance = n_blk // 2, 2
    while tiles > 1:
        tiles //= 2
        out_shape = [f32((rows * tiles, s_width))] * 2
        keep, give = call(
            functools.partial(halve_kernel, rows * tiles), out_shape, (keep, got), 2 * keep.size
        )
        got = exchange(give, "blk", distance)
        distance *= 2
    all_sums = to_all(sums)
    parts = [own, keep, got] + returned
    grad, loss = call(
        functools.partial(final_kernel, t_width, total_rows),
        [f32((rows, s_width)), f32((1, LANES))],
        [packed, totals, all_sums] + parts,
        8 * student.size,
    )
    return grad, loss[0, :1]


def solution(mesh):
    placed = P(("groups", "blk", "sub"), None)
    return jax.shard_map(
        per_device,
        mesh=mesh,
        in_specs=(placed, placed),
        out_specs=(placed, P("groups")),
        check_vma=False,
    )
```
